32 devices in a mesh: groups: 2 (over x), band: 16 (over z, y, core).
Axes of the slice: x: 2, y: 2, z: 4, core: 2. Of those that a mesh axis runs over, the one named last changes fastest.
Arguments:
- grid_latent: bfloat16 [32768, 512], P(('groups', 'band')), parts along dimension 0, may hold values from -6 to 6
- mesh_latent: bfloat16 [8192, 512], P(('groups', 'band')), parts along dimension 0, may hold values from -6 to 6
- edge_latent: bfloat16 [49152, 512], P(('groups', 'band')), parts along dimension 0, may hold values from -6 to 6
- mesh_cot: bfloat16 [8192, 512], P(('groups', 'band')), parts along dimension 0, may hold values from -6 to 6
- send_rows: int32 [16, 128], P('band'), may hold values from 0 to 1023
- edge_slot: int32 [24576], P('band'), may hold values from 0 to 127, as said below
- edge_dst: int32 [24576], P('band'), may hold values from 0 to 255
- w_edge1: bfloat16 [1536, 512], replicated, may hold values from -0.15625 to 0.15625
- w_edge2: bfloat16 [512, 512], replicated, may hold values from -0.25 to 0.25
- w_node1: bfloat16 [1024, 512], replicated, may hold values from -0.1875 to 0.1875
- w_node2: bfloat16 [512, 512], replicated, may hold values from -0.25 to 0.25
Outputs:
- mesh_out: bfloat16 [8192, 512], P(('groups', 'band')), parts along dimension 0
- grid_grad: float32 [32768, 512], P(('groups', 'band')), parts along dimension 0
- grad_edge1: float32 [3072, 512], P('groups'), parts along dimension 0
- grad_edge2: float32 [1024, 512], P('groups'), parts along dimension 0
The draws below stay inside these ranges and needn't reach their ends.
There are 2 independent parts, one for each index of `groups`. The reference program is written for one: setup_inputs(seed, part) draws one part's arguments, and reference() takes and returns one part's arrays. A program takes and returns all parts, laid end to end along the dimension named above; an argument that names none is the same for every part. Nothing has to cross between parts.
Inputs may be any that keep to these rules, and one draw needn't show every extreme that they name: `edge_slot`: for edge e of owner o with slot q = b * 8 + s, slot s holds one of the rows that band b sends to owner o. Owners in the first and last eighth (the polar faces) may read any slot of any band; every other owner reads only from the bands within 16 // 4 of a band drawn for it, counted round the axis.
All inputs are finite; a program needn't handle non-finite values.
Results may differ from the reference program's by a relative error of at most 0.0066.
Values may be sent and summed in bfloat16 or wider, within the bound.
No kernel may reach another device: no remote copies, remote signals or barrier semaphores. Data moves between devices by JAX's collectives and lax.ppermute only.
A program may use at most 64 MiB of HBM per device.

```python
import jax
import jax.numpy as jnp

D = 512
H = 512
G_DEV = 1024
M_DEV = 256
E_DEV = 1536
CAP = 8
GRID = 16384
MESH = 4096
EDGES = 24576
N_BAND = 16


def draw_edge_slot(key, part):
    key = jax.random.fold_in(key, 7)
    center_key, offset_key, polar_key, count_key, slot_key = jax.random.split(key, 5)
    owner_index = jnp.arange(N_BAND, dtype=jnp.int32)
    polar_owner = (owner_index * 8 < N_BAND) | (owner_index * 8 >= 7 * N_BAND)
    reach = N_BAND // 4
    center = jax.random.randint(center_key, (N_BAND, 1), 0, N_BAND)
    offset = jax.random.randint(offset_key, (N_BAND, E_DEV), -reach, reach + 1)
    near_band = (center + offset + N_BAND) % N_BAND
    any_band = jax.random.randint(polar_key, (N_BAND, E_DEV), 0, N_BAND)
    source_band = jnp.where(polar_owner[:, None], any_band, near_band).astype(jnp.int32)
    fewer = jax.random.randint(count_key, (N_BAND, N_BAND), CAP // 2, CAP + 1)
    counts = jnp.where(polar_owner[:, None], CAP, fewer).astype(jnp.int32)
    limit = jnp.take_along_axis(counts, source_band, axis=1)
    slot_index = jax.random.randint(slot_key, (N_BAND, E_DEV), 0, limit)
    chosen = source_band * CAP + slot_index
    chosen = chosen.at[0, 0].set(0)
    chosen = chosen.at[0, E_DEV - 1].set(N_BAND * CAP - 1)
    return chosen.reshape(N_BAND * E_DEV).astype(jnp.int32)


def plant(drawn, key, least, top_value):
    spot = [jax.random.randint(jax.random.fold_in(key, axis), (), 0, length) for axis, length in enumerate(drawn.shape)]
    widest = drawn.shape.index(max(drawn.shape))
    next_to = spot[:widest] + [(spot[widest] + 1) % drawn.shape[widest]] + spot[widest + 1:]
    return drawn.at[tuple(spot)].set(least).at[tuple(next_to)].set(top_value)


def steps_of(own_key, dims, cuts, low, largest):
    def one(axis_at, blocks):
        steps = jax.random.uniform(jax.random.fold_in(jax.random.fold_in(own_key, 6), axis_at), (blocks,), jnp.float32, low / len(cuts), largest / len(cuts))
        return jnp.repeat(jnp.exp(steps), dims[axis_at] // blocks).reshape((-1,) + (1,) * (len(dims) - axis_at - 1))

    factor_of = one(*cuts[0])
    for cut in cuts[1:]:
        factor_of = factor_of * one(*cut)
    return factor_of


def scatter_about(rng, dims, spread, bound, cuts=(), kind=jnp.bfloat16):
    array = jax.random.normal(rng, dims, jnp.float32) * spread
    if len(cuts) > 0:
        array = steps_of(rng, dims, cuts, -0.22, 0.18) * array
    return jnp.clip(array, min=-bound, max=bound).astype(kind)


def setup_inputs(seed: int = 0, part: int = 0) -> dict:
    streams_of = jax.random.split(jax.random.key(seed), 12)
    own_keys = jax.random.split(jax.random.fold_in(streams_of[11], part), 12)
    grid_latent = scatter_about(own_keys[0], (GRID, D), 1.0, 6.0, ((0, 16),))
    mesh_latent = scatter_about(own_keys[1], (MESH, D), 1.0, 6.0, ((0, 16),))
    edge_latent = scatter_about(own_keys[2], (EDGES, D), 1.0, 6.0, ((0, 16),))
    mesh_cot = scatter_about(own_keys[3], (MESH, D), 1.0, 6.0, ((0, 16),))
    send_rows = plant(jax.random.randint(streams_of[4], (N_BAND, N_BAND * CAP), 0, G_DEV), jax.random.fold_in(streams_of[4], 1), 0, G_DEV - 1).astype(jnp.int32)
    edge_slot = draw_edge_slot(jax.random.fold_in(streams_of[11], 71), part)
    edge_dst = plant(jax.random.randint(streams_of[6], (EDGES,), 0, M_DEV), jax.random.fold_in(streams_of[6], 1), 0, M_DEV - 1).astype(jnp.int32)
    w_edge1 = scatter_about(streams_of[7], (3 * D, H), (3 * D) ** -0.5, 0.15625)
    w_edge2 = scatter_about(streams_of[8], (H, D), H ** -0.5, 0.25)
    w_node1 = scatter_about(streams_of[9], (2 * D, H), (2 * D) ** -0.5, 0.1875)
    w_node2 = scatter_about(streams_of[10], (H, D), H ** -0.5, 0.25)
    return {"grid_latent": grid_latent, "mesh_latent": mesh_latent, "edge_latent": edge_latent, "mesh_cot": mesh_cot, "send_rows": send_rows, "edge_slot": edge_slot, "edge_dst": edge_dst, "w_edge1": w_edge1, "w_edge2": w_edge2, "w_node1": w_node1, "w_node2": w_node2}


def silu_slope(value):
    sigma = jax.nn.sigmoid(value)
    return sigma * (1.0 + value * (1.0 - sigma))


def reference(grid_latent, mesh_latent, edge_latent, mesh_cot, send_rows, edge_slot, edge_dst, w_edge1, w_edge2, w_node1, w_node2):
    owner_index = (jnp.arange(EDGES, dtype=jnp.int32) // E_DEV).astype(jnp.int32)
    band_src = (edge_slot // CAP).astype(jnp.int32)
    slot_index = (edge_slot % CAP).astype(jnp.int32)
    local_row = send_rows[band_src, owner_index * CAP + slot_index]
    source = (band_src * G_DEV + local_row).astype(jnp.int32)
    target = (owner_index * M_DEV + edge_dst).astype(jnp.int32)
    inputs = jnp.concatenate([grid_latent[source], mesh_latent[target], edge_latent], axis=1)
    pre_edge = jnp.dot(inputs, w_edge1, preferred_element_type=jnp.float32)
    hidden = jax.nn.silu(pre_edge).astype(jnp.bfloat16)
    message = jnp.dot(hidden, w_edge2, preferred_element_type=jnp.float32).astype(jnp.bfloat16)
    received = jax.ops.segment_sum(message.astype(jnp.float32), target, num_segments=MESH).astype(jnp.bfloat16)
    node_in = jnp.concatenate([mesh_latent, received], axis=1)
    pre_node = jnp.dot(node_in, w_node1, preferred_element_type=jnp.float32)
    node_hidden = jax.nn.silu(pre_node).astype(jnp.bfloat16)
    mesh_out = (mesh_latent.astype(jnp.float32) + jnp.dot(node_hidden, w_node2, preferred_element_type=jnp.float32)).astype(jnp.bfloat16)
    d_pre_node = (jnp.dot(mesh_cot, w_node2.T, preferred_element_type=jnp.float32) * silu_slope(pre_node)).astype(jnp.bfloat16)
    d_received = jnp.dot(d_pre_node, w_node1[D:].T, preferred_element_type=jnp.float32)
    d_message = d_received[target].astype(jnp.bfloat16)
    d_pre_edge = (jnp.dot(d_message, w_edge2.T, preferred_element_type=jnp.float32) * silu_slope(pre_edge)).astype(jnp.bfloat16)
    grad_edge2 = jnp.dot(hidden.T, d_message, preferred_element_type=jnp.float32)
    grad_edge1 = jnp.dot(inputs.T, d_pre_edge, preferred_element_type=jnp.float32)
    d_gathered = jnp.dot(d_pre_edge, w_edge1[:D].T, preferred_element_type=jnp.float32)
    grid_grad = jax.ops.segment_sum(d_gathered, source, num_segments=GRID)
    return mesh_out, grid_grad, grad_edge1, grad_edge2
```

```python
import functools

import jax
import jax.numpy as jnp
from jax import lax
from jax.experimental import pallas as pl
from jax.experimental.pallas import tpu as pltpu
from jax.sharding import PartitionSpec as P

BF16 = jnp.bfloat16
F32 = jnp.float32
VMEM_LIMIT = 50 * 1024 * 1024


def dot_nn(a, b):
    return jnp.dot(a, b, preferred_element_type=F32)


def dot_tn(a, b):
    return lax.dot_general(a, b, (((0,), (0,)), ((), ())), preferred_element_type=F32)


def dot_nt(a, b):
    return lax.dot_general(a, b, (((1,), (1,)), ((), ())), preferred_element_type=F32)


def split(value):
    high = value.astype(BF16)
    low = (value - high.astype(F32)).astype(BF16)
    return high, low


def one_hot_rows(index_row, rows):
    shape = (rows, index_row.shape[1])
    hit = lax.broadcasted_iota(jnp.int32, shape, 0) == index_row
    return jnp.where(hit, 1.0, 0.0).astype(BF16)


def params():
    return pltpu.CompilerParams(vmem_limit_bytes=VMEM_LIMIT)


def cost(flops, nbytes):
    return pl.CostEstimate(flops=flops, bytes_accessed=nbytes, transcendentals=0)


def pick_kernel(rows_ref, grid_ref, out_ref):
    chosen = one_hot_rows(rows_ref[...], grid_ref.shape[0])
    out_ref[...] = dot_tn(chosen, grid_ref[...]).astype(BF16)


def put_kernel(rows_ref, back_ref, out_ref):
    chosen = one_hot_rows(rows_ref[...], out_ref.shape[0])
    out_ref[...] = dot_nn(chosen, back_ref[...])


def base_kernel(tile, dst_ref, mesh_ref, edge_ref, w1_ref, out_ref):
    width = mesh_ref.shape[1]
    mesh_rows = mesh_ref.shape[0]
    high, low = split(dot_nn(mesh_ref[...], w1_ref[width : 2 * width, :]))
    pair = jnp.concatenate([high, low], axis=0)

    def step(at, carry):
        rows = pl.ds(pl.multiple_of(at * tile, tile), tile)
        to_mesh = one_hot_rows(dst_ref[:, rows], mesh_rows)
        twice = jnp.concatenate([to_mesh, to_mesh], axis=0)
        out_ref[rows, :] = dot_nn(edge_ref[rows, :], w1_ref[2 * width :, :]) + dot_tn(twice, pair)
        return carry

    lax.fori_loop(0, edge_ref.shape[0] // tile, step, 0)


def main_kernel(
    tile,
    sizes,
    a_cols,
    slot_ref,
    dst_ref,
    slots_ref,
    base_ref,
    mesh_ref,
    edge_ref,
    cot_ref,
    w1_ref,
    w2_ref,
    wn1_ref,
    wn2_ref,
    mesh_out_ref,
    d_slots_ref,
    a_keep_ref,
    a_send_ref,
    b_keep_ref,
    b_send_ref,
    slope_ref,
    sums_ref,
    grads_ref,
):
    outer, inner = sizes
    width = mesh_ref.shape[1]
    mesh_rows = mesh_ref.shape[0]
    slot_rows = slots_ref.shape[0]
    tiles = edge_ref.shape[0] // tile
    me = lax.axis_index("band")
    my_core = me % 2
    my_inner = (me // 2) % inner
    my_outer = me // (2 * inner)

    high, low = split(dot_nn(slots_ref[...], w1_ref[:width, :]))
    slot_pair = jnp.concatenate([high, low], axis=0)
    sums_ref[...] = jnp.zeros_like(sums_ref)

    def forward(at, carry):
        rows = pl.ds(pl.multiple_of(at * tile, tile), tile)
        from_slot = one_hot_rows(slot_ref[:, rows], slot_rows)
        twice = jnp.concatenate([from_slot, from_slot], axis=0)
        pre = base_ref[rows, :] + dot_tn(twice, slot_pair)
        sigma = 0.5 + 0.5 * jnp.tanh(0.5 * pre)
        hidden = pre * sigma
        slope_ref[rows, :] = sigma + hidden * (1.0 - sigma)
        to_mesh = one_hot_rows(dst_ref[:, rows], mesh_rows)
        sums_ref[slot_rows:, :] += dot_nn(to_mesh, hidden.astype(BF16))
        return carry

    lax.fori_loop(0, tiles, forward, 0)

    hidden_high, hidden_low = split(sums_ref[slot_rows:, :])
    received = (dot_nn(hidden_high, w2_ref[...]) + dot_nn(hidden_low, w2_ref[...])).astype(BF16)
    mesh = mesh_ref[...]
    pre_node = dot_nn(mesh, wn1_ref[:width, :]) + dot_nn(received, wn1_ref[width:, :])
    sigma = 0.5 + 0.5 * jnp.tanh(0.5 * pre_node)
    node = pre_node * sigma
    mesh_out_ref[...] = (mesh.astype(F32) + dot_nn(node.astype(BF16), wn2_ref[...])).astype(BF16)
    slope = sigma + node * (1.0 - sigma)
    d_pre_node = (dot_nt(cot_ref[...], wn2_ref[...]) * slope).astype(BF16)
    d_received = dot_nt(d_pre_node, wn1_ref[width:, :]).astype(BF16)
    grads_ref[3 * width :, :] = dot_tn(hidden_high, d_received) + dot_tn(hidden_low, d_received)
    high, low = split(dot_nt(d_received, w2_ref[...]))
    back_pair = jnp.concatenate([high, low], axis=0)
    sums_ref[...] = jnp.zeros_like(sums_ref)
    grads_ref[2 * width : 3 * width, :] = jnp.zeros((width, grads_ref.shape[1]), F32)

    def backward(at, carry):
        rows = pl.ds(pl.multiple_of(at * tile, tile), tile)
        from_slot = one_hot_rows(slot_ref[:, rows], slot_rows)
        to_mesh = one_hot_rows(dst_ref[:, rows], mesh_rows)
        twice = jnp.concatenate([to_mesh, to_mesh], axis=0)
        d_pre = (dot_tn(twice, back_pair) * slope_ref[rows, :]).astype(BF16)
        both = jnp.concatenate([from_slot, to_mesh], axis=0)
        sums_ref[...] += dot_nn(both, d_pre)
        grads_ref[2 * width : 3 * width, :] += dot_tn(edge_ref[rows, :], d_pre)
        return carry

    lax.fori_loop(0, tiles, backward, 0)

    slot_high, slot_low = split(sums_ref[:slot_rows, :])
    d_slots = dot_nt(slot_high, w1_ref[:width, :]) + dot_nt(slot_low, w1_ref[:width, :])
    d_slots_ref[...] = d_slots.astype(BF16)
    slots = slots_ref[...]
    grads_ref[:width, :] = dot_tn(slots, slot_high) + dot_tn(slots, slot_low)
    mesh_high, mesh_low = split(sums_ref[slot_rows:, :])
    grads_ref[width : 2 * width, :] = dot_tn(mesh, mesh_high) + dot_tn(mesh, mesh_low)

    chunk = grads_ref.shape[0] // (2 * outer * inner)

    def spread(far_core, a_ref, b_ref):
        core = my_core ^ far_core

        def step(at, carry):
            far_inner, far_outer = at // outer, at % outer
            owner = ((my_outer ^ far_outer) * inner + (my_inner ^ far_inner)) * 2 + core
            rows = grads_ref[pl.ds(pl.multiple_of(owner * chunk, chunk), chunk), :].astype(BF16)
            a_ref[pl.ds(pl.multiple_of(at * chunk, chunk), chunk), :] = rows[:, :a_cols]
            other = far_outer * inner + far_inner
            b_ref[pl.ds(pl.multiple_of(other * chunk, chunk), chunk), :] = rows[:, a_cols:]
            return carry

        lax.fori_loop(0, outer * inner, step, 0)

    spread(1, a_send_ref, b_send_ref)
    spread(0, a_keep_ref, b_keep_ref)


def order_kernel(sizes, a_cols, a_ref, b_ref, first_ref, second_ref):
    outer, inner = sizes
    chunk = a_ref.shape[0] // (2 * outer * inner)
    me = lax.axis_index("band")
    my_core = me % 2
    my_inner = (me // 2) % inner
    my_outer = me // (2 * inner)
    first_chunks = first_ref.shape[0] // chunk

    def place(out_ref, start):
        def step(at, carry):
            owner = at + start
            far_core = my_core ^ (owner % 2)
            far_inner = my_inner ^ ((owner // 2) % inner)
            far_outer = my_outer ^ (owner // (2 * inner))
            a_at = (far_core * inner + far_inner) * outer + far_outer
            b_at = (far_core * outer + far_outer) * inner + far_inner
            rows = pl.ds(pl.multiple_of(at * chunk, chunk), chunk)
            a_rows = pl.ds(pl.multiple_of(a_at * chunk, chunk), chunk)
            b_rows = pl.ds(pl.multiple_of(b_at * chunk, chunk), chunk)
            out_ref[rows, :a_cols] = a_ref[a_rows, :].astype(F32)
            out_ref[rows, a_cols:] = b_ref[b_rows, :].astype(F32)
            return carry

        lax.fori_loop(0, out_ref.shape[0] // chunk, step, 0)

    place(first_ref, 0)
    place(second_ref, first_chunks)


def shards(
    sizes,
    grid_latent,
    mesh_latent,
    edge_latent,
    mesh_cot,
    send_rows,
    edge_slot,
    edge_dst,
    w_edge1,
    w_edge2,
    w_node1,
    w_node2,
):
    outer, inner = sizes
    band_count = lax.axis_size("band")
    width = grid_latent.shape[1]
    hidden_width = w_edge1.shape[1]
    edges = edge_latent.shape[0]
    mesh_rows = mesh_latent.shape[0]
    slot_rows = send_rows.shape[1]
    tile = 256
    a_cols = hidden_width * 3 // 4
    b_cols = hidden_width - a_cols
    slot_row = edge_slot.reshape(1, edges)
    dst_row = edge_dst.reshape(1, edges)

    def permute(value, stride, size, shift):
        pairs = []
        for source in range(band_count):
            place = (source // stride) % size
            pairs.append((source, source + ((place ^ shift) - place) * stride))
        return lax.ppermute(value, "band", pairs)

    outgoing = pl.pallas_call(
        pick_kernel,
        out_shape=jax.ShapeDtypeStruct((slot_rows, width), BF16),
        compiler_params=params(),
        name="pick",
    )(send_rows, grid_latent)
    slots = lax.all_to_all(
        outgoing.reshape(band_count, -1, width), "band", split_axis=0, concat_axis=0, tiled=True
    ).reshape(slot_rows, width)

    base = pl.pallas_call(
        functools.partial(base_kernel, tile),
        out_shape=jax.ShapeDtypeStruct((edges, hidden_width), F32),
        compiler_params=params(),
        cost_estimate=cost(2 * edges * width * hidden_width * 2, edges * width * 8),
        name="base",
    )(dst_row, mesh_latent, edge_latent, w_edge1)

    grad_rows = 3 * width + hidden_width
    half = grad_rows // 2
    mesh_out, d_slots, a_keep, a_send, b_keep, b_send = pl.pallas_call(
        functools.partial(main_kernel, tile, sizes, a_cols),
        out_shape=[
            jax.ShapeDtypeStruct((mesh_rows, width), BF16),
            jax.ShapeDtypeStruct((slot_rows, width), BF16),
            jax.ShapeDtypeStruct((half, a_cols), BF16),
            jax.ShapeDtypeStruct((half, a_cols), BF16),
            jax.ShapeDtypeStruct((half, b_cols), BF16),
            jax.ShapeDtypeStruct((half, b_cols), BF16),
        ],
        scratch_shapes=[
            pltpu.VMEM((edges, hidden_width), F32),
            pltpu.VMEM((slot_rows + mesh_rows, hidden_width), F32),
            pltpu.VMEM((grad_rows, hidden_width), F32),
        ],
        compiler_params=params(),
        name="edges",
    )(
        slot_row,
        dst_row,
        slots,
        base,
        mesh_latent,
        edge_latent,
        mesh_cot,
        w_edge1,
        w_edge2,
        w_node1,
        w_node2,
    )

    returned = lax.all_to_all(
        d_slots.reshape(band_count, -1, width), "band", split_axis=0, concat_axis=0, tiled=True
    ).reshape(slot_rows, width)
    grid_grad = pl.pallas_call(
        put_kernel,
        out_shape=jax.ShapeDtypeStruct(grid_latent.shape, F32),
        compiler_params=params(),
        name="put",
    )(send_rows, returned)

    def fold(value, stride, size):
        rows = value.shape[0] // size
        total = value[:rows].astype(F32)
        for shift in range(1, size):
            piece = value[shift * rows : (shift + 1) * rows]
            total = total + permute(piece, stride, size, shift).astype(F32)
        return total.astype(BF16)

    def unfold(value, stride, size):
        pieces = [value] + [permute(value, stride, size, shift) for shift in range(1, size)]
        return jnp.concatenate(pieces, axis=0)

    inner_at, outer_at = (2, inner), (2 * inner, outer)
    a_sum = (a_keep.astype(F32) + permute(a_send, 1, 2, 1).astype(F32)).astype(BF16)
    b_sum = (b_keep.astype(F32) + permute(b_send, 1, 2, 1).astype(F32)).astype(BF16)
    a_own = fold(fold(a_sum, *inner_at), *outer_at)
    b_own = fold(fold(b_sum, *outer_at), *inner_at)
    a_all = unfold(unfold(unfold(a_own, *outer_at), *inner_at), 1, 2)
    b_all = unfold(unfold(unfold(b_own, *inner_at), *outer_at), 1, 2)

    grad_edge1, grad_edge2 = pl.pallas_call(
        functools.partial(order_kernel, sizes, a_cols),
        out_shape=[
            jax.ShapeDtypeStruct((3 * width, hidden_width), F32),
            jax.ShapeDtypeStruct((hidden_width, width), F32),
        ],
        compiler_params=params(),
        name="order",
    )(a_all, b_all)
    return (mesh_out, grid_grad, grad_edge1, grad_edge2)


def solution(mesh):
    chips = mesh.shape["band"] // 2
    inner = 1
    while inner * inner * 4 <= chips:
        inner *= 2
    sizes = (chips // inner, inner)
    in_specs = (
        P(("groups", "band"), None),
        P(("groups", "band"), None),
        P(("groups", "band"), None),
        P(("groups", "band"), None),
        P("band", None),
        P("band"),
        P("band"),
        P(),
        P(),
        P(),
        P(),
    )
    out_specs = (
        P(("groups", "band"), None),
        P(("groups", "band"), None),
        P("groups", None),
        P("groups", None),
    )
    return jax.shard_map(
        functools.partial(shards, sizes), mesh=mesh, in_specs=in_specs, out_specs=out_specs, check_vma=False
    )
```

```python
import functools

import jax
import jax.numpy as jnp
from jax import lax
from jax.experimental import pallas as pl
from jax.experimental.pallas import tpu as pltpu
from jax.sharding import PartitionSpec as P

BF16 = jnp.bfloat16
F32 = jnp.float32
VMEM_LIMIT = 50 * 1024 * 1024


def dot_nn(a, b):
    return jnp.dot(a, b, preferred_element_type=F32)


def dot_tn(a, b):
    return lax.dot_general(a, b, (((0,), (0,)), ((), ())), preferred_element_type=F32)


def dot_nt(a, b):
    return lax.dot_general(a, b, (((1,), (1,)), ((), ())), preferred_element_type=F32)


def split(value):
    high = value.astype(BF16)
    low = (value - high.astype(F32)).astype(BF16)
    return high, low


def one_hot_rows(index_row, rows):
    shape = (rows, index_row.shape[1])
    hit = lax.broadcasted_iota(jnp.int32, shape, 0) == index_row
    return jnp.where(hit, 1.0, 0.0).astype(BF16)


def one_hot_columns(index_row, columns):
    lanes = index_row.shape[1]
    index = jnp.transpose(jnp.broadcast_to(index_row, (lanes, lanes)))
    pieces = []
    for start in range(0, columns, lanes):
        hit = lax.broadcasted_iota(jnp.int32, (lanes, lanes), 1) + start == index
        pieces.append(jnp.where(hit, 1.0, 0.0).astype(BF16))
    return pieces[0] if len(pieces) == 1 else jnp.concatenate(pieces, axis=1)


def tile_rows(index_ref, at, lines, rows):
    found = [one_hot_rows(index_ref[pl.ds(at * lines + k, 1), :], rows) for k in range(lines)]
    return jnp.concatenate(found, axis=1)


def tile_columns(index_ref, at, lines, columns):
    found = [one_hot_columns(index_ref[pl.ds(at * lines + k, 1), :], columns) for k in range(lines)]
    return jnp.concatenate(found, axis=0)


def place_of(sizes):
    outer, inner = sizes
    me = lax.axis_index("band")
    return me // (2 * inner), (me // 2) % inner, me % 2


def owner_at(sizes, far_outer, far_inner, far_core):
    my_outer, my_inner, my_core = place_of(sizes)
    return ((my_outer ^ far_outer) * sizes[1] + (my_inner ^ far_inner)) * 2 + (my_core ^ far_core)


def params():
    return pltpu.CompilerParams(vmem_limit_bytes=VMEM_LIMIT)


def cost(flops, nbytes):
    return pl.CostEstimate(flops=flops, bytes_accessed=nbytes, transcendentals=0)


def pick_kernel(rows_ref, grid_ref, out_ref):
    chosen = one_hot_rows(rows_ref[...], grid_ref.shape[0])
    out_ref[...] = dot_tn(chosen, grid_ref[...]).astype(BF16)


def put_kernel(sizes, rows_ref, back_ref, out_ref, ordered_ref):
    outer, inner = sizes
    cap = back_ref.shape[0] // (2 * outer * inner)
    back = back_ref[...].astype(F32)
    for at in range(2 * outer * inner):
        far_core, far_inner, far_outer = at % 2, at // 2 % inner, at // (2 * inner)
        owner = owner_at(sizes, far_outer, far_inner, far_core)
        ordered_ref[pl.ds(pl.multiple_of(owner * cap, cap), cap), :] = back[at * cap : (at + 1) * cap]
    chosen = one_hot_rows(rows_ref[...], out_ref.shape[0])
    out_ref[...] = dot_nn(chosen, ordered_ref[...].astype(BF16))


def base_kernel(
    lines,
    dst_ref,
    mesh_ref,
    edge_ref,
    cot_ref,
    w1_ref,
    wn1_ref,
    wn2_ref,
    base_ref,
    turned_ref,
    node_ref,
    cot_out_ref,
):
    width = mesh_ref.shape[1]
    mesh_rows = mesh_ref.shape[0]
    tile = lines * 128
    high, low = split(dot_nn(mesh_ref[...], w1_ref[width : 2 * width, :]))
    pair = jnp.concatenate([high, low], axis=0)

    def step(at, carry):
        rows = pl.ds(pl.multiple_of(at * tile, tile), tile)
        to_mesh = tile_columns(dst_ref, at, lines, mesh_rows)
        twice = jnp.concatenate([to_mesh, to_mesh], axis=1)
        edge = edge_ref[rows, :]
        base_ref[rows, :] = dot_nn(edge, w1_ref[2 * width :, :]) + dot_nn(twice, pair)
        turned_ref[:, rows] = jnp.transpose(edge)
        return carry

    lax.fori_loop(0, edge_ref.shape[0] // tile, step, 0)
    node_ref[...] = dot_nn(mesh_ref[...], wn1_ref[:width, :])
    cot_out_ref[...] = dot_nt(cot_ref[...], wn2_ref[...])


def main_kernel(
    lines,
    sizes,
    slot_ref,
    dst_ref,
    slots_ref,
    base_ref,
    turned_ref,
    mesh_ref,
    node_ref,
    cot_ref,
    w1_ref,
    w2_ref,
    wn1_ref,
    wn2_ref,
    *rest,
):
    outer, inner = sizes
    mesh_out_ref, d_slots_ref = rest[:2]
    send_refs, keep_refs = rest[2 : 2 + outer], rest[2 + outer : 2 + 2 * outer]
    slope_ref, value_ref, both_ref, grads_ref, slot_grads_ref, ordered_ref = rest[2 + 2 * outer :]
    width = mesh_ref.shape[1]
    mesh_rows = mesh_ref.shape[0]
    slot_rows = slots_ref.shape[0]
    tile = lines * 128
    tiles = base_ref.shape[0] // tile

    high, low = split(dot_nn(slots_ref[...], w1_ref[:width, :]))
    slot_pair = jnp.concatenate([high, low], axis=0)

    def forward(at, carry):
        rows = pl.ds(pl.multiple_of(at * tile, tile), tile)
        from_slot = tile_columns(slot_ref, at, lines, slot_rows)
        twice = jnp.concatenate([from_slot, from_slot], axis=1)
        pre = base_ref[rows, :] + dot_nn(twice, slot_pair)
        sigma = 0.5 + 0.5 * jnp.tanh(0.5 * pre)
        hidden = pre * sigma
        slope_ref[rows, :] = sigma + hidden * (1.0 - sigma)
        value_ref[rows, :] = hidden.astype(BF16)
        both_ref[:slot_rows, rows] = tile_rows(slot_ref, at, lines, slot_rows)
        both_ref[slot_rows:, rows] = tile_rows(dst_ref, at, lines, mesh_rows)
        return carry

    lax.fori_loop(0, tiles, forward, 0)

    hidden_high, hidden_low = split(dot_nn(both_ref[slot_rows:, :], value_ref[...]))
    received = (dot_nn(hidden_high, w2_ref[...]) + dot_nn(hidden_low, w2_ref[...])).astype(BF16)
    mesh = mesh_ref[...]
    pre_node = node_ref[...] + dot_nn(received, wn1_ref[width:, :])
    sigma = 0.5 + 0.5 * jnp.tanh(0.5 * pre_node)
    node = pre_node * sigma
    slope = sigma + node * (1.0 - sigma)
    d_pre_node = (cot_ref[...] * slope).astype(BF16)
    d_received = dot_nt(d_pre_node, wn1_ref[width:, :]).astype(BF16)
    high, low = split(dot_nt(d_received, w2_ref[...]))
    back_pair = jnp.concatenate([high, low], axis=0)

    def backward(at, carry):
        rows = pl.ds(pl.multiple_of(at * tile, tile), tile)
        to_mesh = tile_columns(dst_ref, at, lines, mesh_rows)
        twice = jnp.concatenate([to_mesh, to_mesh], axis=1)
        value_ref[rows, :] = (dot_nn(twice, back_pair) * slope_ref[rows, :]).astype(BF16)
        return carry

    lax.fori_loop(0, tiles, backward, 0)

    grads_ref[3 * width :, :] = dot_tn(hidden_high, d_received) + dot_tn(hidden_low, d_received)
    mesh_out_ref[...] = (mesh.astype(F32) + dot_nn(node.astype(BF16), wn2_ref[...])).astype(BF16)
    sums = dot_nn(both_ref[...], value_ref[...])
    slot_high, slot_low = split(sums[:slot_rows])
    slot_grads_ref[...] = dot_nt(slot_high, w1_ref[:width, :]) + dot_nt(slot_low, w1_ref[:width, :])
    slots = slots_ref[...]
    grads_ref[:width, :] = dot_tn(slots, slot_high) + dot_tn(slots, slot_low)
    mesh_high, mesh_low = split(sums[slot_rows:])
    grads_ref[width : 2 * width, :] = dot_tn(mesh, mesh_high) + dot_tn(mesh, mesh_low)
    grads_ref[2 * width : 3 * width, :] = dot_nn(turned_ref[...], value_ref[...])

    chunk = grads_ref.shape[0] // (2 * outer * inner)
    cap = slot_rows // (2 * outer * inner)
    for far_core in range(2):
        for far_inner in range(inner):
            for far_outer in range(outer):
                owner = owner_at(sizes, far_outer, far_inner, far_core)
                at = (far_core * inner + far_inner) * outer + far_outer
                from_rows = pl.ds(pl.multiple_of(owner * cap, cap), cap)
                ordered_ref[at * cap : (at + 1) * cap, :] = slot_grads_ref[from_rows, :]
                value = grads_ref[pl.ds(pl.multiple_of(owner * chunk, chunk), chunk), :]
                rows = slice(far_inner * chunk, (far_inner + 1) * chunk)
                if far_core:
                    send_refs[far_outer][rows, :] = value.astype(BF16)
                else:
                    keep_refs[far_outer][rows, :] = value
    d_slots_ref[...] = ordered_ref[...].astype(BF16)


def order_kernel(sizes, *refs):
    outer, inner = sizes
    first_ref, second_ref = refs[-2:]
    pieces = refs[:-2]
    chunk = pieces[0].shape[0]
    first_chunks = first_ref.shape[0] // chunk

    for at, piece in enumerate(pieces):
        far_outer, far_inner, far_core = at % outer, at // outer % inner, at // (outer * inner)
        owner = owner_at(sizes, far_outer, far_inner, far_core)
        value = piece[...].astype(F32)

        @pl.when(owner < first_chunks)
        def _():
            first_ref[pl.ds(pl.multiple_of(owner * chunk, chunk), chunk), :] = value

        @pl.when(owner >= first_chunks)
        def _():
            start = (owner - first_chunks) * chunk
            second_ref[pl.ds(pl.multiple_of(start, chunk), chunk), :] = value


def shards(
    sizes,
    grid_latent,
    mesh_latent,
    edge_latent,
    mesh_cot,
    send_rows,
    edge_slot,
    edge_dst,
    w_edge1,
    w_edge2,
    w_node1,
    w_node2,
):
    outer, inner = sizes
    band_count = lax.axis_size("band")
    width = grid_latent.shape[1]
    hidden_width = w_edge1.shape[1]
    edges = edge_latent.shape[0]
    mesh_rows = mesh_latent.shape[0]
    slot_rows = send_rows.shape[1]
    lines = 2
    slot_index = edge_slot.reshape(edges // 128, 128)
    dst_index = edge_dst.reshape(edges // 128, 128)

    def permute(value, stride, size, shift):
        pairs = []
        for source in range(band_count):
            place = (source // stride) % size
            pairs.append((source, source + ((place ^ shift) - place) * stride))
        return lax.ppermute(value, "band", pairs)

    def to_core(value):
        return permute(value, 1, 2, 1)

    def to_inner(value, shift):
        return permute(value, 2, inner, shift)

    def to_outer(value, shift):
        return permute(value, 2 * inner, outer, shift)

    outgoing = pl.pallas_call(
        pick_kernel,
        out_shape=jax.ShapeDtypeStruct((slot_rows, width), BF16),
        compiler_params=params(),
        name="pick",
    )(send_rows, grid_latent)
    slots = lax.all_to_all(
        outgoing.reshape(band_count, -1, width), "band", split_axis=0, concat_axis=0, tiled=True
    ).reshape(slot_rows, width)

    base, turned, node, cot = pl.pallas_call(
        functools.partial(base_kernel, lines),
        out_shape=[
            jax.ShapeDtypeStruct((edges, hidden_width), F32),
            jax.ShapeDtypeStruct((width, edges), BF16),
            jax.ShapeDtypeStruct((mesh_rows, hidden_width), F32),
            jax.ShapeDtypeStruct((mesh_rows, hidden_width), F32),
        ],
        compiler_params=params(),
        cost_estimate=cost(2 * edges * width * hidden_width * 2, edges * width * 8),
        name="base",
    )(dst_index, mesh_latent, edge_latent, mesh_cot, w_edge1, w_node1, w_node2)

    grad_rows = 3 * width + hidden_width
    chunk = grad_rows // band_count
    group = (inner * chunk, hidden_width)
    mesh_out, d_slots, *sides = pl.pallas_call(
        functools.partial(main_kernel, lines, sizes),
        out_shape=[
            jax.ShapeDtypeStruct((mesh_rows, width), BF16),
            jax.ShapeDtypeStruct((slot_rows, width), BF16),
        ]
        + [jax.ShapeDtypeStruct(group, BF16)] * outer
        + [jax.ShapeDtypeStruct(group, F32)] * outer,
        scratch_shapes=[
            pltpu.VMEM((edges, hidden_width), F32),
            pltpu.VMEM((edges, hidden_width), BF16),
            pltpu.VMEM((slot_rows + mesh_rows, edges), BF16),
            pltpu.VMEM((grad_rows, hidden_width), F32),
            pltpu.VMEM((slot_rows, width), F32),
            pltpu.VMEM((slot_rows, width), F32),
        ],
        compiler_params=params(),
        name="edges",
    )(
        slot_index,
        dst_index,
        slots,
        base,
        turned,
        mesh_latent,
        node,
        cot,
        w_edge1,
        w_edge2,
        w_node1,
        w_node2,
    )
    sends, keeps = sides[:outer], sides[outer:]

    own_sums = None
    arrived = []
    for far_outer in range(outer - 1, -1, -1):
        half = keeps[far_outer] + to_core(sends[far_outer]).astype(F32)
        total = half[:chunk]
        for far_inner in range(1, inner):
            part = half[far_inner * chunk : (far_inner + 1) * chunk].astype(BF16)
            total = total + to_inner(part, far_inner).astype(F32)
        if far_outer:
            arrived.append(to_outer(total.astype(BF16), far_outer))
        else:
            own_sums = total
    for value in arrived:
        own_sums = own_sums + value.astype(F32)
    own = own_sums.astype(BF16)

    pieces = [own] + [to_outer(own, far_outer) for far_outer in range(1, outer)]
    for far_inner in range(1, inner):
        pieces += [to_inner(value, far_inner) for value in pieces[:outer]]
    pieces += [to_core(value) for value in pieces]

    cap = slot_rows // band_count
    back = d_slots.reshape(2, inner, outer, cap, width)
    back = jnp.stack([back[0], to_core(back[1])], axis=2)
    back = jnp.stack([back[0]] + [to_inner(back[k], k) for k in range(1, inner)], axis=1)
    back = jnp.stack([back[0]] + [to_outer(back[k], k) for k in range(1, outer)], axis=0)
    grid_grad = pl.pallas_call(
        functools.partial(put_kernel, sizes),
        out_shape=jax.ShapeDtypeStruct(grid_latent.shape, F32),
        scratch_shapes=[pltpu.VMEM((slot_rows, width), F32)],
        compiler_params=params(),
        name="put",
    )(send_rows, back.reshape(slot_rows, width))

    grad_edge1, grad_edge2 = pl.pallas_call(
        functools.partial(order_kernel, sizes),
        out_shape=[
            jax.ShapeDtypeStruct((3 * width, hidden_width), F32),
            jax.ShapeDtypeStruct((hidden_width, width), F32),
        ],
        compiler_params=params(),
        name="order",
    )(*pieces)
    return (mesh_out, grid_grad, grad_edge1, grad_edge2)


def solution(mesh):
    chips = mesh.shape["band"] // 2
    inner = 1
    while inner * inner * 4 <= chips:
        inner *= 2
    sizes = (chips // inner, inner)
    in_specs = (
        P(("groups", "band"), None),
        P(("groups", "band"), None),
        P(("groups", "band"), None),
        P(("groups", "band"), None),
        P("band", None),
        P("band"),
        P("band"),
        P(),
        P(),
        P(),
        P(),
    )
    out_specs = (
        P(("groups", "band"), None),
        P(("groups", "band"), None),
        P("groups", None),
        P("groups", None),
    )
    return jax.shard_map(
        functools.partial(shards, sizes), mesh=mesh, in_specs=in_specs, out_specs=out_specs, check_vma=False
    )
```

```python
import functools

import jax
import jax.numpy as jnp
from jax import lax
from jax.experimental import pallas as pl
from jax.experimental.pallas import tpu as pltpu
from jax.sharding import PartitionSpec as P

BF16 = jnp.bfloat16
F32 = jnp.float32
MIB = 1024 * 1024


def dot_nn(a, b):
    return jnp.dot(a, b, preferred_element_type=F32)


def dot_tn(a, b):
    return lax.dot_general(a, b, (((0,), (0,)), ((), ())), preferred_element_type=F32)


def dot_nt(a, b):
    return lax.dot_general(a, b, (((1,), (1,)), ((), ())), preferred_element_type=F32)


def split(value):
    high = value.astype(BF16)
    low = (value - high.astype(F32)).astype(BF16)
    return high, low


def one_hot_rows(index_row, rows):
    shape = (rows, index_row.shape[1])
    hit = lax.broadcasted_iota(jnp.int32, shape, 0) == index_row
    return jnp.where(hit, 1.0, 0.0).astype(BF16)


def one_hot_columns(index_row, columns):
    lanes = index_row.shape[1]
    index = jnp.transpose(jnp.broadcast_to(index_row, (lanes, lanes)))
    pieces = []
    for start in range(0, columns, lanes):
        hit = lax.broadcasted_iota(jnp.int32, (lanes, lanes), 1) + start == index
        pieces.append(jnp.where(hit, 1.0, 0.0).astype(BF16))
    return pieces[0] if len(pieces) == 1 else jnp.concatenate(pieces, axis=1)


def tile_rows(index_ref, at, lines, rows):
    found = [one_hot_rows(index_ref[pl.ds(at * lines + k, 1), :], rows) for k in range(lines)]
    return jnp.concatenate(found, axis=1)


def tile_columns(index_ref, at, lines, columns):
    found = [one_hot_columns(index_ref[pl.ds(at * lines + k, 1), :], columns) for k in range(lines)]
    return jnp.concatenate(found, axis=0)


def place_of(sizes):
    outer, inner = sizes
    me = lax.axis_index("band")
    return me // (2 * inner), (me // 2) % inner, me % 2


def owner_at(sizes, far_outer, far_inner, far_core):
    my_outer, my_inner, my_core = place_of(sizes)
    return ((my_outer ^ far_outer) * sizes[1] + (my_inner ^ far_inner)) * 2 + (my_core ^ far_core)


def params(mib):
    return pltpu.CompilerParams(vmem_limit_bytes=mib * MIB)


def specs(space, count):
    return [pl.BlockSpec(memory_space=space)] * count


def cost(flops, nbytes):
    return pl.CostEstimate(flops=flops, bytes_accessed=nbytes, transcendentals=0)


def load(pairs, sems):
    copies = [pltpu.make_async_copy(source, target, sems.at[at]) for at, (source, target) in enumerate(pairs)]
    for copy in copies:
        copy.start()
    return copies


def pick_kernel(rows_hbm, grid_hbm, out_ref, rows_ref, grid_ref, sems):
    rows_copy, grid_copy = load([(rows_hbm, rows_ref), (grid_hbm, grid_ref)], sems)
    rows_copy.wait()
    picked = out_ref.shape[0]
    chosen = [one_hot_columns(rows_ref[:, at : at + 128], grid_ref.shape[0]) for at in range(0, picked, 128)]
    grid_copy.wait()
    for at, some in enumerate(chosen):
        out_ref[at * 128 : (at + 1) * 128, :] = dot_nn(some, grid_ref[...]).astype(BF16)


def put_kernel(sizes, rows_ref, back_ref, out_ref, ordered_ref):
    outer, inner = sizes
    cap = back_ref.shape[0] // (2 * outer * inner)
    back = back_ref[...].astype(F32)
    for at in range(2 * outer * inner):
        far_core, far_inner, far_outer = at % 2, at // 2 % inner, at // (2 * inner)
        owner = owner_at(sizes, far_outer, far_inner, far_core)
        ordered_ref[pl.ds(pl.multiple_of(owner * cap, cap), cap), :] = back[at * cap : (at + 1) * cap]
    chosen = one_hot_rows(rows_ref[...], out_ref.shape[0])
    out_ref[...] = dot_nn(chosen, ordered_ref[...].astype(BF16))


def base_kernel(
    lines,
    dst_hbm,
    mesh_hbm,
    edge_hbm,
    cot_hbm,
    w1_hbm,
    wn1_hbm,
    wn2_hbm,
    base_ref,
    turned_ref,
    hot_ref,
    node_ref,
    cot_out_ref,
    dst_ref,
    mesh_ref,
    edge_ref,
    cot_ref,
    w1_ref,
    wn1_ref,
    wn2_ref,
    sems,
):
    width = mesh_ref.shape[1]
    mesh_rows = mesh_ref.shape[0]
    tile = lines * 128
    tiles = edge_ref.shape[0] // tile
    pairs = [
        (dst_hbm, dst_ref),
        (mesh_hbm, mesh_ref),
        (w1_hbm.at[pl.ds(width, width), :], w1_ref.at[pl.ds(0, width), :]),
        (w1_hbm.at[pl.ds(2 * width, width), :], w1_ref.at[pl.ds(width, width), :]),
    ]
    pairs += [(edge_hbm.at[pl.ds(at * tile, tile), :], edge_ref.at[pl.ds(at * tile, tile), :]) for at in range(tiles)]
    pairs += [(wn1_hbm.at[pl.ds(0, width), :], wn1_ref), (cot_hbm, cot_ref), (wn2_hbm, wn2_ref)]
    copies = load(pairs, sems)
    same = lax.broadcasted_iota(jnp.int32, (256, 256), 0) == lax.broadcasted_iota(jnp.int32, (256, 256), 1)
    eye = jnp.where(same, 1.0, 0.0).astype(BF16)
    for copy in copies[:4]:
        copy.wait()
    moved = dot_nn(mesh_ref[...], w1_ref[:width, :]).astype(BF16)
    for at in range(tiles):
        rows = slice(at * tile, (at + 1) * tile)
        to_mesh = tile_columns(dst_ref, at, lines, mesh_rows)
        hot_ref[rows, :] = to_mesh
        copies[4 + at].wait()
        edge = edge_ref[rows, :]
        base_ref[rows, :] = dot_nn(edge, w1_ref[width:, :]) + dot_nn(to_mesh, moved)
        for start in range(0, width, 256):
            turned_ref[start : start + 256, rows] = dot_nt(eye, edge[:, start : start + 256]).astype(BF16)
    for copy in copies[4 + tiles :]:
        copy.wait()
    node_ref[...] = dot_nn(mesh_ref[...], wn1_ref[...])
    cot_out_ref[...] = dot_nt(cot_ref[...], wn2_ref[...])


def main_kernel(
    lines,
    sizes,
    slot_hbm,
    dst_hbm,
    mesh_hbm,
    w1_hbm,
    w2_hbm,
    wn1_hbm,
    wn2_hbm,
    slots_ref,
    base_ref,
    turned_ref,
    hot_ref,
    node_ref,
    cot_ref,
    *rest,
):
    outer, inner = sizes
    mesh_out_ref, d_slots_ref = rest[:2]
    send_refs, keep_refs = rest[2 : 2 + outer], rest[2 + outer : 2 + 2 * outer]
    slope_ref, value_ref, both_ref, grads_ref, slot_grads_ref, ordered_ref = rest[2 + 2 * outer : 8 + 2 * outer]
    slot_ref, dst_ref, mesh_ref, w1_ref, w2_ref, wn1_ref, wn2_ref, sems = rest[8 + 2 * outer :]
    width = mesh_ref.shape[1]
    mesh_rows = mesh_ref.shape[0]
    slot_rows = slots_ref.shape[0]
    tile = lines * 128
    tiles = base_ref.shape[0] // tile
    pairs = [
        (slot_hbm, slot_ref),
        (w1_hbm.at[pl.ds(0, width), :], w1_ref),
        (dst_hbm, dst_ref),
        (w2_hbm, w2_ref),
        (wn1_hbm.at[pl.ds(width, wn1_ref.shape[0]), :], wn1_ref),
        (mesh_hbm, mesh_ref),
        (wn2_hbm, wn2_ref),
    ]
    copies = load(pairs, sems)
    for copy in copies[:3]:
        copy.wait()

    slot_pair = jnp.concatenate(split(dot_nn(slots_ref[...], w1_ref[...])), axis=0)
    for at in range(tiles):
        rows = slice(at * tile, (at + 1) * tile)
        from_slot = tile_columns(slot_ref, at, lines, slot_rows)
        twice = jnp.concatenate([from_slot, from_slot], axis=1)
        pre = base_ref[rows, :] + dot_nn(twice, slot_pair)
        sigma = 0.5 + 0.5 * jnp.tanh(0.5 * pre)
        hidden = pre * sigma
        slope_ref[rows, :] = sigma + hidden * (1.0 - sigma)
        value_ref[rows, :] = hidden.astype(BF16)
        both_ref[:slot_rows, rows] = tile_rows(slot_ref, at, lines, slot_rows)
        both_ref[slot_rows:, rows] = tile_rows(dst_ref, at, lines, mesh_rows)

    for copy in copies[3:]:
        copy.wait()
    hidden_sums = dot_nn(both_ref[slot_rows:, :], value_ref[...]).astype(BF16)
    received = dot_nn(hidden_sums, w2_ref[...]).astype(BF16)
    mesh = mesh_ref[...]
    pre_node = node_ref[...] + dot_nn(received, wn1_ref[...])
    sigma = 0.5 + 0.5 * jnp.tanh(0.5 * pre_node)
    node = pre_node * sigma
    slope = sigma + node * (1.0 - sigma)
    d_pre_node = (cot_ref[...] * slope).astype(BF16)
    d_received = dot_nt(d_pre_node, wn1_ref[...]).astype(BF16)
    spread = dot_nt(d_received, w2_ref[...]).astype(BF16)

    for at in range(tiles):
        rows = slice(at * tile, (at + 1) * tile)
        value_ref[rows, :] = (dot_nn(hot_ref[rows, :], spread) * slope_ref[rows, :]).astype(BF16)

    grads_ref[3 * width :, :] = dot_tn(hidden_sums, d_received)
    mesh_out_ref[...] = (mesh.astype(F32) + dot_nn(node.astype(BF16), wn2_ref[...])).astype(BF16)
    sums = dot_nn(both_ref[...], value_ref[...]).astype(BF16)
    slot_grads_ref[...] = dot_nt(sums[:slot_rows], w1_ref[...])
    grads_ref[:width, :] = dot_tn(slots_ref[...], sums[:slot_rows])
    grads_ref[width : 2 * width, :] = dot_tn(mesh, sums[slot_rows:])
    grads_ref[2 * width : 3 * width, :] = dot_nn(turned_ref[...], value_ref[...])

    chunk = grads_ref.shape[0] // (2 * outer * inner)
    cap = slot_rows // (2 * outer * inner)
    for far_core in range(2):
        for far_inner in range(inner):
            for far_outer in range(outer):
                owner = owner_at(sizes, far_outer, far_inner, far_core)
                at = (far_core * inner + far_inner) * outer + far_outer
                from_rows = pl.ds(pl.multiple_of(owner * cap, cap), cap)
                ordered_ref[at * cap : (at + 1) * cap, :] = slot_grads_ref[from_rows, :]
                value = grads_ref[pl.ds(pl.multiple_of(owner * chunk, chunk), chunk), :]
                rows = slice(far_inner * chunk, (far_inner + 1) * chunk)
                if far_core:
                    send_refs[far_outer][rows, :] = value.astype(BF16)
                else:
                    keep_refs[far_outer][rows, :] = value
    d_slots_ref[...] = ordered_ref[...].astype(BF16)


def order_kernel(sizes, places, aliased, *refs):
    outer, inner = sizes
    pieces = refs[: len(places)]
    first_hbm, second_hbm, stage_ref, sems = refs[len(places) + aliased :]
    chunk = pieces[0].shape[0]
    first_chunks = first_hbm.shape[0] // chunk

    def send(k, target, start):
        rows = pl.ds(pl.multiple_of(start, chunk), chunk)
        return pltpu.make_async_copy(stage_ref.at[k], target.at[rows, :], sems.at[k])

    for k, (at, piece) in enumerate(zip(places, pieces)):
        owner = owner_at(sizes, at % outer, at // outer % inner, at // (outer * inner))
        stage_ref[k] = piece[...].astype(F32)

        @pl.when(owner < first_chunks)
        def _():
            send(k, first_hbm, owner * chunk).start()

        @pl.when(owner >= first_chunks)
        def _():
            send(k, second_hbm, (owner - first_chunks) * chunk).start()

    for k in range(len(places)):
        send(k, first_hbm, 0).wait()


def shards(
    sizes,
    grid_latent,
    mesh_latent,
    edge_latent,
    mesh_cot,
    send_rows,
    edge_slot,
    edge_dst,
    w_edge1,
    w_edge2,
    w_node1,
    w_node2,
):
    outer, inner = sizes
    band_count = lax.axis_size("band")
    width = grid_latent.shape[1]
    hidden_width = w_edge1.shape[1]
    edges = edge_latent.shape[0]
    mesh_rows = mesh_latent.shape[0]
    slot_rows = send_rows.shape[1]
    lines = 4
    slot_index = edge_slot.reshape(edges // 128, 128)
    dst_index = edge_dst.reshape(edges // 128, 128)

    def permute(value, stride, size, shift):
        pairs = []
        for source in range(band_count):
            place = (source // stride) % size
            pairs.append((source, source + ((place ^ shift) - place) * stride))
        return lax.ppermute(value, "band", pairs)

    def to_core(value):
        return permute(value, 1, 2, 1)

    def to_inner(value, shift):
        return permute(value, 2, inner, shift)

    def to_outer(value, shift):
        return permute(value, 2 * inner, outer, shift)

    outgoing = pl.pallas_call(
        pick_kernel,
        out_shape=jax.ShapeDtypeStruct((slot_rows, width), BF16),
        in_specs=specs(pltpu.HBM, 2),
        out_specs=pl.BlockSpec(memory_space=pltpu.VMEM),
        scratch_shapes=[
            pltpu.VMEM(send_rows.shape, jnp.int32),
            pltpu.VMEM(grid_latent.shape, BF16),
            pltpu.SemaphoreType.DMA((2,)),
        ],
        compiler_params=params(16),
        name="pick",
    )(send_rows, grid_latent)
    slots = lax.all_to_all(
        outgoing.reshape(band_count, -1, width), "band", split_axis=0, concat_axis=0, tiled=True
    ).reshape(slot_rows, width)

    base, turned, hot, node, cot = pl.pallas_call(
        functools.partial(base_kernel, lines),
        out_shape=[
            jax.ShapeDtypeStruct((edges, hidden_width), F32),
            jax.ShapeDtypeStruct((width, edges), BF16),
            jax.ShapeDtypeStruct((edges, mesh_rows), BF16),
            jax.ShapeDtypeStruct((mesh_rows, hidden_width), F32),
            jax.ShapeDtypeStruct((mesh_rows, hidden_width), F32),
        ],
        in_specs=specs(pltpu.HBM, 7),
        out_specs=specs(pltpu.VMEM, 5),
        scratch_shapes=[
            pltpu.VMEM(dst_index.shape, jnp.int32),
            pltpu.VMEM(mesh_latent.shape, BF16),
            pltpu.VMEM(edge_latent.shape, BF16),
            pltpu.VMEM(mesh_cot.shape, BF16),
            pltpu.VMEM((2 * width, hidden_width), BF16),
            pltpu.VMEM((width, hidden_width), BF16),
            pltpu.VMEM(w_node2.shape, BF16),
            pltpu.SemaphoreType.DMA((7 + edges // (128 * lines),)),
        ],
        compiler_params=params(20),
        cost_estimate=cost(2 * edges * width * hidden_width * 2, edges * width * 8),
        name="base",
    )(dst_index, mesh_latent, edge_latent, mesh_cot, w_edge1, w_node1, w_node2)

    grad_rows = 3 * width + hidden_width
    chunk = grad_rows // band_count
    group = (inner * chunk, hidden_width)
    mesh_out, d_slots, *sides = pl.pallas_call(
        functools.partial(main_kernel, lines, sizes),
        out_shape=[
            jax.ShapeDtypeStruct((mesh_rows, width), BF16),
            jax.ShapeDtypeStruct((slot_rows, width), BF16),
        ]
        + [jax.ShapeDtypeStruct(group, BF16)] * outer
        + [jax.ShapeDtypeStruct(group, F32)] * outer,
        in_specs=specs(pltpu.HBM, 7) + specs(pltpu.VMEM, 6),
        out_specs=specs(pltpu.VMEM, 2 + 2 * outer),
        scratch_shapes=[
            pltpu.VMEM((edges, hidden_width), F32),
            pltpu.VMEM((edges, hidden_width), BF16),
            pltpu.VMEM((slot_rows + mesh_rows, edges), BF16),
            pltpu.VMEM((grad_rows, hidden_width), F32),
            pltpu.VMEM((slot_rows, width), F32),
            pltpu.VMEM((slot_rows, width), F32),
            pltpu.VMEM(slot_index.shape, jnp.int32),
            pltpu.VMEM(dst_index.shape, jnp.int32),
            pltpu.VMEM(mesh_latent.shape, BF16),
            pltpu.VMEM((width, hidden_width), BF16),
            pltpu.VMEM(w_edge2.shape, BF16),
            pltpu.VMEM((w_node1.shape[0] - width, w_node1.shape[1]), BF16),
            pltpu.VMEM(w_node2.shape, BF16),
            pltpu.SemaphoreType.DMA((7,)),
        ],
        compiler_params=params(36),
        name="edges",
    )(
        slot_index,
        dst_index,
        mesh_latent,
        w_edge1,
        w_edge2,
        w_node1,
        w_node2,
        slots,
        base,
        turned,
        hot,
        node,
        cot,
    )
    sends, keeps = sides[:outer], sides[outer:]

    def after(value, *others):
        return lax.optimization_barrier((value, *others))[0]

    order = list(range(outer - 1, -1, -1))
    crossed = {order[0]: to_core(sends[order[0]])}
    for far_outer in order[1:]:
        crossed[far_outer] = to_core(after(sends[far_outer], crossed[order[0]]))
    own_sums = None
    arrived = []
    before = None
    for far_outer in order:
        half = keeps[far_outer] + crossed[far_outer].astype(F32)
        total = half[:chunk]
        received = []
        for far_inner in range(1, inner):
            part = half[far_inner * chunk : (far_inner + 1) * chunk].astype(BF16)
            if before is not None:
                part = after(part, *before)
            received.append(to_inner(part, far_inner))
        before = received
        for value in received:
            total = total + value.astype(F32)
        if far_outer:
            arrived.append(to_outer(total.astype(BF16), far_outer))
        else:
            own_sums = total
    for value in arrived:
        own_sums = own_sums + value.astype(F32)
    own = own_sums.astype(BF16)

    turns = []
    for step in range(1, outer // 2 + 1):
        turns += [outer - step] + [step] * (step != outer - step)
    fetched = {0: own}
    for at, far_outer in enumerate(turns):
        value = own if at < 2 else after(own, fetched[turns[at - 2]])
        fetched[far_outer] = to_outer(value, far_outer)
    pieces = [fetched[far_outer] for far_outer in range(outer)]
    for far_inner in range(1, inner):
        pieces += [to_inner(value, far_inner) for value in pieces[:outer]]
    pieces += [to_core(value) for value in pieces]

    cap = slot_rows // band_count
    back = d_slots.reshape(2, inner, outer, cap, width)
    back = jnp.stack([back[0], to_core(back[1])], axis=2)
    back = jnp.stack([back[0]] + [to_inner(back[k], k) for k in range(1, inner)], axis=1)
    back = jnp.stack([back[0]] + [to_outer(back[k], k) for k in range(1, outer)], axis=0)
    grid_grad = pl.pallas_call(
        functools.partial(put_kernel, sizes),
        out_shape=jax.ShapeDtypeStruct(grid_latent.shape, F32),
        scratch_shapes=[pltpu.VMEM((slot_rows, width), F32)],
        compiler_params=params(16),
        name="put",
    )(send_rows, back.reshape(slot_rows, width))

    late = [at for at in range(band_count) if at % outer == turns[-1]]
    early = [at for at in range(band_count) if at % outer != turns[-1]]
    grads = []
    for places in (early, late):
        grads = pl.pallas_call(
            functools.partial(order_kernel, sizes, places, len(grads)),
            out_shape=[
                jax.ShapeDtypeStruct((3 * width, hidden_width), F32),
                jax.ShapeDtypeStruct((hidden_width, width), F32),
            ],
            in_specs=specs(pltpu.VMEM, len(places)) + specs(pltpu.HBM, len(grads)),
            out_specs=specs(pltpu.HBM, 2),
            scratch_shapes=[
                pltpu.VMEM((len(places), chunk, hidden_width), F32),
                pltpu.SemaphoreType.DMA((len(places),)),
            ],
            input_output_aliases={len(places) + k: k for k in range(len(grads))},
            compiler_params=params(16),
            name="order",
        )(*[pieces[at] for at in places], *grads)
    grad_edge1, grad_edge2 = grads
    return (mesh_out, grid_grad, grad_edge1, grad_edge2)


def solution(mesh):
    chips = mesh.shape["band"] // 2
    inner = 1
    while inner * inner * 4 <= chips:
        inner *= 2
    sizes = (chips // inner, inner)
    in_specs = (
        P(("groups", "band"), None),
        P(("groups", "band"), None),
        P(("groups", "band"), None),
        P(("groups", "band"), None),
        P("band", None),
        P("band"),
        P("band"),
        P(),
        P(),
        P(),
        P(),
    )
    out_specs = (
        P(("groups", "band"), None),
        P(("groups", "band"), None),
        P("groups", None),
        P("groups", None),
    )
    return jax.shard_map(
        functools.partial(shards, sizes), mesh=mesh, in_specs=in_specs, out_specs=out_specs, check_vma=False
    )
```

```python
import functools

import jax
import jax.numpy as jnp
from jax import lax
from jax.experimental import pallas as pl
from jax.experimental.pallas import tpu as pltpu
from jax.sharding import PartitionSpec as P

BF16 = jnp.bfloat16
F32 = jnp.float32
MIB = 1024 * 1024


def dot_nn(a, b):
    return jnp.dot(a, b, preferred_element_type=F32)


def dot_tn(a, b):
    return lax.dot_general(a, b, (((0,), (0,)), ((), ())), preferred_element_type=F32)


def dot_nt(a, b):
    return lax.dot_general(a, b, (((1,), (1,)), ((), ())), preferred_element_type=F32)


def split(value):
    high = value.astype(BF16)
    low = (value - high.astype(F32)).astype(BF16)
    return high, low


def one_hot_rows(index_row, rows):
    shape = (rows, index_row.shape[1])
    hit = lax.broadcasted_iota(jnp.int32, shape, 0) == index_row
    return jnp.where(hit, 1.0, 0.0).astype(BF16)


def one_hot_columns(index_row, columns):
    lanes = index_row.shape[1]
    index = jnp.transpose(jnp.broadcast_to(index_row, (lanes, lanes)))
    pieces = []
    for start in range(0, columns, lanes):
        hit = lax.broadcasted_iota(jnp.int32, (lanes, lanes), 1) + start == index
        pieces.append(jnp.where(hit, 1.0, 0.0).astype(BF16))
    return pieces[0] if len(pieces) == 1 else jnp.concatenate(pieces, axis=1)


def tile_rows(index_ref, at, lines, rows):
    found = [one_hot_rows(index_ref[pl.ds(at * lines + k, 1), :], rows) for k in range(lines)]
    return jnp.concatenate(found, axis=1)


def tile_columns(index_ref, at, lines, columns):
    found = [one_hot_columns(index_ref[pl.ds(at * lines + k, 1), :], columns) for k in range(lines)]
    return jnp.concatenate(found, axis=0)


def place_of(sizes):
    outer, inner = sizes
    me = lax.axis_index("band")
    return me // (2 * inner), (me // 2) % inner, me % 2


def owner_at(sizes, far_outer, far_inner, far_core):
    my_outer, my_inner, my_core = place_of(sizes)
    return ((my_outer ^ far_outer) * sizes[1] + (my_inner ^ far_inner)) * 2 + (my_core ^ far_core)


def params(mib):
    return pltpu.CompilerParams(vmem_limit_bytes=mib * MIB)


def pinned(space, *values):
    return [pltpu.with_memory_space_constraint(value, space) for value in values]


def specs(space, count):
    return [pl.BlockSpec(memory_space=space)] * count


def cost(flops, nbytes):
    return pl.CostEstimate(flops=flops, bytes_accessed=nbytes, transcendentals=0)


def load(pairs, sems):
    copies = [pltpu.make_async_copy(source, target, sems.at[at]) for at, (source, target) in enumerate(pairs)]
    for copy in copies:
        copy.start()
    return copies


def pick_kernel(rows_hbm, grid_hbm, out_ref, rows_ref, grid_ref, sems):
    rows_copy, grid_copy = load([(rows_hbm, rows_ref), (grid_hbm, grid_ref)], sems)
    rows_copy.wait()
    picked = out_ref.shape[0]
    chosen = [one_hot_columns(rows_ref[:, at : at + 128], grid_ref.shape[0]) for at in range(0, picked, 128)]
    grid_copy.wait()
    for at, some in enumerate(chosen):
        out_ref[at * 128 : (at + 1) * 128, :] = dot_nn(some, grid_ref[...]).astype(BF16)


def put_kernel(sizes, rows_hbm, back_ref, out_ref, ordered_ref, rows_ref, sems):
    outer, inner = sizes
    (copy,) = load([(rows_hbm, rows_ref)], sems)
    cap = back_ref.shape[0] // (2 * outer * inner)
    back = back_ref[...].astype(F32)
    for at in range(2 * outer * inner):
        far_core, far_inner, far_outer = at % 2, at // 2 % inner, at // (2 * inner)
        owner = owner_at(sizes, far_outer, far_inner, far_core)
        ordered_ref[pl.ds(pl.multiple_of(owner * cap, cap), cap), :] = back[at * cap : (at + 1) * cap]
    copy.wait()
    chosen = one_hot_rows(rows_ref[...], out_ref.shape[0])
    out_ref[...] = dot_nn(chosen, ordered_ref[...].astype(BF16))


def base_kernel(
    lines,
    dst_hbm,
    mesh_hbm,
    edge_hbm,
    cot_hbm,
    w1_hbm,
    wn1_hbm,
    wn2_hbm,
    base_ref,
    turned_ref,
    hot_ref,
    node_ref,
    cot_out_ref,
    dst_ref,
    mesh_ref,
    edge_ref,
    cot_ref,
    w1_ref,
    wn1_ref,
    wn2_ref,
    sems,
):
    width = mesh_ref.shape[1]
    mesh_rows = mesh_ref.shape[0]
    tile = lines * 128
    tiles = edge_ref.shape[0] // tile
    pairs = [
        (dst_hbm, dst_ref),
        (mesh_hbm, mesh_ref),
        (w1_hbm.at[pl.ds(width, width), :], w1_ref.at[pl.ds(0, width), :]),
        (w1_hbm.at[pl.ds(2 * width, width), :], w1_ref.at[pl.ds(width, width), :]),
    ]
    pairs += [(edge_hbm.at[pl.ds(at * tile, tile), :], edge_ref.at[pl.ds(at * tile, tile), :]) for at in range(tiles)]
    pairs += [(wn1_hbm.at[pl.ds(0, width), :], wn1_ref), (cot_hbm, cot_ref), (wn2_hbm, wn2_ref)]
    copies = load(pairs, sems)
    same = lax.broadcasted_iota(jnp.int32, (256, 256), 0) == lax.broadcasted_iota(jnp.int32, (256, 256), 1)
    eye = jnp.where(same, 1.0, 0.0).astype(BF16)
    for copy in copies[:4]:
        copy.wait()
    moved = dot_nn(mesh_ref[...], w1_ref[:width, :]).astype(BF16)
    for at in range(tiles):
        rows = slice(at * tile, (at + 1) * tile)
        to_mesh = tile_columns(dst_ref, at, lines, mesh_rows)
        hot_ref[rows, :] = to_mesh
        copies[4 + at].wait()
        edge = edge_ref[rows, :]
        base_ref[rows, :] = dot_nn(edge, w1_ref[width:, :]) + dot_nn(to_mesh, moved)
        for start in range(0, width, 256):
            turned_ref[start : start + 256, rows] = dot_nt(eye, edge[:, start : start + 256]).astype(BF16)
    for copy in copies[4 + tiles :]:
        copy.wait()
    node_ref[...] = dot_nn(mesh_ref[...], wn1_ref[...])
    cot_out_ref[...] = dot_nt(cot_ref[...], wn2_ref[...])


def main_kernel(
    lines,
    sizes,
    slot_hbm,
    dst_hbm,
    mesh_hbm,
    w1_hbm,
    w2_hbm,
    wn1_hbm,
    wn2_hbm,
    slots_ref,
    base_ref,
    turned_ref,
    hot_ref,
    node_ref,
    cot_ref,
    *rest,
):
    outer, inner = sizes
    mesh_out_ref, d_slots_ref = rest[:2]
    send_refs, keep_refs = rest[2:4], rest[4:6]
    slope_ref, value_ref, both_ref, grads_ref, slot_grads_ref, ordered_ref = rest[6:12]
    slot_ref, dst_ref, mesh_ref, w1_ref, w2_ref, wn1_ref, wn2_ref, sems = rest[12:]
    width = mesh_ref.shape[1]
    mesh_rows = mesh_ref.shape[0]
    slot_rows = slots_ref.shape[0]
    tile = lines * 128
    tiles = base_ref.shape[0] // tile
    pairs = [
        (slot_hbm, slot_ref),
        (w1_hbm.at[pl.ds(0, width), :], w1_ref),
        (dst_hbm, dst_ref),
        (w2_hbm, w2_ref),
        (wn1_hbm.at[pl.ds(width, wn1_ref.shape[0]), :], wn1_ref),
        (mesh_hbm, mesh_ref),
        (wn2_hbm, wn2_ref),
    ]
    copies = load(pairs, sems)
    for copy in copies[:3]:
        copy.wait()

    slot_pair = jnp.concatenate(split(dot_nn(slots_ref[...], w1_ref[...])), axis=0)
    for at in range(tiles):
        rows = slice(at * tile, (at + 1) * tile)
        from_slot = tile_columns(slot_ref, at, lines, slot_rows)
        twice = jnp.concatenate([from_slot, from_slot], axis=1)
        pre = base_ref[rows, :] + dot_nn(twice, slot_pair)
        sigma = 0.5 + 0.5 * jnp.tanh(0.5 * pre)
        hidden = pre * sigma
        slope_ref[rows, :] = sigma + hidden * (1.0 - sigma)
        value_ref[rows, :] = hidden.astype(BF16)
        both_ref[:slot_rows, rows] = tile_rows(slot_ref, at, lines, slot_rows)
        both_ref[slot_rows:, rows] = tile_rows(dst_ref, at, lines, mesh_rows)

    for copy in copies[3:]:
        copy.wait()
    hidden_sums = dot_nn(both_ref[slot_rows:, :], value_ref[...]).astype(BF16)
    received = dot_nn(hidden_sums, w2_ref[...]).astype(BF16)
    mesh = mesh_ref[...]
    pre_node = node_ref[...] + dot_nn(received, wn1_ref[...])
    sigma = 0.5 + 0.5 * jnp.tanh(0.5 * pre_node)
    node = pre_node * sigma
    slope = sigma + node * (1.0 - sigma)
    d_pre_node = (cot_ref[...] * slope).astype(BF16)
    d_received = dot_nt(d_pre_node, wn1_ref[...]).astype(BF16)
    spread = dot_nt(d_received, w2_ref[...]).astype(BF16)

    for at in range(tiles):
        rows = slice(at * tile, (at + 1) * tile)
        value_ref[rows, :] = (dot_nn(hot_ref[rows, :], spread) * slope_ref[rows, :]).astype(BF16)

    grads_ref[3 * width :, :] = dot_tn(hidden_sums, d_received)
    mesh_out_ref[...] = (mesh.astype(F32) + dot_nn(node.astype(BF16), wn2_ref[...])).astype(BF16)
    sums = dot_nn(both_ref[...], value_ref[...]).astype(BF16)
    slot_grads_ref[...] = dot_nt(sums[:slot_rows], w1_ref[...])
    grads_ref[:width, :] = dot_tn(slots_ref[...], sums[:slot_rows])
    grads_ref[width : 2 * width, :] = dot_tn(mesh, sums[slot_rows:])
    grads_ref[2 * width : 3 * width, :] = dot_nn(turned_ref[...], value_ref[...])

    chunk = grads_ref.shape[0] // (2 * outer * inner)
    cap = slot_rows // (2 * outer * inner)
    for far_core in range(2):
        for far_inner in range(inner):
            for far_outer in range(outer):
                owner = owner_at(sizes, far_outer, far_inner, far_core)
                at = (far_core * inner + far_inner) * outer + far_outer
                from_rows = pl.ds(pl.multiple_of(owner * cap, cap), cap)
                ordered_ref[at * cap : (at + 1) * cap, :] = slot_grads_ref[from_rows, :]
                value = grads_ref[pl.ds(pl.multiple_of(owner * chunk, chunk), chunk), :]
                group = 0 if far_outer >= outer // 2 else 1
                line = far_inner * (outer // 2) + far_outer % (outer // 2)
                rows = slice(line * chunk, (line + 1) * chunk)
                if far_core:
                    send_refs[group][rows, :] = value.astype(BF16)
                else:
                    keep_refs[group][rows, :] = value
    d_slots_ref[...] = ordered_ref[...].astype(BF16)


def order_kernel(sizes, places, aliased, *refs):
    outer, inner = sizes
    pieces = refs[: len(places)]
    first_hbm, second_hbm, stage_ref, sems = refs[len(places) + aliased :]
    chunk = pieces[0].shape[0]
    first_chunks = first_hbm.shape[0] // chunk

    def send(k, target, start):
        rows = pl.ds(pl.multiple_of(start, chunk), chunk)
        return pltpu.make_async_copy(stage_ref.at[k], target.at[rows, :], sems.at[k])

    for k, (at, piece) in enumerate(zip(places, pieces)):
        owner = owner_at(sizes, at % outer, at // outer % inner, at // (outer * inner))
        stage_ref[k] = piece[...].astype(F32)

        @pl.when(owner < first_chunks)
        def _():
            send(k, first_hbm, owner * chunk).start()

        @pl.when(owner >= first_chunks)
        def _():
            send(k, second_hbm, (owner - first_chunks) * chunk).start()

    for k in range(len(places)):
        send(k, first_hbm, 0).wait()


def shards(
    sizes,
    grid_latent,
    mesh_latent,
    edge_latent,
    mesh_cot,
    send_rows,
    edge_slot,
    edge_dst,
    w_edge1,
    w_edge2,
    w_node1,
    w_node2,
):
    outer, inner = sizes
    band_count = lax.axis_size("band")
    width = grid_latent.shape[1]
    hidden_width = w_edge1.shape[1]
    edges = edge_latent.shape[0]
    mesh_rows = mesh_latent.shape[0]
    slot_rows = send_rows.shape[1]
    lines = 4
    slot_index = edge_slot.reshape(edges // 128, 128)
    dst_index = edge_dst.reshape(edges // 128, 128)

    def permute(value, stride, size, shift):
        pairs = []
        for source in range(band_count):
            place = (source // stride) % size
            pairs.append((source, source + ((place ^ shift) - place) * stride))
        return lax.ppermute(value, "band", pairs)

    def to_core(value):
        return permute(value, 1, 2, 1)

    def to_inner(value, shift):
        return permute(value, 2, inner, shift)

    def to_outer(value, shift):
        return permute(value, 2 * inner, outer, shift)

    outgoing = pl.pallas_call(
        pick_kernel,
        out_shape=jax.ShapeDtypeStruct((slot_rows, width), BF16),
        in_specs=specs(pltpu.HBM, 2),
        out_specs=pl.BlockSpec(memory_space=pltpu.VMEM),
        scratch_shapes=[
            pltpu.VMEM(send_rows.shape, jnp.int32),
            pltpu.VMEM(grid_latent.shape, BF16),
            pltpu.SemaphoreType.DMA((2,)),
        ],
        compiler_params=params(16),
        name="pick",
    )(*pinned(pltpu.HBM, send_rows, grid_latent))
    slots = lax.all_to_all(
        outgoing.reshape(band_count, -1, width), "band", split_axis=0, concat_axis=0, tiled=True
    ).reshape(slot_rows, width)

    base, turned, hot, node, cot = pl.pallas_call(
        functools.partial(base_kernel, lines),
        out_shape=[
            pltpu.VMEM((edges, hidden_width), F32),
            pltpu.VMEM((width, edges), BF16),
            pltpu.VMEM((edges, mesh_rows), BF16),
            pltpu.VMEM((mesh_rows, hidden_width), F32),
            pltpu.VMEM((mesh_rows, hidden_width), F32),
        ],
        in_specs=specs(pltpu.HBM, 7),
        out_specs=specs(pltpu.VMEM, 5),
        scratch_shapes=[
            pltpu.VMEM(dst_index.shape, jnp.int32),
            pltpu.VMEM(mesh_latent.shape, BF16),
            pltpu.VMEM(edge_latent.shape, BF16),
            pltpu.VMEM(mesh_cot.shape, BF16),
            pltpu.VMEM((2 * width, hidden_width), BF16),
            pltpu.VMEM((width, hidden_width), BF16),
            pltpu.VMEM(w_node2.shape, BF16),
            pltpu.SemaphoreType.DMA((7 + edges // (128 * lines),)),
        ],
        compiler_params=params(20),
        cost_estimate=cost(2 * edges * width * hidden_width * 2, edges * width * 8),
        name="base",
    )(*pinned(pltpu.HBM, dst_index, mesh_latent, edge_latent, mesh_cot, w_edge1, w_node1, w_node2))

    grad_rows = 3 * width + hidden_width
    chunk = grad_rows // band_count
    group = (band_count // 4 * chunk, hidden_width)
    mesh_out, d_slots, *sides = pl.pallas_call(
        functools.partial(main_kernel, lines, sizes),
        out_shape=[
            jax.ShapeDtypeStruct((mesh_rows, width), BF16),
            jax.ShapeDtypeStruct((slot_rows, width), BF16),
        ]
        + [jax.ShapeDtypeStruct(group, BF16)] * 2
        + [jax.ShapeDtypeStruct(group, F32)] * 2,
        in_specs=specs(pltpu.HBM, 7) + specs(pltpu.VMEM, 6),
        out_specs=specs(pltpu.VMEM, 6),
        scratch_shapes=[
            pltpu.VMEM((edges, hidden_width), F32),
            pltpu.VMEM((edges, hidden_width), BF16),
            pltpu.VMEM((slot_rows + mesh_rows, edges), BF16),
            pltpu.VMEM((grad_rows, hidden_width), F32),
            pltpu.VMEM((slot_rows, width), F32),
            pltpu.VMEM((slot_rows, width), F32),
            pltpu.VMEM(slot_index.shape, jnp.int32),
            pltpu.VMEM(dst_index.shape, jnp.int32),
            pltpu.VMEM(mesh_latent.shape, BF16),
            pltpu.VMEM((width, hidden_width), BF16),
            pltpu.VMEM(w_edge2.shape, BF16),
            pltpu.VMEM((w_node1.shape[0] - width, w_node1.shape[1]), BF16),
            pltpu.VMEM(w_node2.shape, BF16),
            pltpu.SemaphoreType.DMA((7,)),
        ],
        compiler_params=params(36),
        name="edges",
    )(
        *pinned(pltpu.HBM, slot_index, dst_index, mesh_latent, w_edge1, w_edge2, w_node1, w_node2),
        slots,
        *pinned(pltpu.VMEM, base, turned, hot, node, cot),
    )
    def after(value, *others):
        return lax.optimization_barrier((value, *others))[0]

    far_send, near_send, far_keep, near_keep = sides
    half = outer // 2
    rows = half * chunk

    def over_inner(total):
        parts = [total[k * rows : (k + 1) * rows].astype(BF16) for k in range(1, inner)]
        received = [to_inner(part, k + 1) for k, part in enumerate(parts)]
        return total[:rows], received

    def joined(total, received):
        for value in received:
            total = total + value.astype(F32)
        return total

    def line(total, k):
        return total[k * chunk : (k + 1) * chunk]

    cap = slot_rows // band_count
    back = d_slots.reshape(2, inner, outer, cap, width)
    far_crossed = to_core(far_send)
    near_crossed, slots_crossed = to_core(after(near_send, far_crossed)), to_core(back[1])
    far_total, far_received = over_inner(far_keep + far_crossed.astype(F32))
    back = jnp.stack([back[0], slots_crossed], axis=2)
    back = jnp.stack([back[0]] + [to_inner(after(back[k], near_crossed), k) for k in range(1, inner)], axis=1)
    near_total, near_received = over_inner(near_keep + near_crossed.astype(F32))
    far_total = joined(far_total, [after(value, back) for value in far_received])
    arrived = [to_outer(line(far_total, k).astype(BF16), half + k) for k in range(half - 1, -1, -1)]
    back = jnp.stack([back[0]] + [to_outer(back[k], k) for k in range(1, outer)], axis=0)
    near_total = joined(near_total, [after(value, back) for value in near_received])
    arrived += [to_outer(line(near_total, k).astype(BF16), k) for k in range(half - 1, 0, -1)]
    own = joined(line(near_total, 0), arrived).astype(BF16)

    turns = []
    for step in range(1, half + 1):
        turns += [outer - step] + [step] * (step != outer - step)
    pieces = {0: own}
    for far_inner in range(1, inner):
        pieces[far_inner * outer] = to_inner(own, far_inner)
    for at, far_outer in enumerate(turns):
        value = own if at < 2 else after(own, pieces[outer])
        pieces[far_outer] = to_outer(value, far_outer)
    for far_inner in range(1, inner):
        for far_outer in turns:
            pieces[far_inner * outer + far_outer] = to_inner(pieces[far_outer], far_inner)
    for at in range(band_count // 2):
        pieces[band_count // 2 + at] = to_core(pieces[at])

    grid_grad = pl.pallas_call(
        functools.partial(put_kernel, sizes),
        out_shape=jax.ShapeDtypeStruct(grid_latent.shape, F32),
        in_specs=specs(pltpu.HBM, 1) + specs(pltpu.VMEM, 1),
        out_specs=pl.BlockSpec(memory_space=pltpu.VMEM),
        scratch_shapes=[
            pltpu.VMEM((slot_rows, width), F32),
            pltpu.VMEM(send_rows.shape, jnp.int32),
            pltpu.SemaphoreType.DMA((1,)),
        ],
        compiler_params=params(16),
        name="put",
    )(*pinned(pltpu.HBM, send_rows), back.reshape(slot_rows, width))

    late = [at for at in range(band_count) if at % outer == turns[-1]]
    early = [at for at in range(band_count) if at % outer != turns[-1]]
    grads = []
    for places in (early, late):
        grads = pl.pallas_call(
            functools.partial(order_kernel, sizes, places, len(grads)),
            out_shape=[
                jax.ShapeDtypeStruct((3 * width, hidden_width), F32),
                jax.ShapeDtypeStruct((hidden_width, width), F32),
            ],
            in_specs=specs(pltpu.VMEM, len(places)) + specs(pltpu.HBM, len(grads)),
            out_specs=specs(pltpu.HBM, 2),
            scratch_shapes=[
                pltpu.VMEM((len(places), chunk, hidden_width), F32),
                pltpu.SemaphoreType.DMA((len(places),)),
            ],
            input_output_aliases={len(places) + k: k for k in range(len(grads))},
            compiler_params=params(16),
            name="order",
        )(*[pieces[at] for at in places], *grads)
    grad_edge1, grad_edge2 = grads
    return (mesh_out, grid_grad, grad_edge1, grad_edge2)


def solution(mesh):
    chips = mesh.shape["band"] // 2
    inner = 1
    while inner * inner * 4 <= chips:
        inner *= 2
    sizes = (chips // inner, inner)
    in_specs = (
        P(("groups", "band"), None),
        P(("groups", "band"), None),
        P(("groups", "band"), None),
        P(("groups", "band"), None),
        P("band", None),
        P("band"),
        P("band"),
        P(),
        P(),
        P(),
        P(),
    )
    out_specs = (
        P(("groups", "band"), None),
        P(("groups", "band"), None),
        P("groups", None),
        P("groups", None),
    )
    return jax.shard_map(
        functools.partial(shards, sizes), mesh=mesh, in_specs=in_specs, out_specs=out_specs, check_vma=False
    )
```

```python
import functools

import jax
import jax.numpy as jnp
from jax import lax
from jax.experimental import pallas as pl
from jax.experimental.pallas import tpu as pltpu
from jax.sharding import PartitionSpec as P

BF16 = jnp.bfloat16
F32 = jnp.float32
MIB = 1024 * 1024


def dot_nn(a, b):
    return jnp.dot(a, b, preferred_element_type=F32)


def dot_tn(a, b):
    return lax.dot_general(a, b, (((0,), (0,)), ((), ())), preferred_element_type=F32)


def dot_nt(a, b):
    return lax.dot_general(a, b, (((1,), (1,)), ((), ())), preferred_element_type=F32)


def split(value):
    high = value.astype(BF16)
    low = (value - high.astype(F32)).astype(BF16)
    return high, low


def one_hot_rows(index_row, rows):
    shape = (rows, index_row.shape[1])
    hit = lax.broadcasted_iota(jnp.int32, shape, 0) == index_row
    return jnp.where(hit, 1.0, 0.0).astype(BF16)


def one_hot_columns(index_row, columns):
    lanes = index_row.shape[1]
    index = jnp.transpose(jnp.broadcast_to(index_row, (lanes, lanes)))
    pieces = []
    for start in range(0, columns, lanes):
        hit = lax.broadcasted_iota(jnp.int32, (lanes, lanes), 1) + start == index
        pieces.append(jnp.where(hit, 1.0, 0.0).astype(BF16))
    return pieces[0] if len(pieces) == 1 else jnp.concatenate(pieces, axis=1)


def tile_rows(index_ref, at, lines, rows):
    found = [one_hot_rows(index_ref[pl.ds(at * lines + k, 1), :], rows) for k in range(lines)]
    return jnp.concatenate(found, axis=1)


def tile_columns(index_ref, at, lines, columns):
    found = [one_hot_columns(index_ref[pl.ds(at * lines + k, 1), :], columns) for k in range(lines)]
    return jnp.concatenate(found, axis=0)


def far_lines(outer):
    return max(1, outer // 4)


def place_of(sizes):
    outer, inner = sizes
    me = lax.axis_index("band")
    return me // (2 * inner), (me // 2) % inner, me % 2


def owner_at(sizes, far_outer, far_inner, far_core):
    my_outer, my_inner, my_core = place_of(sizes)
    return ((my_outer ^ far_outer) * sizes[1] + (my_inner ^ far_inner)) * 2 + (my_core ^ far_core)


def params(mib):
    return pltpu.CompilerParams(vmem_limit_bytes=mib * MIB)


def pinned(space, *values):
    return [pltpu.with_memory_space_constraint(value, space) for value in values]


def specs(space, count):
    return [pl.BlockSpec(memory_space=space)] * count


def cost(flops, nbytes):
    return pl.CostEstimate(flops=flops, bytes_accessed=nbytes, transcendentals=0)


def load(pairs, sems):
    copies = [pltpu.make_async_copy(source, target, sems.at[at]) for at, (source, target) in enumerate(pairs)]
    for copy in copies:
        copy.start()
    return copies


def pick_kernel(rows_hbm, grid_hbm, out_ref, rows_ref, grid_ref, sems):
    rows_copy, grid_copy = load([(rows_hbm, rows_ref), (grid_hbm, grid_ref)], sems)
    rows_copy.wait()
    picked = out_ref.shape[0]
    chosen = [one_hot_columns(rows_ref[:, at : at + 128], grid_ref.shape[0]) for at in range(0, picked, 128)]
    grid_copy.wait()
    for at, some in enumerate(chosen):
        out_ref[at * 128 : (at + 1) * 128, :] = dot_nn(some, grid_ref[...]).astype(BF16)


def put_kernel(sizes, rows_hbm, back_ref, out_ref, ordered_ref, rows_ref, sems):
    outer, inner = sizes
    (copy,) = load([(rows_hbm, rows_ref)], sems)
    cap = back_ref.shape[0] // (2 * outer * inner)
    back = back_ref[...].astype(F32)
    for at in range(2 * outer * inner):
        far_core, far_inner, far_outer = at % 2, at // 2 % inner, at // (2 * inner)
        owner = owner_at(sizes, far_outer, far_inner, far_core)
        ordered_ref[pl.ds(pl.multiple_of(owner * cap, cap), cap), :] = back[at * cap : (at + 1) * cap]
    copy.wait()
    chosen = one_hot_rows(rows_ref[...], out_ref.shape[0])
    out_ref[...] = dot_nn(chosen, ordered_ref[...].astype(BF16))


def base_kernel(
    lines,
    dst_hbm,
    mesh_hbm,
    edge_hbm,
    cot_hbm,
    w1_hbm,
    wn1_hbm,
    wn2_hbm,
    base_ref,
    turned_hbm,
    hot_hbm,
    node_hbm,
    cot_out_hbm,
    dst_ref,
    mesh_ref,
    edge_ref,
    cot_ref,
    w1_ref,
    wn1_ref,
    wn2_ref,
    turned_ref,
    hot_ref,
    node_ref,
    cot_out_ref,
    sems,
    out_sems,
):
    width = mesh_ref.shape[1]
    mesh_rows = mesh_ref.shape[0]
    tile = lines * 128
    tiles = edge_ref.shape[0] // tile
    pairs = [
        (dst_hbm, dst_ref),
        (mesh_hbm, mesh_ref),
        (w1_hbm.at[pl.ds(width, width), :], w1_ref.at[pl.ds(0, width), :]),
        (wn1_hbm.at[pl.ds(0, width), :], wn1_ref),
        (cot_hbm, cot_ref),
        (wn2_hbm, wn2_ref),
        (w1_hbm.at[pl.ds(2 * width, width), :], w1_ref.at[pl.ds(width, width), :]),
    ]
    pairs += [(edge_hbm.at[pl.ds(at * tile, tile), :], edge_ref.at[pl.ds(at * tile, tile), :]) for at in range(tiles)]
    copies = load(pairs, sems)
    same = lax.broadcasted_iota(jnp.int32, (256, 256), 0) == lax.broadcasted_iota(jnp.int32, (256, 256), 1)
    eye = jnp.where(same, 1.0, 0.0).astype(BF16)
    copies[0].wait()
    for at in range(tiles):
        hot_ref[at * tile : (at + 1) * tile, :] = tile_columns(dst_ref, at, lines, mesh_rows)
    for copy in copies[1:6]:
        copy.wait()
    moved = dot_nn(mesh_ref[...], w1_ref[:width, :]).astype(BF16)
    node_ref[...] = dot_nn(mesh_ref[...], wn1_ref[...])
    cot_out_ref[...] = dot_nt(cot_ref[...], wn2_ref[...])
    done = load([(hot_ref, hot_hbm), (node_ref, node_hbm), (cot_out_ref, cot_out_hbm)], out_sems)
    copies[6].wait()
    for at in range(tiles):
        rows = slice(at * tile, (at + 1) * tile)
        copies[7 + at].wait()
        edge = edge_ref[rows, :]
        for start in range(0, width, 256):
            turned_ref[start : start + 256, rows] = dot_nt(eye, edge[:, start : start + 256]).astype(BF16)
        base_ref[rows, :] = dot_nn(edge, w1_ref[width:, :]) + dot_nn(hot_ref[rows, :], moved)
    last = pltpu.make_async_copy(turned_ref, turned_hbm, out_sems.at[3])
    last.start()
    for copy in done + [last]:
        copy.wait()


def main_kernel(
    lines,
    sizes,
    slot_hbm,
    dst_hbm,
    mesh_hbm,
    w1_hbm,
    w2_hbm,
    wn1_hbm,
    wn2_hbm,
    turned_hbm,
    hot_hbm,
    node_hbm,
    cot_hbm,
    slots_ref,
    base_ref,
    *rest,
):
    outer, inner = sizes
    mesh_out_ref, d_slots_ref, far_send_ref, near_send_ref, far_keep_ref, near_keep_ref = rest[:6]
    slope_ref, value_ref, both_ref, grads_ref, slot_grads_ref, ordered_ref = rest[6:12]
    slot_ref, dst_ref, mesh_ref, w1_ref, w2_ref, wn1_ref, wn2_ref = rest[12:19]
    turned_ref, hot_ref, node_ref, cot_ref, sems = rest[19:]
    width = mesh_ref.shape[1]
    mesh_rows = mesh_ref.shape[0]
    slot_rows = slots_ref.shape[0]
    tile = lines * 128
    tiles = base_ref.shape[0] // tile
    pairs = [
        (slot_hbm, slot_ref),
        (w1_hbm.at[pl.ds(0, width), :], w1_ref),
        (dst_hbm, dst_ref),
        (w2_hbm, w2_ref),
        (wn1_hbm.at[pl.ds(width, wn1_ref.shape[0]), :], wn1_ref),
        (mesh_hbm, mesh_ref),
        (node_hbm, node_ref),
        (cot_hbm, cot_ref),
        (hot_hbm, hot_ref),
        (wn2_hbm, wn2_ref),
        (turned_hbm, turned_ref),
    ]
    copies = load(pairs, sems)
    for copy in copies[:3]:
        copy.wait()

    slot_pair = jnp.concatenate(split(dot_nn(slots_ref[...], w1_ref[...])), axis=0)
    for at in range(tiles):
        rows = slice(at * tile, (at + 1) * tile)
        from_slot = tile_columns(slot_ref, at, lines, slot_rows)
        twice = jnp.concatenate([from_slot, from_slot], axis=1)
        pre = base_ref[rows, :] + dot_nn(twice, slot_pair)
        sigma = 0.5 + 0.5 * jnp.tanh(0.5 * pre)
        hidden = pre * sigma
        slope_ref[rows, :] = sigma + hidden * (1.0 - sigma)
        value_ref[rows, :] = hidden.astype(BF16)
        both_ref[:slot_rows, rows] = tile_rows(slot_ref, at, lines, slot_rows)
        both_ref[slot_rows:, rows] = tile_rows(dst_ref, at, lines, mesh_rows)

    for copy in copies[3:-1]:
        copy.wait()
    hidden_sums = dot_nn(both_ref[slot_rows:, :], value_ref[...]).astype(BF16)
    received = dot_nn(hidden_sums, w2_ref[...]).astype(BF16)
    mesh = mesh_ref[...]
    pre_node = node_ref[...] + dot_nn(received, wn1_ref[...])
    sigma = 0.5 + 0.5 * jnp.tanh(0.5 * pre_node)
    node = pre_node * sigma
    slope = sigma + node * (1.0 - sigma)
    d_pre_node = (cot_ref[...] * slope).astype(BF16)
    d_received = dot_nt(d_pre_node, wn1_ref[...]).astype(BF16)
    spread = dot_nt(d_received, w2_ref[...]).astype(BF16)

    for at in range(tiles):
        rows = slice(at * tile, (at + 1) * tile)
        value_ref[rows, :] = (dot_nn(hot_ref[rows, :], spread) * slope_ref[rows, :]).astype(BF16)

    grads_ref[3 * width :, :] = dot_tn(hidden_sums, d_received)
    mesh_out_ref[...] = (mesh.astype(F32) + dot_nn(node.astype(BF16), wn2_ref[...])).astype(BF16)
    sums = dot_nn(both_ref[...], value_ref[...]).astype(BF16)
    slot_grads_ref[...] = dot_nt(sums[:slot_rows], w1_ref[...])
    grads_ref[:width, :] = dot_tn(slots_ref[...], sums[:slot_rows])
    grads_ref[width : 2 * width, :] = dot_tn(mesh, sums[slot_rows:])
    copies[-1].wait()
    grads_ref[2 * width : 3 * width, :] = dot_nn(turned_ref[...], value_ref[...])

    chunk = grads_ref.shape[0] // (2 * outer * inner)
    cap = slot_rows // (2 * outer * inner)
    far_count = far_lines(outer)
    for far_core in range(2):
        for far_inner in range(inner):
            for far_outer in range(outer):
                owner = owner_at(sizes, far_outer, far_inner, far_core)
                at = (far_core * inner + far_inner) * outer + far_outer
                from_rows = pl.ds(pl.multiple_of(owner * cap, cap), cap)
                ordered_ref[at * cap : (at + 1) * cap, :] = slot_grads_ref[from_rows, :]
                value = grads_ref[pl.ds(pl.multiple_of(owner * chunk, chunk), chunk), :]
                if far_outer >= outer - far_count:
                    line = far_inner * far_count + far_outer - (outer - far_count)
                    send_ref, keep_ref = far_send_ref, far_keep_ref
                else:
                    line = far_inner * (outer - far_count) + far_outer
                    send_ref, keep_ref = near_send_ref, near_keep_ref
                rows = slice(line * chunk, (line + 1) * chunk)
                if far_core:
                    send_ref[rows, :] = value.astype(BF16)
                else:
                    keep_ref[rows, :] = value
    halfway = slot_rows // 2
    d_slots_ref[...] = ordered_ref[:halfway, :].astype(BF16)
    near_send_ref[near_keep_ref.shape[0] :, :] = ordered_ref[halfway:, :].astype(BF16)


def join_kernel(sizes, near_count, keep_ref, crossed_ref, d_slots_ref, total_ref, slots_ref, *part_refs):
    outer, inner = sizes
    rows = keep_ref.shape[0]
    size = rows // inner
    cap = d_slots_ref.shape[0] // (inner * outer)
    own, far = d_slots_ref[...].astype(F32), crossed_ref[rows:, :].astype(F32)
    for far_inner in range(inner):
        here = slice(far_inner * size, (far_inner + 1) * size)
        total = keep_ref[here, :] + crossed_ref[here, :].astype(F32)
        mixed = []
        for far_outer in range(outer):
            at = (far_inner * outer + far_outer) * cap
            mixed += [own[at : at + cap], far[at : at + cap]]
        mixed = jnp.concatenate(mixed, axis=0).astype(BF16)
        if far_inner:
            part_refs[far_inner - 1][:size, :] = total.astype(BF16)
            part_refs[far_inner - 1][size:, :] = mixed
        else:
            total_ref[...] = total
            slots_ref[...] = mixed


def order_kernel(sizes, places, aliased, *refs):
    outer, inner = sizes
    pieces = refs[: len(places)]
    first_hbm, second_hbm, stage_ref, sems = refs[len(places) + aliased :]
    chunk = pieces[0].shape[0]
    first_chunks = first_hbm.shape[0] // chunk

    def send(k, target, start):
        rows = pl.ds(pl.multiple_of(start, chunk), chunk)
        return pltpu.make_async_copy(stage_ref.at[k], target.at[rows, :], sems.at[k])

    for k, (at, piece) in enumerate(zip(places, pieces)):
        owner = owner_at(sizes, at % outer, at // outer % inner, at // (outer * inner))
        stage_ref[k] = piece[...].astype(F32)

        @pl.when(owner < first_chunks)
        def _():
            send(k, first_hbm, owner * chunk).start()

        @pl.when(owner >= first_chunks)
        def _():
            send(k, second_hbm, (owner - first_chunks) * chunk).start()

    for k in range(len(places)):
        send(k, first_hbm, 0).wait()


def shards(
    sizes,
    grid_latent,
    mesh_latent,
    edge_latent,
    mesh_cot,
    send_rows,
    edge_slot,
    edge_dst,
    w_edge1,
    w_edge2,
    w_node1,
    w_node2,
):
    outer, inner = sizes
    band_count = lax.axis_size("band")
    width = grid_latent.shape[1]
    hidden_width = w_edge1.shape[1]
    edges = edge_latent.shape[0]
    mesh_rows = mesh_latent.shape[0]
    slot_rows = send_rows.shape[1]
    lines = 4
    slot_index = edge_slot.reshape(edges // 128, 128)
    dst_index = edge_dst.reshape(edges // 128, 128)

    def permute(value, stride, size, shift):
        pairs = []
        for source in range(band_count):
            place = (source // stride) % size
            pairs.append((source, source + ((place ^ shift) - place) * stride))
        return lax.ppermute(value, "band", pairs)

    def to_core(value):
        return permute(value, 1, 2, 1)

    def to_inner(value, shift):
        return permute(value, 2, inner, shift)

    def to_outer(value, shift):
        return permute(value, 2 * inner, outer, shift)

    outgoing = pl.pallas_call(
        pick_kernel,
        out_shape=jax.ShapeDtypeStruct((slot_rows, width), BF16),
        in_specs=specs(pltpu.HBM, 2),
        out_specs=pl.BlockSpec(memory_space=pltpu.VMEM),
        scratch_shapes=[
            pltpu.VMEM(send_rows.shape, jnp.int32),
            pltpu.VMEM(grid_latent.shape, BF16),
            pltpu.SemaphoreType.DMA((2,)),
        ],
        compiler_params=params(16),
        name="pick",
    )(*pinned(pltpu.HBM, send_rows, grid_latent))
    slots = lax.all_to_all(
        outgoing.reshape(band_count, -1, width), "band", split_axis=0, concat_axis=0, tiled=True
    ).reshape(slot_rows, width)

    base, turned, hot, node, cot = pl.pallas_call(
        functools.partial(base_kernel, lines),
        out_shape=[
            pltpu.VMEM((edges, hidden_width), F32),
            pltpu.HBM((width, edges), BF16),
            pltpu.HBM((edges, mesh_rows), BF16),
            pltpu.HBM((mesh_rows, hidden_width), F32),
            pltpu.HBM((mesh_rows, hidden_width), F32),
        ],
        in_specs=specs(pltpu.HBM, 7),
        out_specs=specs(pltpu.VMEM, 1) + specs(pltpu.HBM, 4),
        scratch_shapes=[
            pltpu.VMEM(dst_index.shape, jnp.int32),
            pltpu.VMEM(mesh_latent.shape, BF16),
            pltpu.VMEM(edge_latent.shape, BF16),
            pltpu.VMEM(mesh_cot.shape, BF16),
            pltpu.VMEM((2 * width, hidden_width), BF16),
            pltpu.VMEM((width, hidden_width), BF16),
            pltpu.VMEM(w_node2.shape, BF16),
            pltpu.VMEM((width, edges), BF16),
            pltpu.VMEM((edges, mesh_rows), BF16),
            pltpu.VMEM((mesh_rows, hidden_width), F32),
            pltpu.VMEM((mesh_rows, hidden_width), F32),
            pltpu.SemaphoreType.DMA((7 + edges // (128 * lines),)),
            pltpu.SemaphoreType.DMA((4,)),
        ],
        compiler_params=params(20),
        cost_estimate=cost(2 * edges * width * hidden_width * 2, edges * width * 8),
        name="base",
    )(*pinned(pltpu.HBM, dst_index, mesh_latent, edge_latent, mesh_cot, w_edge1, w_node1, w_node2))

    grad_rows = 3 * width + hidden_width
    chunk = grad_rows // band_count
    far_count = far_lines(outer)
    near_count = outer - far_count
    far_group = (far_count * inner * chunk, hidden_width)
    near_group = (near_count * inner * chunk, hidden_width)
    near_rows, halfway = near_group[0], slot_rows // 2
    mesh_out, d_slots, far_send, near_send, far_keep, near_keep = pl.pallas_call(
        functools.partial(main_kernel, lines, sizes),
        out_shape=[
            jax.ShapeDtypeStruct((mesh_rows, width), BF16),
            jax.ShapeDtypeStruct((halfway, width), BF16),
            jax.ShapeDtypeStruct(far_group, BF16),
            jax.ShapeDtypeStruct((near_rows + halfway, hidden_width), BF16),
            jax.ShapeDtypeStruct(far_group, F32),
            jax.ShapeDtypeStruct(near_group, F32),
        ],
        in_specs=specs(pltpu.HBM, 11) + specs(pltpu.VMEM, 2),
        out_specs=specs(pltpu.VMEM, 6),
        scratch_shapes=[
            pltpu.VMEM((edges, hidden_width), F32),
            pltpu.VMEM((edges, hidden_width), BF16),
            pltpu.VMEM((slot_rows + mesh_rows, edges), BF16),
            pltpu.VMEM((grad_rows, hidden_width), F32),
            pltpu.VMEM((slot_rows, width), F32),
            pltpu.VMEM((slot_rows, width), F32),
            pltpu.VMEM(slot_index.shape, jnp.int32),
            pltpu.VMEM(dst_index.shape, jnp.int32),
            pltpu.VMEM(mesh_latent.shape, BF16),
            pltpu.VMEM((width, hidden_width), BF16),
            pltpu.VMEM(w_edge2.shape, BF16),
            pltpu.VMEM((w_node1.shape[0] - width, w_node1.shape[1]), BF16),
            pltpu.VMEM(w_node2.shape, BF16),
            pltpu.VMEM(turned.shape, BF16),
            pltpu.VMEM(hot.shape, BF16),
            pltpu.VMEM(node.shape, F32),
            pltpu.VMEM(cot.shape, F32),
            pltpu.SemaphoreType.DMA((11,)),
        ],
        compiler_params=params(40),
        name="edges",
    )(
        *pinned(pltpu.HBM, slot_index, dst_index, mesh_latent, w_edge1, w_edge2, w_node1, w_node2),
        *pinned(pltpu.HBM, turned, hot, node, cot),
        slots,
        *pinned(pltpu.VMEM, base),
    )
    cap = slot_rows // band_count

    def line(total, k):
        return total[k * chunk : (k + 1) * chunk].astype(BF16)

    far_crossed, near_crossed = to_core(far_send), to_core(near_send)
    far_rows, size = far_count * chunk, near_count * chunk
    far_half = far_keep + far_crossed.astype(F32)
    far_total = far_half[:far_rows]
    far_parts = [far_half[k * far_rows : (k + 1) * far_rows].astype(BF16) for k in range(1, inner)]
    near_crossed = lax.optimization_barrier((near_crossed, *far_parts))[0]
    for k, part in enumerate(far_parts):
        far_total = far_total + to_inner(part, k + 1).astype(F32)
    mixed_rows = outer * 2 * cap
    near_total, mixed, *parts = pl.pallas_call(
        functools.partial(join_kernel, sizes, near_count),
        out_shape=[
            jax.ShapeDtypeStruct((size, hidden_width), F32),
            jax.ShapeDtypeStruct((mixed_rows, width), BF16),
        ]
        + [jax.ShapeDtypeStruct((size + mixed_rows, width), BF16)] * (inner - 1),
        compiler_params=params(16),
        cost_estimate=cost(2 * 10**10, MIB),
        name="join",
    )(near_keep, near_crossed, d_slots)
    parts = [to_inner(part, k + 1) for k, part in enumerate(parts)]
    for part in parts:
        near_total = near_total + part[:size].astype(F32)
    back = [value.reshape(outer, 2, cap, width) for value in [mixed] + [part[size:] for part in parts]]
    back = jnp.stack(back, axis=1)
    arrived, returned = [], {0: back[0]}
    for k in range(far_count):
        arrived.append(to_outer(line(far_total, k), near_count + k))
    near_total = lax.optimization_barrier((near_total, *arrived))[0]
    for k in range(near_count - 1, 0, -1):
        value = to_outer(jnp.concatenate([line(near_total, k), back[k].reshape(-1, width)], axis=0), k)
        arrived.append(value[:chunk])
        returned[k] = value[chunk:].reshape(back[0].shape)
    for k in range(near_count, outer):
        returned[k] = to_outer(back[k], k)
    own = near_total[:chunk]
    for value in arrived:
        own = own + value.astype(F32)
    own = own.astype(BF16)
    back = jnp.stack([returned[k] for k in range(outer)], axis=0)

    pieces = {0: own}
    stride = outer // 2
    while stride:
        for at in range(0, outer, 2 * stride):
            pieces[at + stride] = to_outer(pieces[at], stride)
        stride //= 2
    for far_inner in range(1, inner):
        for far_outer in range(outer):
            pieces[far_inner * outer + far_outer] = to_inner(pieces[far_outer], far_inner)
    for at in range(band_count // 2):
        pieces[band_count // 2 + at] = to_core(pieces[at])

    grid_grad = pl.pallas_call(
        functools.partial(put_kernel, sizes),
        out_shape=jax.ShapeDtypeStruct(grid_latent.shape, F32),
        in_specs=specs(pltpu.HBM, 1) + specs(pltpu.VMEM, 1),
        out_specs=pl.BlockSpec(memory_space=pltpu.VMEM),
        scratch_shapes=[
            pltpu.VMEM((slot_rows, width), F32),
            pltpu.VMEM(send_rows.shape, jnp.int32),
            pltpu.SemaphoreType.DMA((1,)),
        ],
        compiler_params=params(16),
        name="put",
    )(*pinned(pltpu.HBM, send_rows), back.reshape(slot_rows, width))

    late = [at for at in range(band_count) if at % outer == outer - 1]
    early = [at for at in range(band_count) if at % outer != outer - 1]
    grads = []
    for places in (early, late):
        grads = pl.pallas_call(
            functools.partial(order_kernel, sizes, places, len(grads)),
            out_shape=[
                jax.ShapeDtypeStruct((3 * width, hidden_width), F32),
                jax.ShapeDtypeStruct((hidden_width, width), F32),
            ],
            in_specs=specs(pltpu.VMEM, len(places)) + specs(pltpu.HBM, len(grads)),
            out_specs=specs(pltpu.HBM, 2),
            scratch_shapes=[
                pltpu.VMEM((len(places), chunk, hidden_width), F32),
                pltpu.SemaphoreType.DMA((len(places),)),
            ],
            input_output_aliases={len(places) + k: k for k in range(len(grads))},
            compiler_params=params(16),
            name="order",
        )(*[pieces[at] for at in places], *grads)
    grad_edge1, grad_edge2 = grads
    return (mesh_out, grid_grad, grad_edge1, grad_edge2)


def solution(mesh):
    chips = mesh.shape["band"] // 2
    inner = 1
    while inner * inner * 4 <= chips:
        inner *= 2
    sizes = (chips // inner, inner)
    in_specs = (
        P(("groups", "band"), None),
        P(("groups", "band"), None),
        P(("groups", "band"), None),
        P(("groups", "band"), None),
        P("band", None),
        P("band"),
        P("band"),
        P(),
        P(),
        P(),
        P(),
    )
    out_specs = (
        P(("groups", "band"), None),
        P(("groups", "band"), None),
        P("groups", None),
        P("groups", None),
    )
    return jax.shard_map(
        functools.partial(shards, sizes), mesh=mesh, in_specs=in_specs, out_specs=out_specs, check_vma=False
    )
```

```python
import functools

import jax
import jax.numpy as jnp
from jax import lax
from jax.experimental import pallas as pl
from jax.experimental.pallas import tpu as pltpu
from jax.sharding import PartitionSpec as P

BF16 = jnp.bfloat16
F32 = jnp.float32
MIB = 1024 * 1024


def dot_nn(a, b):
    return jnp.dot(a, b, preferred_element_type=F32)


def dot_tn(a, b):
    return lax.dot_general(a, b, (((0,), (0,)), ((), ())), preferred_element_type=F32)


def dot_nt(a, b):
    return lax.dot_general(a, b, (((1,), (1,)), ((), ())), preferred_element_type=F32)


def split(value):
    high = value.astype(BF16)
    low = (value - high.astype(F32)).astype(BF16)
    return high, low


def one_hot_rows(index_row, rows):
    shape = (rows, index_row.shape[1])
    hit = lax.broadcasted_iota(jnp.int32, shape, 0) == index_row
    return jnp.where(hit, 1.0, 0.0).astype(BF16)


def one_hot_columns(index_row, columns):
    lanes = index_row.shape[1]
    index = jnp.transpose(jnp.broadcast_to(index_row, (lanes, lanes)))
    pieces = []
    for start in range(0, columns, lanes):
        hit = lax.broadcasted_iota(jnp.int32, (lanes, lanes), 1) + start == index
        pieces.append(jnp.where(hit, 1.0, 0.0).astype(BF16))
    return pieces[0] if len(pieces) == 1 else jnp.concatenate(pieces, axis=1)


def tile_rows(index_ref, at, lines, rows):
    found = [one_hot_rows(index_ref[pl.ds(at * lines + k, 1), :], rows) for k in range(lines)]
    return jnp.concatenate(found, axis=1)


def tile_columns(index_ref, at, lines, columns):
    found = [one_hot_columns(index_ref[pl.ds(at * lines + k, 1), :], columns) for k in range(lines)]
    return jnp.concatenate(found, axis=0)


def place_of(sizes):
    outer, inner = sizes
    me = lax.axis_index("band")
    return me // (2 * inner), (me // 2) % inner, me % 2


def owner_at(sizes, far_outer, far_inner, far_core):
    my_outer, my_inner, my_core = place_of(sizes)
    return ((my_outer ^ far_outer) * sizes[1] + (my_inner ^ far_inner)) * 2 + (my_core ^ far_core)


def params(mib):
    return pltpu.CompilerParams(vmem_limit_bytes=mib * MIB)


def pinned(space, *values):
    return [pltpu.with_memory_space_constraint(value, space) for value in values]


def specs(space, count):
    return [pl.BlockSpec(memory_space=space)] * count


def cost(flops, nbytes):
    return pl.CostEstimate(flops=flops, bytes_accessed=nbytes, transcendentals=0)


def load(pairs, sems):
    copies = [pltpu.make_async_copy(source, target, sems.at[at]) for at, (source, target) in enumerate(pairs)]
    for copy in copies:
        copy.start()
    return copies


def pick_kernel(sizes, rows_hbm, grid_hbm, keep_ref, send_ref, rows_ref, grid_ref, picked_ref, sems):
    outer, inner = sizes
    rows_copy, grid_copy = load([(rows_hbm, rows_ref), (grid_hbm, grid_ref)], sems)
    rows_copy.wait()
    picked = picked_ref.shape[0]
    chosen = [one_hot_columns(rows_ref[:, at : at + 128], grid_ref.shape[0]) for at in range(0, picked, 128)]
    grid_copy.wait()
    for at, some in enumerate(chosen):
        picked_ref[at * 128 : (at + 1) * 128, :] = dot_nn(some, grid_ref[...])
    cap = picked // (2 * outer * inner)
    for far_core, target in enumerate((keep_ref, send_ref)):
        blocks = []
        for far_inner in range(inner):
            for far_outer in range(outer):
                owner = owner_at(sizes, far_outer, far_inner, far_core)
                blocks.append(picked_ref[pl.ds(pl.multiple_of(owner * cap, cap), cap), :])
        target[...] = jnp.concatenate(blocks, axis=0).astype(BF16)


def mix_kernel(count, minor, *refs):
    sources, targets = refs[:-count], refs[-count:]
    values = [ref[...].astype(F32) for ref in sources]
    unit = values[0].shape[0] // (count * minor)
    for at, target in enumerate(targets):
        starts = [(at * minor + k) * unit for k in range(minor)]
        blocks = [value[start : start + unit] for start in starts for value in values]
        target[...] = jnp.concatenate(blocks, axis=0).astype(BF16)


def put_kernel(sizes, rows_hbm, *refs):
    outer, inner = sizes
    blocks, (out_ref, ordered_ref, rows_ref, sems) = refs[:outer], refs[outer:]
    (copy,) = load([(rows_hbm, rows_ref)], sems)
    place_rows(sizes, blocks, ordered_ref)
    copy.wait()
    chosen = one_hot_rows(rows_ref[...], out_ref.shape[0])
    out_ref[...] = dot_nn(chosen, ordered_ref[...].astype(BF16))


def place_rows(sizes, blocks, ordered_ref):
    outer, inner = sizes
    cap = ordered_ref.shape[0] // (2 * outer * inner)
    for far_outer, block in enumerate(blocks):
        value = block[block.shape[0] - 2 * inner * cap :, :].astype(F32)
        for at in range(2 * inner):
            owner = owner_at(sizes, far_outer, at // 2, at % 2)
            ordered_ref[pl.ds(pl.multiple_of(owner * cap, cap), cap), :] = value[at * cap : (at + 1) * cap]


def ready_kernel(
    lines,
    dst_hbm,
    mesh_hbm,
    cot_hbm,
    w1_hbm,
    wn1_hbm,
    wn2_hbm,
    hot_hbm,
    node_hbm,
    cot_out_hbm,
    moved_ref,
    dst_ref,
    mesh_ref,
    cot_ref,
    w1_ref,
    wn1_ref,
    wn2_ref,
    hot_ref,
    node_ref,
    cot_out_ref,
    sems,
    out_sems,
):
    width = mesh_ref.shape[1]
    tile = lines * 128
    pairs = [
        (dst_hbm, dst_ref),
        (mesh_hbm, mesh_ref),
        (w1_hbm.at[pl.ds(width, width), :], w1_ref),
        (wn1_hbm.at[pl.ds(0, width), :], wn1_ref),
        (cot_hbm, cot_ref),
        (wn2_hbm, wn2_ref),
    ]
    copies = load(pairs, sems)
    copies[0].wait()
    for at in range(hot_ref.shape[0] // tile):
        hot_ref[at * tile : (at + 1) * tile, :] = tile_columns(dst_ref, at, lines, hot_ref.shape[1])
    for copy in copies[1:]:
        copy.wait()
    moved_ref[...] = dot_nn(mesh_ref[...], w1_ref[...]).astype(BF16)
    node_ref[...] = dot_nn(mesh_ref[...], wn1_ref[...])
    cot_out_ref[...] = dot_nt(cot_ref[...], wn2_ref[...])
    pairs = [(hot_ref, hot_hbm), (node_ref, node_hbm), (cot_out_ref, cot_out_hbm)]
    for copy in load(pairs, out_sems):
        copy.wait()


def base_kernel(
    lines,
    hot_hbm,
    edge_hbm,
    w1_hbm,
    moved_ref,
    base_ref,
    turned_hbm,
    hot_ref,
    edge_ref,
    w1_ref,
    turned_ref,
    sems,
    out_sems,
):
    width = edge_ref.shape[1]
    tile = lines * 128
    tiles = edge_ref.shape[0] // tile
    pairs = [(w1_hbm.at[pl.ds(2 * width, width), :], w1_ref), (hot_hbm, hot_ref)]
    pairs += [(edge_hbm.at[pl.ds(at * tile, tile), :], edge_ref.at[pl.ds(at * tile, tile), :]) for at in range(tiles)]
    copies = load(pairs, sems)
    same = lax.broadcasted_iota(jnp.int32, (256, 256), 0) == lax.broadcasted_iota(jnp.int32, (256, 256), 1)
    eye = jnp.where(same, 1.0, 0.0).astype(BF16)
    copies[0].wait()
    copies[1].wait()
    for at in range(tiles):
        rows = slice(at * tile, (at + 1) * tile)
        copies[2 + at].wait()
        edge = edge_ref[rows, :]
        for start in range(0, width, 256):
            turned_ref[start : start + 256, rows] = dot_nt(eye, edge[:, start : start + 256]).astype(BF16)
        base_ref[rows, :] = dot_nn(edge, w1_ref[...]) + dot_nn(hot_ref[rows, :], moved_ref[...])
    (last,) = load([(turned_ref, turned_hbm)], out_sems)
    last.wait()


def main_kernel(
    lines,
    sizes,
    slot_hbm,
    dst_hbm,
    mesh_hbm,
    w1_hbm,
    w2_hbm,
    wn1_hbm,
    wn2_hbm,
    turned_hbm,
    hot_hbm,
    node_hbm,
    cot_hbm,
    base_ref,
    *rest,
):
    outer, inner = sizes
    slot_blocks, rest = rest[:outer], rest[outer:]
    mesh_out_ref, d_slots_ref = rest[:2]
    send_refs, keep_refs, rest = rest[2 : 2 + outer], rest[2 + outer : 2 + 2 * outer], rest[2 + 2 * outer :]
    slope_ref, value_ref, both_ref, grads_ref, slot_grads_ref, ordered_ref = rest[:6]
    slot_ref, dst_ref, mesh_ref, w1_ref, w2_ref, wn1_ref, wn2_ref = rest[6:13]
    turned_ref, hot_ref, node_ref, cot_ref, sems = rest[13:]
    width = mesh_ref.shape[1]
    mesh_rows = mesh_ref.shape[0]
    slot_rows = ordered_ref.shape[0]
    tile = lines * 128
    tiles = base_ref.shape[0] // tile
    pairs = [
        (slot_hbm, slot_ref),
        (w1_hbm.at[pl.ds(0, width), :], w1_ref),
        (dst_hbm, dst_ref),
        (w2_hbm, w2_ref),
        (wn1_hbm.at[pl.ds(width, wn1_ref.shape[0]), :], wn1_ref),
        (mesh_hbm, mesh_ref),
        (node_hbm, node_ref),
        (cot_hbm, cot_ref),
        (hot_hbm, hot_ref),
        (wn2_hbm, wn2_ref),
        (turned_hbm, turned_ref),
    ]
    copies = load(pairs, sems)
    place_rows(sizes, slot_blocks, ordered_ref)
    slots_value = ordered_ref[...].astype(BF16)
    for copy in copies[:3]:
        copy.wait()

    slots = slots_value
    slot_pair = jnp.concatenate(split(dot_nn(slots, w1_ref[...])), axis=0)
    for at in range(tiles):
        rows = slice(at * tile, (at + 1) * tile)
        from_slot = tile_columns(slot_ref, at, lines, slot_rows)
        twice = jnp.concatenate([from_slot, from_slot], axis=1)
        pre = base_ref[rows, :] + dot_nn(twice, slot_pair)
        sigma = 0.5 + 0.5 * jnp.tanh(0.5 * pre)
        hidden = pre * sigma
        slope_ref[rows, :] = sigma + hidden * (1.0 - sigma)
        value_ref[rows, :] = hidden.astype(BF16)
        both_ref[:slot_rows, rows] = tile_rows(slot_ref, at, lines, slot_rows)
        both_ref[slot_rows:, rows] = tile_rows(dst_ref, at, lines, mesh_rows)

    for copy in copies[3:-1]:
        copy.wait()
    hidden_sums = dot_nn(both_ref[slot_rows:, :], value_ref[...]).astype(BF16)
    received = dot_nn(hidden_sums, w2_ref[...]).astype(BF16)
    mesh = mesh_ref[...]
    pre_node = node_ref[...] + dot_nn(received, wn1_ref[...])
    sigma = 0.5 + 0.5 * jnp.tanh(0.5 * pre_node)
    node = pre_node * sigma
    slope = sigma + node * (1.0 - sigma)
    d_pre_node = (cot_ref[...] * slope).astype(BF16)
    d_received = dot_nt(d_pre_node, wn1_ref[...]).astype(BF16)
    spread = dot_nt(d_received, w2_ref[...]).astype(BF16)

    for at in range(tiles):
        rows = slice(at * tile, (at + 1) * tile)
        value_ref[rows, :] = (dot_nn(hot_ref[rows, :], spread) * slope_ref[rows, :]).astype(BF16)

    grads_ref[3 * width :, :] = dot_tn(hidden_sums, d_received)
    mesh_out_ref[...] = (mesh.astype(F32) + dot_nn(node.astype(BF16), wn2_ref[...])).astype(BF16)
    sums = dot_nn(both_ref[...], value_ref[...]).astype(BF16)
    slot_grads_ref[...] = dot_nt(sums[:slot_rows], w1_ref[...])
    grads_ref[:width, :] = dot_tn(slots, sums[:slot_rows])
    grads_ref[width : 2 * width, :] = dot_tn(mesh, sums[slot_rows:])
    copies[-1].wait()
    grads_ref[2 * width : 3 * width, :] = dot_nn(turned_ref[...], value_ref[...])

    chunk = grads_ref.shape[0] // (2 * outer * inner)
    cap = slot_rows // (2 * outer * inner)
    for far_core in range(2):
        for far_outer in range(outer):
            for far_inner in range(inner):
                owner = owner_at(sizes, far_outer, far_inner, far_core)
                at = (far_core * outer + far_outer) * inner + far_inner
                from_rows = pl.ds(pl.multiple_of(owner * cap, cap), cap)
                ordered_ref[at * cap : (at + 1) * cap, :] = slot_grads_ref[from_rows, :]
                value = grads_ref[pl.ds(pl.multiple_of(owner * chunk, chunk), chunk), :]
                rows = slice(far_inner * chunk, (far_inner + 1) * chunk)
                if far_core:
                    send_refs[far_outer][rows, :] = value.astype(BF16)
                else:
                    keep_refs[far_outer][rows, :] = value
    halfway, share = slot_rows // 2, inner * cap
    d_slots_ref[...] = ordered_ref[:halfway, :].astype(BF16)
    for far_outer, send_ref in enumerate(send_refs):
        start = halfway + far_outer * share
        send_ref[inner * chunk :, :] = ordered_ref[start : start + share, :].astype(BF16)


def core_kernel(sizes, far_outer, keep_ref, crossed_ref, d_slots_ref, total_ref, mixed_ref, *part_refs):
    outer, inner = sizes
    chunk = total_ref.shape[0]
    cap = d_slots_ref.shape[0] // (outer * inner)
    start = far_outer * inner * cap
    own = d_slots_ref[start : start + inner * cap, :].astype(F32)
    far = crossed_ref[inner * chunk :, :].astype(F32)
    for far_inner in range(inner):
        rows, slots = slice(far_inner * chunk, (far_inner + 1) * chunk), slice(far_inner * cap, (far_inner + 1) * cap)
        total = keep_ref[rows, :] + crossed_ref[rows, :].astype(F32)
        mixed = jnp.concatenate([own[slots], far[slots]], axis=0).astype(BF16)
        if far_inner:
            part_refs[far_inner - 1][:chunk, :] = total.astype(BF16)
            part_refs[far_inner - 1][chunk:, :] = mixed
        else:
            total_ref[...] = total
            mixed_ref[...] = mixed


def inner_kernel(parts, arrivals, total_ref, mixed_ref, *refs):
    received, arrived, outs = refs[:parts], refs[parts : parts + arrivals], refs[parts + arrivals :]
    chunk = total_ref.shape[0]
    total = total_ref[...]
    mixed = [mixed_ref[...]]
    for part in received:
        total = total + part[:chunk, :].astype(F32)
        mixed.append(part[chunk:, :])
    for value in arrived:
        total = total + value[:chunk, :].astype(F32)
    mixed = jnp.concatenate(mixed, axis=0)
    if len(outs) == 1:
        outs[0][:chunk, :] = total.astype(BF16)
        outs[0][chunk:, :] = mixed
    else:
        outs[0][...] = total.astype(BF16)
        outs[1][...] = mixed


def order_kernel(sizes, places, aliased, *refs):
    outer, inner = sizes
    pieces = refs[: len(places)]
    first_hbm, second_hbm, stage_ref, sems = refs[len(places) + aliased :]
    chunk = pieces[0].shape[0]
    first_chunks = first_hbm.shape[0] // chunk

    def send(k, target, start):
        rows = pl.ds(pl.multiple_of(start, chunk), chunk)
        return pltpu.make_async_copy(stage_ref.at[k], target.at[rows, :], sems.at[k])

    for k, (at, piece) in enumerate(zip(places, pieces)):
        owner = owner_at(sizes, at % outer, at // outer % inner, at // (outer * inner))
        stage_ref[k] = piece[...].astype(F32)

        @pl.when(owner < first_chunks)
        def _():
            send(k, first_hbm, owner * chunk).start()

        @pl.when(owner >= first_chunks)
        def _():
            send(k, second_hbm, (owner - first_chunks) * chunk).start()

    for k in range(len(places)):
        send(k, first_hbm, 0).wait()


def shards(
    sizes,
    grid_latent,
    mesh_latent,
    edge_latent,
    mesh_cot,
    send_rows,
    edge_slot,
    edge_dst,
    w_edge1,
    w_edge2,
    w_node1,
    w_node2,
):
    outer, inner = sizes
    band_count = lax.axis_size("band")
    width = grid_latent.shape[1]
    hidden_width = w_edge1.shape[1]
    edges = edge_latent.shape[0]
    mesh_rows = mesh_latent.shape[0]
    slot_rows = send_rows.shape[1]
    lines = 4
    slot_index = edge_slot.reshape(edges // 128, 128)
    dst_index = edge_dst.reshape(edges // 128, 128)

    def permute(value, stride, size, shift):
        pairs = []
        for source in range(band_count):
            place = (source // stride) % size
            pairs.append((source, source + ((place ^ shift) - place) * stride))
        return lax.ppermute(value, "band", pairs)

    def to_core(value):
        return permute(value, 1, 2, 1)

    def to_inner(value, shift):
        return permute(value, 2, inner, shift)

    def to_outer(value, shift):
        return permute(value, 2 * inner, outer, shift)

    cap, halfway = slot_rows // band_count, slot_rows // 2
    kept, sent = pl.pallas_call(
        functools.partial(pick_kernel, sizes),
        out_shape=[jax.ShapeDtypeStruct((halfway, width), BF16)] * 2,
        in_specs=specs(pltpu.HBM, 2),
        out_specs=specs(pltpu.VMEM, 2),
        scratch_shapes=[
            pltpu.VMEM(send_rows.shape, jnp.int32),
            pltpu.VMEM(grid_latent.shape, BF16),
            pltpu.VMEM((slot_rows, width), F32),
            pltpu.SemaphoreType.DMA((2,)),
        ],
        compiler_params=params(16),
        name="pick",
    )(*pinned(pltpu.HBM, send_rows, grid_latent))

    def mix(values, count, minor):
        rows = len(values) * values[0].shape[0] // count
        return pl.pallas_call(
            functools.partial(mix_kernel, count, minor),
            out_shape=[jax.ShapeDtypeStruct((rows, width), BF16)] * count,
            compiler_params=params(16),
            name="mix",
        )(*values)

    hot, node, cot, moved = pl.pallas_call(
        functools.partial(ready_kernel, lines),
        out_shape=[
            pltpu.HBM((edges, mesh_rows), BF16),
            pltpu.HBM((mesh_rows, hidden_width), F32),
            pltpu.HBM((mesh_rows, hidden_width), F32),
            pltpu.VMEM((mesh_rows, hidden_width), BF16),
        ],
        in_specs=specs(pltpu.HBM, 6),
        out_specs=specs(pltpu.HBM, 3) + specs(pltpu.VMEM, 1),
        scratch_shapes=[
            pltpu.VMEM(dst_index.shape, jnp.int32),
            pltpu.VMEM(mesh_latent.shape, BF16),
            pltpu.VMEM(mesh_cot.shape, BF16),
            pltpu.VMEM((width, hidden_width), BF16),
            pltpu.VMEM((width, hidden_width), BF16),
            pltpu.VMEM(w_node2.shape, BF16),
            pltpu.VMEM((edges, mesh_rows), BF16),
            pltpu.VMEM((mesh_rows, hidden_width), F32),
            pltpu.VMEM((mesh_rows, hidden_width), F32),
            pltpu.SemaphoreType.DMA((6,)),
            pltpu.SemaphoreType.DMA((3,)),
        ],
        compiler_params=params(16),
        cost_estimate=cost(2 * 10**9, 4 * MIB),
        name="ready",
    )(*pinned(pltpu.HBM, dst_index, mesh_latent, mesh_cot, w_edge1, w_node1, w_node2))
    base, turned = pl.pallas_call(
        functools.partial(base_kernel, lines),
        out_shape=[
            pltpu.VMEM((edges, hidden_width), F32),
            pltpu.HBM((width, edges), BF16),
        ],
        in_specs=specs(pltpu.HBM, 3) + specs(pltpu.VMEM, 1),
        out_specs=specs(pltpu.VMEM, 1) + specs(pltpu.HBM, 1),
        scratch_shapes=[
            pltpu.VMEM((edges, mesh_rows), BF16),
            pltpu.VMEM(edge_latent.shape, BF16),
            pltpu.VMEM((width, hidden_width), BF16),
            pltpu.VMEM((width, edges), BF16),
            pltpu.SemaphoreType.DMA((2 + edges // (128 * lines),)),
            pltpu.SemaphoreType.DMA((1,)),
        ],
        compiler_params=params(16),
        cost_estimate=cost(4 * 10**9, 4 * MIB),
        name="base",
    )(*pinned(pltpu.HBM, hot, edge_latent, w_edge1), *pinned(pltpu.VMEM, moved))

    by_inner = mix([kept, to_core(sent)], inner, outer)
    by_inner = [by_inner[0]] + [to_inner(by_inner[k], k) for k in range(1, inner)]
    by_outer = mix(by_inner, outer, 1)
    slot_blocks = [by_outer[0]] + [to_outer(by_outer[k], k) for k in range(1, outer)]

    grad_rows = 3 * width + hidden_width
    chunk = grad_rows // band_count
    group = (inner * chunk, hidden_width)
    mesh_out, d_slots, *sides = pl.pallas_call(
        functools.partial(main_kernel, lines, sizes),
        out_shape=[
            jax.ShapeDtypeStruct((mesh_rows, width), BF16),
            jax.ShapeDtypeStruct((halfway, width), BF16),
        ]
        + [jax.ShapeDtypeStruct((group[0] + inner * cap, hidden_width), BF16)] * outer
        + [jax.ShapeDtypeStruct(group, F32)] * outer,
        in_specs=specs(pltpu.HBM, 11) + specs(pltpu.VMEM, 1 + outer),
        out_specs=specs(pltpu.VMEM, 2 + 2 * outer),
        scratch_shapes=[
            pltpu.VMEM((edges, hidden_width), F32),
            pltpu.VMEM((edges, hidden_width), BF16),
            pltpu.VMEM((slot_rows + mesh_rows, edges), BF16),
            pltpu.VMEM((grad_rows, hidden_width), F32),
            pltpu.VMEM((slot_rows, width), F32),
            pltpu.VMEM((slot_rows, width), F32),
            pltpu.VMEM(slot_index.shape, jnp.int32),
            pltpu.VMEM(dst_index.shape, jnp.int32),
            pltpu.VMEM(mesh_latent.shape, BF16),
            pltpu.VMEM((width, hidden_width), BF16),
            pltpu.VMEM(w_edge2.shape, BF16),
            pltpu.VMEM((w_node1.shape[0] - width, w_node1.shape[1]), BF16),
            pltpu.VMEM(w_node2.shape, BF16),
            pltpu.VMEM(turned.shape, BF16),
            pltpu.VMEM(hot.shape, BF16),
            pltpu.VMEM(node.shape, F32),
            pltpu.VMEM(cot.shape, F32),
            pltpu.SemaphoreType.DMA((11,)),
        ],
        compiler_params=params(40),
        name="edges",
    )(
        *pinned(pltpu.HBM, slot_index, dst_index, mesh_latent, w_edge1, w_edge2, w_node1, w_node2),
        *pinned(pltpu.HBM, turned, hot, node, cot),
        *pinned(pltpu.VMEM, base),
        *slot_blocks,
    )
    sends, keeps = sides[:outer], sides[outer:]
    small = (2 * cap, width)
    arrived = []
    first = None
    for k in range(outer - 1, -1, -1):
        send = sends[k] if first is None else lax.optimization_barrier((sends[k], first))[0]
        crossed = to_core(send)
        first = crossed if first is None else first
        total, mixed, *parts = pl.pallas_call(
            functools.partial(core_kernel, sizes, k),
            out_shape=[
                jax.ShapeDtypeStruct((chunk, hidden_width), F32),
                jax.ShapeDtypeStruct(small, BF16),
            ]
            + [jax.ShapeDtypeStruct((chunk + 2 * cap, width), BF16)] * (inner - 1),
            compiler_params=params(16),
            cost_estimate=cost(10**9, MIB),
            name="core",
        )(keeps[k], crossed, d_slots)
        parts = [to_inner(part, at + 1) for at, part in enumerate(parts)]
        block = 2 * inner * cap
        if k:
            (out,) = pl.pallas_call(
                functools.partial(inner_kernel, inner - 1, 0),
                out_shape=[jax.ShapeDtypeStruct((chunk + block, width), BF16)],
                compiler_params=params(16),
                name="inner",
            )(total, mixed, *parts)
            arrived.append(to_outer(out, k))
        else:
            own, home = pl.pallas_call(
                functools.partial(inner_kernel, inner - 1, outer - 1),
                out_shape=[
                    jax.ShapeDtypeStruct((chunk, hidden_width), BF16),
                    jax.ShapeDtypeStruct((block, width), BF16),
                ],
                compiler_params=params(16),
                name="own",
            )(total, mixed, *parts, *arrived)

    pieces = {0: own}
    stride = outer // 2
    while stride:
        for at in range(0, outer, 2 * stride):
            pieces[at + stride] = to_outer(pieces[at], stride)
        stride //= 2
    for far_inner in range(1, inner):
        for far_outer in range(outer):
            pieces[far_inner * outer + far_outer] = to_inner(pieces[far_outer], far_inner)
    for at in range(band_count // 2):
        pieces[band_count // 2 + at] = to_core(pieces[at])

    grid_grad = pl.pallas_call(
        functools.partial(put_kernel, sizes),
        out_shape=jax.ShapeDtypeStruct(grid_latent.shape, F32),
        in_specs=specs(pltpu.HBM, 1) + specs(pltpu.VMEM, outer),
        out_specs=pl.BlockSpec(memory_space=pltpu.VMEM),
        scratch_shapes=[
            pltpu.VMEM((slot_rows, width), F32),
            pltpu.VMEM(send_rows.shape, jnp.int32),
            pltpu.SemaphoreType.DMA((1,)),
        ],
        compiler_params=params(16),
        cost_estimate=cost(2 * 10**9, 2 * MIB),
        name="put",
    )(*pinned(pltpu.HBM, send_rows), home, *arrived[::-1])

    late = [at for at in range(band_count) if at % outer == outer - 1]
    early = [at for at in range(band_count) if at % outer != outer - 1]
    grads = []
    for places in (early, late):
        grads = pl.pallas_call(
            functools.partial(order_kernel, sizes, places, len(grads)),
            out_shape=[
                jax.ShapeDtypeStruct((3 * width, hidden_width), F32),
                jax.ShapeDtypeStruct((hidden_width, width), F32),
            ],
            in_specs=specs(pltpu.VMEM, len(places)) + specs(pltpu.HBM, len(grads)),
            out_specs=specs(pltpu.HBM, 2),
            scratch_shapes=[
                pltpu.VMEM((len(places), chunk, hidden_width), F32),
                pltpu.SemaphoreType.DMA((len(places),)),
            ],
            input_output_aliases={len(places) + k: k for k in range(len(grads))},
            compiler_params=params(16),
            cost_estimate=cost(15 * 10**7 * len(places), 2 * MIB),
            name="order",
        )(*[pieces[at] for at in places], *grads)
    grad_edge1, grad_edge2 = grads
    return (mesh_out, grid_grad, grad_edge1, grad_edge2)


def solution(mesh):
    chips = mesh.shape["band"] // 2
    inner = 1
    while inner * inner * 4 <= chips:
        inner *= 2
    sizes = (chips // inner, inner)
    in_specs = (
        P(("groups", "band"), None),
        P(("groups", "band"), None),
        P(("groups", "band"), None),
        P(("groups", "band"), None),
        P("band", None),
        P("band"),
        P("band"),
        P(),
        P(),
        P(),
        P(),
    )
    out_specs = (
        P(("groups", "band"), None),
        P(("groups", "band"), None),
        P("groups", None),
        P("groups", None),
    )
    return jax.shard_map(
        functools.partial(shards, sizes), mesh=mesh, in_specs=in_specs, out_specs=out_specs, check_vma=False
    )
```

```python
import functools

import jax
import jax.numpy as jnp
from jax import lax
from jax.experimental import pallas as pl
from jax.experimental.pallas import tpu as pltpu
from jax.sharding import PartitionSpec as P

BF16 = jnp.bfloat16
F32 = jnp.float32
MIB = 1024 * 1024


def dot_nn(a, b):
    return jnp.dot(a, b, preferred_element_type=F32)


def dot_tn(a, b):
    return lax.dot_general(a, b, (((0,), (0,)), ((), ())), preferred_element_type=F32)


def dot_nt(a, b):
    return lax.dot_general(a, b, (((1,), (1,)), ((), ())), preferred_element_type=F32)


def split(value):
    high = value.astype(BF16)
    low = (value - high.astype(F32)).astype(BF16)
    return high, low


def one_hot_rows(index_row, rows):
    shape = (rows, index_row.shape[1])
    hit = lax.broadcasted_iota(jnp.int32, shape, 0) == index_row
    return jnp.where(hit, 1.0, 0.0).astype(BF16)


def one_hot_columns(index_row, columns):
    lanes = index_row.shape[1]
    index = jnp.transpose(jnp.broadcast_to(index_row, (lanes, lanes)))
    pieces = []
    for start in range(0, columns, lanes):
        hit = lax.broadcasted_iota(jnp.int32, (lanes, lanes), 1) + start == index
        pieces.append(jnp.where(hit, 1.0, 0.0).astype(BF16))
    return pieces[0] if len(pieces) == 1 else jnp.concatenate(pieces, axis=1)


def tile_rows(index_ref, at, lines, rows):
    found = [one_hot_rows(index_ref[pl.ds(at * lines + k, 1), :], rows) for k in range(lines)]
    return jnp.concatenate(found, axis=1)


def tile_columns(index_ref, at, lines, columns):
    found = [one_hot_columns(index_ref[pl.ds(at * lines + k, 1), :], columns) for k in range(lines)]
    return jnp.concatenate(found, axis=0)


def place_of(sizes):
    outer, inner = sizes
    me = lax.axis_index("band")
    return me // (2 * inner), (me // 2) % inner, me % 2


def owner_at(sizes, far_outer, far_inner, far_core):
    my_outer, my_inner, my_core = place_of(sizes)
    return ((my_outer ^ far_outer) * sizes[1] + (my_inner ^ far_inner)) * 2 + (my_core ^ far_core)


def params(mib):
    return pltpu.CompilerParams(vmem_limit_bytes=mib * MIB)


def pinned(space, *values):
    return [pltpu.with_memory_space_constraint(value, space) for value in values]


def specs(space, count):
    return [pl.BlockSpec(memory_space=space)] * count


def cost(flops, nbytes):
    return pl.CostEstimate(flops=flops, bytes_accessed=nbytes, transcendentals=0)


def load(pairs, sems):
    copies = [pltpu.make_async_copy(source, target, sems.at[at]) for at, (source, target) in enumerate(pairs)]
    for copy in copies:
        copy.start()
    return copies


def pick_kernel(sizes, rows_hbm, grid_hbm, keep_ref, send_ref, rows_ref, grid_ref, picked_ref, sems):
    outer, inner = sizes
    rows_copy, grid_copy = load([(rows_hbm, rows_ref), (grid_hbm, grid_ref)], sems)
    rows_copy.wait()
    picked = picked_ref.shape[0]
    chosen = [one_hot_columns(rows_ref[:, at : at + 128], grid_ref.shape[0]) for at in range(0, picked, 128)]
    grid_copy.wait()
    for at, some in enumerate(chosen):
        picked_ref[at * 128 : (at + 1) * 128, :] = dot_nn(some, grid_ref[...])
    cap = picked // (2 * outer * inner)
    for far_core, target in enumerate((keep_ref, send_ref)):
        blocks = []
        for far_inner in range(inner):
            for far_outer in range(outer):
                owner = owner_at(sizes, far_outer, far_inner, far_core)
                blocks.append(picked_ref[pl.ds(pl.multiple_of(owner * cap, cap), cap), :])
        target[...] = jnp.concatenate(blocks, axis=0).astype(BF16)


def mix_kernel(count, minor, *refs):
    sources, targets = refs[:-count], refs[-count:]
    values = [ref[...].astype(F32) for ref in sources]
    unit = values[0].shape[0] // (count * minor)
    for at, target in enumerate(targets):
        starts = [(at * minor + k) * unit for k in range(minor)]
        blocks = [value[start : start + unit] for start in starts for value in values]
        target[...] = jnp.concatenate(blocks, axis=0).astype(BF16)


def put_kernel(sizes, rows_hbm, *refs):
    outer, inner = sizes
    blocks, (out_ref, ordered_ref, rows_ref, sems) = refs[:outer], refs[outer:]
    (copy,) = load([(rows_hbm, rows_ref)], sems)
    place_rows(sizes, blocks, ordered_ref)
    copy.wait()
    chosen = one_hot_rows(rows_ref[...], out_ref.shape[0])
    out_ref[...] = dot_nn(chosen, ordered_ref[...].astype(BF16))


def place_rows(sizes, blocks, ordered_ref):
    outer, inner = sizes
    cap = ordered_ref.shape[0] // (2 * outer * inner)
    for far_outer, block in enumerate(blocks):
        value = block[block.shape[0] - 2 * inner * cap :, :].astype(F32)
        for at in range(2 * inner):
            owner = owner_at(sizes, far_outer, at // 2, at % 2)
            ordered_ref[pl.ds(pl.multiple_of(owner * cap, cap), cap), :] = value[at * cap : (at + 1) * cap]


def ready_kernel(
    lines,
    dst_hbm,
    mesh_hbm,
    cot_hbm,
    w1_hbm,
    wn1_hbm,
    wn2_hbm,
    hot_hbm,
    node_hbm,
    cot_out_hbm,
    moved_ref,
    dst_ref,
    mesh_ref,
    cot_ref,
    w1_ref,
    wn1_ref,
    wn2_ref,
    hot_ref,
    node_ref,
    cot_out_ref,
    sems,
    out_sems,
):
    width = mesh_ref.shape[1]
    tile = lines * 128
    pairs = [
        (dst_hbm, dst_ref),
        (mesh_hbm, mesh_ref),
        (w1_hbm.at[pl.ds(width, width), :], w1_ref),
        (wn1_hbm.at[pl.ds(0, width), :], wn1_ref),
        (cot_hbm, cot_ref),
        (wn2_hbm, wn2_ref),
    ]
    copies = load(pairs, sems)
    outs = [
        pltpu.make_async_copy(source, target, out_sems.at[at])
        for at, (source, target) in enumerate([(hot_ref, hot_hbm), (node_ref, node_hbm), (cot_out_ref, cot_out_hbm)])
    ]
    copies[0].wait()
    for at in range(hot_ref.shape[0] // tile):
        hot_ref[at * tile : (at + 1) * tile, :] = tile_columns(dst_ref, at, lines, hot_ref.shape[1])
    outs[0].start()
    copies[1].wait()
    copies[3].wait()
    node_ref[...] = dot_nn(mesh_ref[...], wn1_ref[...])
    outs[1].start()
    copies[4].wait()
    copies[5].wait()
    cot_out_ref[...] = dot_nt(cot_ref[...], wn2_ref[...])
    outs[2].start()
    copies[2].wait()
    moved_ref[...] = dot_nn(mesh_ref[...], w1_ref[...]).astype(BF16)
    for copy in outs:
        copy.wait()


def base_kernel(
    lines,
    hot_hbm,
    edge_hbm,
    w1_hbm,
    moved_ref,
    base_ref,
    turned_hbm,
    hot_ref,
    edge_ref,
    w1_ref,
    turned_ref,
    sems,
    out_sems,
):
    width = edge_ref.shape[1]
    tile = lines * 128
    tiles = edge_ref.shape[0] // tile
    pairs = [(w1_hbm.at[pl.ds(2 * width, width), :], w1_ref), (hot_hbm, hot_ref)]
    pairs += [(edge_hbm.at[pl.ds(at * tile, tile), :], edge_ref.at[pl.ds(at * tile, tile), :]) for at in range(tiles)]
    copies = load(pairs, sems)
    same = lax.broadcasted_iota(jnp.int32, (256, 256), 0) == lax.broadcasted_iota(jnp.int32, (256, 256), 1)
    eye = jnp.where(same, 1.0, 0.0).astype(BF16)
    copies[0].wait()
    copies[1].wait()
    for at in range(tiles):
        rows = slice(at * tile, (at + 1) * tile)
        copies[2 + at].wait()
        edge = edge_ref[rows, :]
        for start in range(0, width, 256):
            turned_ref[start : start + 256, rows] = dot_nt(eye, edge[:, start : start + 256]).astype(BF16)
        base_ref[rows, :] = dot_nn(edge, w1_ref[...]) + dot_nn(hot_ref[rows, :], moved_ref[...])
    (last,) = load([(turned_ref, turned_hbm)], out_sems)
    last.wait()


def main_kernel(
    lines,
    sizes,
    slot_hbm,
    dst_hbm,
    mesh_hbm,
    w1_hbm,
    w2_hbm,
    wn1_hbm,
    wn2_hbm,
    turned_hbm,
    hot_hbm,
    node_hbm,
    cot_hbm,
    base_ref,
    *rest,
):
    outer, inner = sizes
    slot_blocks, rest = rest[:outer], rest[outer:]
    mesh_out_hbm, d_slots_ref = rest[:2]
    send_refs, keep_refs, rest = rest[2 : 2 + outer], rest[2 + outer : 2 + 2 * outer], rest[2 + 2 * outer :]
    slope_ref, value_ref, both_ref, grads_ref, slot_grads_ref, ordered_ref = rest[:6]
    slot_ref, dst_ref, mesh_ref, w1_ref, w2_ref, wn1_ref, wn2_ref = rest[6:13]
    turned_ref, hot_ref, node_ref, cot_ref, mesh_out_ref, sems, out_sems = rest[13:]
    width = mesh_ref.shape[1]
    mesh_rows = mesh_ref.shape[0]
    slot_rows = ordered_ref.shape[0]
    tile = lines * 128
    tiles = base_ref.shape[0] // tile
    pairs = [
        (slot_hbm, slot_ref),
        (w1_hbm.at[pl.ds(0, width), :], w1_ref),
        (dst_hbm, dst_ref),
        (w2_hbm, w2_ref),
        (wn1_hbm.at[pl.ds(width, wn1_ref.shape[0]), :], wn1_ref),
        (mesh_hbm, mesh_ref),
        (node_hbm, node_ref),
        (cot_hbm, cot_ref),
        (hot_hbm, hot_ref),
        (wn2_hbm, wn2_ref),
        (turned_hbm, turned_ref),
    ]
    copies = load(pairs, sems)
    place_rows(sizes, slot_blocks, ordered_ref)
    slots_value = ordered_ref[...].astype(BF16)
    for copy in copies[:3]:
        copy.wait()

    slots = slots_value
    slot_pair = jnp.concatenate(split(dot_nn(slots, w1_ref[...])), axis=0)
    for at in range(tiles):
        rows = slice(at * tile, (at + 1) * tile)
        from_slot = tile_columns(slot_ref, at, lines, slot_rows)
        twice = jnp.concatenate([from_slot, from_slot], axis=1)
        pre = base_ref[rows, :] + dot_nn(twice, slot_pair)
        sigma = 0.5 + 0.5 * jnp.tanh(0.5 * pre)
        hidden = pre * sigma
        slope_ref[rows, :] = sigma + hidden * (1.0 - sigma)
        value_ref[rows, :] = hidden.astype(BF16)
        both_ref[:slot_rows, rows] = tile_rows(slot_ref, at, lines, slot_rows)
        both_ref[slot_rows:, rows] = tile_rows(dst_ref, at, lines, mesh_rows)

    for copy in copies[3:-1]:
        copy.wait()
    hidden_sums = dot_nn(both_ref[slot_rows:, :], value_ref[...]).astype(BF16)
    received = dot_nn(hidden_sums, w2_ref[...]).astype(BF16)
    mesh = mesh_ref[...]
    pre_node = node_ref[...] + dot_nn(received, wn1_ref[...])
    sigma = 0.5 + 0.5 * jnp.tanh(0.5 * pre_node)
    node = pre_node * sigma
    slope = sigma + node * (1.0 - sigma)
    d_pre_node = (cot_ref[...] * slope).astype(BF16)
    d_received = dot_nt(d_pre_node, wn1_ref[...]).astype(BF16)
    spread = dot_nt(d_received, w2_ref[...]).astype(BF16)

    for at in range(tiles):
        rows = slice(at * tile, (at + 1) * tile)
        value_ref[rows, :] = (dot_nn(hot_ref[rows, :], spread) * slope_ref[rows, :]).astype(BF16)

    grads_ref[3 * width :, :] = dot_tn(hidden_sums, d_received)
    mesh_out_ref[...] = (mesh.astype(F32) + dot_nn(node.astype(BF16), wn2_ref[...])).astype(BF16)
    (mesh_copy,) = load([(mesh_out_ref, mesh_out_hbm)], out_sems)
    sums = dot_nn(both_ref[...], value_ref[...]).astype(BF16)
    slot_grads_ref[...] = dot_nt(sums[:slot_rows], w1_ref[...])
    grads_ref[:width, :] = dot_tn(slots, sums[:slot_rows])
    grads_ref[width : 2 * width, :] = dot_tn(mesh, sums[slot_rows:])
    copies[-1].wait()
    grads_ref[2 * width : 3 * width, :] = dot_nn(turned_ref[...], value_ref[...])

    chunk = grads_ref.shape[0] // (2 * outer * inner)
    cap = slot_rows // (2 * outer * inner)
    for far_core in range(2):
        for far_outer in range(outer):
            for far_inner in range(inner):
                owner = owner_at(sizes, far_outer, far_inner, far_core)
                at = (far_core * outer + far_outer) * inner + far_inner
                from_rows = pl.ds(pl.multiple_of(owner * cap, cap), cap)
                ordered_ref[at * cap : (at + 1) * cap, :] = slot_grads_ref[from_rows, :]
                value = grads_ref[pl.ds(pl.multiple_of(owner * chunk, chunk), chunk), :]
                rows = slice(far_inner * chunk, (far_inner + 1) * chunk)
                if far_core:
                    send_refs[far_outer][rows, :] = value.astype(BF16)
                else:
                    keep_refs[far_outer][rows, :] = value
    halfway, share = slot_rows // 2, inner * cap
    d_slots_ref[...] = ordered_ref[:halfway, :].astype(BF16)
    for far_outer, send_ref in enumerate(send_refs):
        start = halfway + far_outer * share
        send_ref[inner * chunk :, :] = ordered_ref[start : start + share, :].astype(BF16)
    mesh_copy.wait()


def core_kernel(sizes, far_outer, keep_ref, crossed_ref, d_slots_ref, total_ref, mixed_ref, *part_refs):
    outer, inner = sizes
    chunk = total_ref.shape[0]
    cap = d_slots_ref.shape[0] // (outer * inner)
    start = far_outer * inner * cap
    own = d_slots_ref[start : start + inner * cap, :].astype(F32)
    far = crossed_ref[inner * chunk :, :].astype(F32)
    for far_inner in range(inner):
        rows, slots = slice(far_inner * chunk, (far_inner + 1) * chunk), slice(far_inner * cap, (far_inner + 1) * cap)
        total = keep_ref[rows, :] + crossed_ref[rows, :].astype(F32)
        mixed = jnp.concatenate([own[slots], far[slots]], axis=0).astype(BF16)
        if far_inner:
            part_refs[far_inner - 1][:chunk, :] = total.astype(BF16)
            part_refs[far_inner - 1][chunk:, :] = mixed
        else:
            total_ref[...] = total
            mixed_ref[...] = mixed


def inner_kernel(parts, arrivals, total_ref, mixed_ref, *refs):
    received, arrived, outs = refs[:parts], refs[parts : parts + arrivals], refs[parts + arrivals :]
    chunk = total_ref.shape[0]
    total = total_ref[...]
    mixed = [mixed_ref[...]]
    for part in received:
        total = total + part[:chunk, :].astype(F32)
        mixed.append(part[chunk:, :])
    for value in arrived:
        total = total + value[:chunk, :].astype(F32)
    mixed = jnp.concatenate(mixed, axis=0)
    if len(outs) == 1:
        outs[0][:chunk, :] = total.astype(BF16)
        outs[0][chunk:, :] = mixed
    else:
        outs[0][...] = total.astype(BF16)
        outs[1][...] = mixed


def order_kernel(sizes, places, aliased, *refs):
    outer, inner = sizes
    pieces = refs[: len(places)]
    first_hbm, second_hbm, stage_ref, sems = refs[len(places) + aliased :]
    chunk = pieces[0].shape[0]
    first_chunks = first_hbm.shape[0] // chunk

    def send(k, target, start):
        rows = pl.ds(pl.multiple_of(start, chunk), chunk)
        return pltpu.make_async_copy(stage_ref.at[k], target.at[rows, :], sems.at[k])

    for k, (at, piece) in enumerate(zip(places, pieces)):
        owner = owner_at(sizes, at % outer, at // outer % inner, at // (outer * inner))
        stage_ref[k] = piece[...].astype(F32)

        @pl.when(owner < first_chunks)
        def _():
            send(k, first_hbm, owner * chunk).start()

        @pl.when(owner >= first_chunks)
        def _():
            send(k, second_hbm, (owner - first_chunks) * chunk).start()

    for k in range(len(places)):
        send(k, first_hbm, 0).wait()


def shards(
    sizes,
    grid_latent,
    mesh_latent,
    edge_latent,
    mesh_cot,
    send_rows,
    edge_slot,
    edge_dst,
    w_edge1,
    w_edge2,
    w_node1,
    w_node2,
):
    outer, inner = sizes
    band_count = lax.axis_size("band")
    width = grid_latent.shape[1]
    hidden_width = w_edge1.shape[1]
    edges = edge_latent.shape[0]
    mesh_rows = mesh_latent.shape[0]
    slot_rows = send_rows.shape[1]
    lines = 4
    slot_index = edge_slot.reshape(edges // 128, 128)
    dst_index = edge_dst.reshape(edges // 128, 128)

    def permute(value, stride, size, shift):
        pairs = []
        for source in range(band_count):
            place = (source // stride) % size
            pairs.append((source, source + ((place ^ shift) - place) * stride))
        return lax.ppermute(value, "band", pairs)

    def to_core(value):
        return permute(value, 1, 2, 1)

    def to_inner(value, shift):
        return permute(value, 2, inner, shift)

    def to_outer(value, shift):
        return permute(value, 2 * inner, outer, shift)

    cap, halfway = slot_rows // band_count, slot_rows // 2
    kept, sent = pl.pallas_call(
        functools.partial(pick_kernel, sizes),
        out_shape=[jax.ShapeDtypeStruct((halfway, width), BF16)] * 2,
        in_specs=specs(pltpu.HBM, 2),
        out_specs=specs(pltpu.VMEM, 2),
        scratch_shapes=[
            pltpu.VMEM(send_rows.shape, jnp.int32),
            pltpu.VMEM(grid_latent.shape, BF16),
            pltpu.VMEM((slot_rows, width), F32),
            pltpu.SemaphoreType.DMA((2,)),
        ],
        compiler_params=params(16),
        name="pick",
    )(*pinned(pltpu.HBM, send_rows, grid_latent))

    def mix(values, count, minor):
        rows = len(values) * values[0].shape[0] // count
        return pl.pallas_call(
            functools.partial(mix_kernel, count, minor),
            out_shape=[jax.ShapeDtypeStruct((rows, width), BF16)] * count,
            compiler_params=params(16),
            name="mix",
        )(*values)

    hot, node, cot, moved = pl.pallas_call(
        functools.partial(ready_kernel, lines),
        out_shape=[
            pltpu.HBM((edges, mesh_rows), BF16),
            pltpu.HBM((mesh_rows, hidden_width), F32),
            pltpu.HBM((mesh_rows, hidden_width), F32),
            pltpu.VMEM((mesh_rows, hidden_width), BF16),
        ],
        in_specs=specs(pltpu.HBM, 6),
        out_specs=specs(pltpu.HBM, 3) + specs(pltpu.VMEM, 1),
        scratch_shapes=[
            pltpu.VMEM(dst_index.shape, jnp.int32),
            pltpu.VMEM(mesh_latent.shape, BF16),
            pltpu.VMEM(mesh_cot.shape, BF16),
            pltpu.VMEM((width, hidden_width), BF16),
            pltpu.VMEM((width, hidden_width), BF16),
            pltpu.VMEM(w_node2.shape, BF16),
            pltpu.VMEM((edges, mesh_rows), BF16),
            pltpu.VMEM((mesh_rows, hidden_width), F32),
            pltpu.VMEM((mesh_rows, hidden_width), F32),
            pltpu.SemaphoreType.DMA((6,)),
            pltpu.SemaphoreType.DMA((3,)),
        ],
        compiler_params=params(16),
        cost_estimate=cost(2 * 10**9, 4 * MIB),
        name="ready",
    )(*pinned(pltpu.HBM, dst_index, mesh_latent, mesh_cot, w_edge1, w_node1, w_node2))
    base, turned = pl.pallas_call(
        functools.partial(base_kernel, lines),
        out_shape=[
            pltpu.VMEM((edges, hidden_width), F32),
            pltpu.HBM((width, edges), BF16),
        ],
        in_specs=specs(pltpu.HBM, 3) + specs(pltpu.VMEM, 1),
        out_specs=specs(pltpu.VMEM, 1) + specs(pltpu.HBM, 1),
        scratch_shapes=[
            pltpu.VMEM((edges, mesh_rows), BF16),
            pltpu.VMEM(edge_latent.shape, BF16),
            pltpu.VMEM((width, hidden_width), BF16),
            pltpu.VMEM((width, edges), BF16),
            pltpu.SemaphoreType.DMA((2 + edges // (128 * lines),)),
            pltpu.SemaphoreType.DMA((1,)),
        ],
        compiler_params=params(16),
        cost_estimate=cost(4 * 10**9, 4 * MIB),
        name="base",
    )(*pinned(pltpu.HBM, hot, edge_latent, w_edge1), *pinned(pltpu.VMEM, moved))

    by_inner = mix([kept, to_core(sent)], inner, outer)
    by_inner = [by_inner[0]] + [to_inner(by_inner[k], k) for k in range(1, inner)]
    by_outer = mix(by_inner, outer, 1)
    slot_blocks = [by_outer[0]] + [to_outer(by_outer[k], k) for k in range(1, outer)]

    grad_rows = 3 * width + hidden_width
    chunk = grad_rows // band_count
    group = (inner * chunk, hidden_width)
    mesh_out, d_slots, *sides = pl.pallas_call(
        functools.partial(main_kernel, lines, sizes),
        out_shape=[
            jax.ShapeDtypeStruct((mesh_rows, width), BF16),
            jax.ShapeDtypeStruct((halfway, width), BF16),
        ]
        + [jax.ShapeDtypeStruct((group[0] + inner * cap, hidden_width), BF16)] * outer
        + [jax.ShapeDtypeStruct(group, F32)] * outer,
        in_specs=specs(pltpu.HBM, 11) + specs(pltpu.VMEM, 1 + outer),
        out_specs=specs(pltpu.HBM, 1) + specs(pltpu.VMEM, 1 + 2 * outer),
        scratch_shapes=[
            pltpu.VMEM((edges, hidden_width), F32),
            pltpu.VMEM((edges, hidden_width), BF16),
            pltpu.VMEM((slot_rows + mesh_rows, edges), BF16),
            pltpu.VMEM((grad_rows, hidden_width), F32),
            pltpu.VMEM((slot_rows, width), F32),
            pltpu.VMEM((slot_rows, width), F32),
            pltpu.VMEM(slot_index.shape, jnp.int32),
            pltpu.VMEM(dst_index.shape, jnp.int32),
            pltpu.VMEM(mesh_latent.shape, BF16),
            pltpu.VMEM((width, hidden_width), BF16),
            pltpu.VMEM(w_edge2.shape, BF16),
            pltpu.VMEM((w_node1.shape[0] - width, w_node1.shape[1]), BF16),
            pltpu.VMEM(w_node2.shape, BF16),
            pltpu.VMEM(turned.shape, BF16),
            pltpu.VMEM(hot.shape, BF16),
            pltpu.VMEM(node.shape, F32),
            pltpu.VMEM(cot.shape, F32),
            pltpu.VMEM((mesh_rows, width), BF16),
            pltpu.SemaphoreType.DMA((11,)),
            pltpu.SemaphoreType.DMA((1,)),
        ],
        compiler_params=params(40),
        name="edges",
    )(
        *pinned(pltpu.HBM, slot_index, dst_index, mesh_latent, w_edge1, w_edge2, w_node1, w_node2),
        *pinned(pltpu.HBM, turned, hot, node, cot),
        *pinned(pltpu.VMEM, base),
        *slot_blocks,
    )
    sends, keeps = sides[:outer], sides[outer:]
    small = (2 * cap, width)
    arrived, before = [], []
    first = None
    for k in range(outer - 1, -1, -1):
        send = sends[k] if first is None else lax.optimization_barrier((sends[k], first))[0]
        crossed = to_core(send)
        first = crossed if first is None else first
        total, mixed, *parts = pl.pallas_call(
            functools.partial(core_kernel, sizes, k),
            out_shape=[
                jax.ShapeDtypeStruct((chunk, hidden_width), F32),
                jax.ShapeDtypeStruct(small, BF16),
            ]
            + [jax.ShapeDtypeStruct((chunk + 2 * cap, width), BF16)] * (inner - 1),
            compiler_params=params(16),
            cost_estimate=cost(10**9, MIB),
            name="core",
        )(keeps[k], crossed, d_slots)
        parts = [lax.optimization_barrier((part, *before))[0] for part in parts]
        parts = [to_inner(part, at + 1) for at, part in enumerate(parts)]
        before = parts if k >= outer - 2 else before
        block = 2 * inner * cap
        if k:
            (out,) = pl.pallas_call(
                functools.partial(inner_kernel, inner - 1, 0),
                out_shape=[jax.ShapeDtypeStruct((chunk + block, width), BF16)],
                compiler_params=params(16),
                name="inner",
            )(total, mixed, *parts)
            arrived.append(to_outer(out, k))
        else:
            own, home = pl.pallas_call(
                functools.partial(inner_kernel, inner - 1, outer - 1),
                out_shape=[
                    jax.ShapeDtypeStruct((chunk, hidden_width), BF16),
                    jax.ShapeDtypeStruct((block, width), BF16),
                ],
                compiler_params=params(16),
                name="own",
            )(total, mixed, *parts, *arrived)

    pieces = {0: own}
    stride = outer // 2
    while stride:
        for at in range(0, outer, 2 * stride):
            pieces[at + stride] = to_outer(pieces[at], stride)
        stride //= 2
    halfway_at = band_count // 2
    pieces[halfway_at] = to_core(own)
    for far_inner in range(1, inner):
        for far_outer in range(outer):
            value = pieces[far_outer]
            if far_outer == outer // 2:
                value = lax.optimization_barrier((value, pieces[halfway_at]))[0]
            pieces[far_inner * outer + far_outer] = to_inner(value, far_inner)
    for at in range(1, halfway_at):
        pieces[halfway_at + at] = to_core(pieces[at])

    grid_grad = pl.pallas_call(
        functools.partial(put_kernel, sizes),
        out_shape=jax.ShapeDtypeStruct(grid_latent.shape, F32),
        in_specs=specs(pltpu.HBM, 1) + specs(pltpu.VMEM, outer),
        out_specs=pl.BlockSpec(memory_space=pltpu.VMEM),
        scratch_shapes=[
            pltpu.VMEM((slot_rows, width), F32),
            pltpu.VMEM(send_rows.shape, jnp.int32),
            pltpu.SemaphoreType.DMA((1,)),
        ],
        compiler_params=params(16),
        cost_estimate=cost(2 * 10**9, 2 * MIB),
        name="put",
    )(*pinned(pltpu.HBM, send_rows), home, *arrived[::-1])

    last = outer - 1
    stages = [[], [], []]
    for at in range(band_count):
        far_outer, far_inner, far_core = at % outer, at // outer % inner, at // halfway_at
        if far_outer == last:
            stages[2 if far_inner else 1].append(at)
        else:
            stages[1 if far_inner and (far_core or far_outer == outer // 2) else 0].append(at)
    grads = []
    for places in stages:
        grads = pl.pallas_call(
            functools.partial(order_kernel, sizes, places, len(grads)),
            out_shape=[
                jax.ShapeDtypeStruct((3 * width, hidden_width), F32),
                jax.ShapeDtypeStruct((hidden_width, width), F32),
            ],
            in_specs=specs(pltpu.VMEM, len(places)) + specs(pltpu.HBM, len(grads)),
            out_specs=specs(pltpu.HBM, 2),
            scratch_shapes=[
                pltpu.VMEM((len(places), chunk, hidden_width), F32),
                pltpu.SemaphoreType.DMA((len(places),)),
            ],
            input_output_aliases={len(places) + k: k for k in range(len(grads))},
            compiler_params=params(16),
            cost_estimate=cost(15 * 10**7 * len(places), 2 * MIB),
            name="order",
        )(*[pieces[at] for at in places], *grads)
    grad_edge1, grad_edge2 = grads
    return (mesh_out, grid_grad, grad_edge1, grad_edge2)


def solution(mesh):
    chips = mesh.shape["band"] // 2
    inner = 1
    while inner * inner * 4 <= chips:
        inner *= 2
    sizes = (chips // inner, inner)
    in_specs = (
        P(("groups", "band"), None),
        P(("groups", "band"), None),
        P(("groups", "band"), None),
        P(("groups", "band"), None),
        P("band", None),
        P("band"),
        P("band"),
        P(),
        P(),
        P(),
        P(),
    )
    out_specs = (
        P(("groups", "band"), None),
        P(("groups", "band"), None),
        P("groups", None),
        P("groups", None),
    )
    return jax.shard_map(
        functools.partial(shards, sizes), mesh=mesh, in_specs=in_specs, out_specs=out_specs, check_vma=False
    )
```

```python
import functools

import jax
import jax.numpy as jnp
from jax import lax
from jax.experimental import pallas as pl
from jax.experimental.pallas import tpu as pltpu
from jax.sharding import PartitionSpec as P

BF16 = jnp.bfloat16
F32 = jnp.float32
MIB = 1024 * 1024


def dot_nn(a, b):
    return jnp.dot(a, b, preferred_element_type=F32)


def dot_tn(a, b):
    return lax.dot_general(a, b, (((0,), (0,)), ((), ())), preferred_element_type=F32)


def dot_nt(a, b):
    return lax.dot_general(a, b, (((1,), (1,)), ((), ())), preferred_element_type=F32)


def split(value):
    high = value.astype(BF16)
    low = (value - high.astype(F32)).astype(BF16)
    return high, low


def one_hot_rows(index_row, rows):
    shape = (rows, index_row.shape[1])
    hit = lax.broadcasted_iota(jnp.int32, shape, 0) == index_row
    return jnp.where(hit, 1.0, 0.0).astype(BF16)


def one_hot_columns(index_row, columns):
    lanes = index_row.shape[1]
    index = jnp.transpose(jnp.broadcast_to(index_row, (lanes, lanes)))
    pieces = []
    for start in range(0, columns, lanes):
        hit = lax.broadcasted_iota(jnp.int32, (lanes, lanes), 1) + start == index
        pieces.append(jnp.where(hit, 1.0, 0.0).astype(BF16))
    return pieces[0] if len(pieces) == 1 else jnp.concatenate(pieces, axis=1)


def tile_rows(index_ref, at, lines, rows):
    found = [one_hot_rows(index_ref[pl.ds(at * lines + k, 1), :], rows) for k in range(lines)]
    return jnp.concatenate(found, axis=1)


def tile_columns(index_ref, at, lines, columns):
    found = [one_hot_columns(index_ref[pl.ds(at * lines + k, 1), :], columns) for k in range(lines)]
    return jnp.concatenate(found, axis=0)


def place_of(sizes):
    outer, inner = sizes
    me = lax.axis_index("band")
    return me // (2 * inner), (me // 2) % inner, me % 2


def owner_at(sizes, far_outer, far_inner, far_core):
    my_outer, my_inner, my_core = place_of(sizes)
    return ((my_outer ^ far_outer) * sizes[1] + (my_inner ^ far_inner)) * 2 + (my_core ^ far_core)


def params(mib):
    return pltpu.CompilerParams(vmem_limit_bytes=mib * MIB)


def pinned(space, *values):
    return [pltpu.with_memory_space_constraint(value, space) for value in values]


def specs(space, count):
    return [pl.BlockSpec(memory_space=space)] * count


def cost(flops, nbytes):
    return pl.CostEstimate(flops=flops, bytes_accessed=nbytes, transcendentals=0)


def load(pairs, sems):
    copies = [pltpu.make_async_copy(source, target, sems.at[at]) for at, (source, target) in enumerate(pairs)]
    for copy in copies:
        copy.start()
    return copies


def pick_kernel(sizes, rows_hbm, grid_hbm, keep_ref, send_ref, rows_ref, grid_ref, picked_ref, sems):
    outer, inner = sizes
    rows_copy, grid_copy = load([(rows_hbm, rows_ref), (grid_hbm, grid_ref)], sems)
    rows_copy.wait()
    picked = picked_ref.shape[0]
    chosen = [one_hot_columns(rows_ref[:, at : at + 128], grid_ref.shape[0]) for at in range(0, picked, 128)]
    grid_copy.wait()
    for at, some in enumerate(chosen):
        picked_ref[at * 128 : (at + 1) * 128, :] = dot_nn(some, grid_ref[...])
    cap = picked // (2 * outer * inner)
    for far_core, target in enumerate((keep_ref, send_ref)):
        blocks = []
        for far_inner in range(inner):
            for far_outer in range(outer):
                owner = owner_at(sizes, far_outer, far_inner, far_core)
                blocks.append(picked_ref[pl.ds(pl.multiple_of(owner * cap, cap), cap), :])
        target[...] = jnp.concatenate(blocks, axis=0).astype(BF16)


def mix_kernel(count, minor, *refs):
    sources, targets = refs[:-count], refs[-count:]
    values = [ref[...].astype(F32) for ref in sources]
    unit = values[0].shape[0] // (count * minor)
    for at, target in enumerate(targets):
        starts = [(at * minor + k) * unit for k in range(minor)]
        blocks = [value[start : start + unit] for start in starts for value in values]
        target[...] = jnp.concatenate(blocks, axis=0).astype(BF16)


def put_kernel(sizes, rows_hbm, *refs):
    outer, inner = sizes
    blocks, (out_ref, ordered_ref, rows_ref, sems) = refs[:outer], refs[outer:]
    (copy,) = load([(rows_hbm, rows_ref)], sems)
    place_rows(sizes, blocks, ordered_ref)
    copy.wait()
    chosen = one_hot_rows(rows_ref[...], out_ref.shape[0])
    out_ref[...] = dot_nn(chosen, ordered_ref[...].astype(BF16))


def place_rows(sizes, blocks, ordered_ref):
    outer, inner = sizes
    cap = ordered_ref.shape[0] // (2 * outer * inner)
    for far_outer, block in enumerate(blocks):
        value = block[block.shape[0] - 2 * inner * cap :, :].astype(F32)
        for at in range(2 * inner):
            owner = owner_at(sizes, far_outer, at // 2, at % 2)
            ordered_ref[pl.ds(pl.multiple_of(owner * cap, cap), cap), :] = value[at * cap : (at + 1) * cap]


def ready_kernel(
    lines,
    dst_hbm,
    mesh_hbm,
    cot_hbm,
    w1_hbm,
    wn1_hbm,
    wn2_hbm,
    hot_hbm,
    node_hbm,
    cot_out_hbm,
    moved_ref,
    dst_ref,
    mesh_ref,
    cot_ref,
    w1_ref,
    wn1_ref,
    wn2_ref,
    hot_ref,
    node_ref,
    cot_out_ref,
    sems,
    out_sems,
):
    width = mesh_ref.shape[1]
    tile = lines * 128
    pairs = [
        (dst_hbm, dst_ref),
        (mesh_hbm, mesh_ref),
        (w1_hbm.at[pl.ds(width, width), :], w1_ref),
        (wn1_hbm.at[pl.ds(0, width), :], wn1_ref),
        (cot_hbm, cot_ref),
        (wn2_hbm, wn2_ref),
    ]
    copies = load(pairs, sems)
    outs = [
        pltpu.make_async_copy(source, target, out_sems.at[at])
        for at, (source, target) in enumerate([(hot_ref, hot_hbm), (node_ref, node_hbm), (cot_out_ref, cot_out_hbm)])
    ]
    copies[0].wait()
    for at in range(hot_ref.shape[0] // tile):
        hot_ref[at * tile : (at + 1) * tile, :] = tile_columns(dst_ref, at, lines, hot_ref.shape[1])
    outs[0].start()
    copies[1].wait()
    copies[3].wait()
    node_ref[...] = dot_nn(mesh_ref[...], wn1_ref[...])
    outs[1].start()
    copies[4].wait()
    copies[5].wait()
    cot_out_ref[...] = dot_nt(cot_ref[...], wn2_ref[...])
    outs[2].start()
    copies[2].wait()
    moved_ref[...] = dot_nn(mesh_ref[...], w1_ref[...]).astype(BF16)
    for copy in outs:
        copy.wait()


def base_kernel(
    lines,
    hot_hbm,
    edge_hbm,
    w1_hbm,
    moved_ref,
    base_ref,
    turned_hbm,
    hot_ref,
    edge_ref,
    w1_ref,
    turned_ref,
    sems,
    out_sems,
):
    width = edge_ref.shape[1]
    tile = lines * 128
    tiles = edge_ref.shape[0] // tile
    pairs = [(edge_hbm.at[pl.ds(at * tile, tile), :], edge_ref.at[pl.ds(at * tile, tile), :]) for at in range(tiles)]
    pairs[1:1] = [(w1_hbm.at[pl.ds(2 * width, width), :], w1_ref), (hot_hbm, hot_ref)]
    copies = load(pairs, sems)
    same = lax.broadcasted_iota(jnp.int32, (256, 256), 0) == lax.broadcasted_iota(jnp.int32, (256, 256), 1)
    eye = jnp.where(same, 1.0, 0.0).astype(BF16)
    outs = []
    for at in range(tiles):
        rows = slice(at * tile, (at + 1) * tile)
        copies[2 + at if at else 0].wait()
        edge = edge_ref[rows, :]
        for start in range(0, width, 256):
            turned_ref[start : start + 256, rows] = dot_nt(eye, edge[:, start : start + 256]).astype(BF16)
        out = pltpu.make_async_copy(turned_ref.at[:, pl.ds(at * tile, tile)], turned_hbm.at[:, pl.ds(at * tile, tile)], out_sems.at[at])
        out.start()
        outs.append(out)
        if at == 0:
            copies[1].wait()
            copies[2].wait()
        base_ref[rows, :] = dot_nn(edge, w1_ref[...]) + dot_nn(hot_ref[rows, :], moved_ref[...])
    for out in outs:
        out.wait()


def main_kernel(
    lines,
    sizes,
    slot_hbm,
    dst_hbm,
    mesh_hbm,
    w1_hbm,
    w2_hbm,
    wn1_hbm,
    wn2_hbm,
    turned_hbm,
    hot_hbm,
    node_hbm,
    cot_hbm,
    base_ref,
    *rest,
):
    outer, inner = sizes
    slot_blocks, rest = rest[:outer], rest[outer:]
    mesh_out_hbm, d_slots_ref = rest[:2]
    send_refs, keep_refs, rest = rest[2 : 2 + outer], rest[2 + outer : 2 + 2 * outer], rest[2 + 2 * outer :]
    slope_ref, value_ref, both_ref, grads_ref, slot_grads_ref, ordered_ref = rest[:6]
    slot_ref, dst_ref, mesh_ref, w1_ref, w2_ref, wn1_ref, wn2_ref = rest[6:13]
    turned_ref, hot_ref, node_ref, cot_ref, mesh_out_ref, picks_ref, sems, out_sems = rest[13:]
    width = mesh_ref.shape[1]
    mesh_rows = mesh_ref.shape[0]
    slot_rows = ordered_ref.shape[0]
    tile = lines * 128
    tiles = base_ref.shape[0] // tile
    pairs = [
        (slot_hbm, slot_ref),
        (dst_hbm, dst_ref),
        (w1_hbm.at[pl.ds(0, width), :], w1_ref),
        (w2_hbm, w2_ref),
        (wn1_hbm.at[pl.ds(width, wn1_ref.shape[0]), :], wn1_ref),
        (mesh_hbm, mesh_ref),
        (node_hbm, node_ref),
        (cot_hbm, cot_ref),
        (hot_hbm, hot_ref),
        (wn2_hbm, wn2_ref),
        (turned_hbm, turned_ref),
    ]
    copies = load(pairs, sems)
    place_rows(sizes, slot_blocks, ordered_ref)
    slots_value = ordered_ref[...].astype(BF16)
    for copy in copies[:2]:
        copy.wait()
    for at in range(tiles):
        rows = slice(at * tile, (at + 1) * tile)
        picks_ref[rows, :] = tile_columns(slot_ref, at, lines, slot_rows)
        both_ref[:slot_rows, rows] = tile_rows(slot_ref, at, lines, slot_rows)
        both_ref[slot_rows:, rows] = tile_rows(dst_ref, at, lines, mesh_rows)
    copies[2].wait()

    slots = slots_value
    slot_pair = jnp.concatenate(split(dot_nn(slots, w1_ref[...])), axis=0)
    for at in range(tiles):
        rows = slice(at * tile, (at + 1) * tile)
        from_slot = picks_ref[rows, :]
        twice = jnp.concatenate([from_slot, from_slot], axis=1)
        pre = base_ref[rows, :] + dot_nn(twice, slot_pair)
        sigma = 0.5 + 0.5 * jnp.tanh(0.5 * pre)
        hidden = pre * sigma
        slope_ref[rows, :] = sigma + hidden * (1.0 - sigma)
        value_ref[rows, :] = hidden.astype(BF16)

    for copy in copies[3:-1]:
        copy.wait()
    hidden_sums = dot_nn(both_ref[slot_rows:, :], value_ref[...]).astype(BF16)
    received = dot_nn(hidden_sums, w2_ref[...]).astype(BF16)
    mesh = mesh_ref[...]
    pre_node = node_ref[...] + dot_nn(received, wn1_ref[...])
    sigma = 0.5 + 0.5 * jnp.tanh(0.5 * pre_node)
    node = pre_node * sigma
    slope = sigma + node * (1.0 - sigma)
    d_pre_node = (cot_ref[...] * slope).astype(BF16)
    d_received = dot_nt(d_pre_node, wn1_ref[...]).astype(BF16)
    spread = dot_nt(d_received, w2_ref[...]).astype(BF16)

    for at in range(tiles):
        rows = slice(at * tile, (at + 1) * tile)
        value_ref[rows, :] = (dot_nn(hot_ref[rows, :], spread) * slope_ref[rows, :]).astype(BF16)

    grads_ref[3 * width :, :] = dot_tn(hidden_sums, d_received)
    mesh_out_ref[...] = (mesh.astype(F32) + dot_nn(node.astype(BF16), wn2_ref[...])).astype(BF16)
    (mesh_copy,) = load([(mesh_out_ref, mesh_out_hbm)], out_sems)
    sums = dot_nn(both_ref[...], value_ref[...]).astype(BF16)
    slot_grads_ref[...] = dot_nt(sums[:slot_rows], w1_ref[...])
    grads_ref[:width, :] = dot_tn(slots, sums[:slot_rows])
    grads_ref[width : 2 * width, :] = dot_tn(mesh, sums[slot_rows:])
    copies[-1].wait()
    grads_ref[2 * width : 3 * width, :] = dot_nn(turned_ref[...], value_ref[...])

    chunk = grads_ref.shape[0] // (2 * outer * inner)
    cap = slot_rows // (2 * outer * inner)
    for far_core in range(2):
        for far_outer in range(outer):
            for far_inner in range(inner):
                owner = owner_at(sizes, far_outer, far_inner, far_core)
                at = (far_core * outer + far_outer) * inner + far_inner
                from_rows = pl.ds(pl.multiple_of(owner * cap, cap), cap)
                ordered_ref[at * cap : (at + 1) * cap, :] = slot_grads_ref[from_rows, :]
                value = grads_ref[pl.ds(pl.multiple_of(owner * chunk, chunk), chunk), :]
                rows = slice(far_inner * chunk, (far_inner + 1) * chunk)
                if far_core:
                    send_refs[far_outer][rows, :] = value.astype(BF16)
                else:
                    keep_refs[far_outer][rows, :] = value
    halfway, share = slot_rows // 2, inner * cap
    d_slots_ref[...] = ordered_ref[:halfway, :].astype(BF16)
    for far_outer, send_ref in enumerate(send_refs):
        start = halfway + far_outer * share
        send_ref[inner * chunk :, :] = ordered_ref[start : start + share, :].astype(BF16)
    mesh_copy.wait()


def core_kernel(sizes, far_outer, keep_ref, crossed_ref, d_slots_ref, total_ref, mixed_ref, *part_refs):
    outer, inner = sizes
    chunk = total_ref.shape[0]
    cap = d_slots_ref.shape[0] // (outer * inner)
    start = far_outer * inner * cap
    own = d_slots_ref[start : start + inner * cap, :].astype(F32)
    far = crossed_ref[inner * chunk :, :].astype(F32)
    for far_inner in range(inner):
        rows, slots = slice(far_inner * chunk, (far_inner + 1) * chunk), slice(far_inner * cap, (far_inner + 1) * cap)
        total = keep_ref[rows, :] + crossed_ref[rows, :].astype(F32)
        mixed = jnp.concatenate([own[slots], far[slots]], axis=0).astype(BF16)
        if far_inner:
            part_refs[far_inner - 1][:chunk, :] = total.astype(BF16)
            part_refs[far_inner - 1][chunk:, :] = mixed
        else:
            total_ref[...] = total
            mixed_ref[...] = mixed


def inner_kernel(parts, arrivals, total_ref, mixed_ref, *refs):
    received, arrived, outs = refs[:parts], refs[parts : parts + arrivals], refs[parts + arrivals :]
    chunk = total_ref.shape[0]
    total = total_ref[...]
    mixed = [mixed_ref[...]]
    for part in received:
        total = total + part[:chunk, :].astype(F32)
        mixed.append(part[chunk:, :])
    for value in arrived:
        total = total + value[:chunk, :].astype(F32)
    mixed = jnp.concatenate(mixed, axis=0)
    if len(outs) == 1:
        outs[0][:chunk, :] = total.astype(BF16)
        outs[0][chunk:, :] = mixed
    else:
        outs[0][...] = total.astype(BF16)
        outs[1][...] = mixed


def order_kernel(sizes, places, aliased, *refs):
    outer, inner = sizes
    pieces = refs[: len(places)]
    first_hbm, second_hbm, stage_ref, sems = refs[len(places) + aliased :]
    chunk = pieces[0].shape[0]
    first_chunks = first_hbm.shape[0] // chunk

    def send(k, target, start):
        rows = pl.ds(pl.multiple_of(start, chunk), chunk)
        return pltpu.make_async_copy(stage_ref.at[k], target.at[rows, :], sems.at[k])

    for k, (at, piece) in enumerate(zip(places, pieces)):
        owner = owner_at(sizes, at % outer, at // outer % inner, at // (outer * inner))
        stage_ref[k] = piece[...].astype(F32)

        @pl.when(owner < first_chunks)
        def _():
            send(k, first_hbm, owner * chunk).start()

        @pl.when(owner >= first_chunks)
        def _():
            send(k, second_hbm, (owner - first_chunks) * chunk).start()

    for k in range(len(places)):
        send(k, first_hbm, 0).wait()


def shards(
    sizes,
    grid_latent,
    mesh_latent,
    edge_latent,
    mesh_cot,
    send_rows,
    edge_slot,
    edge_dst,
    w_edge1,
    w_edge2,
    w_node1,
    w_node2,
):
    outer, inner = sizes
    band_count = lax.axis_size("band")
    width = grid_latent.shape[1]
    hidden_width = w_edge1.shape[1]
    edges = edge_latent.shape[0]
    mesh_rows = mesh_latent.shape[0]
    slot_rows = send_rows.shape[1]
    lines = 4
    slot_index = edge_slot.reshape(edges // 128, 128)
    dst_index = edge_dst.reshape(edges // 128, 128)

    def permute(value, stride, size, shift):
        pairs = []
        for source in range(band_count):
            place = (source // stride) % size
            pairs.append((source, source + ((place ^ shift) - place) * stride))
        return lax.ppermute(value, "band", pairs)

    def to_core(value):
        return permute(value, 1, 2, 1)

    def to_inner(value, shift):
        return permute(value, 2, inner, shift)

    def to_outer(value, shift):
        return permute(value, 2 * inner, outer, shift)

    cap, halfway = slot_rows // band_count, slot_rows // 2
    kept, sent = pl.pallas_call(
        functools.partial(pick_kernel, sizes),
        out_shape=[jax.ShapeDtypeStruct((halfway, width), BF16)] * 2,
        in_specs=specs(pltpu.HBM, 2),
        out_specs=specs(pltpu.VMEM, 2),
        scratch_shapes=[
            pltpu.VMEM(send_rows.shape, jnp.int32),
            pltpu.VMEM(grid_latent.shape, BF16),
            pltpu.VMEM((slot_rows, width), F32),
            pltpu.SemaphoreType.DMA((2,)),
        ],
        compiler_params=params(16),
        name="pick",
    )(*pinned(pltpu.HBM, send_rows, grid_latent))

    def mix(values, count, minor):
        rows = len(values) * values[0].shape[0] // count
        return pl.pallas_call(
            functools.partial(mix_kernel, count, minor),
            out_shape=[jax.ShapeDtypeStruct((rows, width), BF16)] * count,
            compiler_params=params(16),
            name="mix",
        )(*values)

    hot, node, cot, moved = pl.pallas_call(
        functools.partial(ready_kernel, lines),
        out_shape=[
            pltpu.HBM((edges, mesh_rows), BF16),
            pltpu.HBM((mesh_rows, hidden_width), F32),
            pltpu.HBM((mesh_rows, hidden_width), F32),
            pltpu.VMEM((mesh_rows, hidden_width), BF16),
        ],
        in_specs=specs(pltpu.HBM, 6),
        out_specs=specs(pltpu.HBM, 3) + specs(pltpu.VMEM, 1),
        scratch_shapes=[
            pltpu.VMEM(dst_index.shape, jnp.int32),
            pltpu.VMEM(mesh_latent.shape, BF16),
            pltpu.VMEM(mesh_cot.shape, BF16),
            pltpu.VMEM((width, hidden_width), BF16),
            pltpu.VMEM((width, hidden_width), BF16),
            pltpu.VMEM(w_node2.shape, BF16),
            pltpu.VMEM((edges, mesh_rows), BF16),
            pltpu.VMEM((mesh_rows, hidden_width), F32),
            pltpu.VMEM((mesh_rows, hidden_width), F32),
            pltpu.SemaphoreType.DMA((6,)),
            pltpu.SemaphoreType.DMA((3,)),
        ],
        compiler_params=params(16),
        cost_estimate=cost(2 * 10**9, 4 * MIB),
        name="ready",
    )(*pinned(pltpu.HBM, dst_index, mesh_latent, mesh_cot, w_edge1, w_node1, w_node2))
    base, turned = pl.pallas_call(
        functools.partial(base_kernel, lines),
        out_shape=[
            pltpu.VMEM((edges, hidden_width), F32),
            pltpu.HBM((width, edges), BF16),
        ],
        in_specs=specs(pltpu.HBM, 3) + specs(pltpu.VMEM, 1),
        out_specs=specs(pltpu.VMEM, 1) + specs(pltpu.HBM, 1),
        scratch_shapes=[
            pltpu.VMEM((edges, mesh_rows), BF16),
            pltpu.VMEM(edge_latent.shape, BF16),
            pltpu.VMEM((width, hidden_width), BF16),
            pltpu.VMEM((width, edges), BF16),
            pltpu.SemaphoreType.DMA((2 + edges // (128 * lines),)),
            pltpu.SemaphoreType.DMA((edges // (128 * lines),)),
        ],
        compiler_params=params(16),
        cost_estimate=cost(4 * 10**9, 4 * MIB),
        name="base",
    )(*pinned(pltpu.HBM, hot, edge_latent, w_edge1), *pinned(pltpu.VMEM, moved))

    by_inner = mix([kept, to_core(sent)], inner, outer)
    by_inner = [by_inner[0]] + [to_inner(by_inner[k], k) for k in range(1, inner)]
    by_outer = mix(by_inner, outer, 1)
    slot_blocks = [by_outer[0]] + [to_outer(by_outer[k], k) for k in range(1, outer)]

    grad_rows = 3 * width + hidden_width
    chunk = grad_rows // band_count
    group = (inner * chunk, hidden_width)
    mesh_out, d_slots, *sides = pl.pallas_call(
        functools.partial(main_kernel, lines, sizes),
        out_shape=[
            jax.ShapeDtypeStruct((mesh_rows, width), BF16),
            jax.ShapeDtypeStruct((halfway, width), BF16),
        ]
        + [jax.ShapeDtypeStruct((group[0] + inner * cap, hidden_width), BF16)] * outer
        + [jax.ShapeDtypeStruct(group, F32)] * outer,
        in_specs=specs(pltpu.HBM, 11) + specs(pltpu.VMEM, 1 + outer),
        out_specs=specs(pltpu.HBM, 1) + specs(pltpu.VMEM, 1 + 2 * outer),
        scratch_shapes=[
            pltpu.VMEM((edges, hidden_width), F32),
            pltpu.VMEM((edges, hidden_width), BF16),
            pltpu.VMEM((slot_rows + mesh_rows, edges), BF16),
            pltpu.VMEM((grad_rows, hidden_width), F32),
            pltpu.VMEM((slot_rows, width), F32),
            pltpu.VMEM((slot_rows, width), F32),
            pltpu.VMEM(slot_index.shape, jnp.int32),
            pltpu.VMEM(dst_index.shape, jnp.int32),
            pltpu.VMEM(mesh_latent.shape, BF16),
            pltpu.VMEM((width, hidden_width), BF16),
            pltpu.VMEM(w_edge2.shape, BF16),
            pltpu.VMEM((w_node1.shape[0] - width, w_node1.shape[1]), BF16),
            pltpu.VMEM(w_node2.shape, BF16),
            pltpu.VMEM(turned.shape, BF16),
            pltpu.VMEM(hot.shape, BF16),
            pltpu.VMEM(node.shape, F32),
            pltpu.VMEM(cot.shape, F32),
            pltpu.VMEM((mesh_rows, width), BF16),
            pltpu.VMEM((edges, slot_rows), BF16),
            pltpu.SemaphoreType.DMA((11,)),
            pltpu.SemaphoreType.DMA((1,)),
        ],
        compiler_params=params(40),
        name="edges",
    )(
        *pinned(pltpu.HBM, slot_index, dst_index, mesh_latent, w_edge1, w_edge2, w_node1, w_node2),
        *pinned(pltpu.HBM, turned, hot, node, cot),
        *pinned(pltpu.VMEM, base),
        *slot_blocks,
    )
    sends, keeps = sides[:outer], sides[outer:]
    small = (2 * cap, width)
    arrived = {}
    first = None
    for k in [outer - 1, *range(1, outer - 1), 0]:
        send = sends[k] if first is None else lax.optimization_barrier((sends[k], first))[0]
        crossed = to_core(send)
        first = crossed if first is None else first
        total, mixed, *parts = pl.pallas_call(
            functools.partial(core_kernel, sizes, k),
            out_shape=[
                jax.ShapeDtypeStruct((chunk, hidden_width), F32),
                jax.ShapeDtypeStruct(small, BF16),
            ]
            + [jax.ShapeDtypeStruct((chunk + 2 * cap, width), BF16)] * (inner - 1),
            compiler_params=params(16),
            cost_estimate=cost(10**9, MIB),
            name="core",
        )(keeps[k], crossed, d_slots)
        parts = [to_inner(part, at + 1) for at, part in enumerate(parts)]
        block = 2 * inner * cap
        if k:
            (out,) = pl.pallas_call(
                functools.partial(inner_kernel, inner - 1, 0),
                out_shape=[jax.ShapeDtypeStruct((chunk + block, width), BF16)],
                compiler_params=params(16),
                name="inner",
            )(total, mixed, *parts)
            arrived[k] = to_outer(out, k)
        else:
            own, home = pl.pallas_call(
                functools.partial(inner_kernel, inner - 1, outer - 1),
                out_shape=[
                    jax.ShapeDtypeStruct((chunk, hidden_width), BF16),
                    jax.ShapeDtypeStruct((block, width), BF16),
                ],
                compiler_params=params(16),
                name="own",
            )(total, mixed, *parts, *[arrived[at] for at in range(1, outer)])

    pieces = {0: own}
    stride = outer // 2
    while stride:
        for at in range(0, outer, 2 * stride):
            pieces[at + stride] = to_outer(pieces[at], stride)
        stride //= 2
    halfway_at = band_count // 2
    pieces[halfway_at] = to_core(own)
    for far_inner in range(1, inner):
        for far_outer in range(outer):
            value = pieces[far_outer]
            if far_outer == outer // 2:
                value = lax.optimization_barrier((value, pieces[halfway_at]))[0]
            pieces[far_inner * outer + far_outer] = to_inner(value, far_inner)
    for at in range(1, halfway_at - 1):
        pieces[halfway_at + at] = to_core(pieces[at])

    grid_grad = pl.pallas_call(
        functools.partial(put_kernel, sizes),
        out_shape=jax.ShapeDtypeStruct(grid_latent.shape, F32),
        in_specs=specs(pltpu.HBM, 1) + specs(pltpu.VMEM, outer),
        out_specs=pl.BlockSpec(memory_space=pltpu.VMEM),
        scratch_shapes=[
            pltpu.VMEM((slot_rows, width), F32),
            pltpu.VMEM(send_rows.shape, jnp.int32),
            pltpu.SemaphoreType.DMA((1,)),
        ],
        compiler_params=params(16),
        cost_estimate=cost(2 * 10**9, 2 * MIB),
        name="put",
    )(*pinned(pltpu.HBM, send_rows), home, *[arrived[at] for at in range(1, outer)])

    last = outer - 1
    stages = [[], [], []]
    for at in range(band_count):
        far_outer, far_inner, far_core = at % outer, at // outer % inner, at // halfway_at
        if far_outer == last:
            stages[2 if far_inner else 1].append(at)
        else:
            stages[1 if far_inner and (far_core or far_outer == outer // 2) else 0].append(at)
    grads = []
    for places in stages:
        if places is stages[1]:
            value = lax.optimization_barrier((pieces[halfway_at - 1], grid_grad, *grads))[0]
            pieces[band_count - 1] = to_core(value)
        grads = pl.pallas_call(
            functools.partial(order_kernel, sizes, places, len(grads)),
            out_shape=[
                jax.ShapeDtypeStruct((3 * width, hidden_width), F32),
                jax.ShapeDtypeStruct((hidden_width, width), F32),
            ],
            in_specs=specs(pltpu.VMEM, len(places)) + specs(pltpu.HBM, len(grads)),
            out_specs=specs(pltpu.HBM, 2),
            scratch_shapes=[
                pltpu.VMEM((len(places), chunk, hidden_width), F32),
                pltpu.SemaphoreType.DMA((len(places),)),
            ],
            input_output_aliases={len(places) + k: k for k in range(len(grads))},
            compiler_params=params(16),
            cost_estimate=cost(15 * 10**7 * len(places), 2 * MIB),
            name="order",
        )(*[pieces[at] for at in places], *grads)
    grad_edge1, grad_edge2 = grads
    return (mesh_out, grid_grad, grad_edge1, grad_edge2)


def solution(mesh):
    chips = mesh.shape["band"] // 2
    inner = 1
    while inner * inner * 4 <= chips:
        inner *= 2
    sizes = (chips // inner, inner)
    in_specs = (
        P(("groups", "band"), None),
        P(("groups", "band"), None),
        P(("groups", "band"), None),
        P(("groups", "band"), None),
        P("band", None),
        P("band"),
        P("band"),
        P(),
        P(),
        P(),
        P(),
    )
    out_specs = (
        P(("groups", "band"), None),
        P(("groups", "band"), None),
        P("groups", None),
        P("groups", None),
    )
    return jax.shard_map(
        functools.partial(shards, sizes), mesh=mesh, in_specs=in_specs, out_specs=out_specs, check_vma=False
    )
```

```python
import functools

import jax
import jax.numpy as jnp
from jax import lax
from jax.experimental import pallas as pl
from jax.experimental.pallas import tpu as pltpu
from jax.sharding import PartitionSpec as P

BF16 = jnp.bfloat16
F32 = jnp.float32
MIB = 1024 * 1024


def dot_nn(a, b):
    return jnp.dot(a, b, preferred_element_type=F32)


def dot_tn(a, b):
    return lax.dot_general(a, b, (((0,), (0,)), ((), ())), preferred_element_type=F32)


def dot_nt(a, b):
    return lax.dot_general(a, b, (((1,), (1,)), ((), ())), preferred_element_type=F32)


def split(value):
    high = value.astype(BF16)
    low = (value - high.astype(F32)).astype(BF16)
    return high, low


def one_hot_rows(index_row, rows):
    shape = (rows, index_row.shape[1])
    hit = lax.broadcasted_iota(jnp.int32, shape, 0) == index_row
    return jnp.where(hit, 1.0, 0.0).astype(BF16)


def one_hot_columns(index_row, columns):
    lanes = index_row.shape[1]
    index = jnp.transpose(jnp.broadcast_to(index_row, (lanes, lanes)))
    pieces = []
    for start in range(0, columns, lanes):
        hit = lax.broadcasted_iota(jnp.int32, (lanes, lanes), 1) + start == index
        pieces.append(jnp.where(hit, 1.0, 0.0).astype(BF16))
    return pieces[0] if len(pieces) == 1 else jnp.concatenate(pieces, axis=1)


def tile_rows(index_ref, at, lines, rows):
    found = [one_hot_rows(index_ref[pl.ds(at * lines + k, 1), :], rows) for k in range(lines)]
    return jnp.concatenate(found, axis=1)


def tile_columns(index_ref, at, lines, columns):
    found = [one_hot_columns(index_ref[pl.ds(at * lines + k, 1), :], columns) for k in range(lines)]
    return jnp.concatenate(found, axis=0)


def place_of(sizes):
    outer, inner = sizes
    me = lax.axis_index("band")
    return me // (2 * inner), (me // 2) % inner, me % 2


def owner_at(sizes, far_outer, far_inner, far_core):
    my_outer, my_inner, my_core = place_of(sizes)
    return ((my_outer ^ far_outer) * sizes[1] + (my_inner ^ far_inner)) * 2 + (my_core ^ far_core)


def params(mib):
    return pltpu.CompilerParams(vmem_limit_bytes=mib * MIB)


def pinned(space, *values):
    return [pltpu.with_memory_space_constraint(value, space) for value in values]


def specs(space, count):
    return [pl.BlockSpec(memory_space=space)] * count


def cost(flops, nbytes):
    return pl.CostEstimate(flops=flops, bytes_accessed=nbytes, transcendentals=0)


def load(pairs, sems):
    copies = [pltpu.make_async_copy(source, target, sems.at[at]) for at, (source, target) in enumerate(pairs)]
    for copy in copies:
        copy.start()
    return copies


def pick_kernel(sizes, rows_hbm, grid_hbm, keep_ref, send_ref, rows_ref, grid_ref, picked_ref, sems):
    outer, inner = sizes
    rows_copy, grid_copy = load([(rows_hbm, rows_ref), (grid_hbm, grid_ref)], sems)
    rows_copy.wait()
    picked = picked_ref.shape[0]
    chosen = [one_hot_columns(rows_ref[:, at : at + 128], grid_ref.shape[0]) for at in range(0, picked, 128)]
    grid_copy.wait()
    for at, some in enumerate(chosen):
        picked_ref[at * 128 : (at + 1) * 128, :] = dot_nn(some, grid_ref[...])
    cap = picked // (2 * outer * inner)
    for far_core, target in enumerate((keep_ref, send_ref)):
        blocks = []
        for far_inner in range(inner):
            for far_outer in range(outer):
                owner = owner_at(sizes, far_outer, far_inner, far_core)
                blocks.append(picked_ref[pl.ds(pl.multiple_of(owner * cap, cap), cap), :])
        target[...] = jnp.concatenate(blocks, axis=0).astype(BF16)


def mix_kernel(count, minor, *refs):
    sources, targets = refs[:-count], refs[-count:]
    values = [ref[...].astype(F32) for ref in sources]
    unit = values[0].shape[0] // (count * minor)
    for at, target in enumerate(targets):
        starts = [(at * minor + k) * unit for k in range(minor)]
        blocks = [value[start : start + unit] for start in starts for value in values]
        target[...] = jnp.concatenate(blocks, axis=0).astype(BF16)


def put_kernel(sizes, rows_hbm, *refs):
    outer, inner = sizes
    blocks, (out_ref, ordered_ref, rows_ref, sems) = refs[:outer], refs[outer:]
    (copy,) = load([(rows_hbm, rows_ref)], sems)
    place_rows(sizes, blocks, ordered_ref)
    copy.wait()
    chosen = one_hot_rows(rows_ref[...], out_ref.shape[0])
    out_ref[...] = dot_nn(chosen, ordered_ref[...].astype(BF16))


def place_rows(sizes, blocks, ordered_ref):
    outer, inner = sizes
    cap = ordered_ref.shape[0] // (2 * outer * inner)
    for far_outer, block in enumerate(blocks):
        value = block[block.shape[0] - 2 * inner * cap :, :].astype(F32)
        for at in range(2 * inner):
            owner = owner_at(sizes, far_outer, at // 2, at % 2)
            ordered_ref[pl.ds(pl.multiple_of(owner * cap, cap), cap), :] = value[at * cap : (at + 1) * cap]


def ready_kernel(
    lines,
    dst_hbm,
    mesh_hbm,
    cot_hbm,
    w1_hbm,
    wn1_hbm,
    wn2_hbm,
    hot_hbm,
    node_hbm,
    cot_out_hbm,
    moved_ref,
    dst_ref,
    mesh_ref,
    cot_ref,
    w1_ref,
    wn1_ref,
    wn2_ref,
    hot_ref,
    node_ref,
    cot_out_ref,
    sems,
    out_sems,
):
    width = mesh_ref.shape[1]
    tile = lines * 128
    pairs = [
        (dst_hbm, dst_ref),
        (mesh_hbm, mesh_ref),
        (w1_hbm.at[pl.ds(width, width), :], w1_ref),
        (wn1_hbm.at[pl.ds(0, width), :], wn1_ref),
        (cot_hbm, cot_ref),
        (wn2_hbm, wn2_ref),
    ]
    copies = load(pairs, sems)
    outs = [
        pltpu.make_async_copy(source, target, out_sems.at[at])
        for at, (source, target) in enumerate([(hot_ref, hot_hbm), (node_ref, node_hbm), (cot_out_ref, cot_out_hbm)])
    ]
    copies[0].wait()
    for at in range(hot_ref.shape[0] // tile):
        hot_ref[at * tile : (at + 1) * tile, :] = tile_columns(dst_ref, at, lines, hot_ref.shape[1])
    outs[0].start()
    copies[1].wait()
    copies[3].wait()
    node_ref[...] = dot_nn(mesh_ref[...], wn1_ref[...])
    outs[1].start()
    copies[4].wait()
    copies[5].wait()
    cot_out_ref[...] = dot_nt(cot_ref[...], wn2_ref[...])
    outs[2].start()
    copies[2].wait()
    moved_ref[...] = dot_nn(mesh_ref[...], w1_ref[...]).astype(BF16)
    for copy in outs:
        copy.wait()


def base_kernel(
    lines,
    hot_hbm,
    edge_hbm,
    w1_hbm,
    moved_ref,
    base_ref,
    turned_hbm,
    hot_ref,
    edge_ref,
    w1_ref,
    turned_ref,
    sems,
    out_sems,
):
    width = edge_ref.shape[1]
    tile = lines * 128
    tiles = edge_ref.shape[0] // tile
    pairs = [(edge_hbm.at[pl.ds(at * tile, tile), :], edge_ref.at[pl.ds(at * tile, tile), :]) for at in range(tiles)]
    pairs += [(w1_hbm.at[pl.ds(2 * width, width), :], w1_ref), (hot_hbm, hot_ref)]
    copies = load(pairs, sems)
    same = lax.broadcasted_iota(jnp.int32, (256, 256), 0) == lax.broadcasted_iota(jnp.int32, (256, 256), 1)
    eye = jnp.where(same, 1.0, 0.0).astype(BF16)
    outs = []
    for at in range(tiles):
        rows = slice(at * tile, (at + 1) * tile)
        copies[at].wait()
        for start in range(0, width, 256):
            block = dot_nt(eye, edge_ref[rows, start : start + 256])
            turned_ref[start : start + 256, rows] = block.astype(BF16)
        columns = pl.ds(at * tile, tile)
        out = pltpu.make_async_copy(turned_ref.at[:, columns], turned_hbm.at[:, columns], out_sems.at[at])
        out.start()
        outs.append(out)
    copies[tiles].wait()
    copies[tiles + 1].wait()
    for at in range(tiles):
        rows = slice(at * tile, (at + 1) * tile)
        base_ref[rows, :] = dot_nn(edge_ref[rows, :], w1_ref[...]) + dot_nn(hot_ref[rows, :], moved_ref[...])
    for out in outs:
        out.wait()


def main_kernel(
    lines,
    sizes,
    slot_hbm,
    dst_hbm,
    mesh_hbm,
    w1_hbm,
    w2_hbm,
    wn1_hbm,
    wn2_hbm,
    turned_hbm,
    hot_hbm,
    node_hbm,
    cot_hbm,
    base_ref,
    *rest,
):
    outer, inner = sizes
    slot_blocks, rest = rest[:outer], rest[outer:]
    mesh_out_hbm, d_slots_ref = rest[:2]
    send_refs, keep_refs, rest = rest[2 : 2 + outer], rest[2 + outer : 2 + 2 * outer], rest[2 + 2 * outer :]
    slope_ref, value_ref, both_ref, grads_ref, slot_grads_ref, ordered_ref = rest[:6]
    slot_ref, dst_ref, mesh_ref, w1_ref, w2_ref, wn1_ref, wn2_ref = rest[6:13]
    hot_ref, node_ref, cot_ref, mesh_out_ref, picks_ref, sems, out_sems = rest[13:]
    width = mesh_ref.shape[1]
    mesh_rows = mesh_ref.shape[0]
    slot_rows = ordered_ref.shape[0]
    tile = lines * 128
    tiles = base_ref.shape[0] // tile
    pairs = [
        (slot_hbm, slot_ref),
        (dst_hbm, dst_ref),
        (w1_hbm.at[pl.ds(0, width), :], w1_ref),
        (w2_hbm, w2_ref),
        (wn1_hbm.at[pl.ds(width, wn1_ref.shape[0]), :], wn1_ref),
        (mesh_hbm, mesh_ref),
        (node_hbm, node_ref),
        (cot_hbm, cot_ref),
        (hot_hbm, hot_ref),
        (wn2_hbm, wn2_ref),
        (turned_hbm, both_ref.at[pl.ds(slot_rows + mesh_rows, width), :]),
    ]
    copies = load(pairs, sems)
    place_rows(sizes, slot_blocks, ordered_ref)
    slots_value = ordered_ref[...].astype(BF16)
    for copy in copies[:2]:
        copy.wait()
    for at in range(tiles):
        rows = slice(at * tile, (at + 1) * tile)
        picks_ref[rows, :] = tile_columns(slot_ref, at, lines, slot_rows)
        both_ref[:slot_rows, rows] = tile_rows(slot_ref, at, lines, slot_rows)
        both_ref[slot_rows : slot_rows + mesh_rows, rows] = tile_rows(dst_ref, at, lines, mesh_rows)
    copies[2].wait()

    slots = slots_value
    slot_pair = jnp.concatenate(split(dot_nn(slots, w1_ref[...])), axis=0)
    for at in range(tiles):
        rows = slice(at * tile, (at + 1) * tile)
        from_slot = picks_ref[rows, :]
        twice = jnp.concatenate([from_slot, from_slot], axis=1)
        pre = base_ref[rows, :] + dot_nn(twice, slot_pair)
        sigma = 0.5 + 0.5 * jnp.tanh(0.5 * pre)
        hidden = pre * sigma
        slope_ref[rows, :] = sigma + hidden * (1.0 - sigma)
        value_ref[rows, :] = hidden.astype(BF16)

    for copy in copies[3:-1]:
        copy.wait()
    hidden_sums = dot_nn(both_ref[slot_rows : slot_rows + mesh_rows, :], value_ref[...]).astype(BF16)
    received = dot_nn(hidden_sums, w2_ref[...]).astype(BF16)
    mesh = mesh_ref[...]
    pre_node = node_ref[...] + dot_nn(received, wn1_ref[...])
    sigma = 0.5 + 0.5 * jnp.tanh(0.5 * pre_node)
    node = pre_node * sigma
    slope = sigma + node * (1.0 - sigma)
    d_pre_node = (cot_ref[...] * slope).astype(BF16)
    d_received = dot_nt(d_pre_node, wn1_ref[...]).astype(BF16)
    spread = dot_nt(d_received, w2_ref[...]).astype(BF16)

    for at in range(tiles):
        rows = slice(at * tile, (at + 1) * tile)
        value_ref[rows, :] = (dot_nn(hot_ref[rows, :], spread) * slope_ref[rows, :]).astype(BF16)

    grads_ref[3 * width :, :] = dot_tn(hidden_sums, d_received)
    mesh_out_ref[...] = (mesh.astype(F32) + dot_nn(node.astype(BF16), wn2_ref[...])).astype(BF16)
    (mesh_copy,) = load([(mesh_out_ref, mesh_out_hbm)], out_sems)
    copies[-1].wait()
    product = dot_nn(both_ref[...], value_ref[...])
    sums = product[: slot_rows + mesh_rows].astype(BF16)
    grads_ref[2 * width : 3 * width, :] = product[slot_rows + mesh_rows :]
    slot_grads_ref[...] = dot_nt(sums[:slot_rows], w1_ref[...])
    grads_ref[:width, :] = dot_tn(slots, sums[:slot_rows])
    grads_ref[width : 2 * width, :] = dot_tn(mesh, sums[slot_rows:])

    chunk = grads_ref.shape[0] // (2 * outer * inner)
    cap = slot_rows // (2 * outer * inner)
    for far_core in range(2):
        for far_outer in range(outer):
            for far_inner in range(inner):
                owner = owner_at(sizes, far_outer, far_inner, far_core)
                at = (far_core * outer + far_outer) * inner + far_inner
                from_rows = pl.ds(pl.multiple_of(owner * cap, cap), cap)
                ordered_ref[at * cap : (at + 1) * cap, :] = slot_grads_ref[from_rows, :]
                value = grads_ref[pl.ds(pl.multiple_of(owner * chunk, chunk), chunk), :]
                rows = slice(far_inner * chunk, (far_inner + 1) * chunk)
                if far_core:
                    send_refs[far_outer][rows, :] = value.astype(BF16)
                else:
                    keep_refs[far_outer][rows, :] = value
    halfway, share = slot_rows // 2, inner * cap
    d_slots_ref[...] = ordered_ref[:halfway, :].astype(BF16)
    for far_outer, send_ref in enumerate(send_refs):
        start = halfway + far_outer * share
        send_ref[inner * chunk :, :] = ordered_ref[start : start + share, :].astype(BF16)
    mesh_copy.wait()


def core_kernel(sizes, far_outer, keep_ref, crossed_ref, d_slots_ref, total_ref, mixed_ref, *part_refs):
    outer, inner = sizes
    chunk = total_ref.shape[0]
    cap = d_slots_ref.shape[0] // (outer * inner)
    start = far_outer * inner * cap
    own = d_slots_ref[start : start + inner * cap, :].astype(F32)
    far = crossed_ref[inner * chunk :, :].astype(F32)
    for far_inner in range(inner):
        rows, slots = slice(far_inner * chunk, (far_inner + 1) * chunk), slice(far_inner * cap, (far_inner + 1) * cap)
        total = keep_ref[rows, :] + crossed_ref[rows, :].astype(F32)
        mixed = jnp.concatenate([own[slots], far[slots]], axis=0).astype(BF16)
        if far_inner:
            part_refs[far_inner - 1][:chunk, :] = total.astype(BF16)
            part_refs[far_inner - 1][chunk:, :] = mixed
        else:
            total_ref[...] = total
            mixed_ref[...] = mixed


def inner_kernel(parts, arrivals, total_ref, mixed_ref, *refs):
    received, arrived, outs = refs[:parts], refs[parts : parts + arrivals], refs[parts + arrivals :]
    chunk = total_ref.shape[0]
    total = total_ref[...]
    mixed = [mixed_ref[...]]
    for part in received:
        total = total + part[:chunk, :].astype(F32)
        mixed.append(part[chunk:, :])
    for value in arrived:
        total = total + value[:chunk, :].astype(F32)
    mixed = jnp.concatenate(mixed, axis=0)
    if len(outs) == 1:
        outs[0][:chunk, :] = total.astype(BF16)
        outs[0][chunk:, :] = mixed
    else:
        outs[0][...] = total.astype(BF16)
        outs[1][...] = mixed


def order_kernel(sizes, places, aliased, *refs):
    outer, inner = sizes
    pieces = refs[: len(places)]
    first_hbm, second_hbm, stage_ref, sems = refs[len(places) + aliased :]
    chunk = pieces[0].shape[0]
    first_chunks = first_hbm.shape[0] // chunk

    def send(k, target, start):
        rows = pl.ds(pl.multiple_of(start, chunk), chunk)
        return pltpu.make_async_copy(stage_ref.at[k], target.at[rows, :], sems.at[k])

    for k, (at, piece) in enumerate(zip(places, pieces)):
        owner = owner_at(sizes, at % outer, at // outer % inner, at // (outer * inner))
        stage_ref[k] = piece[...].astype(F32)

        @pl.when(owner < first_chunks)
        def _():
            send(k, first_hbm, owner * chunk).start()

        @pl.when(owner >= first_chunks)
        def _():
            send(k, second_hbm, (owner - first_chunks) * chunk).start()

    for k in range(len(places)):
        send(k, first_hbm, 0).wait()


def shards(
    sizes,
    grid_latent,
    mesh_latent,
    edge_latent,
    mesh_cot,
    send_rows,
    edge_slot,
    edge_dst,
    w_edge1,
    w_edge2,
    w_node1,
    w_node2,
):
    outer, inner = sizes
    band_count = lax.axis_size("band")
    width = grid_latent.shape[1]
    hidden_width = w_edge1.shape[1]
    edges = edge_latent.shape[0]
    mesh_rows = mesh_latent.shape[0]
    slot_rows = send_rows.shape[1]
    lines = 4
    slot_index = edge_slot.reshape(edges // 128, 128)
    dst_index = edge_dst.reshape(edges // 128, 128)

    def permute(value, stride, size, shift):
        pairs = []
        for source in range(band_count):
            place = (source // stride) % size
            pairs.append((source, source + ((place ^ shift) - place) * stride))
        return lax.ppermute(value, "band", pairs)

    def to_core(value):
        return permute(value, 1, 2, 1)

    def to_inner(value, shift):
        return permute(value, 2, inner, shift)

    def to_outer(value, shift):
        return permute(value, 2 * inner, outer, shift)

    cap, halfway = slot_rows // band_count, slot_rows // 2
    kept, sent = pl.pallas_call(
        functools.partial(pick_kernel, sizes),
        out_shape=[jax.ShapeDtypeStruct((halfway, width), BF16)] * 2,
        in_specs=specs(pltpu.HBM, 2),
        out_specs=specs(pltpu.VMEM, 2),
        scratch_shapes=[
            pltpu.VMEM(send_rows.shape, jnp.int32),
            pltpu.VMEM(grid_latent.shape, BF16),
            pltpu.VMEM((slot_rows, width), F32),
            pltpu.SemaphoreType.DMA((2,)),
        ],
        compiler_params=params(16),
        name="pick",
    )(*pinned(pltpu.HBM, send_rows, grid_latent))

    def mix(values, count, minor):
        rows = len(values) * values[0].shape[0] // count
        return pl.pallas_call(
            functools.partial(mix_kernel, count, minor),
            out_shape=[jax.ShapeDtypeStruct((rows, width), BF16)] * count,
            compiler_params=params(16),
            name="mix",
        )(*values)

    hot, node, cot, moved = pl.pallas_call(
        functools.partial(ready_kernel, lines),
        out_shape=[
            pltpu.HBM((edges, mesh_rows), BF16),
            pltpu.HBM((mesh_rows, hidden_width), F32),
            pltpu.HBM((mesh_rows, hidden_width), F32),
            pltpu.VMEM((mesh_rows, hidden_width), BF16),
        ],
        in_specs=specs(pltpu.HBM, 6),
        out_specs=specs(pltpu.HBM, 3) + specs(pltpu.VMEM, 1),
        scratch_shapes=[
            pltpu.VMEM(dst_index.shape, jnp.int32),
            pltpu.VMEM(mesh_latent.shape, BF16),
            pltpu.VMEM(mesh_cot.shape, BF16),
            pltpu.VMEM((width, hidden_width), BF16),
            pltpu.VMEM((width, hidden_width), BF16),
            pltpu.VMEM(w_node2.shape, BF16),
            pltpu.VMEM((edges, mesh_rows), BF16),
            pltpu.VMEM((mesh_rows, hidden_width), F32),
            pltpu.VMEM((mesh_rows, hidden_width), F32),
            pltpu.SemaphoreType.DMA((6,)),
            pltpu.SemaphoreType.DMA((3,)),
        ],
        compiler_params=params(16),
        cost_estimate=cost(2 * 10**9, 4 * MIB),
        name="ready",
    )(*pinned(pltpu.HBM, dst_index, mesh_latent, mesh_cot, w_edge1, w_node1, w_node2))
    base, turned = pl.pallas_call(
        functools.partial(base_kernel, lines),
        out_shape=[
            pltpu.VMEM((edges, hidden_width), F32),
            pltpu.HBM((width, edges), BF16),
        ],
        in_specs=specs(pltpu.HBM, 3) + specs(pltpu.VMEM, 1),
        out_specs=specs(pltpu.VMEM, 1) + specs(pltpu.HBM, 1),
        scratch_shapes=[
            pltpu.VMEM((edges, mesh_rows), BF16),
            pltpu.VMEM(edge_latent.shape, BF16),
            pltpu.VMEM((width, hidden_width), BF16),
            pltpu.VMEM((width, edges), BF16),
            pltpu.SemaphoreType.DMA((2 + edges // (128 * lines),)),
            pltpu.SemaphoreType.DMA((edges // (128 * lines),)),
        ],
        compiler_params=params(16),
        cost_estimate=cost(4 * 10**9, 4 * MIB),
        name="base",
    )(*pinned(pltpu.HBM, hot, edge_latent, w_edge1), *pinned(pltpu.VMEM, moved))

    by_inner = mix([kept, to_core(sent)], inner, outer)
    by_inner = [by_inner[0]] + [to_inner(by_inner[k], k) for k in range(1, inner)]
    by_outer = mix(by_inner, outer, 1)
    slot_blocks = [by_outer[0]] + [to_outer(by_outer[k], k) for k in range(1, outer)]

    grad_rows = 3 * width + hidden_width
    chunk = grad_rows // band_count
    group = (inner * chunk, hidden_width)
    mesh_out, d_slots, *sides = pl.pallas_call(
        functools.partial(main_kernel, lines, sizes),
        out_shape=[
            jax.ShapeDtypeStruct((mesh_rows, width), BF16),
            jax.ShapeDtypeStruct((halfway, width), BF16),
        ]
        + [jax.ShapeDtypeStruct((group[0] + inner * cap, hidden_width), BF16)] * outer
        + [jax.ShapeDtypeStruct(group, F32)] * outer,
        in_specs=specs(pltpu.HBM, 11) + specs(pltpu.VMEM, 1 + outer),
        out_specs=specs(pltpu.HBM, 1) + specs(pltpu.VMEM, 1 + 2 * outer),
        scratch_shapes=[
            pltpu.VMEM((edges, hidden_width), F32),
            pltpu.VMEM((edges, hidden_width), BF16),
            pltpu.VMEM((slot_rows + mesh_rows + width, edges), BF16),
            pltpu.VMEM((grad_rows, hidden_width), F32),
            pltpu.VMEM((slot_rows, width), F32),
            pltpu.VMEM((slot_rows, width), F32),
            pltpu.VMEM(slot_index.shape, jnp.int32),
            pltpu.VMEM(dst_index.shape, jnp.int32),
            pltpu.VMEM(mesh_latent.shape, BF16),
            pltpu.VMEM((width, hidden_width), BF16),
            pltpu.VMEM(w_edge2.shape, BF16),
            pltpu.VMEM((w_node1.shape[0] - width, w_node1.shape[1]), BF16),
            pltpu.VMEM(w_node2.shape, BF16),
            pltpu.VMEM(hot.shape, BF16),
            pltpu.VMEM(node.shape, F32),
            pltpu.VMEM(cot.shape, F32),
            pltpu.VMEM((mesh_rows, width), BF16),
            pltpu.VMEM((edges, slot_rows), BF16),
            pltpu.SemaphoreType.DMA((11,)),
            pltpu.SemaphoreType.DMA((1,)),
        ],
        compiler_params=params(40),
        name="edges",
    )(
        *pinned(pltpu.HBM, slot_index, dst_index, mesh_latent, w_edge1, w_edge2, w_node1, w_node2),
        *pinned(pltpu.HBM, turned, hot, node, cot),
        *pinned(pltpu.VMEM, base),
        *slot_blocks,
    )
    sends, keeps = sides[:outer], sides[outer:]
    small = (2 * cap, width)
    arrived = {}
    first = None
    for k in [outer - 1, *range(1, outer - 1), 0]:
        send = sends[k] if first is None else lax.optimization_barrier((sends[k], first))[0]
        crossed = to_core(send)
        total, mixed, *parts = pl.pallas_call(
            functools.partial(core_kernel, sizes, k),
            out_shape=[
                jax.ShapeDtypeStruct((chunk, hidden_width), F32),
                jax.ShapeDtypeStruct(small, BF16),
            ]
            + [jax.ShapeDtypeStruct((chunk + 2 * cap, width), BF16)] * (inner - 1),
            compiler_params=params(16),
            cost_estimate=cost(10**9, MIB),
            name="core",
        )(keeps[k], crossed, d_slots)
        first = parts[0] if first is None else first
        parts = [to_inner(part, at + 1) for at, part in enumerate(parts)]
        block = 2 * inner * cap
        if k:
            (out,) = pl.pallas_call(
                functools.partial(inner_kernel, inner - 1, 0),
                out_shape=[jax.ShapeDtypeStruct((chunk + block, width), BF16)],
                compiler_params=params(16),
                name="inner",
            )(total, mixed, *parts)
            arrived[k] = to_outer(out, k)
        else:
            own, home = pl.pallas_call(
                functools.partial(inner_kernel, inner - 1, outer - 1),
                out_shape=[
                    jax.ShapeDtypeStruct((chunk, hidden_width), BF16),
                    jax.ShapeDtypeStruct((block, width), BF16),
                ],
                compiler_params=params(16),
                name="own",
            )(total, mixed, *parts, *[arrived[at] for at in range(1, outer)])

    grid_grad = pl.pallas_call(
        functools.partial(put_kernel, sizes),
        out_shape=jax.ShapeDtypeStruct(grid_latent.shape, F32),
        in_specs=specs(pltpu.HBM, 1) + specs(pltpu.VMEM, outer),
        out_specs=pl.BlockSpec(memory_space=pltpu.VMEM),
        scratch_shapes=[
            pltpu.VMEM((slot_rows, width), F32),
            pltpu.VMEM(send_rows.shape, jnp.int32),
            pltpu.SemaphoreType.DMA((1,)),
        ],
        compiler_params=params(16),
        cost_estimate=cost(2 * 10**9, 2 * MIB),
        name="put",
    )(*pinned(pltpu.HBM, send_rows), home, *[arrived[at] for at in range(1, outer)])

    pieces = {0: own}
    stride = outer // 2
    while stride:
        for at in range(0, outer, 2 * stride):
            value = pieces[at]
            if at + stride == 1:
                value = lax.optimization_barrier((value, grid_grad))[0]
            pieces[at + stride] = to_outer(value, stride)
        stride //= 2
    halfway_at = band_count // 2
    pieces[halfway_at] = to_core(own)
    for far_inner in range(1, inner):
        for far_outer in range(outer):
            value = pieces[far_outer]
            if far_outer == outer // 2:
                value = lax.optimization_barrier((value, pieces[halfway_at]))[0]
            pieces[far_inner * outer + far_outer] = to_inner(value, far_inner)
    for at in range(1, halfway_at - 1):
        pieces[halfway_at + at] = to_core(pieces[at])

    last = outer - 1
    stages = [[], [], []]
    for at in range(band_count):
        far_outer, far_inner, far_core = at % outer, at // outer % inner, at // halfway_at
        if far_outer == last:
            stages[2 if far_inner else 1].append(at)
        else:
            stages[1 if far_inner and (far_core or far_outer == outer // 2) else 0].append(at)
    grads = []
    for places in stages:
        if places is stages[1]:
            value = lax.optimization_barrier((pieces[halfway_at - 1], *grads))[0]
            pieces[band_count - 1] = to_core(value)
        grads = pl.pallas_call(
            functools.partial(order_kernel, sizes, places, len(grads)),
            out_shape=[
                jax.ShapeDtypeStruct((3 * width, hidden_width), F32),
                jax.ShapeDtypeStruct((hidden_width, width), F32),
            ],
            in_specs=specs(pltpu.VMEM, len(places)) + specs(pltpu.HBM, len(grads)),
            out_specs=specs(pltpu.HBM, 2),
            scratch_shapes=[
                pltpu.VMEM((len(places), chunk, hidden_width), F32),
                pltpu.SemaphoreType.DMA((len(places),)),
            ],
            input_output_aliases={len(places) + k: k for k in range(len(grads))},
            compiler_params=params(16),
            cost_estimate=cost(15 * 10**7 * len(places), 2 * MIB),
            name="order",
        )(*[pieces[at] for at in places], *grads)
    grad_edge1, grad_edge2 = grads
    return (mesh_out, grid_grad, grad_edge1, grad_edge2)


def solution(mesh):
    chips = mesh.shape["band"] // 2
    inner = 1
    while inner * inner * 4 <= chips:
        inner *= 2
    sizes = (chips // inner, inner)
    in_specs = (
        P(("groups", "band"), None),
        P(("groups", "band"), None),
        P(("groups", "band"), None),
        P(("groups", "band"), None),
        P("band", None),
        P("band"),
        P("band"),
        P(),
        P(),
        P(),
        P(),
    )
    out_specs = (
        P(("groups", "band"), None),
        P(("groups", "band"), None),
        P("groups", None),
        P("groups", None),
    )
    return jax.shard_map(
        functools.partial(shards, sizes), mesh=mesh, in_specs=in_specs, out_specs=out_specs, check_vma=False
    )
```

```python
import functools

import jax
import jax.numpy as jnp
from jax import lax
from jax.experimental import pallas as pl
from jax.experimental.pallas import tpu as pltpu
from jax.sharding import PartitionSpec as P

BF16 = jnp.bfloat16
F32 = jnp.float32
MIB = 1024 * 1024


def dot_nn(a, b):
    return jnp.dot(a, b, preferred_element_type=F32)


def dot_tn(a, b):
    return lax.dot_general(a, b, (((0,), (0,)), ((), ())), preferred_element_type=F32)


def dot_nt(a, b):
    return lax.dot_general(a, b, (((1,), (1,)), ((), ())), preferred_element_type=F32)


def split(value):
    high = value.astype(BF16)
    low = (value - high.astype(F32)).astype(BF16)
    return high, low


def one_hot_rows(index_row, rows):
    shape = (rows, index_row.shape[1])
    hit = lax.broadcasted_iota(jnp.int32, shape, 0) == index_row
    return jnp.where(hit, 1.0, 0.0).astype(BF16)


def one_hot_columns(index_row, columns):
    lanes = index_row.shape[1]
    index = jnp.transpose(jnp.broadcast_to(index_row, (lanes, lanes)))
    pieces = []
    for start in range(0, columns, lanes):
        hit = lax.broadcasted_iota(jnp.int32, (lanes, lanes), 1) + start == index
        pieces.append(jnp.where(hit, 1.0, 0.0).astype(BF16))
    return pieces[0] if len(pieces) == 1 else jnp.concatenate(pieces, axis=1)


def tile_rows(index_ref, at, lines, rows):
    found = [one_hot_rows(index_ref[pl.ds(at * lines + k, 1), :], rows) for k in range(lines)]
    return jnp.concatenate(found, axis=1)


def tile_columns(index_ref, at, lines, columns):
    found = [one_hot_columns(index_ref[pl.ds(at * lines + k, 1), :], columns) for k in range(lines)]
    return jnp.concatenate(found, axis=0)


def place_of(sizes):
    outer, inner = sizes
    me = lax.axis_index("band")
    return me // (2 * inner), (me // 2) % inner, me % 2


def owner_at(sizes, far_outer, far_inner, far_core):
    my_outer, my_inner, my_core = place_of(sizes)
    return ((my_outer ^ far_outer) * sizes[1] + (my_inner ^ far_inner)) * 2 + (my_core ^ far_core)


def params(mib):
    return pltpu.CompilerParams(vmem_limit_bytes=mib * MIB)


def pinned(space, *values):
    return [pltpu.with_memory_space_constraint(value, space) for value in values]


def specs(space, count):
    return [pl.BlockSpec(memory_space=space)] * count


def cost(flops, nbytes):
    return pl.CostEstimate(flops=flops, bytes_accessed=nbytes, transcendentals=0)


def load(pairs, sems):
    copies = [pltpu.make_async_copy(source, target, sems.at[at]) for at, (source, target) in enumerate(pairs)]
    for copy in copies:
        copy.start()
    return copies


def pick_kernel(sizes, rows_hbm, grid_hbm, keep_ref, send_ref, rows_ref, grid_ref, picked_ref, sems):
    outer, inner = sizes
    block = grid_ref.shape[0] // 4
    parts = [pl.ds(at * block, block) for at in range(4)]
    copies = load([(rows_hbm, rows_ref)] + [(grid_hbm.at[part, :], grid_ref.at[part, :]) for part in parts], sems)
    copies[0].wait()
    picked = picked_ref.shape[0]
    chosen = [one_hot_columns(rows_ref[:, at : at + 128], grid_ref.shape[0]) for at in range(0, picked, 128)]
    for copy in copies[1:]:
        copy.wait()
    for at, some in enumerate(chosen):
        picked_ref[at * 128 : (at + 1) * 128, :] = dot_nn(some, grid_ref[...])
    cap = picked // (2 * outer * inner)
    for far_core, target in enumerate((keep_ref, send_ref)):
        blocks = []
        for far_inner in range(inner):
            for far_outer in range(outer):
                owner = owner_at(sizes, far_outer, far_inner, far_core)
                blocks.append(picked_ref[pl.ds(pl.multiple_of(owner * cap, cap), cap), :])
        target[...] = jnp.concatenate(blocks, axis=0).astype(BF16)


def mix_kernel(count, minor, *refs):
    sources, targets = refs[:-count], refs[-count:]
    values = [ref[...].astype(F32) for ref in sources]
    unit = values[0].shape[0] // (count * minor)
    for at, target in enumerate(targets):
        starts = [(at * minor + k) * unit for k in range(minor)]
        blocks = [value[start : start + unit] for start in starts for value in values]
        target[...] = jnp.concatenate(blocks, axis=0).astype(BF16)


def put_kernel(sizes, rows_hbm, *refs):
    outer, inner = sizes
    blocks, (out_ref, ordered_ref, rows_ref, sems) = refs[:outer], refs[outer:]
    (copy,) = load([(rows_hbm, rows_ref)], sems)
    place_rows(sizes, blocks, ordered_ref)
    copy.wait()
    chosen = one_hot_rows(rows_ref[...], out_ref.shape[0])
    out_ref[...] = dot_nn(chosen, ordered_ref[...].astype(BF16))


def place_rows(sizes, blocks, ordered_ref):
    outer, inner = sizes
    cap = ordered_ref.shape[0] // (2 * outer * inner)
    for far_outer, block in enumerate(blocks):
        value = block[block.shape[0] - 2 * inner * cap :, :].astype(F32)
        for at in range(2 * inner):
            owner = owner_at(sizes, far_outer, at // 2, at % 2)
            ordered_ref[pl.ds(pl.multiple_of(owner * cap, cap), cap), :] = value[at * cap : (at + 1) * cap]


def ready_kernel(
    lines,
    dst_hbm,
    mesh_hbm,
    cot_hbm,
    w1_hbm,
    wn1_hbm,
    wn2_hbm,
    hot_hbm,
    node_hbm,
    cot_out_hbm,
    moved_ref,
    dst_ref,
    mesh_ref,
    cot_ref,
    w1_ref,
    wn1_ref,
    wn2_ref,
    hot_ref,
    node_ref,
    cot_out_ref,
    sems,
    out_sems,
):
    width = mesh_ref.shape[1]
    tile = lines * 128
    pairs = [
        (dst_hbm, dst_ref),
        (mesh_hbm, mesh_ref),
        (w1_hbm.at[pl.ds(width, width), :], w1_ref),
        (wn1_hbm.at[pl.ds(0, width), :], wn1_ref),
        (cot_hbm, cot_ref),
        (wn2_hbm, wn2_ref),
    ]
    copies = load(pairs, sems)
    outs = [
        pltpu.make_async_copy(source, target, out_sems.at[at])
        for at, (source, target) in enumerate([(hot_ref, hot_hbm), (node_ref, node_hbm), (cot_out_ref, cot_out_hbm)])
    ]
    copies[0].wait()
    for at in range(hot_ref.shape[0] // tile):
        hot_ref[at * tile : (at + 1) * tile, :] = tile_columns(dst_ref, at, lines, hot_ref.shape[1])
    outs[0].start()
    copies[1].wait()
    copies[3].wait()
    node_ref[...] = dot_nn(mesh_ref[...], wn1_ref[...])
    outs[1].start()
    copies[4].wait()
    copies[5].wait()
    cot_out_ref[...] = dot_nt(cot_ref[...], wn2_ref[...])
    outs[2].start()
    copies[2].wait()
    moved_ref[...] = dot_nn(mesh_ref[...], w1_ref[...]).astype(BF16)
    for copy in outs:
        copy.wait()


def base_kernel(
    lines,
    hot_hbm,
    edge_hbm,
    w1_hbm,
    slot_hbm,
    dst_hbm,
    moved_ref,
    base_ref,
    slot_ref,
    dst_ref,
    top_ref,
    turned_hbm,
    hot_ref,
    edge_ref,
    w1_ref,
    turned_ref,
    sems,
    out_sems,
):
    width = edge_ref.shape[1]
    tile = lines * 128
    tiles = edge_ref.shape[0] // tile
    pairs = [(edge_hbm.at[pl.ds(at * tile, tile), :], edge_ref.at[pl.ds(at * tile, tile), :]) for at in range(tiles)]
    pairs += [(w1_hbm.at[pl.ds(2 * width, width), :], w1_ref), (hot_hbm, hot_ref)]
    pairs += [(w1_hbm.at[pl.ds(0, width), :], top_ref), (slot_hbm, slot_ref), (dst_hbm, dst_ref)]
    copies = load(pairs, sems)
    same = lax.broadcasted_iota(jnp.int32, (256, 256), 0) == lax.broadcasted_iota(jnp.int32, (256, 256), 1)
    eye = jnp.where(same, 1.0, 0.0).astype(BF16)
    outs = []
    for at in range(tiles):
        rows = slice(at * tile, (at + 1) * tile)
        copies[at].wait()
        for start in range(0, width, 256):
            block = dot_nt(eye, edge_ref[rows, start : start + 256])
            turned_ref[start : start + 256, rows] = block.astype(BF16)
        columns = pl.ds(at * tile, tile)
        out = pltpu.make_async_copy(turned_ref.at[:, columns], turned_hbm.at[:, columns], out_sems.at[at])
        out.start()
        outs.append(out)
    copies[tiles].wait()
    copies[tiles + 1].wait()
    for at in range(tiles):
        rows = slice(at * tile, (at + 1) * tile)
        base_ref[rows, :] = dot_nn(edge_ref[rows, :], w1_ref[...]) + dot_nn(hot_ref[rows, :], moved_ref[...])
    for out in outs + copies[tiles + 2 :]:
        out.wait()


def main_kernel(
    lines,
    sizes,
    mesh_hbm,
    w2_hbm,
    wn1_hbm,
    turned_hbm,
    hot_hbm,
    node_hbm,
    cot_hbm,
    base_ref,
    slot_ref,
    dst_ref,
    w1_ref,
    *rest,
):
    outer, inner = sizes
    slot_blocks, rest = rest[:outer], rest[outer:]
    node_out_ref, d_slots_ref = rest[:2]
    send_refs, keep_refs, rest = rest[2 : 2 + outer], rest[2 + outer : 2 + 2 * outer], rest[2 + 2 * outer :]
    slope_ref, value_ref, both_ref, grads_ref, slot_grads_ref, ordered_ref = rest[:6]
    mesh_ref, w2_ref, wn1_ref, hot_ref, node_ref, cot_ref, picks_ref, sems = rest[6:]
    width = mesh_ref.shape[1]
    mesh_rows = mesh_ref.shape[0]
    slot_rows = ordered_ref.shape[0]
    tile = lines * 128
    tiles = base_ref.shape[0] // tile
    pairs = [
        (w2_hbm, w2_ref),
        (wn1_hbm.at[pl.ds(width, wn1_ref.shape[0]), :], wn1_ref),
        (mesh_hbm, mesh_ref),
        (node_hbm, node_ref),
        (cot_hbm, cot_ref),
        (hot_hbm, hot_ref),
        (turned_hbm, both_ref.at[pl.ds(slot_rows + mesh_rows, width), :]),
    ]
    copies = load(pairs, sems)
    place_rows(sizes, slot_blocks, ordered_ref)
    slots_value = ordered_ref[...].astype(BF16)
    for at in range(tiles):
        rows = slice(at * tile, (at + 1) * tile)
        picks_ref[rows, :] = tile_columns(slot_ref, at, lines, slot_rows)
        both_ref[:slot_rows, rows] = tile_rows(slot_ref, at, lines, slot_rows)
        both_ref[slot_rows : slot_rows + mesh_rows, rows] = tile_rows(dst_ref, at, lines, mesh_rows)

    slots = slots_value
    slot_pair = jnp.concatenate(split(dot_nn(slots, w1_ref[...])), axis=0)
    for at in range(tiles):
        rows = slice(at * tile, (at + 1) * tile)
        from_slot = picks_ref[rows, :]
        twice = jnp.concatenate([from_slot, from_slot], axis=1)
        pre = base_ref[rows, :] + dot_nn(twice, slot_pair)
        sigma = 0.5 + 0.5 * jnp.tanh(0.5 * pre)
        hidden = pre * sigma
        slope_ref[rows, :] = sigma + hidden * (1.0 - sigma)
        value_ref[rows, :] = hidden.astype(BF16)

    for copy in copies[:-1]:
        copy.wait()
    hidden_sums = dot_nn(both_ref[slot_rows : slot_rows + mesh_rows, :], value_ref[...]).astype(BF16)
    received = dot_nn(hidden_sums, w2_ref[...]).astype(BF16)
    mesh = mesh_ref[...]
    pre_node = node_ref[...] + dot_nn(received, wn1_ref[...])
    sigma = 0.5 + 0.5 * jnp.tanh(0.5 * pre_node)
    node = pre_node * sigma
    slope = sigma + node * (1.0 - sigma)
    d_pre_node = (cot_ref[...] * slope).astype(BF16)
    d_received = dot_nt(d_pre_node, wn1_ref[...]).astype(BF16)
    spread = dot_nt(d_received, w2_ref[...]).astype(BF16)

    for at in range(tiles):
        rows = slice(at * tile, (at + 1) * tile)
        value_ref[rows, :] = (dot_nn(hot_ref[rows, :], spread) * slope_ref[rows, :]).astype(BF16)

    grads_ref[3 * width :, :] = dot_tn(hidden_sums, d_received)
    node_out_ref[...] = node.astype(BF16)
    copies[-1].wait()
    product = dot_nn(both_ref[...], value_ref[...])
    sums = product[: slot_rows + mesh_rows].astype(BF16)
    grads_ref[2 * width : 3 * width, :] = product[slot_rows + mesh_rows :]
    slot_grads_ref[...] = dot_nt(sums[:slot_rows], w1_ref[...])
    grads_ref[:width, :] = dot_tn(slots, sums[:slot_rows])
    grads_ref[width : 2 * width, :] = dot_tn(mesh, sums[slot_rows:])

    chunk = grads_ref.shape[0] // (2 * outer * inner)
    cap = slot_rows // (2 * outer * inner)
    for far_core in range(2):
        for far_outer in range(outer):
            for far_inner in range(inner):
                owner = owner_at(sizes, far_outer, far_inner, far_core)
                at = (far_core * outer + far_outer) * inner + far_inner
                from_rows = pl.ds(pl.multiple_of(owner * cap, cap), cap)
                ordered_ref[at * cap : (at + 1) * cap, :] = slot_grads_ref[from_rows, :]
                value = grads_ref[pl.ds(pl.multiple_of(owner * chunk, chunk), chunk), :]
                rows = slice(far_inner * chunk, (far_inner + 1) * chunk)
                if far_core:
                    send_refs[far_outer][rows, :] = value.astype(BF16)
                else:
                    keep_refs[far_outer][rows, :] = value
    halfway, share = slot_rows // 2, inner * cap
    d_slots_ref[...] = ordered_ref[:halfway, :].astype(BF16)
    for far_outer, send_ref in enumerate(send_refs):
        start = halfway + far_outer * share
        send_ref[inner * chunk :, :] = ordered_ref[start : start + share, :].astype(BF16)


def mesh_kernel(mesh_hbm, wn2_hbm, node_ref, out_ref, mesh_ref, wn2_ref, sems):
    for copy in load([(mesh_hbm, mesh_ref), (wn2_hbm, wn2_ref)], sems):
        copy.wait()
    out_ref[...] = (mesh_ref[...].astype(F32) + dot_nn(node_ref[...], wn2_ref[...])).astype(BF16)


def core_kernel(sizes, far_outer, keep_ref, crossed_ref, d_slots_ref, total_ref, mixed_ref, *part_refs):
    outer, inner = sizes
    chunk = total_ref.shape[0]
    cap = d_slots_ref.shape[0] // (outer * inner)
    start = far_outer * inner * cap
    own = d_slots_ref[start : start + inner * cap, :].astype(F32)
    far = crossed_ref[inner * chunk :, :].astype(F32)
    for far_inner in range(inner):
        rows, slots = slice(far_inner * chunk, (far_inner + 1) * chunk), slice(far_inner * cap, (far_inner + 1) * cap)
        total = keep_ref[rows, :] + crossed_ref[rows, :].astype(F32)
        mixed = jnp.concatenate([own[slots], far[slots]], axis=0).astype(BF16)
        if far_inner:
            part_refs[far_inner - 1][:chunk, :] = total.astype(BF16)
            part_refs[far_inner - 1][chunk:, :] = mixed
        else:
            total_ref[...] = total
            mixed_ref[...] = mixed


def inner_kernel(parts, arrivals, total_ref, mixed_ref, *refs):
    received, arrived, outs = refs[:parts], refs[parts : parts + arrivals], refs[parts + arrivals :]
    chunk = total_ref.shape[0]
    total = total_ref[...]
    mixed = [mixed_ref[...]]
    for part in received:
        total = total + part[:chunk, :].astype(F32)
        mixed.append(part[chunk:, :])
    for value in arrived:
        total = total + value[:chunk, :].astype(F32)
    mixed = jnp.concatenate(mixed, axis=0)
    if len(outs) == 1:
        outs[0][:chunk, :] = total.astype(BF16)
        outs[0][chunk:, :] = mixed
    else:
        outs[0][...] = total.astype(BF16)
        outs[1][...] = mixed


def order_kernel(sizes, places, aliased, *refs):
    outer, inner = sizes
    pieces = refs[: len(places)]
    first_hbm, second_hbm, stage_ref, sems = refs[len(places) + aliased :]
    chunk = pieces[0].shape[0]
    first_chunks = first_hbm.shape[0] // chunk

    def send(k, target, start):
        rows = pl.ds(pl.multiple_of(start, chunk), chunk)
        return pltpu.make_async_copy(stage_ref.at[k], target.at[rows, :], sems.at[k])

    for k, (at, piece) in enumerate(zip(places, pieces)):
        owner = owner_at(sizes, at % outer, at // outer % inner, at // (outer * inner))
        stage_ref[k] = piece[...].astype(F32)

        @pl.when(owner < first_chunks)
        def _():
            send(k, first_hbm, owner * chunk).start()

        @pl.when(owner >= first_chunks)
        def _():
            send(k, second_hbm, (owner - first_chunks) * chunk).start()

    for k in range(len(places)):
        send(k, first_hbm, 0).wait()


def shards(
    sizes,
    grid_latent,
    mesh_latent,
    edge_latent,
    mesh_cot,
    send_rows,
    edge_slot,
    edge_dst,
    w_edge1,
    w_edge2,
    w_node1,
    w_node2,
):
    outer, inner = sizes
    band_count = lax.axis_size("band")
    width = grid_latent.shape[1]
    hidden_width = w_edge1.shape[1]
    edges = edge_latent.shape[0]
    mesh_rows = mesh_latent.shape[0]
    slot_rows = send_rows.shape[1]
    lines = 4
    slot_index = edge_slot.reshape(edges // 128, 128)
    dst_index = edge_dst.reshape(edges // 128, 128)

    def permute(value, stride, size, shift):
        pairs = []
        for source in range(band_count):
            place = (source // stride) % size
            pairs.append((source, source + ((place ^ shift) - place) * stride))
        return lax.ppermute(value, "band", pairs)

    def to_core(value):
        return permute(value, 1, 2, 1)

    def to_inner(value, shift):
        return permute(value, 2, inner, shift)

    def to_outer(value, shift):
        return permute(value, 2 * inner, outer, shift)

    cap, halfway = slot_rows // band_count, slot_rows // 2
    kept, sent = pl.pallas_call(
        functools.partial(pick_kernel, sizes),
        out_shape=[jax.ShapeDtypeStruct((halfway, width), BF16)] * 2,
        in_specs=specs(pltpu.HBM, 2),
        out_specs=specs(pltpu.VMEM, 2),
        scratch_shapes=[
            pltpu.VMEM(send_rows.shape, jnp.int32),
            pltpu.VMEM(grid_latent.shape, BF16),
            pltpu.VMEM((slot_rows, width), F32),
            pltpu.SemaphoreType.DMA((5,)),
        ],
        compiler_params=params(16),
        name="pick",
    )(*pinned(pltpu.HBM, send_rows, grid_latent))

    def mix(values, count, minor):
        rows = len(values) * values[0].shape[0] // count
        return pl.pallas_call(
            functools.partial(mix_kernel, count, minor),
            out_shape=[jax.ShapeDtypeStruct((rows, width), BF16)] * count,
            compiler_params=params(16),
            name="mix",
        )(*values)

    hot, node, cot, moved = pl.pallas_call(
        functools.partial(ready_kernel, lines),
        out_shape=[
            pltpu.HBM((edges, mesh_rows), BF16),
            pltpu.HBM((mesh_rows, hidden_width), F32),
            pltpu.HBM((mesh_rows, hidden_width), F32),
            pltpu.VMEM((mesh_rows, hidden_width), BF16),
        ],
        in_specs=specs(pltpu.HBM, 6),
        out_specs=specs(pltpu.HBM, 3) + specs(pltpu.VMEM, 1),
        scratch_shapes=[
            pltpu.VMEM(dst_index.shape, jnp.int32),
            pltpu.VMEM(mesh_latent.shape, BF16),
            pltpu.VMEM(mesh_cot.shape, BF16),
            pltpu.VMEM((width, hidden_width), BF16),
            pltpu.VMEM((width, hidden_width), BF16),
            pltpu.VMEM(w_node2.shape, BF16),
            pltpu.VMEM((edges, mesh_rows), BF16),
            pltpu.VMEM((mesh_rows, hidden_width), F32),
            pltpu.VMEM((mesh_rows, hidden_width), F32),
            pltpu.SemaphoreType.DMA((6,)),
            pltpu.SemaphoreType.DMA((3,)),
        ],
        compiler_params=params(16),
        cost_estimate=cost(2 * 10**9, 4 * MIB),
        name="ready",
    )(*pinned(pltpu.HBM, dst_index, mesh_latent, mesh_cot, w_edge1, w_node1, w_node2))
    base, *ahead, turned = pl.pallas_call(
        functools.partial(base_kernel, lines),
        out_shape=[
            pltpu.VMEM((edges, hidden_width), F32),
            pltpu.VMEM(slot_index.shape, jnp.int32),
            pltpu.VMEM(dst_index.shape, jnp.int32),
            pltpu.VMEM((width, hidden_width), BF16),
            pltpu.HBM((width, edges), BF16),
        ],
        in_specs=specs(pltpu.HBM, 5) + specs(pltpu.VMEM, 1),
        out_specs=specs(pltpu.VMEM, 4) + specs(pltpu.HBM, 1),
        scratch_shapes=[
            pltpu.VMEM((edges, mesh_rows), BF16),
            pltpu.VMEM(edge_latent.shape, BF16),
            pltpu.VMEM((width, hidden_width), BF16),
            pltpu.VMEM((width, edges), BF16),
            pltpu.SemaphoreType.DMA((5 + edges // (128 * lines),)),
            pltpu.SemaphoreType.DMA((edges // (128 * lines),)),
        ],
        compiler_params=params(16),
        cost_estimate=cost(4 * 10**9, 4 * MIB),
        name="base",
    )(*pinned(pltpu.HBM, hot, edge_latent, w_edge1, slot_index, dst_index), *pinned(pltpu.VMEM, moved))

    by_inner = mix([kept, to_core(sent)], inner, outer)
    by_inner = [by_inner[0]] + [to_inner(by_inner[k], k) for k in range(1, inner)]
    by_outer = mix(by_inner, outer, 1)
    slot_blocks = [by_outer[0]] + [to_outer(by_outer[k], k) for k in range(1, outer)]

    grad_rows = 3 * width + hidden_width
    chunk = grad_rows // band_count
    group = (inner * chunk, hidden_width)
    node_out, d_slots, *sides = pl.pallas_call(
        functools.partial(main_kernel, lines, sizes),
        out_shape=[
            jax.ShapeDtypeStruct((mesh_rows, width), BF16),
            jax.ShapeDtypeStruct((halfway, width), BF16),
        ]
        + [jax.ShapeDtypeStruct((group[0] + inner * cap, hidden_width), BF16)] * outer
        + [jax.ShapeDtypeStruct(group, F32)] * outer,
        in_specs=specs(pltpu.HBM, 7) + specs(pltpu.VMEM, 4 + outer),
        out_specs=specs(pltpu.VMEM, 2 + 2 * outer),
        scratch_shapes=[
            pltpu.VMEM((edges, hidden_width), F32),
            pltpu.VMEM((edges, hidden_width), BF16),
            pltpu.VMEM((slot_rows + mesh_rows + width, edges), BF16),
            pltpu.VMEM((grad_rows, hidden_width), F32),
            pltpu.VMEM((slot_rows, width), F32),
            pltpu.VMEM((slot_rows, width), F32),
            pltpu.VMEM(mesh_latent.shape, BF16),
            pltpu.VMEM(w_edge2.shape, BF16),
            pltpu.VMEM((w_node1.shape[0] - width, w_node1.shape[1]), BF16),
            pltpu.VMEM(hot.shape, BF16),
            pltpu.VMEM(node.shape, F32),
            pltpu.VMEM(cot.shape, F32),
            pltpu.VMEM((edges, slot_rows), BF16),
            pltpu.SemaphoreType.DMA((7,)),
        ],
        compiler_params=params(40),
        name="edges",
    )(
        *pinned(pltpu.HBM, mesh_latent, w_edge2, w_node1, turned, hot, node, cot),
        *pinned(pltpu.VMEM, base, *ahead),
        *slot_blocks,
    )
    mesh_out = pl.pallas_call(
        mesh_kernel,
        out_shape=jax.ShapeDtypeStruct((mesh_rows, width), BF16),
        in_specs=specs(pltpu.HBM, 2) + specs(pltpu.VMEM, 1),
        out_specs=pl.BlockSpec(memory_space=pltpu.VMEM),
        scratch_shapes=[
            pltpu.VMEM(mesh_latent.shape, BF16),
            pltpu.VMEM(w_node2.shape, BF16),
            pltpu.SemaphoreType.DMA((2,)),
        ],
        compiler_params=params(16),
        cost_estimate=cost(10**9, MIB),
        name="mesh",
    )(*pinned(pltpu.HBM, mesh_latent, w_node2), node_out)
    sends, keeps = sides[:outer], sides[outer:]
    small = (2 * cap, width)
    arrived = {}
    first = None
    for k in [outer - 1, *range(1, outer - 1), 0]:
        send = sends[k] if first is None else lax.optimization_barrier((sends[k], first))[0]
        crossed = to_core(send)
        if first is None:
            crossed = lax.optimization_barrier((crossed, mesh_out))[0]
        total, mixed, *parts = pl.pallas_call(
            functools.partial(core_kernel, sizes, k),
            out_shape=[
                jax.ShapeDtypeStruct((chunk, hidden_width), F32),
                jax.ShapeDtypeStruct(small, BF16),
            ]
            + [jax.ShapeDtypeStruct((chunk + 2 * cap, width), BF16)] * (inner - 1),
            compiler_params=params(16),
            cost_estimate=cost(10**9, MIB),
            name="core",
        )(keeps[k], crossed, d_slots)
        first = parts[0] if first is None else first
        parts = [to_inner(part, at + 1) for at, part in enumerate(parts)]
        block = 2 * inner * cap
        if k:
            (out,) = pl.pallas_call(
                functools.partial(inner_kernel, inner - 1, 0),
                out_shape=[jax.ShapeDtypeStruct((chunk + block, width), BF16)],
                compiler_params=params(16),
                name="inner",
            )(total, mixed, *parts)
            arrived[k] = to_outer(out, k)
        else:
            own, home = pl.pallas_call(
                functools.partial(inner_kernel, inner - 1, outer - 1),
                out_shape=[
                    jax.ShapeDtypeStruct((chunk, hidden_width), BF16),
                    jax.ShapeDtypeStruct((block, width), BF16),
                ],
                compiler_params=params(16),
                name="own",
            )(total, mixed, *parts, *[arrived[at] for at in range(1, outer)])

    grid_grad = pl.pallas_call(
        functools.partial(put_kernel, sizes),
        out_shape=jax.ShapeDtypeStruct(grid_latent.shape, F32),
        in_specs=specs(pltpu.HBM, 1) + specs(pltpu.VMEM, outer),
        out_specs=pl.BlockSpec(memory_space=pltpu.VMEM),
        scratch_shapes=[
            pltpu.VMEM((slot_rows, width), F32),
            pltpu.VMEM(send_rows.shape, jnp.int32),
            pltpu.SemaphoreType.DMA((1,)),
        ],
        compiler_params=params(16),
        cost_estimate=cost(2 * 10**9, 2 * MIB),
        name="put",
    )(*pinned(pltpu.HBM, send_rows), home, *[arrived[at] for at in range(1, outer)])

    pieces = {0: own}
    stride = outer // 2
    while stride:
        for at in range(0, outer, 2 * stride):
            value = pieces[at]
            if at + stride == 1:
                value = lax.optimization_barrier((value, grid_grad))[0]
            pieces[at + stride] = to_outer(value, stride)
        stride //= 2
    halfway_at = band_count // 2
    pieces[halfway_at] = to_core(own)
    for far_inner in range(1, inner):
        for far_outer in range(outer):
            value = pieces[far_outer]
            if far_outer == outer // 2:
                value = lax.optimization_barrier((value, pieces[halfway_at]))[0]
            pieces[far_inner * outer + far_outer] = to_inner(value, far_inner)
    for at in range(1, halfway_at - 1):
        pieces[halfway_at + at] = to_core(pieces[at])

    last = outer - 1
    stages = [[], [], []]
    for at in range(band_count):
        far_outer, far_inner, far_core = at % outer, at // outer % inner, at // halfway_at
        if far_outer == last:
            stages[2 if far_inner else 1].append(at)
        else:
            stages[1 if far_inner and (far_core or far_outer == outer // 2) else 0].append(at)
    grads = []
    for places in stages:
        if places is stages[1]:
            value = lax.optimization_barrier((pieces[halfway_at - 1], *grads))[0]
            pieces[band_count - 1] = to_core(value)
        grads = pl.pallas_call(
            functools.partial(order_kernel, sizes, places, len(grads)),
            out_shape=[
                jax.ShapeDtypeStruct((3 * width, hidden_width), F32),
                jax.ShapeDtypeStruct((hidden_width, width), F32),
            ],
            in_specs=specs(pltpu.VMEM, len(places)) + specs(pltpu.HBM, len(grads)),
            out_specs=specs(pltpu.HBM, 2),
            scratch_shapes=[
                pltpu.VMEM((len(places), chunk, hidden_width), F32),
                pltpu.SemaphoreType.DMA((len(places),)),
            ],
            input_output_aliases={len(places) + k: k for k in range(len(grads))},
            compiler_params=params(16),
            cost_estimate=cost(15 * 10**7 * len(places), 2 * MIB),
            name="order",
        )(*[pieces[at] for at in places], *grads)
    grad_edge1, grad_edge2 = grads
    return (mesh_out, grid_grad, grad_edge1, grad_edge2)


def solution(mesh):
    chips = mesh.shape["band"] // 2
    inner = 1
    while inner * inner * 4 <= chips:
        inner *= 2
    sizes = (chips // inner, inner)
    in_specs = (
        P(("groups", "band"), None),
        P(("groups", "band"), None),
        P(("groups", "band"), None),
        P(("groups", "band"), None),
        P("band", None),
        P("band"),
        P("band"),
        P(),
        P(),
        P(),
        P(),
    )
    out_specs = (
        P(("groups", "band"), None),
        P(("groups", "band"), None),
        P("groups", None),
        P("groups", None),
    )
    return jax.shard_map(
        functools.partial(shards, sizes), mesh=mesh, in_specs=in_specs, out_specs=out_specs, check_vma=False
    )
```

```python
import functools

import jax
import jax.numpy as jnp
from jax import lax
from jax.experimental import pallas as pl
from jax.experimental.pallas import tpu as pltpu
from jax.sharding import PartitionSpec as P

BF16 = jnp.bfloat16
F32 = jnp.float32
MIB = 1024 * 1024


def dot_nn(a, b):
    return jnp.dot(a, b, preferred_element_type=F32)


def dot_tn(a, b):
    return lax.dot_general(a, b, (((0,), (0,)), ((), ())), preferred_element_type=F32)


def dot_nt(a, b):
    return lax.dot_general(a, b, (((1,), (1,)), ((), ())), preferred_element_type=F32)


def split(value):
    high = value.astype(BF16)
    low = (value - high.astype(F32)).astype(BF16)
    return high, low


def one_hot_rows(index_row, rows):
    shape = (rows, index_row.shape[1])
    hit = lax.broadcasted_iota(jnp.int32, shape, 0) == index_row
    return jnp.where(hit, 1.0, 0.0).astype(BF16)


def one_hot_columns(index_row, columns):
    lanes = index_row.shape[1]
    index = jnp.transpose(jnp.broadcast_to(index_row, (lanes, lanes)))
    pieces = []
    for start in range(0, columns, lanes):
        hit = lax.broadcasted_iota(jnp.int32, (lanes, lanes), 1) + start == index
        pieces.append(jnp.where(hit, 1.0, 0.0).astype(BF16))
    return pieces[0] if len(pieces) == 1 else jnp.concatenate(pieces, axis=1)


def tile_rows(index_ref, at, lines, rows):
    found = [one_hot_rows(index_ref[pl.ds(at * lines + k, 1), :], rows) for k in range(lines)]
    return jnp.concatenate(found, axis=1)


def tile_columns(index_ref, at, lines, columns):
    found = [one_hot_columns(index_ref[pl.ds(at * lines + k, 1), :], columns) for k in range(lines)]
    return jnp.concatenate(found, axis=0)


def place_of(sizes):
    outer, inner = sizes
    me = lax.axis_index("band")
    return me // (2 * inner), (me // 2) % inner, me % 2


def owner_at(sizes, far_outer, far_inner, far_core):
    my_outer, my_inner, my_core = place_of(sizes)
    return ((my_outer ^ far_outer) * sizes[1] + (my_inner ^ far_inner)) * 2 + (my_core ^ far_core)


def params(mib):
    return pltpu.CompilerParams(vmem_limit_bytes=mib * MIB)


def pinned(space, *values):
    return [pltpu.with_memory_space_constraint(value, space) for value in values]


def specs(space, count):
    return [pl.BlockSpec(memory_space=space)] * count


def cost(flops, nbytes):
    return pl.CostEstimate(flops=flops, bytes_accessed=nbytes, transcendentals=0)


def load(pairs, sems):
    copies = [pltpu.make_async_copy(source, target, sems.at[at]) for at, (source, target) in enumerate(pairs)]
    for copy in copies:
        copy.start()
    return copies


def pick_kernel(sizes, rows_hbm, grid_hbm, keep_ref, send_ref, rows_ref, grid_ref, picked_ref, sems):
    outer, inner = sizes
    block = grid_ref.shape[0] // 4
    parts = [pl.ds(at * block, block) for at in range(4)]
    copies = load([(rows_hbm, rows_ref)] + [(grid_hbm.at[part, :], grid_ref.at[part, :]) for part in parts], sems)
    copies[0].wait()
    picked = picked_ref.shape[0]
    chosen = [one_hot_columns(rows_ref[:, at : at + 128], grid_ref.shape[0]) for at in range(0, picked, 128)]
    for copy in copies[1:]:
        copy.wait()
    for at, some in enumerate(chosen):
        picked_ref[at * 128 : (at + 1) * 128, :] = dot_nn(some, grid_ref[...])
    cap = picked // (2 * outer * inner)
    for far_core, target in enumerate((keep_ref, send_ref)):
        blocks = []
        for far_inner in range(inner):
            for far_outer in range(outer):
                owner = owner_at(sizes, far_outer, far_inner, far_core)
                blocks.append(picked_ref[pl.ds(pl.multiple_of(owner * cap, cap), cap), :])
        target[...] = jnp.concatenate(blocks, axis=0).astype(BF16)


def mix_kernel(count, minor, *refs):
    sources, targets = refs[:-count], refs[-count:]
    values = [ref[...].astype(F32) for ref in sources]
    unit = values[0].shape[0] // (count * minor)
    for at, target in enumerate(targets):
        starts = [(at * minor + k) * unit for k in range(minor)]
        blocks = [value[start : start + unit] for start in starts for value in values]
        target[...] = jnp.concatenate(blocks, axis=0).astype(BF16)


def put_kernel(sizes, rows_hbm, *refs):
    outer, inner = sizes
    blocks, (out_ref, ordered_ref, rows_ref, sems) = refs[:outer], refs[outer:]
    (copy,) = load([(rows_hbm, rows_ref)], sems)
    place_rows(sizes, blocks, ordered_ref)
    copy.wait()
    chosen = one_hot_rows(rows_ref[...], out_ref.shape[0])
    out_ref[...] = dot_nn(chosen, ordered_ref[...].astype(BF16))


def place_rows(sizes, blocks, ordered_ref):
    outer, inner = sizes
    cap = ordered_ref.shape[0] // (2 * outer * inner)
    for far_outer, block in enumerate(blocks):
        value = block[block.shape[0] - 2 * inner * cap :, :].astype(F32)
        for at in range(2 * inner):
            owner = owner_at(sizes, far_outer, at // 2, at % 2)
            ordered_ref[pl.ds(pl.multiple_of(owner * cap, cap), cap), :] = value[at * cap : (at + 1) * cap]


def ready_kernel(
    lines,
    dst_hbm,
    mesh_hbm,
    cot_hbm,
    w1_hbm,
    wn1_hbm,
    wn2_hbm,
    hot_hbm,
    node_hbm,
    cot_out_hbm,
    moved_ref,
    dst_ref,
    mesh_ref,
    cot_ref,
    w1_ref,
    wn1_ref,
    wn2_ref,
    hot_ref,
    node_ref,
    cot_out_ref,
    sems,
    out_sems,
):
    width = mesh_ref.shape[1]
    tile = lines * 128
    pairs = [
        (dst_hbm, dst_ref),
        (mesh_hbm, mesh_ref),
        (w1_hbm.at[pl.ds(width, width), :], w1_ref),
        (wn1_hbm.at[pl.ds(0, width), :], wn1_ref),
        (cot_hbm, cot_ref),
        (wn2_hbm, wn2_ref),
    ]
    copies = load(pairs, sems)
    outs = [
        pltpu.make_async_copy(source, target, out_sems.at[at])
        for at, (source, target) in enumerate([(hot_ref, hot_hbm), (node_ref, node_hbm), (cot_out_ref, cot_out_hbm)])
    ]
    copies[0].wait()
    for at in range(hot_ref.shape[0] // tile):
        hot_ref[at * tile : (at + 1) * tile, :] = tile_columns(dst_ref, at, lines, hot_ref.shape[1])
    outs[0].start()
    copies[1].wait()
    copies[3].wait()
    node_ref[...] = dot_nn(mesh_ref[...], wn1_ref[...])
    outs[1].start()
    copies[4].wait()
    copies[5].wait()
    cot_out_ref[...] = dot_nt(cot_ref[...], wn2_ref[...])
    outs[2].start()
    copies[2].wait()
    moved_ref[...] = dot_nn(mesh_ref[...], w1_ref[...]).astype(BF16)
    for copy in outs:
        copy.wait()


def base_kernel(
    lines,
    hot_hbm,
    edge_hbm,
    w1_hbm,
    slot_hbm,
    dst_hbm,
    moved_ref,
    base_ref,
    slot_ref,
    dst_ref,
    top_ref,
    turned_hbm,
    hot_ref,
    edge_ref,
    w1_ref,
    turned_ref,
    sems,
    out_sems,
):
    width = edge_ref.shape[1]
    tile = lines * 128
    tiles = edge_ref.shape[0] // tile
    pairs = [(edge_hbm.at[pl.ds(at * tile, tile), :], edge_ref.at[pl.ds(at * tile, tile), :]) for at in range(tiles)]
    pairs += [(w1_hbm.at[pl.ds(2 * width, width), :], w1_ref), (hot_hbm, hot_ref)]
    pairs += [(w1_hbm.at[pl.ds(0, width), :], top_ref), (slot_hbm, slot_ref), (dst_hbm, dst_ref)]
    copies = load(pairs, sems)
    same = lax.broadcasted_iota(jnp.int32, (256, 256), 0) == lax.broadcasted_iota(jnp.int32, (256, 256), 1)
    eye = jnp.where(same, 1.0, 0.0).astype(BF16)
    outs = []
    for at in range(tiles):
        rows = slice(at * tile, (at + 1) * tile)
        copies[at].wait()
        for start in range(0, width, 256):
            block = dot_nt(eye, edge_ref[rows, start : start + 256])
            turned_ref[start : start + 256, rows] = block.astype(BF16)
        columns = pl.ds(at * tile, tile)
        out = pltpu.make_async_copy(turned_ref.at[:, columns], turned_hbm.at[:, columns], out_sems.at[at])
        out.start()
        outs.append(out)
    copies[tiles].wait()
    copies[tiles + 1].wait()
    for at in range(tiles):
        rows = slice(at * tile, (at + 1) * tile)
        base_ref[rows, :] = dot_nn(edge_ref[rows, :], w1_ref[...]) + dot_nn(hot_ref[rows, :], moved_ref[...])
    for out in outs + copies[tiles + 2 :]:
        out.wait()


def main_kernel(
    lines,
    sizes,
    mesh_hbm,
    w2_hbm,
    wn1_hbm,
    turned_hbm,
    hot_hbm,
    node_hbm,
    cot_hbm,
    base_ref,
    slot_ref,
    dst_ref,
    w1_ref,
    *rest,
):
    outer, inner = sizes
    slot_blocks, rest = rest[:outer], rest[outer:]
    node_out_ref, d_slots_ref = rest[:2]
    send_refs, keep_refs, rest = rest[2 : 2 + outer], rest[2 + outer : 2 + 2 * outer], rest[2 + 2 * outer :]
    slope_ref, value_ref, both_ref, grads_ref, slot_grads_ref, ordered_ref = rest[:6]
    mesh_ref, w2_ref, wn1_ref, hot_ref, node_ref, cot_ref, picks_ref, sems = rest[6:]
    width = mesh_ref.shape[1]
    mesh_rows = mesh_ref.shape[0]
    slot_rows = ordered_ref.shape[0]
    tile = lines * 128
    tiles = base_ref.shape[0] // tile
    pairs = [
        (w2_hbm, w2_ref),
        (wn1_hbm.at[pl.ds(width, wn1_ref.shape[0]), :], wn1_ref),
        (mesh_hbm, mesh_ref),
        (node_hbm, node_ref),
        (cot_hbm, cot_ref),
        (hot_hbm, hot_ref),
        (turned_hbm, both_ref.at[pl.ds(slot_rows + mesh_rows, width), :]),
    ]
    copies = load(pairs, sems)
    place_rows(sizes, slot_blocks, ordered_ref)
    slots_value = ordered_ref[...].astype(BF16)
    for at in range(tiles):
        rows = slice(at * tile, (at + 1) * tile)
        picks_ref[rows, :] = tile_columns(slot_ref, at, lines, slot_rows)
        both_ref[:slot_rows, rows] = tile_rows(slot_ref, at, lines, slot_rows)
        both_ref[slot_rows : slot_rows + mesh_rows, rows] = tile_rows(dst_ref, at, lines, mesh_rows)

    slots = slots_value
    slot_pair = jnp.concatenate(split(dot_nn(slots, w1_ref[...])), axis=0)
    for at in range(tiles):
        rows = slice(at * tile, (at + 1) * tile)
        from_slot = picks_ref[rows, :]
        twice = jnp.concatenate([from_slot, from_slot], axis=1)
        pre = base_ref[rows, :] + dot_nn(twice, slot_pair)
        sigma = 0.5 + 0.5 * jnp.tanh(0.5 * pre)
        hidden = pre * sigma
        slope_ref[rows, :] = sigma + hidden * (1.0 - sigma)
        value_ref[rows, :] = hidden.astype(BF16)

    for copy in copies[:-1]:
        copy.wait()
    hidden_sums = dot_nn(both_ref[slot_rows : slot_rows + mesh_rows, :], value_ref[...]).astype(BF16)
    received = dot_nn(hidden_sums, w2_ref[...]).astype(BF16)
    mesh = mesh_ref[...]
    pre_node = node_ref[...] + dot_nn(received, wn1_ref[...])
    sigma = 0.5 + 0.5 * jnp.tanh(0.5 * pre_node)
    node = pre_node * sigma
    slope = sigma + node * (1.0 - sigma)
    d_pre_node = (cot_ref[...] * slope).astype(BF16)
    d_received = dot_nt(d_pre_node, wn1_ref[...]).astype(BF16)
    spread = dot_nt(d_received, w2_ref[...]).astype(BF16)

    for at in range(tiles):
        rows = slice(at * tile, (at + 1) * tile)
        value_ref[rows, :] = (dot_nn(hot_ref[rows, :], spread) * slope_ref[rows, :]).astype(BF16)

    grads_ref[3 * width :, :] = dot_tn(hidden_sums, d_received)
    node_out_ref[...] = node.astype(BF16)
    copies[-1].wait()
    product = dot_nn(both_ref[...], value_ref[...])
    sums = product[: slot_rows + mesh_rows].astype(BF16)
    grads_ref[2 * width : 3 * width, :] = product[slot_rows + mesh_rows :]
    slot_grads_ref[...] = dot_nt(sums[:slot_rows], w1_ref[...])
    grads_ref[:width, :] = dot_tn(slots, sums[:slot_rows])
    grads_ref[width : 2 * width, :] = dot_tn(mesh, sums[slot_rows:])

    chunk = grads_ref.shape[0] // (2 * outer * inner)
    cap = slot_rows // (2 * outer * inner)
    for far_core in range(2):
        for far_outer in range(outer):
            for far_inner in range(inner):
                owner = owner_at(sizes, far_outer, far_inner, far_core)
                at = (far_core * outer + far_outer) * inner + far_inner
                from_rows = pl.ds(pl.multiple_of(owner * cap, cap), cap)
                ordered_ref[at * cap : (at + 1) * cap, :] = slot_grads_ref[from_rows, :]
                value = grads_ref[pl.ds(pl.multiple_of(owner * chunk, chunk), chunk), :]
                rows = slice(far_inner * chunk, (far_inner + 1) * chunk)
                if far_core:
                    send_refs[far_outer][rows, :] = value.astype(BF16)
                else:
                    keep_refs[far_outer][rows, :] = value
    halfway, share = slot_rows // 2, inner * cap
    d_slots_ref[...] = ordered_ref[:halfway, :].astype(BF16)
    for far_outer, send_ref in enumerate(send_refs):
        start = halfway + far_outer * share
        send_ref[inner * chunk :, :] = ordered_ref[start : start + share, :].astype(BF16)


def mesh_kernel(mesh_hbm, wn2_hbm, node_ref, out_ref, mesh_ref, wn2_ref, sems):
    for copy in load([(mesh_hbm, mesh_ref), (wn2_hbm, wn2_ref)], sems):
        copy.wait()
    out_ref[...] = (mesh_ref[...].astype(F32) + dot_nn(node_ref[...], wn2_ref[...])).astype(BF16)


def core_kernel(sizes, far_outer, keep_ref, crossed_ref, d_slots_ref, total_ref, mixed_ref, *part_refs):
    outer, inner = sizes
    chunk = total_ref.shape[0]
    cap = d_slots_ref.shape[0] // (outer * inner)
    start = far_outer * inner * cap
    own = d_slots_ref[start : start + inner * cap, :].astype(F32)
    far = crossed_ref[inner * chunk :, :].astype(F32)
    for far_inner in range(inner):
        rows, slots = slice(far_inner * chunk, (far_inner + 1) * chunk), slice(far_inner * cap, (far_inner + 1) * cap)
        total = keep_ref[rows, :] + crossed_ref[rows, :].astype(F32)
        mixed = jnp.concatenate([own[slots], far[slots]], axis=0).astype(BF16)
        if far_inner:
            part_refs[far_inner - 1][:chunk, :] = total.astype(BF16)
            part_refs[far_inner - 1][chunk:, :] = mixed
        else:
            total_ref[...] = total
            mixed_ref[...] = mixed


def inner_kernel(parts, arrivals, total_ref, mixed_ref, *refs):
    received, arrived, outs = refs[:parts], refs[parts : parts + arrivals], refs[parts + arrivals :]
    chunk = total_ref.shape[0]
    total = total_ref[...]
    mixed = [mixed_ref[...]]
    for part in received:
        total = total + part[:chunk, :].astype(F32)
        mixed.append(part[chunk:, :])
    for value in arrived:
        total = total + value[:chunk, :].astype(F32)
    mixed = jnp.concatenate(mixed, axis=0)
    if len(outs) == 1:
        outs[0][:chunk, :] = total.astype(BF16)
        outs[0][chunk:, :] = mixed
    else:
        outs[0][...] = total.astype(BF16)
        outs[1][...] = mixed


def order_kernel(sizes, places, aliased, *refs):
    outer, inner = sizes
    pieces = refs[: len(places)]
    first_hbm, second_hbm, stage_ref, sems = refs[len(places) + aliased :]
    chunk = pieces[0].shape[0]
    first_chunks = first_hbm.shape[0] // chunk

    def send(k, target, start):
        rows = pl.ds(pl.multiple_of(start, chunk), chunk)
        return pltpu.make_async_copy(stage_ref.at[k], target.at[rows, :], sems.at[k])

    for k, (at, piece) in enumerate(zip(places, pieces)):
        owner = owner_at(sizes, at % outer, at // outer % inner, at // (outer * inner))
        stage_ref[k] = piece[...].astype(F32)

        @pl.when(owner < first_chunks)
        def _():
            send(k, first_hbm, owner * chunk).start()

        @pl.when(owner >= first_chunks)
        def _():
            send(k, second_hbm, (owner - first_chunks) * chunk).start()

    for k in range(len(places)):
        send(k, first_hbm, 0).wait()


def shards(
    sizes,
    grid_latent,
    mesh_latent,
    edge_latent,
    mesh_cot,
    send_rows,
    edge_slot,
    edge_dst,
    w_edge1,
    w_edge2,
    w_node1,
    w_node2,
):
    outer, inner = sizes
    band_count = lax.axis_size("band")
    width = grid_latent.shape[1]
    hidden_width = w_edge1.shape[1]
    edges = edge_latent.shape[0]
    mesh_rows = mesh_latent.shape[0]
    slot_rows = send_rows.shape[1]
    lines = 4
    slot_index = edge_slot.reshape(edges // 128, 128)
    dst_index = edge_dst.reshape(edges // 128, 128)

    def permute(value, stride, size, shift):
        pairs = []
        for source in range(band_count):
            place = (source // stride) % size
            pairs.append((source, source + ((place ^ shift) - place) * stride))
        return lax.ppermute(value, "band", pairs)

    def to_core(value):
        return permute(value, 1, 2, 1)

    def to_inner(value, shift):
        return permute(value, 2, inner, shift)

    def to_outer(value, shift):
        return permute(value, 2 * inner, outer, shift)

    cap, halfway = slot_rows // band_count, slot_rows // 2
    kept, sent = pl.pallas_call(
        functools.partial(pick_kernel, sizes),
        out_shape=[jax.ShapeDtypeStruct((halfway, width), BF16)] * 2,
        in_specs=specs(pltpu.HBM, 2),
        out_specs=specs(pltpu.VMEM, 2),
        scratch_shapes=[
            pltpu.VMEM(send_rows.shape, jnp.int32),
            pltpu.VMEM(grid_latent.shape, BF16),
            pltpu.VMEM((slot_rows, width), F32),
            pltpu.SemaphoreType.DMA((5,)),
        ],
        compiler_params=params(16),
        name="pick",
    )(*pinned(pltpu.HBM, send_rows, grid_latent))

    def mix(values, count, minor):
        rows = len(values) * values[0].shape[0] // count
        return pl.pallas_call(
            functools.partial(mix_kernel, count, minor),
            out_shape=[jax.ShapeDtypeStruct((rows, width), BF16)] * count,
            compiler_params=params(16),
            name="mix",
        )(*values)

    hot, node, cot, moved = pl.pallas_call(
        functools.partial(ready_kernel, lines),
        out_shape=[
            pltpu.HBM((edges, mesh_rows), BF16),
            pltpu.HBM((mesh_rows, hidden_width), F32),
            pltpu.HBM((mesh_rows, hidden_width), F32),
            pltpu.VMEM((mesh_rows, hidden_width), BF16),
        ],
        in_specs=specs(pltpu.HBM, 6),
        out_specs=specs(pltpu.HBM, 3) + specs(pltpu.VMEM, 1),
        scratch_shapes=[
            pltpu.VMEM(dst_index.shape, jnp.int32),
            pltpu.VMEM(mesh_latent.shape, BF16),
            pltpu.VMEM(mesh_cot.shape, BF16),
            pltpu.VMEM((width, hidden_width), BF16),
            pltpu.VMEM((width, hidden_width), BF16),
            pltpu.VMEM(w_node2.shape, BF16),
            pltpu.VMEM((edges, mesh_rows), BF16),
            pltpu.VMEM((mesh_rows, hidden_width), F32),
            pltpu.VMEM((mesh_rows, hidden_width), F32),
            pltpu.SemaphoreType.DMA((6,)),
            pltpu.SemaphoreType.DMA((3,)),
        ],
        compiler_params=params(16),
        cost_estimate=cost(2 * 10**9, 4 * MIB),
        name="ready",
    )(*pinned(pltpu.HBM, dst_index, mesh_latent, mesh_cot, w_edge1, w_node1, w_node2))
    base, *ahead, turned = pl.pallas_call(
        functools.partial(base_kernel, lines),
        out_shape=[
            pltpu.VMEM((edges, hidden_width), F32),
            pltpu.VMEM(slot_index.shape, jnp.int32),
            pltpu.VMEM(dst_index.shape, jnp.int32),
            pltpu.VMEM((width, hidden_width), BF16),
            pltpu.HBM((width, edges), BF16),
        ],
        in_specs=specs(pltpu.HBM, 5) + specs(pltpu.VMEM, 1),
        out_specs=specs(pltpu.VMEM, 4) + specs(pltpu.HBM, 1),
        scratch_shapes=[
            pltpu.VMEM((edges, mesh_rows), BF16),
            pltpu.VMEM(edge_latent.shape, BF16),
            pltpu.VMEM((width, hidden_width), BF16),
            pltpu.VMEM((width, edges), BF16),
            pltpu.SemaphoreType.DMA((5 + edges // (128 * lines),)),
            pltpu.SemaphoreType.DMA((edges // (128 * lines),)),
        ],
        compiler_params=params(16),
        cost_estimate=cost(4 * 10**9, 4 * MIB),
        name="base",
    )(*pinned(pltpu.HBM, hot, edge_latent, w_edge1, slot_index, dst_index), *pinned(pltpu.VMEM, moved))

    by_inner = mix([kept, to_core(sent)], inner, outer)
    by_inner = [by_inner[0]] + [to_inner(by_inner[k], k) for k in range(1, inner)]
    by_outer = mix(by_inner, outer, 1)
    slot_blocks = [by_outer[0]] + [to_outer(by_outer[k], k) for k in range(1, outer)]

    grad_rows = 3 * width + hidden_width
    chunk = grad_rows // band_count
    group = (inner * chunk, hidden_width)
    node_out, d_slots, *sides = pl.pallas_call(
        functools.partial(main_kernel, lines, sizes),
        out_shape=[
            jax.ShapeDtypeStruct((mesh_rows, width), BF16),
            jax.ShapeDtypeStruct((halfway, width), BF16),
        ]
        + [jax.ShapeDtypeStruct((group[0] + inner * cap, hidden_width), BF16)] * outer
        + [jax.ShapeDtypeStruct(group, F32)] * outer,
        in_specs=specs(pltpu.HBM, 7) + specs(pltpu.VMEM, 4 + outer),
        out_specs=specs(pltpu.VMEM, 2 + 2 * outer),
        scratch_shapes=[
            pltpu.VMEM((edges, hidden_width), F32),
            pltpu.VMEM((edges, hidden_width), BF16),
            pltpu.VMEM((slot_rows + mesh_rows + width, edges), BF16),
            pltpu.VMEM((grad_rows, hidden_width), F32),
            pltpu.VMEM((slot_rows, width), F32),
            pltpu.VMEM((slot_rows, width), F32),
            pltpu.VMEM(mesh_latent.shape, BF16),
            pltpu.VMEM(w_edge2.shape, BF16),
            pltpu.VMEM((w_node1.shape[0] - width, w_node1.shape[1]), BF16),
            pltpu.VMEM(hot.shape, BF16),
            pltpu.VMEM(node.shape, F32),
            pltpu.VMEM(cot.shape, F32),
            pltpu.VMEM((edges, slot_rows), BF16),
            pltpu.SemaphoreType.DMA((7,)),
        ],
        compiler_params=params(40),
        name="edges",
    )(
        *pinned(pltpu.HBM, mesh_latent, w_edge2, w_node1, turned, hot, node, cot),
        *pinned(pltpu.VMEM, base, *ahead),
        *slot_blocks,
    )
    mesh_out = pl.pallas_call(
        mesh_kernel,
        out_shape=jax.ShapeDtypeStruct((mesh_rows, width), BF16),
        in_specs=specs(pltpu.HBM, 2) + specs(pltpu.VMEM, 1),
        out_specs=pl.BlockSpec(memory_space=pltpu.VMEM),
        scratch_shapes=[
            pltpu.VMEM(mesh_latent.shape, BF16),
            pltpu.VMEM(w_node2.shape, BF16),
            pltpu.SemaphoreType.DMA((2,)),
        ],
        compiler_params=params(16),
        cost_estimate=cost(10**9, MIB),
        name="mesh",
    )(*pinned(pltpu.HBM, mesh_latent, w_node2), node_out)
    sends, keeps = sides[:outer], sides[outer:]
    small = (2 * cap, width)
    arrived = {}
    first = None
    for k in [outer - 1, *range(1, outer - 1), 0]:
        send = sends[k] if first is None else lax.optimization_barrier((sends[k], first))[0]
        crossed = to_core(send)
        total, mixed, *parts = pl.pallas_call(
            functools.partial(core_kernel, sizes, k),
            out_shape=[
                jax.ShapeDtypeStruct((chunk, hidden_width), F32),
                jax.ShapeDtypeStruct(small, BF16),
            ]
            + [jax.ShapeDtypeStruct((chunk + 2 * cap, width), BF16)] * (inner - 1),
            compiler_params=params(16),
            cost_estimate=cost(10**9, MIB),
            name="core",
        )(keeps[k], crossed, d_slots)
        first = parts[0] if first is None else first
        parts = [to_inner(part, at + 1) for at, part in enumerate(parts)]
        block = 2 * inner * cap
        if k:
            (out,) = pl.pallas_call(
                functools.partial(inner_kernel, inner - 1, 0),
                out_shape=[jax.ShapeDtypeStruct((chunk + block, width), BF16)],
                compiler_params=params(16),
                name="inner",
            )(total, mixed, *parts)
            arrived[k] = to_outer(out, k)
        else:
            total = lax.optimization_barrier((total, mesh_out))[0]
            own, home = pl.pallas_call(
                functools.partial(inner_kernel, inner - 1, outer - 1),
                out_shape=[
                    jax.ShapeDtypeStruct((chunk, hidden_width), BF16),
                    jax.ShapeDtypeStruct((block, width), BF16),
                ],
                compiler_params=params(16),
                name="own",
            )(total, mixed, *parts, *[arrived[at] for at in range(1, outer)])

    grid_grad = pl.pallas_call(
        functools.partial(put_kernel, sizes),
        out_shape=jax.ShapeDtypeStruct(grid_latent.shape, F32),
        in_specs=specs(pltpu.HBM, 1) + specs(pltpu.VMEM, outer),
        out_specs=pl.BlockSpec(memory_space=pltpu.VMEM),
        scratch_shapes=[
            pltpu.VMEM((slot_rows, width), F32),
            pltpu.VMEM(send_rows.shape, jnp.int32),
            pltpu.SemaphoreType.DMA((1,)),
        ],
        compiler_params=params(16),
        cost_estimate=cost(2 * 10**9, 2 * MIB),
        name="put",
    )(*pinned(pltpu.HBM, send_rows), home, *[arrived[at] for at in range(1, outer)])

    pieces = {0: own}
    stride = outer // 2
    while stride:
        for at in range(0, outer, 2 * stride):
            value = pieces[at]
            if at == outer // 2 and stride == outer // 4:
                value = lax.optimization_barrier((value, grid_grad))[0]
            pieces[at + stride] = to_outer(value, stride)
        stride //= 2
    halfway_at = band_count // 2
    pieces[halfway_at] = to_core(own)
    for far_inner in range(1, inner):
        for far_outer in range(outer):
            value = pieces[far_outer]
            if far_outer == outer // 2:
                value = lax.optimization_barrier((value, pieces[halfway_at]))[0]
            pieces[far_inner * outer + far_outer] = to_inner(value, far_inner)
    for at in range(1, halfway_at - 1):
        pieces[halfway_at + at] = to_core(pieces[at])

    last = outer - 1
    stages = [[], [], []]
    for at in range(band_count):
        far_outer, far_inner, far_core = at % outer, at // outer % inner, at // halfway_at
        if far_outer == last:
            stages[2 if far_inner else 1].append(at)
        else:
            stages[1 if far_inner and (far_core or far_outer == outer // 2) else 0].append(at)
    grads = []
    for places in stages:
        if places is stages[1]:
            value = lax.optimization_barrier((pieces[halfway_at - 1], *grads))[0]
            pieces[band_count - 1] = to_core(value)
        grads = pl.pallas_call(
            functools.partial(order_kernel, sizes, places, len(grads)),
            out_shape=[
                jax.ShapeDtypeStruct((3 * width, hidden_width), F32),
                jax.ShapeDtypeStruct((hidden_width, width), F32),
            ],
            in_specs=specs(pltpu.VMEM, len(places)) + specs(pltpu.HBM, len(grads)),
            out_specs=specs(pltpu.HBM, 2),
            scratch_shapes=[
                pltpu.VMEM((len(places), chunk, hidden_width), F32),
                pltpu.SemaphoreType.DMA((len(places),)),
            ],
            input_output_aliases={len(places) + k: k for k in range(len(grads))},
            compiler_params=params(16),
            cost_estimate=cost(15 * 10**7 * len(places), 2 * MIB),
            name="order",
        )(*[pieces[at] for at in places], *grads)
    grad_edge1, grad_edge2 = grads
    return (mesh_out, grid_grad, grad_edge1, grad_edge2)


def solution(mesh):
    chips = mesh.shape["band"] // 2
    inner = 1
    while inner * inner * 4 <= chips:
        inner *= 2
    sizes = (chips // inner, inner)
    in_specs = (
        P(("groups", "band"), None),
        P(("groups", "band"), None),
        P(("groups", "band"), None),
        P(("groups", "band"), None),
        P("band", None),
        P("band"),
        P("band"),
        P(),
        P(),
        P(),
        P(),
    )
    out_specs = (
        P(("groups", "band"), None),
        P(("groups", "band"), None),
        P("groups", None),
        P("groups", None),
    )
    return jax.shard_map(
        functools.partial(shards, sizes), mesh=mesh, in_specs=in_specs, out_specs=out_specs, check_vma=False
    )
```

```python
import functools

import jax
import jax.numpy as jnp
from jax import lax
from jax.experimental import pallas as pl
from jax.experimental.pallas import tpu as pltpu
from jax.sharding import PartitionSpec as P

BF16 = jnp.bfloat16
F32 = jnp.float32
MIB = 1024 * 1024


def dot_nn(a, b):
    return jnp.dot(a, b, preferred_element_type=F32)


def dot_tn(a, b):
    return lax.dot_general(a, b, (((0,), (0,)), ((), ())), preferred_element_type=F32)


def dot_nt(a, b):
    return lax.dot_general(a, b, (((1,), (1,)), ((), ())), preferred_element_type=F32)


def split(value):
    high = value.astype(BF16)
    low = (value - high.astype(F32)).astype(BF16)
    return high, low


def one_hot_rows(index_row, rows):
    shape = (rows, index_row.shape[1])
    hit = lax.broadcasted_iota(jnp.int32, shape, 0) == index_row
    return jnp.where(hit, 1.0, 0.0).astype(BF16)


def one_hot_columns(index_row, columns):
    lanes = index_row.shape[1]
    index = jnp.transpose(jnp.broadcast_to(index_row, (lanes, lanes)))
    pieces = []
    for start in range(0, columns, lanes):
        hit = lax.broadcasted_iota(jnp.int32, (lanes, lanes), 1) + start == index
        pieces.append(jnp.where(hit, 1.0, 0.0).astype(BF16))
    return pieces[0] if len(pieces) == 1 else jnp.concatenate(pieces, axis=1)


def tile_rows(index_ref, at, lines, rows):
    found = [one_hot_rows(index_ref[pl.ds(at * lines + k, 1), :], rows) for k in range(lines)]
    return jnp.concatenate(found, axis=1)


def tile_columns(index_ref, at, lines, columns):
    found = [one_hot_columns(index_ref[pl.ds(at * lines + k, 1), :], columns) for k in range(lines)]
    return jnp.concatenate(found, axis=0)


def place_of(sizes):
    outer, inner = sizes
    me = lax.axis_index("band")
    return me // (2 * inner), (me // 2) % inner, me % 2


def owner_at(sizes, far_outer, far_inner, far_core):
    my_outer, my_inner, my_core = place_of(sizes)
    return ((my_outer ^ far_outer) * sizes[1] + (my_inner ^ far_inner)) * 2 + (my_core ^ far_core)


def params(mib):
    return pltpu.CompilerParams(vmem_limit_bytes=mib * MIB)


def pinned(space, *values):
    return [pltpu.with_memory_space_constraint(value, space) for value in values]


def specs(space, count):
    return [pl.BlockSpec(memory_space=space)] * count


def cost(flops, nbytes):
    return pl.CostEstimate(flops=flops, bytes_accessed=nbytes, transcendentals=0)


def load(pairs, sems):
    copies = [pltpu.make_async_copy(source, target, sems.at[at]) for at, (source, target) in enumerate(pairs)]
    for copy in copies:
        copy.start()
    return copies


def pick_kernel(sizes, rows_hbm, grid_hbm, keep_ref, send_ref, rows_ref, grid_ref, picked_ref, sems):
    outer, inner = sizes
    block = grid_ref.shape[0] // 4
    parts = [pl.ds(at * block, block) for at in range(4)]
    copies = load([(rows_hbm, rows_ref)] + [(grid_hbm.at[part, :], grid_ref.at[part, :]) for part in parts], sems)
    copies[0].wait()
    picked = picked_ref.shape[0]
    chosen = [one_hot_columns(rows_ref[:, at : at + 128], grid_ref.shape[0]) for at in range(0, picked, 128)]
    for copy in copies[1:]:
        copy.wait()
    for at, some in enumerate(chosen):
        picked_ref[at * 128 : (at + 1) * 128, :] = dot_nn(some, grid_ref[...])
    cap = picked // (2 * outer * inner)
    for far_core, target in enumerate((keep_ref, send_ref)):
        blocks = []
        for far_inner in range(inner):
            for far_outer in range(outer):
                owner = owner_at(sizes, far_outer, far_inner, far_core)
                blocks.append(picked_ref[pl.ds(pl.multiple_of(owner * cap, cap), cap), :])
        target[...] = jnp.concatenate(blocks, axis=0).astype(BF16)


def mix_kernel(count, minor, *refs):
    sources, targets = refs[:-count], refs[-count:]
    values = [ref[...].astype(F32) for ref in sources]
    unit = values[0].shape[0] // (count * minor)
    for at, target in enumerate(targets):
        starts = [(at * minor + k) * unit for k in range(minor)]
        blocks = [value[start : start + unit] for start in starts for value in values]
        target[...] = jnp.concatenate(blocks, axis=0).astype(BF16)


def put_kernel(sizes, rows_hbm, *refs):
    outer, inner = sizes
    blocks, (out_ref, ordered_ref, rows_ref, sems) = refs[:outer], refs[outer:]
    (copy,) = load([(rows_hbm, rows_ref)], sems)
    place_rows(sizes, blocks, ordered_ref)
    copy.wait()
    chosen = one_hot_rows(rows_ref[...], out_ref.shape[0])
    out_ref[...] = dot_nn(chosen, ordered_ref[...].astype(BF16))


def place_rows(sizes, blocks, ordered_ref):
    outer, inner = sizes
    cap = ordered_ref.shape[0] // (2 * outer * inner)
    for far_outer, block in enumerate(blocks):
        value = block[block.shape[0] - 2 * inner * cap :, :].astype(F32)
        for at in range(2 * inner):
            owner = owner_at(sizes, far_outer, at // 2, at % 2)
            ordered_ref[pl.ds(pl.multiple_of(owner * cap, cap), cap), :] = value[at * cap : (at + 1) * cap]


def ready_kernel(
    lines,
    dst_hbm,
    mesh_hbm,
    cot_hbm,
    w1_hbm,
    wn1_hbm,
    wn2_hbm,
    hot_hbm,
    node_hbm,
    cot_out_hbm,
    moved_ref,
    dst_ref,
    mesh_ref,
    cot_ref,
    w1_ref,
    wn1_ref,
    wn2_ref,
    hot_ref,
    node_ref,
    cot_out_ref,
    sems,
    out_sems,
):
    width = mesh_ref.shape[1]
    tile = lines * 128
    pairs = [
        (dst_hbm, dst_ref),
        (mesh_hbm, mesh_ref),
        (w1_hbm.at[pl.ds(width, width), :], w1_ref),
        (wn1_hbm.at[pl.ds(0, width), :], wn1_ref),
        (cot_hbm, cot_ref),
        (wn2_hbm, wn2_ref),
    ]
    copies = load(pairs, sems)
    outs = [
        pltpu.make_async_copy(source, target, out_sems.at[at])
        for at, (source, target) in enumerate([(hot_ref, hot_hbm), (node_ref, node_hbm), (cot_out_ref, cot_out_hbm)])
    ]
    copies[0].wait()
    for at in range(hot_ref.shape[0] // tile):
        hot_ref[at * tile : (at + 1) * tile, :] = tile_columns(dst_ref, at, lines, hot_ref.shape[1])
    outs[0].start()
    copies[1].wait()
    copies[3].wait()
    node_ref[...] = dot_nn(mesh_ref[...], wn1_ref[...])
    outs[1].start()
    copies[4].wait()
    copies[5].wait()
    cot_out_ref[...] = dot_nt(cot_ref[...], wn2_ref[...])
    outs[2].start()
    copies[2].wait()
    moved_ref[...] = dot_nn(mesh_ref[...], w1_ref[...]).astype(BF16)
    for copy in outs:
        copy.wait()


def base_kernel(
    lines,
    hot_hbm,
    edge_hbm,
    w1_hbm,
    slot_hbm,
    dst_hbm,
    moved_ref,
    base_ref,
    slot_ref,
    dst_ref,
    top_ref,
    turned_hbm,
    hot_ref,
    edge_ref,
    w1_ref,
    turned_ref,
    sems,
    out_sems,
):
    width = edge_ref.shape[1]
    tile = lines * 128
    tiles = edge_ref.shape[0] // tile
    pairs = [(edge_hbm.at[pl.ds(at * tile, tile), :], edge_ref.at[pl.ds(at * tile, tile), :]) for at in range(tiles)]
    pairs += [(w1_hbm.at[pl.ds(2 * width, width), :], w1_ref), (hot_hbm, hot_ref)]
    pairs += [(w1_hbm.at[pl.ds(0, width), :], top_ref), (slot_hbm, slot_ref), (dst_hbm, dst_ref)]
    copies = load(pairs, sems)
    same = lax.broadcasted_iota(jnp.int32, (256, 256), 0) == lax.broadcasted_iota(jnp.int32, (256, 256), 1)
    eye = jnp.where(same, 1.0, 0.0).astype(BF16)
    outs = []
    for at in range(tiles):
        rows = slice(at * tile, (at + 1) * tile)
        copies[at].wait()
        for start in range(0, width, 256):
            block = dot_nt(eye, edge_ref[rows, start : start + 256])
            turned_ref[start : start + 256, rows] = block.astype(BF16)
        columns = pl.ds(at * tile, tile)
        out = pltpu.make_async_copy(turned_ref.at[:, columns], turned_hbm.at[:, columns], out_sems.at[at])
        out.start()
        outs.append(out)
    copies[tiles].wait()
    copies[tiles + 1].wait()
    for at in range(tiles):
        rows = slice(at * tile, (at + 1) * tile)
        base_ref[rows, :] = dot_nn(edge_ref[rows, :], w1_ref[...]) + dot_nn(hot_ref[rows, :], moved_ref[...])
    for out in outs + copies[tiles + 2 :]:
        out.wait()


def main_kernel(
    lines,
    sizes,
    mesh_hbm,
    w2_hbm,
    wn1_hbm,
    turned_hbm,
    hot_hbm,
    node_hbm,
    cot_hbm,
    base_ref,
    slot_ref,
    dst_ref,
    w1_ref,
    *rest,
):
    outer, inner = sizes
    slot_blocks, rest = rest[:outer], rest[outer:]
    node_out_ref, d_slots_ref = rest[:2]
    send_refs, keep_refs, rest = rest[2 : 2 + outer], rest[2 + outer : 2 + 2 * outer], rest[2 + 2 * outer :]
    slope_ref, value_ref, both_ref, grads_ref, slot_grads_ref, ordered_ref = rest[:6]
    mesh_ref, w2_ref, wn1_ref, hot_ref, node_ref, cot_ref, picks_ref, sems = rest[6:]
    width = mesh_ref.shape[1]
    mesh_rows = mesh_ref.shape[0]
    slot_rows = ordered_ref.shape[0]
    tile = lines * 128
    tiles = base_ref.shape[0] // tile
    pairs = [
        (w2_hbm, w2_ref),
        (wn1_hbm.at[pl.ds(width, wn1_ref.shape[0]), :], wn1_ref),
        (mesh_hbm, mesh_ref),
        (node_hbm, node_ref),
        (cot_hbm, cot_ref),
        (hot_hbm, hot_ref),
        (turned_hbm, both_ref.at[pl.ds(slot_rows + mesh_rows, width), :]),
    ]
    copies = load(pairs, sems)
    place_rows(sizes, slot_blocks, ordered_ref)
    slots_value = ordered_ref[...].astype(BF16)
    for at in range(tiles):
        rows = slice(at * tile, (at + 1) * tile)
        picks_ref[rows, :] = tile_columns(slot_ref, at, lines, slot_rows)
        both_ref[:slot_rows, rows] = tile_rows(slot_ref, at, lines, slot_rows)
        both_ref[slot_rows : slot_rows + mesh_rows, rows] = tile_rows(dst_ref, at, lines, mesh_rows)

    slots = slots_value
    slot_pair = jnp.concatenate(split(dot_nn(slots, w1_ref[...])), axis=0)
    for at in range(tiles):
        rows = slice(at * tile, (at + 1) * tile)
        from_slot = picks_ref[rows, :]
        twice = jnp.concatenate([from_slot, from_slot], axis=1)
        pre = base_ref[rows, :] + dot_nn(twice, slot_pair)
        sigma = 0.5 + 0.5 * jnp.tanh(0.5 * pre)
        hidden = pre * sigma
        slope_ref[rows, :] = sigma + hidden * (1.0 - sigma)
        value_ref[rows, :] = hidden.astype(BF16)

    for copy in copies[:-1]:
        copy.wait()
    hidden_sums = dot_nn(both_ref[slot_rows : slot_rows + mesh_rows, :], value_ref[...]).astype(BF16)
    received = dot_nn(hidden_sums, w2_ref[...]).astype(BF16)
    mesh = mesh_ref[...]
    pre_node = node_ref[...] + dot_nn(received, wn1_ref[...])
    sigma = 0.5 + 0.5 * jnp.tanh(0.5 * pre_node)
    node = pre_node * sigma
    slope = sigma + node * (1.0 - sigma)
    d_pre_node = (cot_ref[...] * slope).astype(BF16)
    d_received = dot_nt(d_pre_node, wn1_ref[...]).astype(BF16)
    spread = dot_nt(d_received, w2_ref[...]).astype(BF16)

    for at in range(tiles):
        rows = slice(at * tile, (at + 1) * tile)
        value_ref[rows, :] = (dot_nn(hot_ref[rows, :], spread) * slope_ref[rows, :]).astype(BF16)

    grads_ref[3 * width :, :] = dot_tn(hidden_sums, d_received)
    node_out_ref[...] = node.astype(BF16)
    copies[-1].wait()
    product = dot_nn(both_ref[...], value_ref[...])
    sums = product[: slot_rows + mesh_rows].astype(BF16)
    grads_ref[2 * width : 3 * width, :] = product[slot_rows + mesh_rows :]
    slot_grads_ref[...] = dot_nt(sums[:slot_rows], w1_ref[...])
    grads_ref[:width, :] = dot_tn(slots, sums[:slot_rows])
    grads_ref[width : 2 * width, :] = dot_tn(mesh, sums[slot_rows:])

    chunk = grads_ref.shape[0] // (2 * outer * inner)
    cap = slot_rows // (2 * outer * inner)
    for far_core in range(2):
        for far_outer in range(outer):
            for far_inner in range(inner):
                owner = owner_at(sizes, far_outer, far_inner, far_core)
                at = (far_core * outer + far_outer) * inner + far_inner
                from_rows = pl.ds(pl.multiple_of(owner * cap, cap), cap)
                ordered_ref[at * cap : (at + 1) * cap, :] = slot_grads_ref[from_rows, :]
                value = grads_ref[pl.ds(pl.multiple_of(owner * chunk, chunk), chunk), :]
                rows = slice(far_inner * chunk, (far_inner + 1) * chunk)
                if far_core:
                    send_refs[far_outer][rows, :] = value.astype(BF16)
                else:
                    keep_refs[far_outer][rows, :] = value
    halfway, share = slot_rows // 2, inner * cap
    d_slots_ref[...] = ordered_ref[:halfway, :].astype(BF16)
    for far_outer, send_ref in enumerate(send_refs):
        start = halfway + far_outer * share
        send_ref[inner * chunk :, :] = ordered_ref[start : start + share, :].astype(BF16)


def mesh_kernel(mesh_hbm, wn2_hbm, node_ref, out_ref, mesh_ref, wn2_ref, sems):
    for copy in load([(mesh_hbm, mesh_ref), (wn2_hbm, wn2_ref)], sems):
        copy.wait()
    out_ref[...] = (mesh_ref[...].astype(F32) + dot_nn(node_ref[...], wn2_ref[...])).astype(BF16)


def core_kernel(sizes, far_outer, keep_ref, crossed_ref, d_slots_ref, total_ref, mixed_ref, *part_refs):
    outer, inner = sizes
    chunk = total_ref.shape[0]
    cap = d_slots_ref.shape[0] // (outer * inner)
    start = far_outer * inner * cap
    own = d_slots_ref[start : start + inner * cap, :].astype(F32)
    far = crossed_ref[inner * chunk :, :].astype(F32)
    for far_inner in range(inner):
        rows, slots = slice(far_inner * chunk, (far_inner + 1) * chunk), slice(far_inner * cap, (far_inner + 1) * cap)
        total = keep_ref[rows, :] + crossed_ref[rows, :].astype(F32)
        mixed = jnp.concatenate([own[slots], far[slots]], axis=0).astype(BF16)
        if far_inner:
            part_refs[far_inner - 1][:chunk, :] = total.astype(BF16)
            part_refs[far_inner - 1][chunk:, :] = mixed
        else:
            total_ref[...] = total
            mixed_ref[...] = mixed


def inner_kernel(parts, arrivals, total_ref, mixed_ref, *refs):
    received, arrived, outs = refs[:parts], refs[parts : parts + arrivals], refs[parts + arrivals :]
    chunk = total_ref.shape[0]
    total = total_ref[...]
    mixed = [mixed_ref[...]]
    for part in received:
        total = total + part[:chunk, :].astype(F32)
        mixed.append(part[chunk:, :])
    for value in arrived:
        total = total + value[:chunk, :].astype(F32)
    mixed = jnp.concatenate(mixed, axis=0)
    if len(outs) == 1:
        outs[0][:chunk, :] = total.astype(BF16)
        outs[0][chunk:, :] = mixed
    else:
        outs[0][...] = total.astype(BF16)
        outs[1][...] = mixed


def order_kernel(sizes, places, aliased, *refs):
    outer, inner = sizes
    pieces = refs[: len(places)]
    first_hbm, second_hbm, stage_ref, sems = refs[len(places) + aliased :]
    chunk = pieces[0].shape[0]
    first_chunks = first_hbm.shape[0] // chunk

    def send(k, target, start):
        rows = pl.ds(pl.multiple_of(start, chunk), chunk)
        return pltpu.make_async_copy(stage_ref.at[k], target.at[rows, :], sems.at[k])

    for k, (at, piece) in enumerate(zip(places, pieces)):
        owner = owner_at(sizes, at % outer, at // outer % inner, at // (outer * inner))
        stage_ref[k] = piece[...].astype(F32)

        @pl.when(owner < first_chunks)
        def _():
            send(k, first_hbm, owner * chunk).start()

        @pl.when(owner >= first_chunks)
        def _():
            send(k, second_hbm, (owner - first_chunks) * chunk).start()

    for k in range(len(places)):
        send(k, first_hbm, 0).wait()


def shards(
    sizes,
    grid_latent,
    mesh_latent,
    edge_latent,
    mesh_cot,
    send_rows,
    edge_slot,
    edge_dst,
    w_edge1,
    w_edge2,
    w_node1,
    w_node2,
):
    outer, inner = sizes
    band_count = lax.axis_size("band")
    width = grid_latent.shape[1]
    hidden_width = w_edge1.shape[1]
    edges = edge_latent.shape[0]
    mesh_rows = mesh_latent.shape[0]
    slot_rows = send_rows.shape[1]
    lines = 4
    slot_index = edge_slot.reshape(edges // 128, 128)
    dst_index = edge_dst.reshape(edges // 128, 128)

    def permute(value, stride, size, shift):
        pairs = []
        for source in range(band_count):
            place = (source // stride) % size
            pairs.append((source, source + ((place ^ shift) - place) * stride))
        return lax.ppermute(value, "band", pairs)

    def to_core(value):
        return permute(value, 1, 2, 1)

    def to_inner(value, shift):
        return permute(value, 2, inner, shift)

    def to_outer(value, shift):
        return permute(value, 2 * inner, outer, shift)

    cap, halfway = slot_rows // band_count, slot_rows // 2
    kept, sent = pl.pallas_call(
        functools.partial(pick_kernel, sizes),
        out_shape=[jax.ShapeDtypeStruct((halfway, width), BF16)] * 2,
        in_specs=specs(pltpu.HBM, 2),
        out_specs=specs(pltpu.VMEM, 2),
        scratch_shapes=[
            pltpu.VMEM(send_rows.shape, jnp.int32),
            pltpu.VMEM(grid_latent.shape, BF16),
            pltpu.VMEM((slot_rows, width), F32),
            pltpu.SemaphoreType.DMA((5,)),
        ],
        compiler_params=params(16),
        name="pick",
    )(*pinned(pltpu.HBM, send_rows, grid_latent))

    def mix(values, count, minor):
        rows = len(values) * values[0].shape[0] // count
        return pl.pallas_call(
            functools.partial(mix_kernel, count, minor),
            out_shape=[jax.ShapeDtypeStruct((rows, width), BF16)] * count,
            compiler_params=params(16),
            name="mix",
        )(*values)

    hot, node, cot, moved = pl.pallas_call(
        functools.partial(ready_kernel, lines),
        out_shape=[
            pltpu.HBM((edges, mesh_rows), BF16),
            pltpu.HBM((mesh_rows, hidden_width), F32),
            pltpu.HBM((mesh_rows, hidden_width), F32),
            pltpu.VMEM((mesh_rows, hidden_width), BF16),
        ],
        in_specs=specs(pltpu.HBM, 6),
        out_specs=specs(pltpu.HBM, 3) + specs(pltpu.VMEM, 1),
        scratch_shapes=[
            pltpu.VMEM(dst_index.shape, jnp.int32),
            pltpu.VMEM(mesh_latent.shape, BF16),
            pltpu.VMEM(mesh_cot.shape, BF16),
            pltpu.VMEM((width, hidden_width), BF16),
            pltpu.VMEM((width, hidden_width), BF16),
            pltpu.VMEM(w_node2.shape, BF16),
            pltpu.VMEM((edges, mesh_rows), BF16),
            pltpu.VMEM((mesh_rows, hidden_width), F32),
            pltpu.VMEM((mesh_rows, hidden_width), F32),
            pltpu.SemaphoreType.DMA((6,)),
            pltpu.SemaphoreType.DMA((3,)),
        ],
        compiler_params=params(16),
        cost_estimate=cost(2 * 10**9, 4 * MIB),
        name="ready",
    )(*pinned(pltpu.HBM, dst_index, mesh_latent, mesh_cot, w_edge1, w_node1, w_node2))
    base, *ahead, turned = pl.pallas_call(
        functools.partial(base_kernel, lines),
        out_shape=[
            pltpu.VMEM((edges, hidden_width), F32),
            pltpu.VMEM(slot_index.shape, jnp.int32),
            pltpu.VMEM(dst_index.shape, jnp.int32),
            pltpu.VMEM((width, hidden_width), BF16),
            pltpu.HBM((width, edges), BF16),
        ],
        in_specs=specs(pltpu.HBM, 5) + specs(pltpu.VMEM, 1),
        out_specs=specs(pltpu.VMEM, 4) + specs(pltpu.HBM, 1),
        scratch_shapes=[
            pltpu.VMEM((edges, mesh_rows), BF16),
            pltpu.VMEM(edge_latent.shape, BF16),
            pltpu.VMEM((width, hidden_width), BF16),
            pltpu.VMEM((width, edges), BF16),
            pltpu.SemaphoreType.DMA((5 + edges // (128 * lines),)),
            pltpu.SemaphoreType.DMA((edges // (128 * lines),)),
        ],
        compiler_params=params(16),
        cost_estimate=cost(4 * 10**9, 4 * MIB),
        name="base",
    )(*pinned(pltpu.HBM, hot, edge_latent, w_edge1, slot_index, dst_index), *pinned(pltpu.VMEM, moved))

    by_inner = mix([kept, to_core(sent)], inner, outer)
    by_inner = [by_inner[0]] + [to_inner(by_inner[k], k) for k in range(1, inner)]
    by_outer = mix(by_inner, outer, 1)
    slot_blocks = [by_outer[0]] + [to_outer(by_outer[k], k) for k in range(1, outer)]

    grad_rows = 3 * width + hidden_width
    chunk = grad_rows // band_count
    group = (inner * chunk, hidden_width)
    node_out, d_slots, *sides = pl.pallas_call(
        functools.partial(main_kernel, lines, sizes),
        out_shape=[
            jax.ShapeDtypeStruct((mesh_rows, width), BF16),
            jax.ShapeDtypeStruct((halfway, width), BF16),
        ]
        + [jax.ShapeDtypeStruct((group[0] + inner * cap, hidden_width), BF16)] * outer
        + [jax.ShapeDtypeStruct(group, F32)] * outer,
        in_specs=specs(pltpu.HBM, 7) + specs(pltpu.VMEM, 4 + outer),
        out_specs=specs(pltpu.VMEM, 2 + 2 * outer),
        scratch_shapes=[
            pltpu.VMEM((edges, hidden_width), F32),
            pltpu.VMEM((edges, hidden_width), BF16),
            pltpu.VMEM((slot_rows + mesh_rows + width, edges), BF16),
            pltpu.VMEM((grad_rows, hidden_width), F32),
            pltpu.VMEM((slot_rows, width), F32),
            pltpu.VMEM((slot_rows, width), F32),
            pltpu.VMEM(mesh_latent.shape, BF16),
            pltpu.VMEM(w_edge2.shape, BF16),
            pltpu.VMEM((w_node1.shape[0] - width, w_node1.shape[1]), BF16),
            pltpu.VMEM(hot.shape, BF16),
            pltpu.VMEM(node.shape, F32),
            pltpu.VMEM(cot.shape, F32),
            pltpu.VMEM((edges, slot_rows), BF16),
            pltpu.SemaphoreType.DMA((7,)),
        ],
        compiler_params=params(40),
        name="edges",
    )(
        *pinned(pltpu.HBM, mesh_latent, w_edge2, w_node1, turned, hot, node, cot),
        *pinned(pltpu.VMEM, base, *ahead),
        *slot_blocks,
    )
    mesh_out = pl.pallas_call(
        mesh_kernel,
        out_shape=jax.ShapeDtypeStruct((mesh_rows, width), BF16),
        in_specs=specs(pltpu.HBM, 2) + specs(pltpu.VMEM, 1),
        out_specs=pl.BlockSpec(memory_space=pltpu.VMEM),
        scratch_shapes=[
            pltpu.VMEM(mesh_latent.shape, BF16),
            pltpu.VMEM(w_node2.shape, BF16),
            pltpu.SemaphoreType.DMA((2,)),
        ],
        compiler_params=params(16),
        cost_estimate=cost(10**9, MIB),
        name="mesh",
    )(*pinned(pltpu.HBM, mesh_latent, w_node2), node_out)
    sends, keeps = sides[:outer], sides[outer:]
    small = (2 * cap, width)
    arrived = {}
    first = None
    for k in [outer - 1, *range(1, outer - 1), 0]:
        send = sends[k] if first is None else lax.optimization_barrier((sends[k], first))[0]
        crossed = to_core(send)
        total, mixed, *parts = pl.pallas_call(
            functools.partial(core_kernel, sizes, k),
            out_shape=[
                jax.ShapeDtypeStruct((chunk, hidden_width), F32),
                jax.ShapeDtypeStruct(small, BF16),
            ]
            + [jax.ShapeDtypeStruct((chunk + 2 * cap, width), BF16)] * (inner - 1),
            compiler_params=params(16),
            cost_estimate=cost(10**9, MIB),
            name="core",
        )(keeps[k], crossed, d_slots)
        first = parts[0] if first is None else first
        parts = [to_inner(part, at + 1) for at, part in enumerate(parts)]
        block = 2 * inner * cap
        if k:
            (out,) = pl.pallas_call(
                functools.partial(inner_kernel, inner - 1, 0),
                out_shape=[jax.ShapeDtypeStruct((chunk + block, width), BF16)],
                compiler_params=params(16),
                name="inner",
            )(total, mixed, *parts)
            arrived[k] = to_outer(out, k)
        else:
            total = lax.optimization_barrier((total, mesh_out))[0]
            own, home = pl.pallas_call(
                functools.partial(inner_kernel, inner - 1, outer - 1),
                out_shape=[
                    jax.ShapeDtypeStruct((chunk, hidden_width), BF16),
                    jax.ShapeDtypeStruct((block, width), BF16),
                ],
                compiler_params=params(16),
                name="own",
            )(total, mixed, *parts, *[arrived[at] for at in range(1, outer)])

    grid_grad = pl.pallas_call(
        functools.partial(put_kernel, sizes),
        out_shape=jax.ShapeDtypeStruct(grid_latent.shape, F32),
        in_specs=specs(pltpu.HBM, 1) + specs(pltpu.VMEM, outer),
        out_specs=pl.BlockSpec(memory_space=pltpu.VMEM),
        scratch_shapes=[
            pltpu.VMEM((slot_rows, width), F32),
            pltpu.VMEM(send_rows.shape, jnp.int32),
            pltpu.SemaphoreType.DMA((1,)),
        ],
        compiler_params=params(16),
        cost_estimate=cost(2 * 10**9, 2 * MIB),
        name="put",
    )(*pinned(pltpu.HBM, send_rows), home, *[arrived[at] for at in range(1, outer)])

    pieces = {0: own}
    stride = outer // 2
    while stride:
        for at in range(0, outer, 2 * stride):
            value = pieces[at]
            if at == outer // 2 and stride == outer // 4:
                value = lax.optimization_barrier((value, grid_grad))[0]
            pieces[at + stride] = to_outer(value, stride)
        stride //= 2
    halfway_at = band_count // 2
    pieces[halfway_at] = to_core(own)
    for far_inner in range(1, inner):
        for far_outer in range(outer):
            value = pieces[far_outer]
            if far_outer == outer // 2:
                value = lax.optimization_barrier((value, pieces[halfway_at]))[0]
            pieces[far_inner * outer + far_outer] = to_inner(value, far_inner)
    late = [at for at in range(halfway_at) if at > outer or at == 1]
    for at in range(1, halfway_at):
        if at not in late:
            pieces[halfway_at + at] = to_core(pieces[at])

    last = outer - 1
    stages = [[], [], []]
    for at in range(band_count):
        far_outer, far_inner = at % outer, at // outer % inner
        if far_outer == last:
            stages[2 if far_inner else 1].append(at)
        else:
            stages[1 if at - halfway_at in late or at in late and at > 1 else 0].append(at)
    grads = []
    for places in stages:
        if places is stages[1]:
            for at in late:
                value = lax.optimization_barrier((pieces[at], *grads))[0]
                pieces[halfway_at + at] = to_core(value)
        grads = pl.pallas_call(
            functools.partial(order_kernel, sizes, places, len(grads)),
            out_shape=[
                jax.ShapeDtypeStruct((3 * width, hidden_width), F32),
                jax.ShapeDtypeStruct((hidden_width, width), F32),
            ],
            in_specs=specs(pltpu.VMEM, len(places)) + specs(pltpu.HBM, len(grads)),
            out_specs=specs(pltpu.HBM, 2),
            scratch_shapes=[
                pltpu.VMEM((len(places), chunk, hidden_width), F32),
                pltpu.SemaphoreType.DMA((len(places),)),
            ],
            input_output_aliases={len(places) + k: k for k in range(len(grads))},
            compiler_params=params(16),
            cost_estimate=cost(15 * 10**7 * len(places), 2 * MIB),
            name="order",
        )(*[pieces[at] for at in places], *grads)
    grad_edge1, grad_edge2 = grads
    return (mesh_out, grid_grad, grad_edge1, grad_edge2)


def solution(mesh):
    chips = mesh.shape["band"] // 2
    inner = 1
    while inner * inner * 4 <= chips:
        inner *= 2
    sizes = (chips // inner, inner)
    in_specs = (
        P(("groups", "band"), None),
        P(("groups", "band"), None),
        P(("groups", "band"), None),
        P(("groups", "band"), None),
        P("band", None),
        P("band"),
        P("band"),
        P(),
        P(),
        P(),
        P(),
    )
    out_specs = (
        P(("groups", "band"), None),
        P(("groups", "band"), None),
        P("groups", None),
        P("groups", None),
    )
    return jax.shard_map(
        functools.partial(shards, sizes), mesh=mesh, in_specs=in_specs, out_specs=out_specs, check_vma=False
    )
```

```python
import functools

import jax
import jax.numpy as jnp
from jax import lax
from jax.experimental import pallas as pl
from jax.experimental.pallas import tpu as pltpu
from jax.sharding import PartitionSpec as P

BF16 = jnp.bfloat16
F32 = jnp.float32
MIB = 1024 * 1024


def dot_nn(a, b):
    return jnp.dot(a, b, preferred_element_type=F32)


def dot_nt(a, b):
    return lax.dot_general(a, b, (((1,), (1,)), ((), ())), preferred_element_type=F32)


def split(value):
    high = value.astype(BF16)
    low = (value - high.astype(F32)).astype(BF16)
    return high, low


def identity():
    same = lax.broadcasted_iota(jnp.int32, (256, 256), 0) == lax.broadcasted_iota(jnp.int32, (256, 256), 1)
    return jnp.where(same, 1.0, 0.0).astype(BF16)


def turn(eye, value):
    blocks = [dot_nt(eye, value[:, at : at + 256]).astype(BF16) for at in range(0, value.shape[1], 256)]
    return jnp.concatenate(blocks, axis=0)


def one_hot_rows(index_row, rows):
    shape = (rows, index_row.shape[1])
    hit = lax.broadcasted_iota(jnp.int32, shape, 0) == index_row
    return jnp.where(hit, 1.0, 0.0).astype(BF16)


def one_hot_columns(index_row, columns):
    lanes = index_row.shape[1]
    index = jnp.transpose(jnp.broadcast_to(index_row, (lanes, lanes)))
    pieces = []
    for start in range(0, columns, lanes):
        hit = lax.broadcasted_iota(jnp.int32, (lanes, lanes), 1) + start == index
        pieces.append(jnp.where(hit, 1.0, 0.0).astype(BF16))
    return pieces[0] if len(pieces) == 1 else jnp.concatenate(pieces, axis=1)


def tile_rows(index_ref, at, lines, rows):
    found = [one_hot_rows(index_ref[pl.ds(at * lines + k, 1), :], rows) for k in range(lines)]
    return jnp.concatenate(found, axis=1)


def tile_columns(index_ref, at, lines, columns):
    found = [one_hot_columns(index_ref[pl.ds(at * lines + k, 1), :], columns) for k in range(lines)]
    return jnp.concatenate(found, axis=0)


def place_of(sizes):
    outer, inner = sizes
    me = lax.axis_index("band")
    return me // (2 * inner), (me // 2) % inner, me % 2


def owner_at(sizes, far_outer, far_inner, far_core):
    my_outer, my_inner, my_core = place_of(sizes)
    return ((my_outer ^ far_outer) * sizes[1] + (my_inner ^ far_inner)) * 2 + (my_core ^ far_core)


def params(mib):
    return pltpu.CompilerParams(vmem_limit_bytes=mib * MIB)


def pinned(space, *values):
    return [pltpu.with_memory_space_constraint(value, space) for value in values]


def specs(space, count):
    return [pl.BlockSpec(memory_space=space)] * count


def cost(flops, nbytes):
    return pl.CostEstimate(flops=flops, bytes_accessed=nbytes, transcendentals=0)


def load(pairs, sems):
    copies = [pltpu.make_async_copy(source, target, sems.at[at]) for at, (source, target) in enumerate(pairs)]
    for copy in copies:
        copy.start()
    return copies


def pick_kernel(sizes, rows_hbm, grid_hbm, keep_ref, send_ref, rows_ref, grid_ref, picked_ref, sems):
    outer, inner = sizes
    block = grid_ref.shape[0] // 4
    parts = [pl.ds(at * block, block) for at in range(4)]
    copies = load([(rows_hbm, rows_ref)] + [(grid_hbm.at[part, :], grid_ref.at[part, :]) for part in parts], sems)
    copies[0].wait()
    picked = picked_ref.shape[0]
    chosen = [one_hot_columns(rows_ref[:, at : at + 128], grid_ref.shape[0]) for at in range(0, picked, 128)]
    for copy in copies[1:]:
        copy.wait()
    for at, some in enumerate(chosen):
        picked_ref[at * 128 : (at + 1) * 128, :] = dot_nn(some, grid_ref[...])
    cap = picked // (2 * outer * inner)
    for far_core, target in enumerate((keep_ref, send_ref)):
        blocks = []
        for far_inner in range(inner):
            for far_outer in range(outer):
                owner = owner_at(sizes, far_outer, far_inner, far_core)
                blocks.append(picked_ref[pl.ds(pl.multiple_of(owner * cap, cap), cap), :])
        target[...] = jnp.concatenate(blocks, axis=0).astype(BF16)


def mix_kernel(count, minor, *refs):
    sources, targets = refs[:-count], refs[-count:]
    values = [ref[...].astype(F32) for ref in sources]
    unit = values[0].shape[0] // (count * minor)
    for at, target in enumerate(targets):
        starts = [(at * minor + k) * unit for k in range(minor)]
        blocks = [value[start : start + unit] for start in starts for value in values]
        target[...] = jnp.concatenate(blocks, axis=0).astype(BF16)


def put_kernel(sizes, rows_hbm, *refs):
    outer, inner = sizes
    blocks, (out_ref, ordered_ref, rows_ref, sems) = refs[:outer], refs[outer:]
    (copy,) = load([(rows_hbm, rows_ref)], sems)
    place_rows(sizes, blocks, ordered_ref)
    copy.wait()
    chosen = one_hot_rows(rows_ref[...], out_ref.shape[0])
    out_ref[...] = dot_nn(chosen, ordered_ref[...].astype(BF16))


def place_rows(sizes, blocks, ordered_ref):
    outer, inner = sizes
    cap = ordered_ref.shape[0] // (2 * outer * inner)
    for far_outer, block in enumerate(blocks):
        value = block[block.shape[0] - 2 * inner * cap :, :].astype(F32)
        for at in range(2 * inner):
            owner = owner_at(sizes, far_outer, at // 2, at % 2)
            ordered_ref[pl.ds(pl.multiple_of(owner * cap, cap), cap), :] = value[at * cap : (at + 1) * cap]


def ready_kernel(
    lines,
    dst_hbm,
    mesh_hbm,
    cot_hbm,
    w1_hbm,
    wn1_hbm,
    wn2_hbm,
    hot_hbm,
    node_hbm,
    cot_out_hbm,
    mesh_out_hbm,
    moved_ref,
    dst_ref,
    mesh_ref,
    cot_ref,
    w1_ref,
    wn1_ref,
    wn2_ref,
    hot_ref,
    node_ref,
    cot_out_ref,
    mesh_out_ref,
    sems,
    out_sems,
):
    width = mesh_ref.shape[1]
    tile = lines * 128
    pairs = [
        (dst_hbm, dst_ref),
        (mesh_hbm, mesh_ref),
        (w1_hbm.at[pl.ds(width, width), :], w1_ref),
        (wn1_hbm.at[pl.ds(0, width), :], wn1_ref),
        (cot_hbm, cot_ref),
        (wn2_hbm, wn2_ref),
    ]
    copies = load(pairs, sems)
    pairs = [(hot_ref, hot_hbm), (node_ref, node_hbm), (cot_out_ref, cot_out_hbm), (mesh_out_ref, mesh_out_hbm)]
    outs = [
        pltpu.make_async_copy(source, target, out_sems.at[at]) for at, (source, target) in enumerate(pairs)
    ]
    copies[0].wait()
    for at in range(hot_ref.shape[0] // tile):
        hot_ref[at * tile : (at + 1) * tile, :] = tile_columns(dst_ref, at, lines, hot_ref.shape[1])
    outs[0].start()
    copies[1].wait()
    mesh_out_ref[...] = turn(identity(), mesh_ref[...])
    outs[3].start()
    copies[3].wait()
    node_ref[...] = dot_nn(mesh_ref[...], wn1_ref[...])
    outs[1].start()
    copies[4].wait()
    copies[5].wait()
    cot_out_ref[...] = dot_nt(cot_ref[...], wn2_ref[...])
    outs[2].start()
    copies[2].wait()
    moved_ref[...] = dot_nn(mesh_ref[...], w1_ref[...]).astype(BF16)
    for copy in outs:
        copy.wait()


def base_kernel(
    lines,
    hot_hbm,
    edge_hbm,
    w1_hbm,
    slot_hbm,
    dst_hbm,
    moved_ref,
    base_ref,
    slot_ref,
    dst_ref,
    top_ref,
    turned_hbm,
    hot_ref,
    edge_ref,
    w1_ref,
    turned_ref,
    sems,
    out_sems,
):
    width = edge_ref.shape[1]
    tile = lines * 128
    tiles = edge_ref.shape[0] // tile
    pairs = [(edge_hbm.at[pl.ds(at * tile, tile), :], edge_ref.at[pl.ds(at * tile, tile), :]) for at in range(tiles)]
    pairs += [(w1_hbm.at[pl.ds(2 * width, width), :], w1_ref), (hot_hbm, hot_ref)]
    pairs += [(w1_hbm.at[pl.ds(0, width), :], top_ref), (slot_hbm, slot_ref), (dst_hbm, dst_ref)]
    copies = load(pairs, sems)
    eye = identity()
    outs = []
    for at in range(tiles):
        rows = slice(at * tile, (at + 1) * tile)
        copies[at].wait()
        for start in range(0, width, 256):
            block = dot_nt(eye, edge_ref[rows, start : start + 256])
            turned_ref[start : start + 256, rows] = block.astype(BF16)
        columns = pl.ds(at * tile, tile)
        out = pltpu.make_async_copy(turned_ref.at[:, columns], turned_hbm.at[:, columns], out_sems.at[at])
        out.start()
        outs.append(out)
    copies[tiles].wait()
    copies[tiles + 1].wait()
    for at in range(tiles):
        rows = slice(at * tile, (at + 1) * tile)
        base_ref[rows, :] = dot_nn(edge_ref[rows, :], w1_ref[...]) + dot_nn(hot_ref[rows, :], moved_ref[...])
    for out in outs + copies[tiles + 2 :]:
        out.wait()


def main_kernel(
    lines,
    sizes,
    mesh_hbm,
    w2_hbm,
    wn1_hbm,
    turned_hbm,
    hot_hbm,
    node_hbm,
    cot_hbm,
    base_ref,
    slot_ref,
    dst_ref,
    w1_ref,
    *rest,
):
    outer, inner = sizes
    slot_blocks, rest = rest[:outer], rest[outer:]
    node_out_ref, d_slots_ref = rest[:2]
    send_refs, keep_refs, rest = rest[2 : 2 + outer], rest[2 + outer : 2 + 2 * outer], rest[2 + 2 * outer :]
    slope_ref, value_ref, both_ref, grads_ref, slot_grads_ref, ordered_ref = rest[:6]
    mesh_ref, w2_ref, wn1_ref, hot_ref, node_ref, cot_ref, picks_ref, sems = rest[6:]
    width, mesh_rows = mesh_ref.shape
    slot_rows = ordered_ref.shape[0]
    tile = lines * 128
    tiles = base_ref.shape[0] // tile
    pairs = [
        (w2_hbm, w2_ref),
        (wn1_hbm.at[pl.ds(width, wn1_ref.shape[0]), :], wn1_ref),
        (mesh_hbm, mesh_ref),
        (node_hbm, node_ref),
        (cot_hbm, cot_ref),
        (hot_hbm, hot_ref),
        (turned_hbm, both_ref.at[pl.ds(slot_rows + mesh_rows, width), :]),
    ]
    copies = load(pairs, sems)
    place_rows(sizes, slot_blocks, ordered_ref)
    slots_value = ordered_ref[...].astype(BF16)
    for at in range(tiles):
        rows = slice(at * tile, (at + 1) * tile)
        picks_ref[rows, :] = tile_columns(slot_ref, at, lines, slot_rows)
        both_ref[:slot_rows, rows] = tile_rows(slot_ref, at, lines, slot_rows)
        both_ref[slot_rows : slot_rows + mesh_rows, rows] = tile_rows(dst_ref, at, lines, mesh_rows)

    eye = identity()
    slots = slots_value
    slot_pair = jnp.concatenate(split(dot_nn(slots, w1_ref[...])), axis=0)
    for at in range(tiles):
        rows = slice(at * tile, (at + 1) * tile)
        from_slot = picks_ref[rows, :]
        twice = jnp.concatenate([from_slot, from_slot], axis=1)
        pre = base_ref[rows, :] + dot_nn(twice, slot_pair)
        sigma = 0.5 + 0.5 * jnp.tanh(0.5 * pre)
        hidden = pre * sigma
        slope_ref[rows, :] = sigma + hidden * (1.0 - sigma)
        value_ref[rows, :] = hidden.astype(BF16)

    for copy in copies[:-1]:
        copy.wait()
    hidden_sums = dot_nn(both_ref[slot_rows : slot_rows + mesh_rows, :], value_ref[...]).astype(BF16)
    received = dot_nn(hidden_sums, w2_ref[...]).astype(BF16)
    pre_node = node_ref[...] + dot_nn(received, wn1_ref[...])
    sigma = 0.5 + 0.5 * jnp.tanh(0.5 * pre_node)
    node = pre_node * sigma
    slope = sigma + node * (1.0 - sigma)
    d_pre_node = (cot_ref[...] * slope).astype(BF16)
    d_received = dot_nt(d_pre_node, wn1_ref[...]).astype(BF16)
    spread = dot_nt(d_received, w2_ref[...]).astype(BF16)

    for at in range(tiles):
        rows = slice(at * tile, (at + 1) * tile)
        value_ref[rows, :] = (dot_nn(hot_ref[rows, :], spread) * slope_ref[rows, :]).astype(BF16)

    grads_ref[3 * width :, :] = dot_nn(turn(eye, hidden_sums), d_received)
    node_out_ref[...] = node.astype(BF16)
    copies[-1].wait()
    product = dot_nn(both_ref[...], value_ref[...])
    sums = product[: slot_rows + mesh_rows].astype(BF16)
    grads_ref[2 * width : 3 * width, :] = product[slot_rows + mesh_rows :]
    slot_grads_ref[...] = dot_nt(sums[:slot_rows], w1_ref[...])
    grads_ref[:width, :] = dot_nn(turn(eye, slots), sums[:slot_rows])
    grads_ref[width : 2 * width, :] = dot_nn(mesh_ref[...], sums[slot_rows:])

    chunk = grads_ref.shape[0] // (2 * outer * inner)
    cap = slot_rows // (2 * outer * inner)
    for far_core in range(2):
        for far_outer in range(outer):
            for far_inner in range(inner):
                owner = owner_at(sizes, far_outer, far_inner, far_core)
                at = (far_core * outer + far_outer) * inner + far_inner
                from_rows = pl.ds(pl.multiple_of(owner * cap, cap), cap)
                ordered_ref[at * cap : (at + 1) * cap, :] = slot_grads_ref[from_rows, :]
                value = grads_ref[pl.ds(pl.multiple_of(owner * chunk, chunk), chunk), :]
                rows = slice(far_inner * chunk, (far_inner + 1) * chunk)
                if far_core:
                    send_refs[far_outer][rows, :] = value.astype(BF16)
                else:
                    keep_refs[far_outer][rows, :] = value
    halfway, share = slot_rows // 2, inner * cap
    d_slots_ref[...] = ordered_ref[:halfway, :].astype(BF16)
    for far_outer, send_ref in enumerate(send_refs):
        start = halfway + far_outer * share
        send_ref[inner * chunk :, :] = ordered_ref[start : start + share, :].astype(BF16)


def mesh_kernel(mesh_hbm, wn2_hbm, node_ref, out_ref, mesh_ref, wn2_ref, sems):
    for copy in load([(mesh_hbm, mesh_ref), (wn2_hbm, wn2_ref)], sems):
        copy.wait()
    out_ref[...] = (mesh_ref[...].astype(F32) + dot_nn(node_ref[...], wn2_ref[...])).astype(BF16)


def core_kernel(sizes, far_outer, keep_ref, crossed_ref, d_slots_ref, total_ref, mixed_ref, *part_refs):
    outer, inner = sizes
    chunk = total_ref.shape[0]
    cap = d_slots_ref.shape[0] // (outer * inner)
    start = far_outer * inner * cap
    own = d_slots_ref[start : start + inner * cap, :].astype(F32)
    far = crossed_ref[inner * chunk :, :].astype(F32)
    for far_inner in range(inner):
        rows, slots = slice(far_inner * chunk, (far_inner + 1) * chunk), slice(far_inner * cap, (far_inner + 1) * cap)
        total = keep_ref[rows, :] + crossed_ref[rows, :].astype(F32)
        mixed = jnp.concatenate([own[slots], far[slots]], axis=0).astype(BF16)
        if far_inner:
            part_refs[far_inner - 1][:chunk, :] = total.astype(BF16)
            part_refs[far_inner - 1][chunk:, :] = mixed
        else:
            total_ref[...] = total
            mixed_ref[...] = mixed


def inner_kernel(parts, arrivals, total_ref, mixed_ref, *refs):
    received, arrived, outs = refs[:parts], refs[parts : parts + arrivals], refs[parts + arrivals :]
    chunk = total_ref.shape[0]
    total = total_ref[...]
    mixed = [mixed_ref[...]]
    for part in received:
        total = total + part[:chunk, :].astype(F32)
        mixed.append(part[chunk:, :])
    for value in arrived:
        total = total + value[:chunk, :].astype(F32)
    mixed = jnp.concatenate(mixed, axis=0)
    if len(outs) == 1:
        outs[0][:chunk, :] = total.astype(BF16)
        outs[0][chunk:, :] = mixed
    else:
        outs[0][...] = total.astype(BF16)
        outs[1][...] = mixed


def order_kernel(sizes, places, aliased, *refs):
    outer, inner = sizes
    pieces = refs[: len(places)]
    first_hbm, second_hbm, stage_ref, sems = refs[len(places) + aliased :]
    chunk = pieces[0].shape[0]
    first_chunks = first_hbm.shape[0] // chunk

    def send(k, target, start):
        rows = pl.ds(pl.multiple_of(start, chunk), chunk)
        return pltpu.make_async_copy(stage_ref.at[k], target.at[rows, :], sems.at[k])

    for k, (at, piece) in enumerate(zip(places, pieces)):
        owner = owner_at(sizes, at % outer, at // outer % inner, at // (outer * inner))
        stage_ref[k] = piece[...].astype(F32)

        @pl.when(owner < first_chunks)
        def _():
            send(k, first_hbm, owner * chunk).start()

        @pl.when(owner >= first_chunks)
        def _():
            send(k, second_hbm, (owner - first_chunks) * chunk).start()

    for k in range(len(places)):
        send(k, first_hbm, 0).wait()


def shards(
    sizes,
    grid_latent,
    mesh_latent,
    edge_latent,
    mesh_cot,
    send_rows,
    edge_slot,
    edge_dst,
    w_edge1,
    w_edge2,
    w_node1,
    w_node2,
):
    outer, inner = sizes
    band_count = lax.axis_size("band")
    width = grid_latent.shape[1]
    hidden_width = w_edge1.shape[1]
    edges = edge_latent.shape[0]
    mesh_rows = mesh_latent.shape[0]
    slot_rows = send_rows.shape[1]
    lines = 4
    slot_index = edge_slot.reshape(edges // 128, 128)
    dst_index = edge_dst.reshape(edges // 128, 128)

    def permute(value, stride, size, shift):
        pairs = []
        for source in range(band_count):
            place = (source // stride) % size
            pairs.append((source, source + ((place ^ shift) - place) * stride))
        return lax.ppermute(value, "band", pairs)

    def to_core(value):
        return permute(value, 1, 2, 1)

    def to_inner(value, shift):
        return permute(value, 2, inner, shift)

    def to_outer(value, shift):
        return permute(value, 2 * inner, outer, shift)

    cap, halfway = slot_rows // band_count, slot_rows // 2
    kept, sent = pl.pallas_call(
        functools.partial(pick_kernel, sizes),
        out_shape=[jax.ShapeDtypeStruct((halfway, width), BF16)] * 2,
        in_specs=specs(pltpu.HBM, 2),
        out_specs=specs(pltpu.VMEM, 2),
        scratch_shapes=[
            pltpu.VMEM(send_rows.shape, jnp.int32),
            pltpu.VMEM(grid_latent.shape, BF16),
            pltpu.VMEM((slot_rows, width), F32),
            pltpu.SemaphoreType.DMA((5,)),
        ],
        compiler_params=params(16),
        name="pick",
    )(*pinned(pltpu.HBM, send_rows, grid_latent))

    def mix(values, count, minor):
        rows = len(values) * values[0].shape[0] // count
        return pl.pallas_call(
            functools.partial(mix_kernel, count, minor),
            out_shape=[jax.ShapeDtypeStruct((rows, width), BF16)] * count,
            compiler_params=params(16),
            name="mix",
        )(*values)

    hot, node, cot, mesh_turned, moved = pl.pallas_call(
        functools.partial(ready_kernel, lines),
        out_shape=[
            pltpu.HBM((edges, mesh_rows), BF16),
            pltpu.HBM((mesh_rows, hidden_width), F32),
            pltpu.HBM((mesh_rows, hidden_width), F32),
            pltpu.HBM((width, mesh_rows), BF16),
            pltpu.VMEM((mesh_rows, hidden_width), BF16),
        ],
        in_specs=specs(pltpu.HBM, 6),
        out_specs=specs(pltpu.HBM, 4) + specs(pltpu.VMEM, 1),
        scratch_shapes=[
            pltpu.VMEM(dst_index.shape, jnp.int32),
            pltpu.VMEM(mesh_latent.shape, BF16),
            pltpu.VMEM(mesh_cot.shape, BF16),
            pltpu.VMEM((width, hidden_width), BF16),
            pltpu.VMEM((width, hidden_width), BF16),
            pltpu.VMEM(w_node2.shape, BF16),
            pltpu.VMEM((edges, mesh_rows), BF16),
            pltpu.VMEM((mesh_rows, hidden_width), F32),
            pltpu.VMEM((mesh_rows, hidden_width), F32),
            pltpu.VMEM((width, mesh_rows), BF16),
            pltpu.SemaphoreType.DMA((6,)),
            pltpu.SemaphoreType.DMA((4,)),
        ],
        compiler_params=params(16),
        cost_estimate=cost(2 * 10**9, 4 * MIB),
        name="ready",
    )(*pinned(pltpu.HBM, dst_index, mesh_latent, mesh_cot, w_edge1, w_node1, w_node2))
    base, *ahead, turned = pl.pallas_call(
        functools.partial(base_kernel, lines),
        out_shape=[
            pltpu.VMEM((edges, hidden_width), F32),
            pltpu.VMEM(slot_index.shape, jnp.int32),
            pltpu.VMEM(dst_index.shape, jnp.int32),
            pltpu.VMEM((width, hidden_width), BF16),
            pltpu.HBM((width, edges), BF16),
        ],
        in_specs=specs(pltpu.HBM, 5) + specs(pltpu.VMEM, 1),
        out_specs=specs(pltpu.VMEM, 4) + specs(pltpu.HBM, 1),
        scratch_shapes=[
            pltpu.VMEM((edges, mesh_rows), BF16),
            pltpu.VMEM(edge_latent.shape, BF16),
            pltpu.VMEM((width, hidden_width), BF16),
            pltpu.VMEM((width, edges), BF16),
            pltpu.SemaphoreType.DMA((5 + edges // (128 * lines),)),
            pltpu.SemaphoreType.DMA((edges // (128 * lines),)),
        ],
        compiler_params=params(16),
        cost_estimate=cost(4 * 10**9, 4 * MIB),
        name="base",
    )(*pinned(pltpu.HBM, hot, edge_latent, w_edge1, slot_index, dst_index), *pinned(pltpu.VMEM, moved))

    by_inner = mix([kept, to_core(sent)], inner, outer)
    by_inner = [by_inner[0]] + [to_inner(by_inner[k], k) for k in range(1, inner)]
    by_outer = mix(by_inner, outer, 1)
    slot_blocks = [by_outer[0]] + [to_outer(by_outer[k], k) for k in range(1, outer)]

    grad_rows = 3 * width + hidden_width
    chunk = grad_rows // band_count
    group = (inner * chunk, hidden_width)
    node_out, d_slots, *sides = pl.pallas_call(
        functools.partial(main_kernel, lines, sizes),
        out_shape=[
            jax.ShapeDtypeStruct((mesh_rows, width), BF16),
            jax.ShapeDtypeStruct((halfway, width), BF16),
        ]
        + [jax.ShapeDtypeStruct((group[0] + inner * cap, hidden_width), BF16)] * outer
        + [jax.ShapeDtypeStruct(group, F32)] * outer,
        in_specs=specs(pltpu.HBM, 7) + specs(pltpu.VMEM, 4 + outer),
        out_specs=specs(pltpu.VMEM, 2 + 2 * outer),
        scratch_shapes=[
            pltpu.VMEM((edges, hidden_width), F32),
            pltpu.VMEM((edges, hidden_width), BF16),
            pltpu.VMEM((slot_rows + mesh_rows + width, edges), BF16),
            pltpu.VMEM((grad_rows, hidden_width), F32),
            pltpu.VMEM((slot_rows, width), F32),
            pltpu.VMEM((slot_rows, width), F32),
            pltpu.VMEM((width, mesh_rows), BF16),
            pltpu.VMEM(w_edge2.shape, BF16),
            pltpu.VMEM((w_node1.shape[0] - width, w_node1.shape[1]), BF16),
            pltpu.VMEM(hot.shape, BF16),
            pltpu.VMEM(node.shape, F32),
            pltpu.VMEM(cot.shape, F32),
            pltpu.VMEM((edges, slot_rows), BF16),
            pltpu.SemaphoreType.DMA((7,)),
        ],
        compiler_params=params(40),
        name="edges",
    )(
        *pinned(pltpu.HBM, mesh_turned, w_edge2, w_node1, turned, hot, node, cot),
        *pinned(pltpu.VMEM, base, *ahead),
        *slot_blocks,
    )
    mesh_out = pl.pallas_call(
        mesh_kernel,
        out_shape=jax.ShapeDtypeStruct((mesh_rows, width), BF16),
        in_specs=specs(pltpu.HBM, 2) + specs(pltpu.VMEM, 1),
        out_specs=pl.BlockSpec(memory_space=pltpu.VMEM),
        scratch_shapes=[
            pltpu.VMEM(mesh_latent.shape, BF16),
            pltpu.VMEM(w_node2.shape, BF16),
            pltpu.SemaphoreType.DMA((2,)),
        ],
        compiler_params=params(16),
        cost_estimate=cost(10**9, MIB),
        name="mesh",
    )(*pinned(pltpu.HBM, mesh_latent, w_node2), node_out)
    sends, keeps = sides[:outer], sides[outer:]
    small = (2 * cap, width)
    arrived = {}
    first = None
    for k in [outer - 1, *range(1, outer - 1), 0]:
        send = sends[k] if first is None else lax.optimization_barrier((sends[k], first))[0]
        crossed = to_core(send)
        total, mixed, *parts = pl.pallas_call(
            functools.partial(core_kernel, sizes, k),
            out_shape=[
                jax.ShapeDtypeStruct((chunk, hidden_width), F32),
                jax.ShapeDtypeStruct(small, BF16),
            ]
            + [jax.ShapeDtypeStruct((chunk + 2 * cap, width), BF16)] * (inner - 1),
            compiler_params=params(16),
            cost_estimate=cost(10**9, MIB),
            name="core",
        )(keeps[k], crossed, d_slots)
        first = parts[0] if first is None else first
        parts = [to_inner(part, at + 1) for at, part in enumerate(parts)]
        block = 2 * inner * cap
        if k:
            (out,) = pl.pallas_call(
                functools.partial(inner_kernel, inner - 1, 0),
                out_shape=[jax.ShapeDtypeStruct((chunk + block, width), BF16)],
                compiler_params=params(16),
                name="inner",
            )(total, mixed, *parts)
            arrived[k] = to_outer(out, k)
        else:
            total = lax.optimization_barrier((total, mesh_out))[0]
            own, home = pl.pallas_call(
                functools.partial(inner_kernel, inner - 1, outer - 1),
                out_shape=[
                    jax.ShapeDtypeStruct((chunk, hidden_width), BF16),
                    jax.ShapeDtypeStruct((block, width), BF16),
                ],
                compiler_params=params(16),
                name="own",
            )(total, mixed, *parts, *[arrived[at] for at in range(1, outer)])

    grid_grad = pl.pallas_call(
        functools.partial(put_kernel, sizes),
        out_shape=jax.ShapeDtypeStruct(grid_latent.shape, F32),
        in_specs=specs(pltpu.HBM, 1) + specs(pltpu.VMEM, outer),
        out_specs=pl.BlockSpec(memory_space=pltpu.VMEM),
        scratch_shapes=[
            pltpu.VMEM((slot_rows, width), F32),
            pltpu.VMEM(send_rows.shape, jnp.int32),
            pltpu.SemaphoreType.DMA((1,)),
        ],
        compiler_params=params(16),
        cost_estimate=cost(2 * 10**9, 2 * MIB),
        name="put",
    )(*pinned(pltpu.HBM, send_rows), home, *[arrived[at] for at in range(1, outer)])

    pieces = {0: own}
    stride = outer // 2
    while stride:
        for at in range(0, outer, 2 * stride):
            value = pieces[at]
            if at == outer // 2 and stride == outer // 4:
                value = lax.optimization_barrier((value, grid_grad))[0]
            pieces[at + stride] = to_outer(value, stride)
        stride //= 2
    halfway_at = band_count // 2
    pieces[halfway_at] = to_core(own)
    for far_inner in range(1, inner):
        for far_outer in range(outer):
            value = pieces[far_outer]
            if far_outer == outer // 2:
                value = lax.optimization_barrier((value, pieces[halfway_at]))[0]
            pieces[far_inner * outer + far_outer] = to_inner(value, far_inner)
    for at in range(1, halfway_at - 1):
        pieces[halfway_at + at] = to_core(pieces[at])

    last = outer - 1
    stages = [[], [], []]
    for at in range(band_count):
        far_outer, far_inner, far_core = at % outer, at // outer % inner, at // halfway_at
        if far_outer == last:
            stages[2 if far_inner else 1].append(at)
        else:
            stages[1 if far_inner and (far_core or far_outer == outer // 2) else 0].append(at)
    grads = []
    for places in stages:
        if places is stages[1]:
            value = lax.optimization_barrier((pieces[halfway_at - 1], *grads))[0]
            pieces[band_count - 1] = to_core(value)
        grads = pl.pallas_call(
            functools.partial(order_kernel, sizes, places, len(grads)),
            out_shape=[
                jax.ShapeDtypeStruct((3 * width, hidden_width), F32),
                jax.ShapeDtypeStruct((hidden_width, width), F32),
            ],
            in_specs=specs(pltpu.VMEM, len(places)) + specs(pltpu.HBM, len(grads)),
            out_specs=specs(pltpu.HBM, 2),
            scratch_shapes=[
                pltpu.VMEM((len(places), chunk, hidden_width), F32),
                pltpu.SemaphoreType.DMA((len(places),)),
            ],
            input_output_aliases={len(places) + k: k for k in range(len(grads))},
            compiler_params=params(16),
            cost_estimate=cost(15 * 10**7 * len(places), 2 * MIB),
            name="order",
        )(*[pieces[at] for at in places], *grads)
    grad_edge1, grad_edge2 = grads
    return (mesh_out, grid_grad, grad_edge1, grad_edge2)


def solution(mesh):
    chips = mesh.shape["band"] // 2
    inner = 1
    while inner * inner * 4 <= chips:
        inner *= 2
    sizes = (chips // inner, inner)
    in_specs = (
        P(("groups", "band"), None),
        P(("groups", "band"), None),
        P(("groups", "band"), None),
        P(("groups", "band"), None),
        P("band", None),
        P("band"),
        P("band"),
        P(),
        P(),
        P(),
        P(),
    )
    out_specs = (
        P(("groups", "band"), None),
        P(("groups", "band"), None),
        P("groups", None),
        P("groups", None),
    )
    return jax.shard_map(
        functools.partial(shards, sizes), mesh=mesh, in_specs=in_specs, out_specs=out_specs, check_vma=False
    )
```

```python
import functools

import jax
import jax.numpy as jnp
from jax import lax
from jax.experimental import pallas as pl
from jax.experimental.pallas import tpu as pltpu
from jax.sharding import PartitionSpec as P

BF16 = jnp.bfloat16
F32 = jnp.float32
MIB = 1024 * 1024


def dot_nn(a, b):
    return jnp.dot(a, b, preferred_element_type=F32)


def dot_tn(a, b):
    return lax.dot_general(a, b, (((0,), (0,)), ((), ())), preferred_element_type=F32)


def dot_nt(a, b):
    return lax.dot_general(a, b, (((1,), (1,)), ((), ())), preferred_element_type=F32)


def split(value):
    high = value.astype(BF16)
    low = (value - high.astype(F32)).astype(BF16)
    return high, low


def one_hot_rows(index_row, rows):
    shape = (rows, index_row.shape[1])
    hit = lax.broadcasted_iota(jnp.int32, shape, 0) == index_row
    return jnp.where(hit, 1.0, 0.0).astype(BF16)


def one_hot_columns(index_row, columns):
    lanes = index_row.shape[1]
    index = jnp.transpose(jnp.broadcast_to(index_row, (lanes, lanes)))
    pieces = []
    for start in range(0, columns, lanes):
        hit = lax.broadcasted_iota(jnp.int32, (lanes, lanes), 1) + start == index
        pieces.append(jnp.where(hit, 1.0, 0.0).astype(BF16))
    return pieces[0] if len(pieces) == 1 else jnp.concatenate(pieces, axis=1)


def tile_rows(index_ref, at, lines, rows):
    found = [one_hot_rows(index_ref[pl.ds(at * lines + k, 1), :], rows) for k in range(lines)]
    return jnp.concatenate(found, axis=1)


def tile_columns(index_ref, at, lines, columns):
    found = [one_hot_columns(index_ref[pl.ds(at * lines + k, 1), :], columns) for k in range(lines)]
    return jnp.concatenate(found, axis=0)


def place_of(sizes):
    outer, inner = sizes
    me = lax.axis_index("band")
    return me // (2 * inner), (me // 2) % inner, me % 2


def owner_at(sizes, far_outer, far_inner, far_core):
    my_outer, my_inner, my_core = place_of(sizes)
    return ((my_outer ^ far_outer) * sizes[1] + (my_inner ^ far_inner)) * 2 + (my_core ^ far_core)


def params(mib):
    return pltpu.CompilerParams(vmem_limit_bytes=mib * MIB)


def pinned(space, *values):
    return [pltpu.with_memory_space_constraint(value, space) for value in values]


def specs(space, count):
    return [pl.BlockSpec(memory_space=space)] * count


def cost(flops, nbytes):
    return pl.CostEstimate(flops=flops, bytes_accessed=nbytes, transcendentals=0)


def load(pairs, sems):
    copies = [pltpu.make_async_copy(source, target, sems.at[at]) for at, (source, target) in enumerate(pairs)]
    for copy in copies:
        copy.start()
    return copies


def pick_kernel(sizes, rows_hbm, grid_hbm, keep_ref, send_ref, rows_ref, grid_ref, picked_ref, sems):
    outer, inner = sizes
    block = grid_ref.shape[0] // 4
    parts = [pl.ds(at * block, block) for at in range(4)]
    copies = load([(rows_hbm, rows_ref)] + [(grid_hbm.at[part, :], grid_ref.at[part, :]) for part in parts], sems)
    copies[0].wait()
    picked = picked_ref.shape[0]
    chosen = [one_hot_columns(rows_ref[:, at : at + 128], grid_ref.shape[0]) for at in range(0, picked, 128)]
    for copy in copies[1:]:
        copy.wait()
    for at, some in enumerate(chosen):
        picked_ref[at * 128 : (at + 1) * 128, :] = dot_nn(some, grid_ref[...])
    cap = picked // (2 * outer * inner)
    for far_core, target in enumerate((keep_ref, send_ref)):
        blocks = []
        for far_inner in range(inner):
            for far_outer in range(outer):
                owner = owner_at(sizes, far_outer, far_inner, far_core)
                blocks.append(picked_ref[pl.ds(pl.multiple_of(owner * cap, cap), cap), :])
        target[...] = jnp.concatenate(blocks, axis=0).astype(BF16)


def mix_kernel(count, minor, *refs):
    sources, targets = refs[:-count], refs[-count:]
    values = [ref[...].astype(F32) for ref in sources]
    unit = values[0].shape[0] // (count * minor)
    for at, target in enumerate(targets):
        starts = [(at * minor + k) * unit for k in range(minor)]
        blocks = [value[start : start + unit] for start in starts for value in values]
        target[...] = jnp.concatenate(blocks, axis=0).astype(BF16)


def put_kernel(sizes, rows_hbm, *refs):
    outer, inner = sizes
    blocks, (out_ref, ordered_ref, rows_ref, sems) = refs[:outer], refs[outer:]
    (copy,) = load([(rows_hbm, rows_ref)], sems)
    place_rows(sizes, blocks, ordered_ref)
    copy.wait()
    chosen = one_hot_rows(rows_ref[...], out_ref.shape[0])
    out_ref[...] = dot_nn(chosen, ordered_ref[...].astype(BF16))


def place_rows(sizes, blocks, ordered_ref):
    outer, inner = sizes
    cap = ordered_ref.shape[0] // (2 * outer * inner)
    for far_outer, block in enumerate(blocks):
        value = block[block.shape[0] - 2 * inner * cap :, :].astype(F32)
        for at in range(2 * inner):
            owner = owner_at(sizes, far_outer, at // 2, at % 2)
            ordered_ref[pl.ds(pl.multiple_of(owner * cap, cap), cap), :] = value[at * cap : (at + 1) * cap]


def ready_kernel(lines, dst_hbm, mesh_hbm, w1_hbm, hot_hbm, moved_ref, dst_ref, mesh_ref, w1_ref, hot_ref, sems, out_sems):
    width = mesh_ref.shape[1]
    tile = lines * 128
    pairs = [(dst_hbm, dst_ref), (mesh_hbm, mesh_ref), (w1_hbm.at[pl.ds(width, width), :], w1_ref)]
    copies = load(pairs, sems)
    copies[0].wait()
    for at in range(hot_ref.shape[0] // tile):
        hot_ref[at * tile : (at + 1) * tile, :] = tile_columns(dst_ref, at, lines, hot_ref.shape[1])
    (out,) = load([(hot_ref, hot_hbm)], out_sems)
    copies[1].wait()
    copies[2].wait()
    moved_ref[...] = dot_nn(mesh_ref[...], w1_ref[...]).astype(BF16)
    out.wait()


def base_kernel(
    lines,
    hot_hbm,
    edge_hbm,
    w1_hbm,
    slot_hbm,
    dst_hbm,
    mesh_hbm,
    cot_hbm,
    wn1_hbm,
    wn2_hbm,
    moved_ref,
    base_ref,
    slot_ref,
    dst_ref,
    top_ref,
    turned_hbm,
    node_hbm,
    cot_out_hbm,
    hot_ref,
    edge_ref,
    w1_ref,
    turned_ref,
    mesh_ref,
    cot_ref,
    wn1_ref,
    wn2_ref,
    node_ref,
    cot_out_ref,
    sems,
    out_sems,
):
    width = edge_ref.shape[1]
    tile = lines * 128
    tiles = edge_ref.shape[0] // tile
    pairs = [(edge_hbm.at[pl.ds(at * tile, tile), :], edge_ref.at[pl.ds(at * tile, tile), :]) for at in range(tiles)]
    pairs += [(w1_hbm.at[pl.ds(2 * width, width), :], w1_ref), (hot_hbm, hot_ref)]
    pairs += [(mesh_hbm, mesh_ref), (wn1_hbm.at[pl.ds(0, width), :], wn1_ref), (cot_hbm, cot_ref), (wn2_hbm, wn2_ref)]
    pairs += [(w1_hbm.at[pl.ds(0, width), :], top_ref), (slot_hbm, slot_ref), (dst_hbm, dst_ref)]
    copies = load(pairs, sems)
    same = lax.broadcasted_iota(jnp.int32, (256, 256), 0) == lax.broadcasted_iota(jnp.int32, (256, 256), 1)
    eye = jnp.where(same, 1.0, 0.0).astype(BF16)
    outs = []
    for at in range(tiles):
        rows = slice(at * tile, (at + 1) * tile)
        copies[at].wait()
        for start in range(0, width, 256):
            block = dot_nt(eye, edge_ref[rows, start : start + 256])
            turned_ref[start : start + 256, rows] = block.astype(BF16)
        columns = pl.ds(at * tile, tile)
        out = pltpu.make_async_copy(turned_ref.at[:, columns], turned_hbm.at[:, columns], out_sems.at[at])
        out.start()
        outs.append(out)
    for copy in copies[tiles : tiles + 6]:
        copy.wait()
    node_ref[...] = dot_nn(mesh_ref[...], wn1_ref[...])
    cot_out_ref[...] = dot_nt(cot_ref[...], wn2_ref[...])
    for at, (source, target) in enumerate([(node_ref, node_hbm), (cot_out_ref, cot_out_hbm)]):
        out = pltpu.make_async_copy(source, target, out_sems.at[tiles + at])
        out.start()
        outs.append(out)
    for at in range(tiles):
        rows = slice(at * tile, (at + 1) * tile)
        base_ref[rows, :] = dot_nn(edge_ref[rows, :], w1_ref[...]) + dot_nn(hot_ref[rows, :], moved_ref[...])
    for out in outs + copies[tiles + 6 :]:
        out.wait()


def main_kernel(
    lines,
    sizes,
    mesh_hbm,
    w2_hbm,
    wn1_hbm,
    turned_hbm,
    hot_hbm,
    node_hbm,
    cot_hbm,
    base_ref,
    slot_ref,
    dst_ref,
    w1_ref,
    *rest,
):
    outer, inner = sizes
    slot_blocks, rest = rest[:outer], rest[outer:]
    node_out_ref, d_slots_ref = rest[:2]
    send_refs, keep_refs, rest = rest[2 : 2 + outer], rest[2 + outer : 2 + 2 * outer], rest[2 + 2 * outer :]
    slope_ref, value_ref, both_ref, grads_ref, slot_grads_ref, ordered_ref = rest[:6]
    mesh_ref, w2_ref, wn1_ref, hot_ref, node_ref, cot_ref, picks_ref, sems = rest[6:]
    width = mesh_ref.shape[1]
    mesh_rows = mesh_ref.shape[0]
    slot_rows = ordered_ref.shape[0]
    tile = lines * 128
    tiles = base_ref.shape[0] // tile
    pairs = [
        (w2_hbm, w2_ref),
        (wn1_hbm.at[pl.ds(width, wn1_ref.shape[0]), :], wn1_ref),
        (mesh_hbm, mesh_ref),
        (node_hbm, node_ref),
        (cot_hbm, cot_ref),
        (hot_hbm, hot_ref),
        (turned_hbm, both_ref.at[pl.ds(slot_rows + mesh_rows, width), :]),
    ]
    copies = load(pairs, sems)
    place_rows(sizes, slot_blocks, ordered_ref)
    slots_value = ordered_ref[...].astype(BF16)
    for at in range(tiles):
        rows = slice(at * tile, (at + 1) * tile)
        picks_ref[rows, :] = tile_columns(slot_ref, at, lines, slot_rows)
        both_ref[:slot_rows, rows] = tile_rows(slot_ref, at, lines, slot_rows)
        both_ref[slot_rows : slot_rows + mesh_rows, rows] = tile_rows(dst_ref, at, lines, mesh_rows)

    slots = slots_value
    slot_pair = jnp.concatenate(split(dot_nn(slots, w1_ref[...])), axis=0)
    for at in range(tiles):
        rows = slice(at * tile, (at + 1) * tile)
        from_slot = picks_ref[rows, :]
        twice = jnp.concatenate([from_slot, from_slot], axis=1)
        pre = base_ref[rows, :] + dot_nn(twice, slot_pair)
        sigma = 0.5 + 0.5 * jnp.tanh(0.5 * pre)
        hidden = pre * sigma
        slope_ref[rows, :] = sigma + hidden * (1.0 - sigma)
        value_ref[rows, :] = hidden.astype(BF16)

    for copy in copies[:-1]:
        copy.wait()
    hidden_sums = dot_nn(both_ref[slot_rows : slot_rows + mesh_rows, :], value_ref[...]).astype(BF16)
    received = dot_nn(hidden_sums, w2_ref[...]).astype(BF16)
    mesh = mesh_ref[...]
    pre_node = node_ref[...] + dot_nn(received, wn1_ref[...])
    sigma = 0.5 + 0.5 * jnp.tanh(0.5 * pre_node)
    node = pre_node * sigma
    slope = sigma + node * (1.0 - sigma)
    d_pre_node = (cot_ref[...] * slope).astype(BF16)
    d_received = dot_nt(d_pre_node, wn1_ref[...]).astype(BF16)
    spread = dot_nt(d_received, w2_ref[...]).astype(BF16)

    for at in range(tiles):
        rows = slice(at * tile, (at + 1) * tile)
        value_ref[rows, :] = (dot_nn(hot_ref[rows, :], spread) * slope_ref[rows, :]).astype(BF16)

    grads_ref[3 * width :, :] = dot_tn(hidden_sums, d_received)
    node_out_ref[...] = node.astype(BF16)
    copies[-1].wait()
    product = dot_nn(both_ref[...], value_ref[...])
    sums = product[: slot_rows + mesh_rows].astype(BF16)
    grads_ref[2 * width : 3 * width, :] = product[slot_rows + mesh_rows :]
    slot_grads_ref[...] = dot_nt(sums[:slot_rows], w1_ref[...])
    grads_ref[:width, :] = dot_tn(slots, sums[:slot_rows])
    grads_ref[width : 2 * width, :] = dot_tn(mesh, sums[slot_rows:])

    chunk = grads_ref.shape[0] // (2 * outer * inner)
    cap = slot_rows // (2 * outer * inner)
    for far_core in range(2):
        for far_outer in range(outer):
            for far_inner in range(inner):
                owner = owner_at(sizes, far_outer, far_inner, far_core)
                at = (far_core * outer + far_outer) * inner + far_inner
                from_rows = pl.ds(pl.multiple_of(owner * cap, cap), cap)
                ordered_ref[at * cap : (at + 1) * cap, :] = slot_grads_ref[from_rows, :]
                value = grads_ref[pl.ds(pl.multiple_of(owner * chunk, chunk), chunk), :]
                rows = slice(far_inner * chunk, (far_inner + 1) * chunk)
                if far_core:
                    send_refs[far_outer][rows, :] = value.astype(BF16)
                else:
                    keep_refs[far_outer][rows, :] = value
    halfway, share = slot_rows // 2, inner * cap
    d_slots_ref[...] = ordered_ref[:halfway, :].astype(BF16)
    for far_outer, send_ref in enumerate(send_refs):
        start = halfway + far_outer * share
        send_ref[inner * chunk :, :] = ordered_ref[start : start + share, :].astype(BF16)


def mesh_kernel(mesh_hbm, wn2_hbm, node_ref, out_ref, mesh_ref, wn2_ref, sems):
    for copy in load([(mesh_hbm, mesh_ref), (wn2_hbm, wn2_ref)], sems):
        copy.wait()
    out_ref[...] = (mesh_ref[...].astype(F32) + dot_nn(node_ref[...], wn2_ref[...])).astype(BF16)


def core_kernel(sizes, far_outer, keep_ref, crossed_ref, d_slots_ref, total_ref, mixed_ref, *part_refs):
    outer, inner = sizes
    chunk = total_ref.shape[0]
    cap = d_slots_ref.shape[0] // (outer * inner)
    start = far_outer * inner * cap
    own = d_slots_ref[start : start + inner * cap, :].astype(F32)
    far = crossed_ref[inner * chunk :, :].astype(F32)
    for far_inner in range(inner):
        rows, slots = slice(far_inner * chunk, (far_inner + 1) * chunk), slice(far_inner * cap, (far_inner + 1) * cap)
        total = keep_ref[rows, :] + crossed_ref[rows, :].astype(F32)
        mixed = jnp.concatenate([own[slots], far[slots]], axis=0).astype(BF16)
        if far_inner:
            part_refs[far_inner - 1][:chunk, :] = total.astype(BF16)
            part_refs[far_inner - 1][chunk:, :] = mixed
        else:
            total_ref[...] = total
            mixed_ref[...] = mixed


def inner_kernel(parts, arrivals, total_ref, mixed_ref, *refs):
    received, arrived, outs = refs[:parts], refs[parts : parts + arrivals], refs[parts + arrivals :]
    chunk = total_ref.shape[0]
    total = total_ref[...]
    mixed = [mixed_ref[...]]
    for part in received:
        total = total + part[:chunk, :].astype(F32)
        mixed.append(part[chunk:, :])
    for value in arrived:
        total = total + value[:chunk, :].astype(F32)
    mixed = jnp.concatenate(mixed, axis=0)
    if len(outs) == 1:
        outs[0][:chunk, :] = total.astype(BF16)
        outs[0][chunk:, :] = mixed
    else:
        outs[0][...] = total.astype(BF16)
        outs[1][...] = mixed


def order_kernel(sizes, places, aliased, *refs):
    outer, inner = sizes
    pieces = refs[: len(places)]
    first_hbm, second_hbm, stage_ref, sems = refs[len(places) + aliased :]
    chunk = pieces[0].shape[0]
    first_chunks = first_hbm.shape[0] // chunk

    def send(k, target, start):
        rows = pl.ds(pl.multiple_of(start, chunk), chunk)
        return pltpu.make_async_copy(stage_ref.at[k], target.at[rows, :], sems.at[k])

    for k, (at, piece) in enumerate(zip(places, pieces)):
        owner = owner_at(sizes, at % outer, at // outer % inner, at // (outer * inner))
        stage_ref[k] = piece[...].astype(F32)

        @pl.when(owner < first_chunks)
        def _():
            send(k, first_hbm, owner * chunk).start()

        @pl.when(owner >= first_chunks)
        def _():
            send(k, second_hbm, (owner - first_chunks) * chunk).start()

    for k in range(len(places)):
        send(k, first_hbm, 0).wait()


def shards(
    sizes,
    grid_latent,
    mesh_latent,
    edge_latent,
    mesh_cot,
    send_rows,
    edge_slot,
    edge_dst,
    w_edge1,
    w_edge2,
    w_node1,
    w_node2,
):
    outer, inner = sizes
    band_count = lax.axis_size("band")
    width = grid_latent.shape[1]
    hidden_width = w_edge1.shape[1]
    edges = edge_latent.shape[0]
    mesh_rows = mesh_latent.shape[0]
    slot_rows = send_rows.shape[1]
    lines = 4
    slot_index = edge_slot.reshape(edges // 128, 128)
    dst_index = edge_dst.reshape(edges // 128, 128)

    def permute(value, stride, size, shift):
        pairs = []
        for source in range(band_count):
            place = (source // stride) % size
            pairs.append((source, source + ((place ^ shift) - place) * stride))
        return lax.ppermute(value, "band", pairs)

    def to_core(value):
        return permute(value, 1, 2, 1)

    def to_inner(value, shift):
        return permute(value, 2, inner, shift)

    def to_outer(value, shift):
        return permute(value, 2 * inner, outer, shift)

    cap, halfway = slot_rows // band_count, slot_rows // 2
    kept, sent = pl.pallas_call(
        functools.partial(pick_kernel, sizes),
        out_shape=[jax.ShapeDtypeStruct((halfway, width), BF16)] * 2,
        in_specs=specs(pltpu.HBM, 2),
        out_specs=specs(pltpu.VMEM, 2),
        scratch_shapes=[
            pltpu.VMEM(send_rows.shape, jnp.int32),
            pltpu.VMEM(grid_latent.shape, BF16),
            pltpu.VMEM((slot_rows, width), F32),
            pltpu.SemaphoreType.DMA((5,)),
        ],
        compiler_params=params(16),
        name="pick",
    )(*pinned(pltpu.HBM, send_rows, grid_latent))

    def mix(values, count, minor):
        rows = len(values) * values[0].shape[0] // count
        return pl.pallas_call(
            functools.partial(mix_kernel, count, minor),
            out_shape=[jax.ShapeDtypeStruct((rows, width), BF16)] * count,
            compiler_params=params(16),
            name="mix",
        )(*values)

    hot, moved = pl.pallas_call(
        functools.partial(ready_kernel, lines),
        out_shape=[
            pltpu.HBM((edges, mesh_rows), BF16),
            pltpu.VMEM((mesh_rows, hidden_width), BF16),
        ],
        in_specs=specs(pltpu.HBM, 3),
        out_specs=specs(pltpu.HBM, 1) + specs(pltpu.VMEM, 1),
        scratch_shapes=[
            pltpu.VMEM(dst_index.shape, jnp.int32),
            pltpu.VMEM(mesh_latent.shape, BF16),
            pltpu.VMEM((width, hidden_width), BF16),
            pltpu.VMEM((edges, mesh_rows), BF16),
            pltpu.SemaphoreType.DMA((3,)),
            pltpu.SemaphoreType.DMA((1,)),
        ],
        compiler_params=params(16),
        cost_estimate=cost(2 * 10**9, 4 * MIB),
        name="ready",
    )(*pinned(pltpu.HBM, dst_index, mesh_latent, w_edge1))
    tiles = edges // (128 * lines)
    base, *ahead, turned, node, cot = pl.pallas_call(
        functools.partial(base_kernel, lines),
        out_shape=[
            pltpu.VMEM((edges, hidden_width), F32),
            pltpu.VMEM(slot_index.shape, jnp.int32),
            pltpu.VMEM(dst_index.shape, jnp.int32),
            pltpu.VMEM((width, hidden_width), BF16),
            pltpu.HBM((width, edges), BF16),
            pltpu.HBM((mesh_rows, hidden_width), F32),
            pltpu.HBM((mesh_rows, hidden_width), F32),
        ],
        in_specs=specs(pltpu.HBM, 9) + specs(pltpu.VMEM, 1),
        out_specs=specs(pltpu.VMEM, 4) + specs(pltpu.HBM, 3),
        scratch_shapes=[
            pltpu.VMEM((edges, mesh_rows), BF16),
            pltpu.VMEM(edge_latent.shape, BF16),
            pltpu.VMEM((width, hidden_width), BF16),
            pltpu.VMEM((width, edges), BF16),
            pltpu.VMEM(mesh_latent.shape, BF16),
            pltpu.VMEM(mesh_cot.shape, BF16),
            pltpu.VMEM((width, hidden_width), BF16),
            pltpu.VMEM(w_node2.shape, BF16),
            pltpu.VMEM((mesh_rows, hidden_width), F32),
            pltpu.VMEM((mesh_rows, hidden_width), F32),
            pltpu.SemaphoreType.DMA((9 + tiles,)),
            pltpu.SemaphoreType.DMA((2 + tiles,)),
        ],
        compiler_params=params(20),
        cost_estimate=cost(4 * 10**9, 4 * MIB),
        name="base",
    )(
        *pinned(pltpu.HBM, hot, edge_latent, w_edge1, slot_index, dst_index, mesh_latent, mesh_cot, w_node1, w_node2),
        *pinned(pltpu.VMEM, moved),
    )

    by_inner = mix([kept, to_core(sent)], inner, outer)
    by_inner = [by_inner[0]] + [to_inner(by_inner[k], k) for k in range(1, inner)]
    by_outer = mix(by_inner, outer, 1)
    slot_blocks = [by_outer[0]] + [to_outer(by_outer[k], k) for k in range(1, outer)]

    grad_rows = 3 * width + hidden_width
    chunk = grad_rows // band_count
    group = (inner * chunk, hidden_width)
    node_out, d_slots, *sides = pl.pallas_call(
        functools.partial(main_kernel, lines, sizes),
        out_shape=[
            jax.ShapeDtypeStruct((mesh_rows, width), BF16),
            jax.ShapeDtypeStruct((halfway, width), BF16),
        ]
        + [jax.ShapeDtypeStruct((group[0] + inner * cap, hidden_width), BF16)] * outer
        + [jax.ShapeDtypeStruct(group, F32)] * outer,
        in_specs=specs(pltpu.HBM, 7) + specs(pltpu.VMEM, 4 + outer),
        out_specs=specs(pltpu.VMEM, 2 + 2 * outer),
        scratch_shapes=[
            pltpu.VMEM((edges, hidden_width), F32),
            pltpu.VMEM((edges, hidden_width), BF16),
            pltpu.VMEM((slot_rows + mesh_rows + width, edges), BF16),
            pltpu.VMEM((grad_rows, hidden_width), F32),
            pltpu.VMEM((slot_rows, width), F32),
            pltpu.VMEM((slot_rows, width), F32),
            pltpu.VMEM(mesh_latent.shape, BF16),
            pltpu.VMEM(w_edge2.shape, BF16),
            pltpu.VMEM((w_node1.shape[0] - width, w_node1.shape[1]), BF16),
            pltpu.VMEM(hot.shape, BF16),
            pltpu.VMEM(node.shape, F32),
            pltpu.VMEM(cot.shape, F32),
            pltpu.VMEM((edges, slot_rows), BF16),
            pltpu.SemaphoreType.DMA((7,)),
        ],
        compiler_params=params(40),
        name="edges",
    )(
        *pinned(pltpu.HBM, mesh_latent, w_edge2, w_node1, turned, hot, node, cot),
        *pinned(pltpu.VMEM, base, *ahead),
        *slot_blocks,
    )
    mesh_out = pl.pallas_call(
        mesh_kernel,
        out_shape=jax.ShapeDtypeStruct((mesh_rows, width), BF16),
        in_specs=specs(pltpu.HBM, 2) + specs(pltpu.VMEM, 1),
        out_specs=pl.BlockSpec(memory_space=pltpu.VMEM),
        scratch_shapes=[
            pltpu.VMEM(mesh_latent.shape, BF16),
            pltpu.VMEM(w_node2.shape, BF16),
            pltpu.SemaphoreType.DMA((2,)),
        ],
        compiler_params=params(16),
        cost_estimate=cost(10**9, MIB),
        name="mesh",
    )(*pinned(pltpu.HBM, mesh_latent, w_node2), node_out)
    sends, keeps = sides[:outer], sides[outer:]
    small = (2 * cap, width)
    arrived = {}
    first = None
    for k in range(outer - 1, -1, -1):
        send = sends[k] if first is None else lax.optimization_barrier((sends[k], first))[0]
        crossed = to_core(send)
        total, mixed, *parts = pl.pallas_call(
            functools.partial(core_kernel, sizes, k),
            out_shape=[
                jax.ShapeDtypeStruct((chunk, hidden_width), F32),
                jax.ShapeDtypeStruct(small, BF16),
            ]
            + [jax.ShapeDtypeStruct((chunk + 2 * cap, width), BF16)] * (inner - 1),
            compiler_params=params(16),
            cost_estimate=cost(10**9, MIB),
            name="core",
        )(keeps[k], crossed, d_slots)
        first = parts[0] if first is None else first
        parts = [to_inner(part, at + 1) for at, part in enumerate(parts)]
        block = 2 * inner * cap
        if k:
            (out,) = pl.pallas_call(
                functools.partial(inner_kernel, inner - 1, 0),
                out_shape=[jax.ShapeDtypeStruct((chunk + block, width), BF16)],
                compiler_params=params(16),
                name="inner",
            )(total, mixed, *parts)
            arrived[k] = to_outer(out, k)
        else:
            total = lax.optimization_barrier((total, mesh_out))[0]
            own, home = pl.pallas_call(
                functools.partial(inner_kernel, inner - 1, outer - 1),
                out_shape=[
                    jax.ShapeDtypeStruct((chunk, hidden_width), BF16),
                    jax.ShapeDtypeStruct((block, width), BF16),
                ],
                compiler_params=params(16),
                name="own",
            )(total, mixed, *parts, *[arrived[at] for at in range(outer - 1, 0, -1)])

    grid_grad = pl.pallas_call(
        functools.partial(put_kernel, sizes),
        out_shape=jax.ShapeDtypeStruct(grid_latent.shape, F32),
        in_specs=specs(pltpu.HBM, 1) + specs(pltpu.VMEM, outer),
        out_specs=pl.BlockSpec(memory_space=pltpu.VMEM),
        scratch_shapes=[
            pltpu.VMEM((slot_rows, width), F32),
            pltpu.VMEM(send_rows.shape, jnp.int32),
            pltpu.SemaphoreType.DMA((1,)),
        ],
        compiler_params=params(16),
        cost_estimate=cost(2 * 10**9, 2 * MIB),
        name="put",
    )(*pinned(pltpu.HBM, send_rows), home, *[arrived[at] for at in range(1, outer)])

    pieces = {0: own}
    stride = outer // 2
    while stride:
        for at in range(0, outer, 2 * stride):
            value = pieces[at]
            if at == outer // 2 and stride == outer // 4:
                value = lax.optimization_barrier((value, grid_grad))[0]
            pieces[at + stride] = to_outer(value, stride)
        stride //= 2
    halfway_at = band_count // 2
    pieces[halfway_at] = to_core(own)
    for far_inner in range(1, inner):
        for far_outer in range(outer):
            value = pieces[far_outer]
            if far_outer == outer // 2:
                value = lax.optimization_barrier((value, pieces[halfway_at]))[0]
            pieces[far_inner * outer + far_outer] = to_inner(value, far_inner)
    for at in range(1, halfway_at - 1):
        pieces[halfway_at + at] = to_core(pieces[at])

    last = outer - 1
    stages = [[], [], []]
    for at in range(band_count):
        far_outer, far_inner, far_core = at % outer, at // outer % inner, at // halfway_at
        if far_outer == last:
            stages[2 if far_inner else 1].append(at)
        else:
            stages[1 if far_inner and (far_core or far_outer == outer // 2) else 0].append(at)
    grads = []
    for places in stages:
        if places is stages[1]:
            value = lax.optimization_barrier((pieces[halfway_at - 1], *grads))[0]
            pieces[band_count - 1] = to_core(value)
        grads = pl.pallas_call(
            functools.partial(order_kernel, sizes, places, len(grads)),
            out_shape=[
                jax.ShapeDtypeStruct((3 * width, hidden_width), F32),
                jax.ShapeDtypeStruct((hidden_width, width), F32),
            ],
            in_specs=specs(pltpu.VMEM, len(places)) + specs(pltpu.HBM, len(grads)),
            out_specs=specs(pltpu.HBM, 2),
            scratch_shapes=[
                pltpu.VMEM((len(places), chunk, hidden_width), F32),
                pltpu.SemaphoreType.DMA((len(places),)),
            ],
            input_output_aliases={len(places) + k: k for k in range(len(grads))},
            compiler_params=params(16),
            cost_estimate=cost(15 * 10**7 * len(places), 2 * MIB),
            name="order",
        )(*[pieces[at] for at in places], *grads)
    grad_edge1, grad_edge2 = grads
    return (mesh_out, grid_grad, grad_edge1, grad_edge2)


def solution(mesh):
    chips = mesh.shape["band"] // 2
    inner = 1
    while inner * inner * 4 <= chips:
        inner *= 2
    sizes = (chips // inner, inner)
    in_specs = (
        P(("groups", "band"), None),
        P(("groups", "band"), None),
        P(("groups", "band"), None),
        P(("groups", "band"), None),
        P("band", None),
        P("band"),
        P("band"),
        P(),
        P(),
        P(),
        P(),
    )
    out_specs = (
        P(("groups", "band"), None),
        P(("groups", "band"), None),
        P("groups", None),
        P("groups", None),
    )
    return jax.shard_map(
        functools.partial(shards, sizes), mesh=mesh, in_specs=in_specs, out_specs=out_specs, check_vma=False
    )
```

```python
import functools

import jax
import jax.numpy as jnp
from jax import lax
from jax.experimental import pallas as pl
from jax.experimental.pallas import tpu as pltpu
from jax.sharding import PartitionSpec as P

BF16 = jnp.bfloat16
F32 = jnp.float32
MIB = 1024 * 1024


def dot_nn(a, b):
    return jnp.dot(a, b, preferred_element_type=F32)


def dot_tn(a, b):
    return lax.dot_general(a, b, (((0,), (0,)), ((), ())), preferred_element_type=F32)


def dot_nt(a, b):
    return lax.dot_general(a, b, (((1,), (1,)), ((), ())), preferred_element_type=F32)


def split(value):
    high = value.astype(BF16)
    low = (value - high.astype(F32)).astype(BF16)
    return high, low


def one_hot_rows(index_row, rows):
    shape = (rows, index_row.shape[1])
    hit = lax.broadcasted_iota(jnp.int32, shape, 0) == index_row
    return jnp.where(hit, 1.0, 0.0).astype(BF16)


def one_hot_columns(index_row, columns):
    lanes = index_row.shape[1]
    index = jnp.transpose(jnp.broadcast_to(index_row, (lanes, lanes)))
    pieces = []
    for start in range(0, columns, lanes):
        hit = lax.broadcasted_iota(jnp.int32, (lanes, lanes), 1) + start == index
        pieces.append(jnp.where(hit, 1.0, 0.0).astype(BF16))
    return pieces[0] if len(pieces) == 1 else jnp.concatenate(pieces, axis=1)


def tile_rows(index_ref, at, lines, rows):
    found = [one_hot_rows(index_ref[pl.ds(at * lines + k, 1), :], rows) for k in range(lines)]
    return jnp.concatenate(found, axis=1)


def tile_columns(index_ref, at, lines, columns):
    found = [one_hot_columns(index_ref[pl.ds(at * lines + k, 1), :], columns) for k in range(lines)]
    return jnp.concatenate(found, axis=0)


def place_of(sizes):
    outer, inner = sizes
    me = lax.axis_index("band")
    return me // (2 * inner), (me // 2) % inner, me % 2


def owner_at(sizes, far_outer, far_inner, far_core):
    my_outer, my_inner, my_core = place_of(sizes)
    return ((my_outer ^ far_outer) * sizes[1] + (my_inner ^ far_inner)) * 2 + (my_core ^ far_core)


def params(mib):
    return pltpu.CompilerParams(vmem_limit_bytes=mib * MIB)


def pinned(space, *values):
    return [pltpu.with_memory_space_constraint(value, space) for value in values]


def specs(space, count):
    return [pl.BlockSpec(memory_space=space)] * count


def cost(flops, nbytes):
    return pl.CostEstimate(flops=flops, bytes_accessed=nbytes, transcendentals=0)


def load(pairs, sems):
    copies = [pltpu.make_async_copy(source, target, sems.at[at]) for at, (source, target) in enumerate(pairs)]
    for copy in copies:
        copy.start()
    return copies


def pick_kernel(sizes, rows_hbm, grid_hbm, keep_ref, send_ref, rows_ref, grid_ref, picked_ref, sems):
    outer, inner = sizes
    block = grid_ref.shape[0] // 4
    parts = [pl.ds(at * block, block) for at in range(4)]
    copies = load([(rows_hbm, rows_ref)] + [(grid_hbm.at[part, :], grid_ref.at[part, :]) for part in parts], sems)
    copies[0].wait()
    picked = picked_ref.shape[0]
    chosen = [one_hot_columns(rows_ref[:, at : at + 128], grid_ref.shape[0]) for at in range(0, picked, 128)]
    for copy in copies[1:]:
        copy.wait()
    for at, some in enumerate(chosen):
        picked_ref[at * 128 : (at + 1) * 128, :] = dot_nn(some, grid_ref[...])
    cap = picked // (2 * outer * inner)
    for far_core, target in enumerate((keep_ref, send_ref)):
        blocks = []
        for far_inner in range(inner):
            for far_outer in range(outer):
                owner = owner_at(sizes, far_outer, far_inner, far_core)
                blocks.append(picked_ref[pl.ds(pl.multiple_of(owner * cap, cap), cap), :])
        target[...] = jnp.concatenate(blocks, axis=0).astype(BF16)


def mix_kernel(count, minor, *refs):
    sources, targets = refs[:-count], refs[-count:]
    values = [ref[...].astype(F32) for ref in sources]
    unit = values[0].shape[0] // (count * minor)
    for at, target in enumerate(targets):
        starts = [(at * minor + k) * unit for k in range(minor)]
        blocks = [value[start : start + unit] for start in starts for value in values]
        target[...] = jnp.concatenate(blocks, axis=0).astype(BF16)


def put_kernel(sizes, rows_hbm, *refs):
    outer, inner = sizes
    blocks, (out_ref, ordered_ref, rows_ref, sems) = refs[:outer], refs[outer:]
    (copy,) = load([(rows_hbm, rows_ref)], sems)
    place_rows(sizes, blocks, ordered_ref)
    copy.wait()
    chosen = one_hot_rows(rows_ref[...], out_ref.shape[0])
    out_ref[...] = dot_nn(chosen, ordered_ref[...].astype(BF16))


def place_rows(sizes, blocks, ordered_ref):
    outer, inner = sizes
    cap = ordered_ref.shape[0] // (2 * outer * inner)
    for far_outer, block in enumerate(blocks):
        value = block[block.shape[0] - 2 * inner * cap :, :].astype(F32)
        for at in range(2 * inner):
            owner = owner_at(sizes, far_outer, at // 2, at % 2)
            ordered_ref[pl.ds(pl.multiple_of(owner * cap, cap), cap), :] = value[at * cap : (at + 1) * cap]


def ready_kernel(
    lines,
    dst_hbm,
    mesh_hbm,
    cot_hbm,
    w1_hbm,
    wn1_hbm,
    wn2_hbm,
    hot_hbm,
    node_hbm,
    cot_out_hbm,
    moved_ref,
    dst_ref,
    mesh_ref,
    cot_ref,
    w1_ref,
    wn1_ref,
    wn2_ref,
    hot_ref,
    node_ref,
    cot_out_ref,
    sems,
    out_sems,
):
    width = mesh_ref.shape[1]
    tile = lines * 128
    pairs = [
        (dst_hbm, dst_ref),
        (mesh_hbm, mesh_ref),
        (w1_hbm.at[pl.ds(width, width), :], w1_ref),
        (wn1_hbm.at[pl.ds(0, width), :], wn1_ref),
        (cot_hbm, cot_ref),
        (wn2_hbm, wn2_ref),
    ]
    copies = load(pairs, sems)
    outs = [
        pltpu.make_async_copy(source, target, out_sems.at[at])
        for at, (source, target) in enumerate([(hot_ref, hot_hbm), (node_ref, node_hbm), (cot_out_ref, cot_out_hbm)])
    ]
    copies[0].wait()
    for at in range(hot_ref.shape[0] // tile):
        hot_ref[at * tile : (at + 1) * tile, :] = tile_columns(dst_ref, at, lines, hot_ref.shape[1])
    outs[0].start()
    copies[1].wait()
    copies[3].wait()
    node_ref[...] = dot_nn(mesh_ref[...], wn1_ref[...])
    outs[1].start()
    copies[4].wait()
    copies[5].wait()
    cot_out_ref[...] = dot_nt(cot_ref[...], wn2_ref[...])
    outs[2].start()
    copies[2].wait()
    moved_ref[...] = dot_nn(mesh_ref[...], w1_ref[...]).astype(BF16)
    for copy in outs:
        copy.wait()


def base_kernel(
    lines,
    hot_hbm,
    edge_hbm,
    w1_hbm,
    slot_hbm,
    dst_hbm,
    moved_ref,
    base_ref,
    slot_ref,
    dst_ref,
    top_ref,
    turned_hbm,
    hot_ref,
    edge_ref,
    w1_ref,
    turned_ref,
    sems,
    out_sems,
):
    width = edge_ref.shape[1]
    tile = lines * 128
    tiles = edge_ref.shape[0] // tile
    pairs = [(edge_hbm.at[pl.ds(at * tile, tile), :], edge_ref.at[pl.ds(at * tile, tile), :]) for at in range(tiles)]
    pairs += [(w1_hbm.at[pl.ds(2 * width, width), :], w1_ref), (hot_hbm, hot_ref)]
    pairs += [(w1_hbm.at[pl.ds(0, width), :], top_ref), (slot_hbm, slot_ref), (dst_hbm, dst_ref)]
    copies = load(pairs, sems)
    same = lax.broadcasted_iota(jnp.int32, (256, 256), 0) == lax.broadcasted_iota(jnp.int32, (256, 256), 1)
    eye = jnp.where(same, 1.0, 0.0).astype(BF16)
    outs = []
    for at in range(tiles):
        rows = slice(at * tile, (at + 1) * tile)
        copies[at].wait()
        for start in range(0, width, 256):
            block = dot_nt(eye, edge_ref[rows, start : start + 256])
            turned_ref[start : start + 256, rows] = block.astype(BF16)
        columns = pl.ds(at * tile, tile)
        out = pltpu.make_async_copy(turned_ref.at[:, columns], turned_hbm.at[:, columns], out_sems.at[at])
        out.start()
        outs.append(out)
    copies[tiles].wait()
    copies[tiles + 1].wait()
    for at in range(tiles):
        rows = slice(at * tile, (at + 1) * tile)
        base_ref[rows, :] = dot_nn(edge_ref[rows, :], w1_ref[...]) + dot_nn(hot_ref[rows, :], moved_ref[...])
    for out in outs + copies[tiles + 2 :]:
        out.wait()


def main_kernel(
    lines,
    sizes,
    mesh_hbm,
    w2_hbm,
    wn1_hbm,
    turned_hbm,
    hot_hbm,
    node_hbm,
    cot_hbm,
    base_ref,
    slot_ref,
    dst_ref,
    w1_ref,
    *rest,
):
    outer, inner = sizes
    slot_blocks, rest = rest[:outer], rest[outer:]
    node_out_ref, d_slots_ref = rest[:2]
    send_refs, keep_refs, rest = rest[2 : 2 + outer], rest[2 + outer : 2 + 2 * outer], rest[2 + 2 * outer :]
    slope_ref, value_ref, both_ref, grads_ref, slot_grads_ref, ordered_ref = rest[:6]
    mesh_ref, w2_ref, wn1_ref, hot_ref, node_ref, cot_ref, picks_ref, sems = rest[6:]
    width = mesh_ref.shape[1]
    mesh_rows = mesh_ref.shape[0]
    slot_rows = ordered_ref.shape[0]
    tile = lines * 128
    tiles = base_ref.shape[0] // tile
    pairs = [
        (w2_hbm, w2_ref),
        (wn1_hbm.at[pl.ds(width, wn1_ref.shape[0]), :], wn1_ref),
        (mesh_hbm, mesh_ref),
        (node_hbm, node_ref),
        (cot_hbm, cot_ref),
        (hot_hbm, hot_ref),
        (turned_hbm, both_ref.at[pl.ds(slot_rows + mesh_rows, width), :]),
    ]
    copies = load(pairs, sems)
    place_rows(sizes, slot_blocks, ordered_ref)
    slots_value = ordered_ref[...].astype(BF16)
    for at in range(tiles):
        rows = slice(at * tile, (at + 1) * tile)
        picks_ref[rows, :] = tile_columns(slot_ref, at, lines, slot_rows)
        both_ref[:slot_rows, rows] = tile_rows(slot_ref, at, lines, slot_rows)
        both_ref[slot_rows : slot_rows + mesh_rows, rows] = tile_rows(dst_ref, at, lines, mesh_rows)

    slots = slots_value
    slot_pair = jnp.concatenate(split(dot_nn(slots, w1_ref[...])), axis=0)
    for at in range(tiles):
        rows = slice(at * tile, (at + 1) * tile)
        from_slot = picks_ref[rows, :]
        twice = jnp.concatenate([from_slot, from_slot], axis=1)
        pre = base_ref[rows, :] + dot_nn(twice, slot_pair)
        sigma = 0.5 + 0.5 * jnp.tanh(0.5 * pre)
        hidden = pre * sigma
        slope_ref[rows, :] = sigma + hidden * (1.0 - sigma)
        value_ref[rows, :] = hidden.astype(BF16)

    for copy in copies[:-1]:
        copy.wait()
    hidden_sums = dot_nn(both_ref[slot_rows : slot_rows + mesh_rows, :], value_ref[...]).astype(BF16)
    received = dot_nn(hidden_sums, w2_ref[...]).astype(BF16)
    mesh = mesh_ref[...]
    pre_node = node_ref[...] + dot_nn(received, wn1_ref[...])
    sigma = 0.5 + 0.5 * jnp.tanh(0.5 * pre_node)
    node = pre_node * sigma
    slope = sigma + node * (1.0 - sigma)
    d_pre_node = (cot_ref[...] * slope).astype(BF16)
    d_received = dot_nt(d_pre_node, wn1_ref[...]).astype(BF16)
    spread = dot_nt(d_received, w2_ref[...]).astype(BF16)

    for at in range(tiles):
        rows = slice(at * tile, (at + 1) * tile)
        value_ref[rows, :] = (dot_nn(hot_ref[rows, :], spread) * slope_ref[rows, :]).astype(BF16)

    grads_ref[3 * width :, :] = dot_tn(hidden_sums, d_received)
    node_out_ref[...] = node.astype(BF16)
    copies[-1].wait()
    product = dot_nn(both_ref[...], value_ref[...])
    sums = product[: slot_rows + mesh_rows].astype(BF16)
    grads_ref[2 * width : 3 * width, :] = product[slot_rows + mesh_rows :]
    slot_grads_ref[...] = dot_nt(sums[:slot_rows], w1_ref[...])
    grads_ref[:width, :] = dot_tn(slots, sums[:slot_rows])
    grads_ref[width : 2 * width, :] = dot_tn(mesh, sums[slot_rows:])

    chunk = grads_ref.shape[0] // (2 * outer * inner)
    cap = slot_rows // (2 * outer * inner)
    for far_core in range(2):
        for far_outer in range(outer):
            for far_inner in range(inner):
                owner = owner_at(sizes, far_outer, far_inner, far_core)
                at = (far_core * outer + far_outer) * inner + far_inner
                from_rows = pl.ds(pl.multiple_of(owner * cap, cap), cap)
                ordered_ref[at * cap : (at + 1) * cap, :] = slot_grads_ref[from_rows, :]
                value = grads_ref[pl.ds(pl.multiple_of(owner * chunk, chunk), chunk), :]
                rows = slice(far_inner * chunk, (far_inner + 1) * chunk)
                if far_core:
                    send_refs[far_outer][rows, :] = value.astype(BF16)
                else:
                    keep_refs[far_outer][rows, :] = value
    halfway, share = slot_rows // 2, inner * cap
    d_slots_ref[...] = ordered_ref[:halfway, :].astype(BF16)
    for far_outer, send_ref in enumerate(send_refs):
        start = halfway + far_outer * share
        send_ref[inner * chunk :, :] = ordered_ref[start : start + share, :].astype(BF16)


def mesh_kernel(mesh_hbm, wn2_hbm, node_ref, out_ref, mesh_ref, wn2_ref, sems):
    for copy in load([(mesh_hbm, mesh_ref), (wn2_hbm, wn2_ref)], sems):
        copy.wait()
    out_ref[...] = (mesh_ref[...].astype(F32) + dot_nn(node_ref[...], wn2_ref[...])).astype(BF16)


def core_kernel(sizes, far_outer, keep_ref, crossed_ref, d_slots_ref, total_ref, mixed_ref, *part_refs):
    outer, inner = sizes
    chunk = total_ref.shape[0]
    cap = d_slots_ref.shape[0] // (outer * inner)
    start = far_outer * inner * cap
    own = d_slots_ref[start : start + inner * cap, :].astype(F32)
    far = crossed_ref[inner * chunk :, :].astype(F32)
    for far_inner in range(inner):
        rows, slots = slice(far_inner * chunk, (far_inner + 1) * chunk), slice(far_inner * cap, (far_inner + 1) * cap)
        total = keep_ref[rows, :] + crossed_ref[rows, :].astype(F32)
        mixed = jnp.concatenate([own[slots], far[slots]], axis=0).astype(BF16)
        if far_inner:
            part_refs[far_inner - 1][:chunk, :] = total.astype(BF16)
            part_refs[far_inner - 1][chunk:, :] = mixed
        else:
            total_ref[...] = total
            mixed_ref[...] = mixed


def inner_kernel(parts, arrivals, total_ref, mixed_ref, *refs):
    received, arrived, outs = refs[:parts], refs[parts : parts + arrivals], refs[parts + arrivals :]
    chunk = total_ref.shape[0]
    total = total_ref[...]
    mixed = [mixed_ref[...]]
    for part in received:
        total = total + part[:chunk, :].astype(F32)
        mixed.append(part[chunk:, :])
    for value in arrived:
        total = total + value[:chunk, :].astype(F32)
    mixed = jnp.concatenate(mixed, axis=0)
    if len(outs) == 1:
        outs[0][:chunk, :] = total.astype(BF16)
        outs[0][chunk:, :] = mixed
    else:
        outs[0][...] = total.astype(BF16)
        outs[1][...] = mixed


def order_kernel(sizes, places, aliased, *refs):
    outer, inner = sizes
    pieces = refs[: len(places)]
    first_hbm, second_hbm, stage_ref, sems = refs[len(places) + aliased :]
    chunk = pieces[0].shape[0]
    first_chunks = first_hbm.shape[0] // chunk

    def send(k, target, start):
        rows = pl.ds(pl.multiple_of(start, chunk), chunk)
        return pltpu.make_async_copy(stage_ref.at[k], target.at[rows, :], sems.at[k])

    for k, (at, piece) in enumerate(zip(places, pieces)):
        owner = owner_at(sizes, at % outer, at // outer % inner, at // (outer * inner))
        stage_ref[k] = piece[...].astype(F32)

        @pl.when(owner < first_chunks)
        def _():
            send(k, first_hbm, owner * chunk).start()

        @pl.when(owner >= first_chunks)
        def _():
            send(k, second_hbm, (owner - first_chunks) * chunk).start()

    for k in range(len(places)):
        send(k, first_hbm, 0).wait()


def shards(
    sizes,
    grid_latent,
    mesh_latent,
    edge_latent,
    mesh_cot,
    send_rows,
    edge_slot,
    edge_dst,
    w_edge1,
    w_edge2,
    w_node1,
    w_node2,
):
    outer, inner = sizes
    band_count = lax.axis_size("band")
    width = grid_latent.shape[1]
    hidden_width = w_edge1.shape[1]
    edges = edge_latent.shape[0]
    mesh_rows = mesh_latent.shape[0]
    slot_rows = send_rows.shape[1]
    lines = 6
    slot_index = edge_slot.reshape(edges // 128, 128)
    dst_index = edge_dst.reshape(edges // 128, 128)

    def permute(value, stride, size, shift):
        pairs = []
        for source in range(band_count):
            place = (source // stride) % size
            pairs.append((source, source + ((place ^ shift) - place) * stride))
        return lax.ppermute(value, "band", pairs)

    def to_core(value):
        return permute(value, 1, 2, 1)

    def to_inner(value, shift):
        return permute(value, 2, inner, shift)

    def to_outer(value, shift):
        return permute(value, 2 * inner, outer, shift)

    cap, halfway = slot_rows // band_count, slot_rows // 2
    kept, sent = pl.pallas_call(
        functools.partial(pick_kernel, sizes),
        out_shape=[jax.ShapeDtypeStruct((halfway, width), BF16)] * 2,
        in_specs=specs(pltpu.HBM, 2),
        out_specs=specs(pltpu.VMEM, 2),
        scratch_shapes=[
            pltpu.VMEM(send_rows.shape, jnp.int32),
            pltpu.VMEM(grid_latent.shape, BF16),
            pltpu.VMEM((slot_rows, width), F32),
            pltpu.SemaphoreType.DMA((5,)),
        ],
        compiler_params=params(16),
        name="pick",
    )(*pinned(pltpu.HBM, send_rows, grid_latent))

    def mix(values, count, minor):
        rows = len(values) * values[0].shape[0] // count
        return pl.pallas_call(
            functools.partial(mix_kernel, count, minor),
            out_shape=[jax.ShapeDtypeStruct((rows, width), BF16)] * count,
            compiler_params=params(16),
            name="mix",
        )(*values)

    hot, node, cot, moved = pl.pallas_call(
        functools.partial(ready_kernel, lines),
        out_shape=[
            pltpu.HBM((edges, mesh_rows), BF16),
            pltpu.HBM((mesh_rows, hidden_width), F32),
            pltpu.HBM((mesh_rows, hidden_width), F32),
            pltpu.VMEM((mesh_rows, hidden_width), BF16),
        ],
        in_specs=specs(pltpu.HBM, 6),
        out_specs=specs(pltpu.HBM, 3) + specs(pltpu.VMEM, 1),
        scratch_shapes=[
            pltpu.VMEM(dst_index.shape, jnp.int32),
            pltpu.VMEM(mesh_latent.shape, BF16),
            pltpu.VMEM(mesh_cot.shape, BF16),
            pltpu.VMEM((width, hidden_width), BF16),
            pltpu.VMEM((width, hidden_width), BF16),
            pltpu.VMEM(w_node2.shape, BF16),
            pltpu.VMEM((edges, mesh_rows), BF16),
            pltpu.VMEM((mesh_rows, hidden_width), F32),
            pltpu.VMEM((mesh_rows, hidden_width), F32),
            pltpu.SemaphoreType.DMA((6,)),
            pltpu.SemaphoreType.DMA((3,)),
        ],
        compiler_params=params(16),
        cost_estimate=cost(2 * 10**9, 4 * MIB),
        name="ready",
    )(*pinned(pltpu.HBM, dst_index, mesh_latent, mesh_cot, w_edge1, w_node1, w_node2))
    base, *ahead, turned = pl.pallas_call(
        functools.partial(base_kernel, lines),
        out_shape=[
            pltpu.VMEM((edges, hidden_width), F32),
            pltpu.VMEM(slot_index.shape, jnp.int32),
            pltpu.VMEM(dst_index.shape, jnp.int32),
            pltpu.VMEM((width, hidden_width), BF16),
            pltpu.HBM((width, edges), BF16),
        ],
        in_specs=specs(pltpu.HBM, 5) + specs(pltpu.VMEM, 1),
        out_specs=specs(pltpu.VMEM, 4) + specs(pltpu.HBM, 1),
        scratch_shapes=[
            pltpu.VMEM((edges, mesh_rows), BF16),
            pltpu.VMEM(edge_latent.shape, BF16),
            pltpu.VMEM((width, hidden_width), BF16),
            pltpu.VMEM((width, edges), BF16),
            pltpu.SemaphoreType.DMA((5 + edges // (128 * lines),)),
            pltpu.SemaphoreType.DMA((edges // (128 * lines),)),
        ],
        compiler_params=params(16),
        cost_estimate=cost(4 * 10**9, 4 * MIB),
        name="base",
    )(*pinned(pltpu.HBM, hot, edge_latent, w_edge1, slot_index, dst_index), *pinned(pltpu.VMEM, moved))

    by_inner = mix([kept, to_core(sent)], inner, outer)
    by_inner = [by_inner[0]] + [to_inner(by_inner[k], k) for k in range(1, inner)]
    by_outer = mix(by_inner, outer, 1)
    slot_blocks = [by_outer[0]] + [to_outer(by_outer[k], k) for k in range(1, outer)]

    grad_rows = 3 * width + hidden_width
    chunk = grad_rows // band_count
    group = (inner * chunk, hidden_width)
    node_out, d_slots, *sides = pl.pallas_call(
        functools.partial(main_kernel, lines, sizes),
        out_shape=[
            jax.ShapeDtypeStruct((mesh_rows, width), BF16),
            jax.ShapeDtypeStruct((halfway, width), BF16),
        ]
        + [jax.ShapeDtypeStruct((group[0] + inner * cap, hidden_width), BF16)] * outer
        + [jax.ShapeDtypeStruct(group, F32)] * outer,
        in_specs=specs(pltpu.HBM, 7) + specs(pltpu.VMEM, 4 + outer),
        out_specs=specs(pltpu.VMEM, 2 + 2 * outer),
        scratch_shapes=[
            pltpu.VMEM((edges, hidden_width), F32),
            pltpu.VMEM((edges, hidden_width), BF16),
            pltpu.VMEM((slot_rows + mesh_rows + width, edges), BF16),
            pltpu.VMEM((grad_rows, hidden_width), F32),
            pltpu.VMEM((slot_rows, width), F32),
            pltpu.VMEM((slot_rows, width), F32),
            pltpu.VMEM(mesh_latent.shape, BF16),
            pltpu.VMEM(w_edge2.shape, BF16),
            pltpu.VMEM((w_node1.shape[0] - width, w_node1.shape[1]), BF16),
            pltpu.VMEM(hot.shape, BF16),
            pltpu.VMEM(node.shape, F32),
            pltpu.VMEM(cot.shape, F32),
            pltpu.VMEM((edges, slot_rows), BF16),
            pltpu.SemaphoreType.DMA((7,)),
        ],
        compiler_params=params(40),
        name="edges",
    )(
        *pinned(pltpu.HBM, mesh_latent, w_edge2, w_node1, turned, hot, node, cot),
        *pinned(pltpu.VMEM, base, *ahead),
        *slot_blocks,
    )
    mesh_out = pl.pallas_call(
        mesh_kernel,
        out_shape=jax.ShapeDtypeStruct((mesh_rows, width), BF16),
        in_specs=specs(pltpu.HBM, 2) + specs(pltpu.VMEM, 1),
        out_specs=pl.BlockSpec(memory_space=pltpu.VMEM),
        scratch_shapes=[
            pltpu.VMEM(mesh_latent.shape, BF16),
            pltpu.VMEM(w_node2.shape, BF16),
            pltpu.SemaphoreType.DMA((2,)),
        ],
        compiler_params=params(16),
        cost_estimate=cost(10**9, MIB),
        name="mesh",
    )(*pinned(pltpu.HBM, mesh_latent, w_node2), node_out)
    sends, keeps = sides[:outer], sides[outer:]
    small = (2 * cap, width)
    arrived = {}
    first = None
    for k in [outer - 1, *range(1, outer - 1), 0]:
        send = sends[k] if first is None else lax.optimization_barrier((sends[k], first))[0]
        crossed = to_core(send)
        total, mixed, *parts = pl.pallas_call(
            functools.partial(core_kernel, sizes, k),
            out_shape=[
                jax.ShapeDtypeStruct((chunk, hidden_width), F32),
                jax.ShapeDtypeStruct(small, BF16),
            ]
            + [jax.ShapeDtypeStruct((chunk + 2 * cap, width), BF16)] * (inner - 1),
            compiler_params=params(16),
            cost_estimate=cost(10**9, MIB),
            name="core",
        )(keeps[k], crossed, d_slots)
        first = parts[0] if first is None else first
        parts = [to_inner(part, at + 1) for at, part in enumerate(parts)]
        block = 2 * inner * cap
        if k:
            (out,) = pl.pallas_call(
                functools.partial(inner_kernel, inner - 1, 0),
                out_shape=[jax.ShapeDtypeStruct((chunk + block, width), BF16)],
                compiler_params=params(16),
                name="inner",
            )(total, mixed, *parts)
            arrived[k] = to_outer(out, k)
        else:
            total = lax.optimization_barrier((total, mesh_out))[0]
            own, home = pl.pallas_call(
                functools.partial(inner_kernel, inner - 1, outer - 1),
                out_shape=[
                    jax.ShapeDtypeStruct((chunk, hidden_width), BF16),
                    jax.ShapeDtypeStruct((block, width), BF16),
                ],
                compiler_params=params(16),
                name="own",
            )(total, mixed, *parts, *[arrived[at] for at in range(1, outer)])

    grid_grad = pl.pallas_call(
        functools.partial(put_kernel, sizes),
        out_shape=jax.ShapeDtypeStruct(grid_latent.shape, F32),
        in_specs=specs(pltpu.HBM, 1) + specs(pltpu.VMEM, outer),
        out_specs=pl.BlockSpec(memory_space=pltpu.VMEM),
        scratch_shapes=[
            pltpu.VMEM((slot_rows, width), F32),
            pltpu.VMEM(send_rows.shape, jnp.int32),
            pltpu.SemaphoreType.DMA((1,)),
        ],
        compiler_params=params(16),
        cost_estimate=cost(2 * 10**9, 2 * MIB),
        name="put",
    )(*pinned(pltpu.HBM, send_rows), home, *[arrived[at] for at in range(1, outer)])

    pieces = {0: own}
    stride = outer // 2
    while stride:
        for at in range(0, outer, 2 * stride):
            value = pieces[at]
            if at == outer // 2 and stride == outer // 4:
                value = lax.optimization_barrier((value, grid_grad))[0]
            pieces[at + stride] = to_outer(value, stride)
        stride //= 2
    halfway_at = band_count // 2
    pieces[halfway_at] = to_core(own)
    for far_inner in range(1, inner):
        for far_outer in range(outer):
            value = pieces[far_outer]
            if far_outer == outer // 2:
                value = lax.optimization_barrier((value, pieces[halfway_at]))[0]
            pieces[far_inner * outer + far_outer] = to_inner(value, far_inner)
    for at in range(1, halfway_at - 1):
        pieces[halfway_at + at] = to_core(pieces[at])

    last = outer - 1
    stages = [[], [], []]
    for at in range(band_count):
        far_outer, far_inner, far_core = at % outer, at // outer % inner, at // halfway_at
        if far_outer == last:
            stages[2 if far_inner else 1].append(at)
        else:
            stages[1 if far_inner and (far_core or far_outer == outer // 2) else 0].append(at)
    grads = []
    for places in stages:
        if places is stages[1]:
            value = lax.optimization_barrier((pieces[halfway_at - 1], *grads))[0]
            pieces[band_count - 1] = to_core(value)
        grads = pl.pallas_call(
            functools.partial(order_kernel, sizes, places, len(grads)),
            out_shape=[
                jax.ShapeDtypeStruct((3 * width, hidden_width), F32),
                jax.ShapeDtypeStruct((hidden_width, width), F32),
            ],
            in_specs=specs(pltpu.VMEM, len(places)) + specs(pltpu.HBM, len(grads)),
            out_specs=specs(pltpu.HBM, 2),
            scratch_shapes=[
                pltpu.VMEM((len(places), chunk, hidden_width), F32),
                pltpu.SemaphoreType.DMA((len(places),)),
            ],
            input_output_aliases={len(places) + k: k for k in range(len(grads))},
            compiler_params=params(16),
            cost_estimate=cost(15 * 10**7 * len(places), 2 * MIB),
            name="order",
        )(*[pieces[at] for at in places], *grads)
    grad_edge1, grad_edge2 = grads
    return (mesh_out, grid_grad, grad_edge1, grad_edge2)


def solution(mesh):
    chips = mesh.shape["band"] // 2
    inner = 1
    while inner * inner * 4 <= chips:
        inner *= 2
    sizes = (chips // inner, inner)
    in_specs = (
        P(("groups", "band"), None),
        P(("groups", "band"), None),
        P(("groups", "band"), None),
        P(("groups", "band"), None),
        P("band", None),
        P("band"),
        P("band"),
        P(),
        P(),
        P(),
        P(),
    )
    out_specs = (
        P(("groups", "band"), None),
        P(("groups", "band"), None),
        P("groups", None),
        P("groups", None),
    )
    return jax.shard_map(
        functools.partial(shards, sizes), mesh=mesh, in_specs=in_specs, out_specs=out_specs, check_vma=False
    )
```
